32 devices in a mesh: group: 2 (over core), cuts: 4 (over y, x), sub: 4 (over z).
Axes of the slice: x: 2, y: 2, z: 4, core: 2. Of those that a mesh axis runs over, the one named last changes fastest.
Arguments:
- disp_now: float32 [2, 3, 128, 1089], P('group', None, ('cuts', 'sub')), may hold values from -6 to 6
- disp_prev: float32 [2, 3, 128, 1089], P('group', None, ('cuts', 'sub')), may hold values from -6 to 6
- memory_init: float32 [2, 3, 5, 125, 2048], P('group', None, None, None, ('cuts', 'sub')), may hold values from -6 to 6
- density: float32 [128, 1089], P(('cuts', 'sub')), may hold values from 0.8 to 1.6
- lame_lambda: float32 [125, 2048], P(None, ('cuts', 'sub')), may hold values from 0.4 to 1.6
- shear_mu: float32 [125, 2048], P(None, ('cuts', 'sub')), may hold values from 0.4 to 1.2
- sls_decay: float32 [3, 2048], P(None, ('cuts', 'sub')), may hold values from 0.3 to 0.98
- owner_map: int32 [32, 64, 1], P(('cuts', 'sub')), may hold values from 0 to 3; in each aligned block of 64 rows (0 to 63, 64 to 127, ..., all dimensions but the last counted through in order) at most 32 rows name the same one
Outputs:
- disp_final: float32 [2, 3, 128, 1089], P('group', None, ('cuts', 'sub'))
- kernels: float32 [2, 4096, 250], P('group', ('cuts', 'sub'))
The draws below stay inside these ranges and needn't reach their ends.
Inputs may be any that keep to these rules, and one draw needn't show every extreme that they name: `owner_map`: among the 64 elements of one slab, no sub-slice owns more than 32; in some slab one owns exactly 32.
All inputs are finite; a program needn't handle non-finite values.
Results may differ from the reference program's by a relative error of at most 0.0004.
The reference program's roundings to bfloat16 on the way (of `kernel_part`) count: a program that leaves them out, or rounds other values in their place, can miss the bound.
Values may be sent and summed in bfloat16 or wider, within the bound.
No kernel may reach another device: no remote copies, remote signals or barrier semaphores. Data moves between devices by JAX's collectives and lax.ppermute only.
A program may use at most 64 MiB of HBM per device.

```python
import math
import jax
import jax.numpy as jnp
import numpy as np
from jax import lax

EX = 2
EY = 8
EZ = 8
NODES = 125
N_SLS = 3
STEPS = 3
EYZ = 64
YZ = 1089
ELX = 32
ELEMS = 2048
NXG = 128
MOST = 32
KROWS = 4096
FIELDS = 2
N_GROUP = 2
N_CUTS = 4
N_SUB = 4


def block_levels(rng, dims, split, smallest, top_value):
    loudness = 1.0
    for axis_at, blocks in split:
        draws = jax.random.uniform(jax.random.fold_in(jax.random.fold_in(rng, 6), axis_at), (blocks,), jnp.float32, smallest / len(split), top_value / len(split))
        loudness = loudness * jnp.repeat(jnp.exp(draws), dims[axis_at] // blocks).reshape((-1,) + (1,) * (len(dims) - 1 - axis_at))
    return loudness


def shared_out(stream_key, own, number, rows, amount, top, reach, slope):
    ranking = jax.random.permutation(stream_key, amount)
    crowded, ordinary = shares(amount, rows * top, reach, slope, True), shares(amount, rows * top, reach, slope, False)
    places = jnp.arange(amount)

    def named(sizes, offset_by):
        used = int((sizes > 0).sum())
        fixed = max(1, used // 4)
        moved = fixed + (places - fixed + offset_by * (used - fixed)) % max(1, amount - fixed)
        return jnp.zeros((amount,), jnp.int32).at[ranking[jnp.where(places < fixed, places, moved)]].set(jnp.asarray(sizes, jnp.int32))

    sizes = jnp.where(number % 4 == 0, named(crowded, number // 4), named(ordinary, number - number // 4 - 1))
    mixed = jax.random.permutation(jax.random.fold_in(own, 3), amount)
    donor, sink = mixed[0:amount // 2 * 2:2], mixed[1:amount // 2 * 2:2]
    slack = jnp.minimum(sizes[donor] - 1, reach - sizes[sink]) // 2
    slack = jnp.where((donor == ranking[0]) | (sink == ranking[0]) | (sizes[sink] == 0), 0, jnp.maximum(slack, 0))
    moved = jax.random.randint(jax.random.fold_in(own, 4), (amount // 2,), 0, 1 << 20) % (slack + 1)
    sizes = sizes.at[donor].add(-moved).at[sink].add(moved)
    items = jnp.searchsorted(jnp.cumsum(sizes), jnp.arange(rows * top), side="right").astype(jnp.int32)
    listing = items.reshape(top, rows).T
    listing = listing[jax.random.permutation(jax.random.fold_in(own, 1), rows)]
    offset_by = jax.random.randint(jax.random.fold_in(own, 2), (rows, 1), 0, top)
    return jnp.take_along_axis(listing, (jnp.arange(top)[None, :] + offset_by) % top, axis=1)


def shares(count, total, reach, slope, full):
    loads = [(1 << 20) // math.isqrt(rank ** slope) + 1 for rank in range(1, count + 1)]
    largest = reach if full else min(reach, max(-(-total // count), total * loads[0] // sum(loads)))
    least = 1 if total - largest >= count - 1 else 0
    counts, spare = [largest] + [least] * (count - 1), total - largest - least * (count - 1)
    while spare > 0:
        free = [i for i in range(1, count) if counts[i] < largest] or [i for i in range(1, count) if counts[i] < reach]
        pool, budget = sum([loads[i] for i in free]), spare
        for i in free:
            more = min(reach - counts[i], max(1, budget * loads[i] // pool), spare)
            counts[i] = counts[i] + more
            spare = spare - more
    return np.array(counts)


def bell_draw(stream_key, dims, spread, reach, shards=(), kind=jnp.bfloat16):
    entries = jax.random.normal(stream_key, dims, jnp.float32) * spread
    if len(shards) > 0:
        entries = block_levels(stream_key, dims, shards, -0.22, 0.18) * entries
    return jnp.clip(entries, min=-reach, max=reach).astype(kind)


def setup_inputs(seed: int = 0) -> dict:
    seeds = jax.random.split(jax.random.key(seed), 9)
    disp_now = bell_draw(seeds[0], (FIELDS, 3, NXG, YZ), 1.0, 6.0, ((0, 2), (2, 16)), jnp.float32)
    disp_prev = bell_draw(seeds[1], (FIELDS, 3, NXG, YZ), 1.0, 6.0, ((0, 2), (2, 16)), jnp.float32)
    memory_init = bell_draw(seeds[2], (FIELDS, N_SLS, 5, NODES, ELEMS), 1.0, 6.0, ((0, 2), (4, 16)), jnp.float32)
    density = jnp.clip(jnp.exp(math.log(1.6) - 0.6931472 * jax.random.uniform(seeds[3], (NXG, YZ), jnp.float32) ** block_levels(seeds[3], (NXG, YZ), ((0, 16),), -0.2, 0.2)), 0.8, 1.6)
    lame_lambda = jnp.clip(jnp.exp(math.log(1.6) - 1.3862944 * jax.random.uniform(seeds[4], (NODES, ELEMS), jnp.float32) ** block_levels(seeds[4], (NODES, ELEMS), ((1, 16),), -0.2, 0.2)), 0.4, 1.6)
    shear_mu = jnp.clip(jnp.exp(math.log(1.2) - 1.0986123 * jax.random.uniform(seeds[5], (NODES, ELEMS), jnp.float32) ** block_levels(seeds[5], (NODES, ELEMS), ((1, 16),), -0.2, 0.2)), 0.4, 1.2)
    sls_decay = jnp.clip(jnp.exp(math.log(0.98) - 1.1837701 * jax.random.uniform(seeds[6], (N_SLS, ELEMS), jnp.float32) ** block_levels(seeds[6], (N_SLS, ELEMS), ((1, 16),), -0.2, 0.2)), 0.3, 0.98)
    owner_map_keys = jax.random.split(jax.random.fold_in(seeds[7], 1), ELX * EYZ // EYZ)
    owner_map_turns = jax.random.permutation(jax.random.fold_in(seeds[7], 3), ELX * EYZ // EYZ)
    owner_map = jax.vmap(lambda own, number: shared_out(jax.random.fold_in(seeds[7], 2), own, number, EYZ, N_SUB, 1, MOST, 2))(owner_map_keys, owner_map_turns).reshape((ELX, EYZ, 1))
    return dict(disp_now=disp_now, disp_prev=disp_prev, memory_init=memory_init, density=density, lame_lambda=lame_lambda, shear_mu=shear_mu, sls_decay=sls_decay, owner_map=owner_map)


time_step = 0.03
step_square = 0.0009
relax_strength = (0.12, 0.08, 0.05)

def gll_tables():
    root_value = math.sqrt(3.0 / 7.0)
    points = [-1.0, -root_value, 0.0, root_value, 1.0]
    weights = [0.1, 49.0 / 90.0, 32.0 / 45.0, 49.0 / 90.0, 0.1]
    derivative = np.zeros((5, 5))
    for p in range(5):
        for a in range(5):
            accum = 0.0
            for m in range(5):
                if m != a:
                    factor = 1.0 / (points[a] - points[m])
                    for k in range(5):
                        if k != a and k != m:
                            factor = factor * (points[p] - points[k]) / (points[a] - points[k])
                    accum = accum + factor
            derivative[p, a] = accum
    return (jnp.asarray(derivative, jnp.float32), jnp.asarray(np.array(weights), jnp.float32))

def split_line(values, elem_count):
    leading = values[..., :4 * elem_count].reshape(values.shape[:-1] + (elem_count, 4))
    trailing = values[..., 4::4]
    return jnp.concatenate([leading, trailing[..., None]], axis=-1)

def join_line(values):
    elem_count = values.shape[-2]
    leading = values[..., :4].reshape(values.shape[:-2] + (4 * elem_count,))
    padding = jnp.zeros(values.shape[:-1] + (3,), values.dtype)
    trailing = jnp.concatenate([padding, values[..., 4:]], axis=-1).reshape(values.shape[:-2] + (4 * elem_count,))
    border = jnp.zeros(values.shape[:-2] + (1,), values.dtype)
    return jnp.concatenate([leading, border], axis=-1) + jnp.concatenate([border, trailing], axis=-1)

def to_elements(extended, count_y, count_z):
    components, layers = (extended.shape[0], extended.shape[1])
    node_grid = extended.reshape(components, layers, 5, 4 * count_y + 1, 4 * count_z + 1)
    along_z = split_line(node_grid, count_z)
    reordered = jnp.transpose(along_z, (0, 1, 2, 4, 5, 3))
    along_y = split_line(reordered, count_y)
    ordered = jnp.transpose(along_y, (0, 2, 6, 4, 1, 5, 3))
    return ordered.reshape(components, 5, 5, 5, layers * count_y * count_z)

def to_nodes(elem_force, layers, count_y, count_z):
    components = elem_force.shape[0]
    shaped = elem_force.reshape(components, 5, 5, 5, layers, count_y, count_z)
    ordered = jnp.transpose(shaped, (0, 4, 1, 6, 3, 5, 2))
    along_y = join_line(ordered)
    reordered = jnp.transpose(along_y, (0, 1, 2, 5, 3, 4))
    along_z = join_line(reordered)
    return along_z.reshape(components, layers, 5, -1)

def strain_parts(elem_disp, derivative):
    highest = lax.Precision.HIGHEST
    grad_x = jnp.einsum('pa,cabde->cpbde', derivative, elem_disp, precision=highest)
    grad_y = jnp.einsum('qb,cabde->caqde', derivative, elem_disp, precision=highest)
    grad_z = jnp.einsum('rd,cabde->cabre', derivative, elem_disp, precision=highest)
    parts = jnp.stack([grad_x[0], grad_y[1], grad_z[2], 0.5 * (grad_y[0] + grad_x[1]), 0.5 * (grad_z[0] + grad_x[2]), 0.5 * (grad_z[1] + grad_y[2])])
    return parts.reshape(6, 125, -1)

def node_weights(count_y, count_z):
    derivative, weights = gll_tables()
    line_y = join_line(jnp.broadcast_to(weights, (count_y, 5)))
    line_z = join_line(jnp.broadcast_to(weights, (count_z, 5)))
    face_weight = (line_y[:, None] * line_z[None, :]).reshape(-1)
    layer_weight = jnp.stack([weights[0] + weights[4], weights[1], weights[2], weights[3]])
    return layer_weight[:, None] * face_weight[None, :]

def element_pass(extended, forward, memory, lame_lambda, shear_mu, sls_decay, count_y, count_z):
    highest = lax.Precision.HIGHEST
    derivative, weights = gll_tables()
    layers = extended.shape[1]
    own_strain = strain_parts(to_elements(extended, count_y, count_z), derivative)
    far_strain = strain_parts(to_elements(forward, count_y, count_z), derivative)
    trace_own = own_strain[0] + own_strain[1] + own_strain[2]
    trace_far = far_strain[0] + far_strain[1] + far_strain[2]
    deviator = jnp.stack([own_strain[0] - trace_own / 3.0, own_strain[1] - trace_own / 3.0, own_strain[3], own_strain[4], own_strain[5]])
    twice_mu = 2.0 * shear_mu
    strengths = jnp.asarray(relax_strength, jnp.float32)[:, None, None, None]
    decay_full = sls_decay[:, None, None, :]
    memory_new = decay_full * memory + (1.0 - decay_full) * strengths * (twice_mu * deviator)[None]
    relax_sum = lax.optimization_barrier(jnp.sum(memory_new, axis=0))
    bulk_part = lame_lambda * trace_own
    sigma_xx = bulk_part + twice_mu * own_strain[0] - relax_sum[0]
    sigma_yy = bulk_part + twice_mu * own_strain[1] - relax_sum[1]
    sigma_zz = bulk_part + twice_mu * own_strain[2] + relax_sum[0] + relax_sum[1]
    sigma_xy = twice_mu * own_strain[3] - relax_sum[2]
    sigma_xz = twice_mu * own_strain[4] - relax_sum[3]
    sigma_yz = twice_mu * own_strain[5] - relax_sum[4]
    weight_cube = (weights[:, None, None] * weights[None, :, None] * weights[None, None, :]).reshape(5, 5, 5, 1)
    stack_x = jnp.stack([sigma_xx, sigma_xy, sigma_xz]).reshape(3, 5, 5, 5, -1) * weight_cube
    stack_y = jnp.stack([sigma_xy, sigma_yy, sigma_yz]).reshape(3, 5, 5, 5, -1) * weight_cube
    stack_z = jnp.stack([sigma_xz, sigma_yz, sigma_zz]).reshape(3, 5, 5, 5, -1) * weight_cube
    elem_force = -(jnp.einsum('pa,cpbde->cabde', derivative, stack_x, precision=highest) + jnp.einsum('qb,caqde->cabde', derivative, stack_y, precision=highest) + jnp.einsum('rd,cabre->cabde', derivative, stack_z, precision=highest))
    kappa = lame_lambda + twice_mu / 3.0
    bulk_kernel = time_step * kappa * trace_far * trace_own
    shear_product = (own_strain[0] - trace_own / 3.0) * (far_strain[0] - trace_far / 3.0) + (own_strain[1] - trace_own / 3.0) * (far_strain[1] - trace_far / 3.0) + (own_strain[2] - trace_own / 3.0) * (far_strain[2] - trace_far / 3.0) + 2.0 * (own_strain[3] * far_strain[3] + own_strain[4] * far_strain[4] + own_strain[5] * far_strain[5])
    shear_kernel = time_step * twice_mu * shear_product
    kernel_part = jnp.stack([bulk_kernel, shear_kernel]).astype(jnp.bfloat16)
    node_force = to_nodes(elem_force.reshape(3, 125, -1), layers, count_y, count_z)
    return (node_force, memory_new, kernel_part)

def reference(disp_now, disp_prev, memory_init, density, lame_lambda, shear_mu, sls_decay, owner_map):
    slab_total = N_CUTS * N_SUB * EX
    block_size = math.gcd(slab_total, 16)
    block_count = slab_total // block_size
    elem_slab = EY * EZ
    lambda_blocks = lame_lambda.reshape(125, block_count, -1).transpose(1, 0, 2)
    mu_blocks = shear_mu.reshape(125, block_count, -1).transpose(1, 0, 2)
    decay_blocks = sls_decay.reshape(N_SLS, block_count, -1).transpose(1, 0, 2)
    node_mass = density.reshape(slab_total, 4, -1) * node_weights(EY, EZ)[None]

    def one_block(items):
        return element_pass(items[0], items[1], items[2], items[3], items[4], items[5], EY, EZ)

    def run_field(field_index, forward_list):
        current = disp_now[field_index].reshape(3, slab_total, 4, -1)
        previous = disp_prev[field_index].reshape(3, slab_total, 4, -1)
        memory = memory_init[field_index].reshape(N_SLS, 5, 125, block_count, -1).transpose(3, 0, 1, 2, 4)
        kernel_sum = jnp.zeros((block_count, 2, 125, block_size * elem_slab), jnp.float32)
        collected = []
        for step_index in range(STEPS):
            extended = jnp.concatenate([current, jnp.roll(current[:, :, 0:1], -1, axis=1)], axis=2)
            if forward_list is None:
                forward_low = lax.optimization_barrier(extended.astype(jnp.bfloat16))
                collected.append(forward_low)
            else:
                forward_low = forward_list[step_index]
            forward = forward_low.astype(jnp.float32)
            ext_blocks = extended.reshape(3, block_count, block_size, 5, -1).transpose(1, 0, 2, 3, 4)
            far_blocks = forward.reshape(3, block_count, block_size, 5, -1).transpose(1, 0, 2, 3, 4)
            force_blocks, memory, kernel_part = lax.map(one_block, (ext_blocks, far_blocks, memory, lambda_blocks, mu_blocks, decay_blocks))
            force_ext = force_blocks.transpose(1, 0, 2, 3, 4).reshape(3, slab_total, 5, -1)
            passed = jnp.roll(force_ext[:, :, 4:5], 1, axis=1)
            zeros_rest = jnp.zeros((3, slab_total, 3, force_ext.shape[-1]), jnp.float32)
            node_force = force_ext[:, :, 0:4] + jnp.concatenate([passed, zeros_rest], axis=2)
            updated = 2.0 * current - previous + step_square * node_force / node_mass
            previous = current
            current = updated
            kernel_sum = kernel_sum + kernel_part.astype(jnp.float32)
        return (current, kernel_sum, collected)
    owners = owner_map[:, :, 0]
    onehot = (owners[:, :, None] == jnp.arange(N_SUB, dtype=jnp.int32)[None, None, :]).astype(jnp.int32)
    rank = lax.optimization_barrier(jnp.sum((jnp.cumsum(onehot, axis=1) - onehot) * onehot, axis=2))
    slab_index = jnp.arange(slab_total, dtype=jnp.int32)[:, None]
    device_slab = slab_index // EX
    local_slab = slab_index % EX
    rows = (device_slab // N_SUB * N_SUB + owners) * (N_SUB * EX * MOST) + device_slab % N_SUB * (EX * MOST) + local_slab * MOST + rank
    rows = rows.reshape(-1).astype(jnp.int32)
    finals = []
    placed_all = []
    forward_list = None
    for field_index in range(N_GROUP):
        final_disp, kernel_sum, collected = run_field(field_index, forward_list)
        if field_index == 0:
            forward_list = collected
        payload = kernel_sum.reshape(block_count, 2, 125, block_size, elem_slab).transpose(0, 3, 4, 1, 2)
        payload = payload.reshape(-1, 250)
        placed = jnp.zeros((KROWS, 250), jnp.float32).at[rows].set(payload)
        finals.append(final_disp.reshape(3, NXG, -1))
        placed_all.append(placed)
    return (jnp.stack(finals), jnp.stack(placed_all))
```

```python
import math

import jax
import jax.numpy as jnp
import numpy as np
from jax import lax
from jax.experimental import pallas as pl
from jax.experimental.pallas import tpu as pltpu
from jax.sharding import PartitionSpec as P

STEPS = 3
EY = 8
EZ = 8
LANES = 128
SIDE = 33
FACE = SIDE * SIDE
BLOCKS = 26
ROWS = 8 * BLOCKS
WIDE = 64 * BLOCKS
JUMP = 4 * SIDE
WINDOW = 256

time_step = 0.03
step_square = 0.0009
relax_strength = (0.12, 0.08, 0.05)

F32 = jnp.float32
BF16 = jnp.bfloat16


def gll_tables():
    root_value = math.sqrt(3.0 / 7.0)
    points = [-1.0, -root_value, 0.0, root_value, 1.0]
    weights = [0.1, 49.0 / 90.0, 32.0 / 45.0, 49.0 / 90.0, 0.1]
    derivative = np.zeros((5, 5))
    for p in range(5):
        for a in range(5):
            accum = 0.0
            for m in range(5):
                if m != a:
                    factor = 1.0 / (points[a] - points[m])
                    for k in range(5):
                        if k != a and k != m:
                            factor = factor * (points[p] - points[k]) / (points[a] - points[k])
                    accum = accum + factor
            derivative[p, a] = accum
    return derivative.astype(np.float32).astype(np.float64), np.array(weights).astype(np.float32).astype(np.float64)


def node(a, b, d):
    return a * 25 + b * 5 + d


def place(a, b, d):
    return (b * 5 + d) * 8 + a


def make_tables():
    derivative, weights = gll_tables()
    grad = np.zeros((3 * 128, ROWS))
    force = np.zeros((ROWS, 3 * 128))
    for a in range(5):
        for b in range(5):
            for d in range(5):
                for m in range(5):
                    grad[node(a, b, d), place(m, b, d)] = derivative[a, m]
                    grad[128 + node(a, b, d), place(a, m, d)] = derivative[b, m]
                    grad[256 + node(a, b, d), place(a, b, m)] = derivative[d, m]
                    row = place(a, b, d)
                    force[row, node(m, b, d)] = -derivative[m, a] * weights[m] * weights[b] * weights[d]
                    force[row, 128 + node(a, m, d)] = -derivative[m, b] * weights[a] * weights[m] * weights[d]
                    force[row, 256 + node(a, b, m)] = -derivative[m, d] * weights[a] * weights[b] * weights[m]
    face = np.zeros((64, 3 * 128))
    face[0:25] = force[0:200:8]
    face[32:57] = force[4:200:8]
    spread = np.zeros((WINDOW, WIDE), np.float32)
    collect = np.zeros((WIDE, WINDOW), np.float32)
    line = np.zeros(SIDE)
    for e in range(8):
        line[4 * e : 4 * e + 5] += weights
    layer = np.array([2 * weights[0], weights[1], weights[2], weights[3], 2 * weights[0], 1.0, 1.0, 1.0])
    mass = np.ones((ROWS, LANES), np.float32)
    for b in range(5):
        for d in range(5):
            for ey in range(8):
                for ez in range(8):
                    column = (b * 5 + d) * 64 + ey * 8 + ez
                    spot = b * SIDE + 4 * ez + d
                    spread[spot, column] = 1.0
                    if d < 4 or ez == 7:
                        collect[column, spot] = 1.0
                    for slab in range(2):
                        at = (b * 5 + d) * 8
                        mass[at : at + 8, slab * 64 + ey * 8 + ez] = layer * line[4 * ey + b] * line[4 * ez + d]
    return grad, force, face, spread, collect, mass


def cut_table(table):
    value = table.astype(np.float32)
    pieces = []
    for _ in range(3):
        piece = value.astype(jnp.bfloat16)
        pieces.append(piece)
        value = value - piece.astype(np.float32)
    return np.stack(pieces)


GRAD, FORCE, FACES, SPREAD, COLLECT, MASS = make_tables()


def cut(value):
    high = value.astype(BF16)
    rest = value - high.astype(F32)
    middle = rest.astype(BF16)
    low = (rest - middle.astype(F32)).astype(BF16)
    return high, middle, low


def dot(left, right):
    return jnp.dot(left, right, preferred_element_type=F32)


def dot_six(table, value):
    high, middle, low = cut(value)
    small = dot(table[2], high) + dot(table[1], middle) + dot(table[0], low)
    return dot(table[0], high) + (dot(table[0], middle) + dot(table[1], high) + small)


def lanes_of(shape):
    return lax.broadcasted_iota(jnp.int32, shape, len(shape) - 1)


def rolled(value, shift, axis):
    return pltpu.roll(value, shift % value.shape[axis], axis)


def window_rows(value, window_ref):
    for ey in range(EY):
        width = min(WINDOW, FACE - JUMP * ey)
        if width < WINDOW:
            window_ref[ey] = jnp.zeros(window_ref.shape[1:], F32)
        window_ref[ey, :, 0:width] = value[:, JUMP * ey : JUMP * ey + width]
    return window_ref[...].reshape(-1, WINDOW)


def to_columns(value, window_ref, spread_ref):
    rows = value.shape[0]
    high, middle, low = cut(window_rows(value, window_ref))
    spread = spread_ref[...]
    wide = dot(high, spread) + dot(middle, spread) + dot(low, spread)
    own = (lanes_of((rows, WIDE)) // 8) % 8
    picked = wide[0:rows]
    for ey in range(1, EY):
        picked = jnp.where(own == ey, wide[ey * rows : (ey + 1) * rows], picked)
    return picked


def assembled(blocks):
    lane = lanes_of((8, LANES))
    blocks = dict(blocks)
    for shift, at, pairs in (
        (1, lane % 8, [((b, 0), (b, 4)) for b in range(5)]),
        (8, (lane // 8) % 8, [((0, d), (4, d)) for d in range(5)]),
    ):
        for c in range(3):
            for near, far in pairs:
                first, last = blocks[(c,) + near], blocks[(c,) + far]
                blocks[(c,) + near] = first + jnp.where(at > 0, rolled(last, shift, 1), 0.0)
                blocks[(c,) + far] = last + jnp.where(at < 7, rolled(first, -shift, 1), 0.0)
    return blocks


def block_rows(b, d):
    return slice((b * 5 + d) * 8, (b * 5 + d) * 8 + 8)


def beside(value):
    return jnp.concatenate([value[0], value[1], value[2]], axis=1)


def prologue_kernel(
    index_ref, now_ref, prev_ref, density_ref, memory_ref, decay_ref, owner_col_ref, owner_row_ref, spread_ref, mass_ref,
    u_ref, p_ref, scale_ref, m1_ref, m2_ref, m3_ref, select_ref, window_ref,
):
    rows = jnp.concatenate([now_ref[0].reshape(24, FACE), prev_ref[0].reshape(24, FACE), density_ref[...]], axis=0)
    columns = to_columns(rows, window_ref, spread_ref)
    lane = lanes_of((8, LANES))
    for group in range(7):
        for pair in range(BLOCKS // 2):
            tile = columns[8 * group : 8 * group + 8, LANES * pair : LANES * pair + LANES]
            swapped = rolled(tile, 64, 1)
            even = jnp.where(lane < 64, tile, rolled(swapped, 4, 0))
            odd = jnp.where(lane < 64, swapped, rolled(tile, 4, 0))
            for block, value in ((2 * pair, even), (2 * pair + 1, odd)):
                at = slice(8 * block, 8 * block + 8)
                if group < 3:
                    u_ref[group, at, :] = value
                elif group < 6:
                    p_ref[group - 3, at, :] = value
                elif block < 25:
                    scale_ref[at, :] = step_square / (value * mass_ref[at, :])
                else:
                    scale_ref[at, :] = jnp.zeros((8, LANES), F32)
    decays = [decay_ref[l : l + 1, :] for l in range(3)]
    for part in range(5):
        terms = [decays[l] * memory_ref[0, l, part] for l in range(3)]
        m1_ref[part] = terms[0] + terms[1] + terms[2]
        terms = [decays[l] * terms[l] for l in range(3)]
        m2_ref[part] = terms[0] + terms[1] + terms[2]
        terms = [decays[l] * terms[l] for l in range(3)]
        m3_ref[part] = terms[0] + terms[1] + terms[2]
    owner_row = owner_row_ref[...]
    earlier = lax.broadcasted_iota(jnp.int32, (LANES, LANES), 0)
    later = lax.broadcasted_iota(jnp.int32, (LANES, LANES), 1)
    ahead = (owner_col_ref[...] == owner_row) & (earlier < later) & ((earlier // 64) == (later // 64))
    rank = jnp.sum(jnp.where(ahead, 1.0, 0.0), axis=0, keepdims=True).astype(jnp.int32)
    total = select_ref.shape[0]
    subs = index_ref[2]
    slots = total // subs
    slot = lax.broadcasted_iota(jnp.int32, (total, LANES), 0)
    toward = (slot // slots) ^ index_ref[0]
    wanted = (lanes_of((1, LANES)) // 64) * (slots // 2) + rank
    chosen = (owner_row == toward) & (wanted == slot % slots)
    select_ref[...] = jnp.where(chosen, 1.0, 0.0).astype(BF16)


def rim_kernel(rim_ref, u_in, p_in, scale_in, spread_ref, mass_ref, u_ref, p_ref, scale_ref, low_ref, window_ref, rows_ref):
    columns = to_columns(rim_ref[...], window_ref, spread_ref)
    for pair in range(BLOCKS // 2):
        tile = columns[:, LANES * pair : LANES * pair + LANES]
        rows_ref[16 * pair : 16 * pair + 8, :] = rolled(tile, 64, 1)
        rows_ref[16 * pair + 8 : 16 * pair + 16, :] = tile
    u_ref[...] = u_in[...]
    p_ref[...] = p_in[...]
    scale_ref[...] = scale_in[...]
    upper = lanes_of((25, LANES)) >= 64
    last = pl.ds(4, 25, stride=8)
    for c in range(3):
        u_ref[c, last, :] = jnp.where(upper, rows_ref[pl.ds(c, 25, stride=8), :], u_ref[c, last, :])
        p_ref[c, last, :] = jnp.where(upper, rows_ref[pl.ds(3 + c, 25, stride=8), :], p_ref[c, last, :])
    rim = step_square / (rows_ref[pl.ds(6, 25, stride=8), :] * mass_ref[last, :])
    scale_ref[last, :] = jnp.where(upper, rim, scale_ref[last, :])
    low_ref[...] = u_ref[...].astype(BF16)


def strains(grad, rows):
    def at(direction, c):
        return grad[direction * 128 + rows.start : direction * 128 + rows.stop, c * LANES : (c + 1) * LANES]

    return [
        at(0, 0),
        at(1, 1),
        at(2, 2),
        0.5 * (at(1, 0) + at(0, 1)),
        0.5 * (at(2, 0) + at(0, 2)),
        0.5 * (at(2, 1) + at(1, 2)),
    ]


CHUNKS = [slice(0, 32), slice(32, 64), slice(64, 96), slice(96, 125)]


def pack_face(face, upper):
    parts = [face[:, c * LANES : (c + 1) * LANES] for c in range(3)]
    lower_lane = lanes_of((16, LANES)) < 64
    lower_lanes = lanes_of((32, LANES)) < 64
    if upper:
        first = jnp.where(lower_lanes, rolled(parts[0], 64, 1), parts[1])
        second = jnp.where(lower_lane, rolled(parts[2][0:16], 64, 1), parts[2][16:32])
    else:
        first = jnp.where(lower_lanes, parts[0], rolled(parts[1], 64, 1))
        second = jnp.where(lower_lane, parts[2][0:16], rolled(parts[2][16:32], 64, 1))
    return jnp.concatenate([first, second], axis=0)


def step_kernel(step, *refs):
    u_ref, lame_ref, mu_ref, m_ref, decay_ref, grad_table, face_table = refs[0:7]
    older = refs[7 : 7 + step]
    refs = refs[7 + step :]
    strain_ref, sigma_ref, first_ref, last_ref = refs[0:4]
    keep_ref = refs[4] if step < STEPS - 1 else None
    grad_ref = refs[-1]
    grad_ref[...] = dot_six(grad_table, beside(u_ref))
    for block in range(9):
        sigma_ref[(block // 3) * 128 + 120 : (block // 3) * 128 + 128, (block % 3) * LANES : (block % 3) * LANES + LANES] = (
            jnp.zeros((8, LANES), F32)
        )
    decays = [decay_ref[l : l + 1, :] for l in range(3)]
    shares = [(1.0 - decays[l]) * relax_strength[l] for l in range(3)]
    factors = []
    for _ in range(step + 1):
        factors.append(shares[0] + shares[1] + shares[2])
        shares = [decays[l] * shares[l] for l in range(3)]
    for rows in CHUNKS:
        strain = strains(grad_ref, rows)
        for part in range(6):
            strain_ref[part, rows, :] = strain[part]
        lame = lame_ref[rows, :]
        twice_mu = 2.0 * mu_ref[rows, :]
        trace = strain[0] + strain[1] + strain[2]
        third = trace * (1.0 / 3.0)
        pulls = [twice_mu * s for s in strain]
        pull_third = twice_mu * third
        fresh = [pulls[0] - pull_third, pulls[1] - pull_third, pulls[3], pulls[4], pulls[5]]
        relax = []
        for part in range(5):
            value = m_ref[part, rows, :] + factors[0] * fresh[part]
            for back in range(step):
                value = value + factors[back + 1] * older[step - 1 - back][part, rows, :]
            relax.append(value)
            if keep_ref is not None:
                keep_ref[part, rows, :] = fresh[part]
        bulk = lame * trace
        xx = bulk + pulls[0] - relax[0]
        yy = bulk + pulls[1] - relax[1]
        zz = bulk + pulls[2] + relax[0] + relax[1]
        xy = pulls[3] - relax[2]
        xz = pulls[4] - relax[3]
        yz = pulls[5] - relax[4]
        for direction, values in enumerate(((xx, xy, xz), (xy, yy, yz), (xz, yz, zz))):
            for c in range(3):
                sigma_ref[direction * 128 + rows.start : direction * 128 + rows.stop, c * LANES : (c + 1) * LANES] = values[c]
    faces = dot_six(face_table, sigma_ref[...])
    first_ref[...] = pack_face(faces[0:32], False)
    last_ref[...] = pack_face(faces[32:64], True)


def rest_kernel(sigma_ref, u_ref, p_ref, scale_ref, force_table, next_ref):
    force = dot_six(force_table, sigma_ref[...])
    blocks = {}
    for c in range(3):
        for b in range(5):
            for d in range(5):
                blocks[(c, b, d)] = force[block_rows(b, d), c * LANES : (c + 1) * LANES]
    blocks = assembled(blocks)
    lane = lanes_of((8, LANES))
    sub = lax.broadcasted_iota(jnp.int32, (8, LANES), 0)
    inner = ((sub == 4) & (lane < 64)) | ((sub == 0) & (lane >= 64))
    for c in range(3):
        for b in range(5):
            for d in range(5):
                value = blocks[(c, b, d)]
                value = value + jnp.where(inner, rolled(rolled(value, 4, 0), 64, 1), 0.0)
                at = block_rows(b, d)
                next_ref[c, at, :] = 2.0 * u_ref[c, at, :] - p_ref[c, at, :] + scale_ref[at, :] * value
        next_ref[c, 200:208, :] = jnp.zeros((8, LANES), F32)


def add_faces(from_before, from_after, partial_ref, scale_ref, u_ref, delta_ref):
    delta_ref[...] = jnp.zeros(delta_ref.shape, F32)
    lower = lanes_of((25, LANES)) < 64
    if from_before is not None:
        packed = from_before[...]
        turned = rolled(packed, 64, 1)
        values = [packed[0:32], turned[0:32], jnp.concatenate([packed[32:48], turned[32:48]], axis=0)]
        for c in range(3):
            delta_ref[c, pl.ds(0, 25, stride=8), :] = jnp.where(lower, values[c][0:25], 0.0)
    if from_after is not None:
        packed = from_after[...]
        turned = rolled(packed, 64, 1)
        values = [turned[0:32], packed[0:32], jnp.concatenate([turned[32:48], packed[32:48]], axis=0)]
        for c in range(3):
            delta_ref[c, pl.ds(4, 25, stride=8), :] = jnp.where(lower, 0.0, values[c][0:25])
    blocks = {}
    for c in range(3):
        for b in range(5):
            for d in range(5):
                blocks[(c, b, d)] = delta_ref[c, block_rows(b, d), :]
    blocks = assembled(blocks)
    for c in range(3):
        for b in range(5):
            for d in range(5):
                at = block_rows(b, d)
                u_ref[c, at, :] = partial_ref[c, at, :] + scale_ref[at, :] * blocks[(c, b, d)]
        u_ref[c, 200:208, :] = jnp.zeros((8, LANES), F32)


def update_kernel(before_ref, after_ref, partial_ref, scale_ref, u_ref, low_ref, delta_ref):
    add_faces(before_ref, after_ref, partial_ref, scale_ref, u_ref, delta_ref)
    low_ref[...] = u_ref[...].astype(BF16)


def parts_kernel(index_ref, strain_ref, low_ref, far_ref, lame_ref, mu_ref, select_ref, grad_table, *refs):
    out_refs, (grad_ref, kernel_ref) = refs[:-2], refs[-2:]
    forward = jnp.where(index_ref[1] == 0, beside(low_ref), beside(far_ref))
    grad_ref[...] = dot(grad_table[0], forward) + (dot(grad_table[1], forward) + dot(grad_table[2], forward))
    for rows in CHUNKS:
        far = strains(grad_ref, rows)
        own = [strain_ref[part, rows, :] for part in range(6)]
        trace_own = own[0] + own[1] + own[2]
        trace_far = far[0] + far[1] + far[2]
        third_own, third_far = trace_own * (1.0 / 3.0), trace_far * (1.0 / 3.0)
        twice_mu = 2.0 * mu_ref[rows, :]
        kappa = lame_ref[rows, :] + twice_mu * (1.0 / 3.0)
        kernel_ref[rows, :] = time_step * kappa * trace_far * trace_own
        product = (
            (own[0] - third_own) * (far[0] - third_far)
            + (own[1] - third_own) * (far[1] - third_far)
            + (own[2] - third_own) * (far[2] - third_far)
            + 2.0 * (own[3] * far[3] + own[4] * far[4] + own[5] * far[5])
        )
        kernel_ref[125 + rows.start : 125 + rows.stop, :] = time_step * twice_mu * product
    kernel_ref[250:256, :] = jnp.zeros((6, LANES), F32)
    outgoing = lax.dot_general(
        select_ref[...], kernel_ref[...].astype(BF16), (((1,), (1,)), ((), ())), preferred_element_type=F32
    ).astype(BF16)
    slots = out_refs[0].shape[0]
    for k, ref in enumerate(out_refs):
        ref[...] = outgoing[k * slots : (k + 1) * slots]


def sum_kernel(index_ref, *refs):
    in_refs, out_ref = refs[:-1], refs[-1]
    subs = len(in_refs) // STEPS
    slots = in_refs[0].shape[0]
    for k in range(subs):
        value = in_refs[k][...].astype(F32) + in_refs[subs + k][...].astype(F32) + in_refs[2 * subs + k][...].astype(F32)
        start = pl.multiple_of((index_ref[0] ^ k) * slots, 16)
        out_ref[0, pl.ds(start, slots), :] = value[:, 0:250]


def finish_kernel(before_ref, partial_ref, scale_ref, collect_ref, out_ref, u_ref, delta_ref):
    add_faces(before_ref, None, partial_ref, scale_ref, u_ref, delta_ref)
    lane = lanes_of((8, LANES))
    sub = lax.broadcasted_iota(jnp.int32, (8, LANES), 0)
    tiles = []
    for c in range(3):
        row = []
        for pair in range(BLOCKS // 2):
            even = u_ref[c, 16 * pair : 16 * pair + 8, :]
            odd = u_ref[c, 16 * pair + 8 : 16 * pair + 16, :]
            low = jnp.where(sub < 4, even, rolled(rolled(even, 64, 1), 4, 0))
            high = jnp.where(sub < 4, rolled(odd, 64, 1), rolled(odd, 4, 0))
            row.append(jnp.where(lane < 64, low, high))
        tiles.append(jnp.concatenate(row, axis=1))
    columns = jnp.concatenate(tiles, axis=0)
    own = (lanes_of((24, WIDE)) // 8) % 8
    spread = jnp.concatenate([jnp.where(own == ey, columns, 0.0) for ey in range(EY)], axis=0)
    high, middle, low = cut(spread)
    collect = collect_ref[...]
    windows = dot(high, collect) + dot(middle, collect) + dot(low, collect)
    for ey in range(EY):
        width = JUMP if ey < EY - 1 else JUMP + SIDE
        for c in range(3):
            out_ref[0, c, :, JUMP * ey : JUMP * ey + width] = windows[24 * ey + 8 * c : 24 * ey + 8 * c + 8, 0:width]


VMEM = pl.BlockSpec(memory_space=pltpu.VMEM)
SMEM = pl.BlockSpec(memory_space=pltpu.SMEM)


def shaped(*shape, dtype=F32):
    return jax.ShapeDtypeStruct(shape, dtype)


def call(kernel, name, outs, scratch, *args, scalars=0, micros=1):
    return pl.pallas_call(
        kernel,
        name=name,
        out_shape=outs,
        in_specs=[SMEM] * scalars + [VMEM] * (len(args) - scalars),
        out_specs=jax.tree.map(lambda _: VMEM, outs),
        scratch_shapes=scratch,
        compiler_params=pltpu.CompilerParams(vmem_limit_bytes=32 * 1024 * 1024),
        cost_estimate=pl.CostEstimate(flops=0, bytes_accessed=micros * 3000000, transcendentals=0),
    )(*args)


def passed_along(value, axis, steps):
    count = lax.axis_size(axis)
    return lax.ppermute(value, axis, [(source, (source + steps) % count) for source in range(count)])


def per_device(disp_now, disp_prev, memory_init, density, lame_lambda, shear_mu, sls_decay, owner_map):
    ring = ("cuts", "sub")
    subs = lax.axis_size("sub")
    groups = lax.axis_size("group")
    slots = 2 * EY * EZ * 2 // subs
    index = jnp.stack([lax.axis_index("sub"), lax.axis_index("group"), jnp.int32(subs)]).astype(jnp.int32)

    rim = jnp.concatenate(
        [disp_now[0, :, 0, :], disp_prev[0, :, 0, :], density[0:1, :], jnp.ones((1, FACE), F32)], axis=0
    )
    rim = passed_along(rim, ring, -1)

    grad_table = jnp.asarray(cut_table(GRAD))
    force_table = jnp.asarray(cut_table(FORCE))
    face_table = jnp.asarray(cut_table(FACES))
    spread = jnp.asarray(SPREAD, BF16)
    collect = jnp.asarray(COLLECT, BF16)
    mass = jnp.asarray(MASS)

    state = shaped(3, ROWS, LANES)
    state_low = shaped(3, ROWS, LANES, dtype=BF16)
    scale_shape = shaped(ROWS, LANES)
    five = shaped(5, 125, LANES)
    u, p, scale, m1, m2, m3, select = call(
        prologue_kernel, "prologue",
        [state, state, scale_shape, five, five, five, shaped(subs * slots, LANES, dtype=BF16)],
        [pltpu.VMEM((8, 56, WINDOW), F32)],
        index, disp_now, disp_prev, density, memory_init, sls_decay,
        owner_map.reshape(2 * EY * EZ, 1), owner_map.reshape(1, 2 * EY * EZ), spread, mass,
        scalars=1, micros=3,
    )
    u, p, scale, low = call(
        rim_kernel, "rim", [state, state, scale_shape, state_low],
        [pltpu.VMEM((8, 8, WINDOW), F32), pltpu.VMEM((ROWS, LANES), F32)],
        rim, u, p, scale, spread, mass,
    )
    memories = (m1, m2, m3)
    kept = []
    parts = []
    for step in range(STEPS):
        far = None
        for k in range(1, groups):
            moved = passed_along(low, "group", k)
            far = moved if far is None else jnp.where(lax.axis_index("group") == k, moved, far)
        outs = [shaped(6, 125, LANES), shaped(384, 384), shaped(48, LANES), shaped(48, LANES)]
        if step < STEPS - 1:
            outs.append(five)
        results = call(
            lambda *refs, step=step: step_kernel(step, *refs), "step", outs, [pltpu.VMEM((384, 384), F32)],
            u, lame_lambda, shear_mu, memories[step], sls_decay, grad_table, face_table, *kept,
        )
        strain, sigma, first, last = results[0:4]
        kept.extend(results[4:])
        from_before = passed_along(last, ring, 1)
        if step < STEPS - 1:
            from_after = passed_along(first, ring, -1)
        partial = call(rest_kernel, "rest", state, [], sigma, u, p, scale, force_table)
        sent = call(
            parts_kernel, "parts", [shaped(slots, WINDOW, dtype=BF16)] * subs,
            [pltpu.VMEM((384, 384), F32), pltpu.VMEM((256, LANES), F32)],
            index, strain, low, far, lame_lambda, shear_mu, select, grad_table, scalars=1,
        )
        parts.append(sent[0])
        for k in range(1, subs):
            parts.append(lax.ppermute(sent[k], "sub", [(j, j ^ k) for j in range(subs)]))
        p = u
        if step < STEPS - 1:
            u, low = call(
                update_kernel, "update", [state, state_low], [pltpu.VMEM((3, ROWS, LANES), F32)],
                from_before, from_after, partial, scale,
            )
    final = call(
        finish_kernel, "finish", shaped(1, 3, 8, FACE),
        [pltpu.VMEM((3, ROWS, LANES), F32), pltpu.VMEM((3, ROWS, LANES), F32)],
        from_before, partial, scale, collect,
    )
    kernels = call(sum_kernel, "sum", shaped(1, subs * slots, 250), [], index, *parts, scalars=1)
    return final, kernels


def solution(mesh):
    in_specs = (
        P("group", None, ("cuts", "sub"), None),
        P("group", None, ("cuts", "sub"), None),
        P("group", None, None, None, ("cuts", "sub")),
        P(("cuts", "sub"), None),
        P(None, ("cuts", "sub")),
        P(None, ("cuts", "sub")),
        P(None, ("cuts", "sub")),
        P(("cuts", "sub"), None, None),
    )
    out_specs = (P("group", None, ("cuts", "sub"), None), P("group", ("cuts", "sub"), None))
    return jax.shard_map(
        per_device, mesh=mesh, in_specs=in_specs, out_specs=out_specs, check_vma=False
    )
```

```python
import math

import jax
import jax.numpy as jnp
import numpy as np
from jax import lax
from jax.experimental import pallas as pl
from jax.experimental.pallas import tpu as pltpu
from jax.sharding import PartitionSpec as P

STEPS = 3
EY = 8
EZ = 8
LANES = 128
SIDE = 33
FACE = SIDE * SIDE
BLOCKS = 26
ROWS = 8 * BLOCKS
WIDE = 64 * BLOCKS
JUMP = 4 * SIDE
WINDOW = 256

time_step = 0.03
step_square = 0.0009
relax_strength = (0.12, 0.08, 0.05)

F32 = jnp.float32
BF16 = jnp.bfloat16


def gll_tables():
    root_value = math.sqrt(3.0 / 7.0)
    points = [-1.0, -root_value, 0.0, root_value, 1.0]
    weights = [0.1, 49.0 / 90.0, 32.0 / 45.0, 49.0 / 90.0, 0.1]
    derivative = np.zeros((5, 5))
    for p in range(5):
        for a in range(5):
            accum = 0.0
            for m in range(5):
                if m != a:
                    factor = 1.0 / (points[a] - points[m])
                    for k in range(5):
                        if k != a and k != m:
                            factor = factor * (points[p] - points[k]) / (points[a] - points[k])
                    accum = accum + factor
            derivative[p, a] = accum
    return derivative.astype(np.float32).astype(np.float64), np.array(weights).astype(np.float32).astype(np.float64)


def node(a, b, d):
    return a * 25 + b * 5 + d


def place(a, b, d):
    return (b * 5 + d) * 8 + a


def make_tables():
    derivative, weights = gll_tables()
    grad = np.zeros((3 * 128, ROWS))
    force = np.zeros((ROWS, 3 * 128))
    for a in range(5):
        for b in range(5):
            for d in range(5):
                for m in range(5):
                    grad[node(a, b, d), place(m, b, d)] = derivative[a, m]
                    grad[128 + node(a, b, d), place(a, m, d)] = derivative[b, m]
                    grad[256 + node(a, b, d), place(a, b, m)] = derivative[d, m]
                    row = place(a, b, d)
                    force[row, node(m, b, d)] = -derivative[m, a] * weights[m] * weights[b] * weights[d]
                    force[row, 128 + node(a, m, d)] = -derivative[m, b] * weights[a] * weights[m] * weights[d]
                    force[row, 256 + node(a, b, m)] = -derivative[m, d] * weights[a] * weights[b] * weights[m]
    face = np.zeros((64, 3 * 128))
    face[0:25] = force[0:200:8]
    face[32:57] = force[4:200:8]
    spread = np.zeros((WINDOW, WIDE), np.float32)
    collect = np.zeros((WIDE, WINDOW), np.float32)
    line = np.zeros(SIDE)
    for e in range(8):
        line[4 * e : 4 * e + 5] += weights
    layer = np.array([2 * weights[0], weights[1], weights[2], weights[3], 2 * weights[0], 1.0, 1.0, 1.0])
    mass = np.ones((ROWS, LANES), np.float32)
    for b in range(5):
        for d in range(5):
            for ey in range(8):
                for ez in range(8):
                    column = (b * 5 + d) * 64 + ey * 8 + ez
                    spot = b * SIDE + 4 * ez + d
                    spread[spot, column] = 1.0
                    if d < 4 or ez == 7:
                        collect[column, spot] = 1.0
                    for slab in range(2):
                        at = (b * 5 + d) * 8
                        mass[at : at + 8, slab * 64 + ey * 8 + ez] = layer * line[4 * ey + b] * line[4 * ez + d]
    return grad, force, face, spread, collect, mass


def cut_table(table):
    value = table.astype(np.float32)
    pieces = []
    for _ in range(3):
        piece = value.astype(jnp.bfloat16)
        pieces.append(piece)
        value = value - piece.astype(np.float32)
    return np.stack(pieces)


GRAD, FORCE, FACES, SPREAD, COLLECT, MASS = make_tables()


def cut(value):
    high = value.astype(BF16)
    rest = value - high.astype(F32)
    middle = rest.astype(BF16)
    low = (rest - middle.astype(F32)).astype(BF16)
    return high, middle, low


def dot(left, right):
    return jnp.dot(left, right, preferred_element_type=F32)


def dot_six(table, value):
    high, middle, low = cut(value)
    small = dot(table[2], high) + dot(table[1], middle) + dot(table[0], low)
    return dot(table[0], high) + (dot(table[0], middle) + dot(table[1], high) + small)


def lanes_of(shape):
    return lax.broadcasted_iota(jnp.int32, shape, len(shape) - 1)


def rolled(value, shift, axis):
    return pltpu.roll(value, shift % value.shape[axis], axis)


def window_rows(value, window_ref):
    for ey in range(EY):
        width = min(WINDOW, FACE - JUMP * ey)
        if width < WINDOW:
            window_ref[ey] = jnp.zeros(window_ref.shape[1:], F32)
        window_ref[ey, :, 0:width] = value[:, JUMP * ey : JUMP * ey + width]
    return window_ref[...].reshape(-1, WINDOW)


def to_columns(value, window_ref, spread_ref):
    rows = value.shape[0]
    high, middle, low = cut(window_rows(value, window_ref))
    spread = spread_ref[...]
    wide = dot(high, spread) + dot(middle, spread) + dot(low, spread)
    own = (lanes_of((rows, WIDE)) // 8) % 8
    picked = wide[0:rows]
    for ey in range(1, EY):
        picked = jnp.where(own == ey, wide[ey * rows : (ey + 1) * rows], picked)
    return picked


def assembled(blocks):
    lane = lanes_of((8, LANES))
    blocks = dict(blocks)
    for shift, at, pairs in (
        (1, lane % 8, [((b, 0), (b, 4)) for b in range(5)]),
        (8, (lane // 8) % 8, [((0, d), (4, d)) for d in range(5)]),
    ):
        for c in range(3):
            for near, far in pairs:
                first, last = blocks[(c,) + near], blocks[(c,) + far]
                blocks[(c,) + near] = first + jnp.where(at > 0, rolled(last, shift, 1), 0.0)
                blocks[(c,) + far] = last + jnp.where(at < 7, rolled(first, -shift, 1), 0.0)
    return blocks


def block_rows(b, d):
    return slice((b * 5 + d) * 8, (b * 5 + d) * 8 + 8)


def beside(value):
    return jnp.concatenate([value[0], value[1], value[2]], axis=1)


def gather_kernel(now_ref, prev_ref, density_ref, rim_ref):
    for c in range(3):
        rim_ref[c : c + 1, :] = now_ref[0, c, 0:1, :]
        rim_ref[3 + c : 4 + c, :] = prev_ref[0, c, 0:1, :]
    rim_ref[6:7, :] = density_ref[0:1, :]
    rim_ref[7:8, :] = density_ref[0:1, :]


def weighted_memory(memory_ref, decays, part, power):
    value = 0.0
    for l in range(3):
        factor = decays[l]
        for _ in range(power - 1):
            factor = factor * decays[l]
        value = value + factor * memory_ref[l, part, :, 0, :]
    return value


def prologue_kernel(
    now_ref, prev_ref, density_ref, memory_ref, decay_ref, spread_ref, mass_ref, u_ref, p_ref, scale_ref, m1_ref, window_ref
):
    rows = jnp.concatenate([now_ref[0].reshape(24, FACE), prev_ref[0].reshape(24, FACE), density_ref[...]], axis=0)
    columns = to_columns(rows, window_ref, spread_ref)
    lane = lanes_of((8, LANES))
    for group in range(7):
        for pair in range(BLOCKS // 2):
            tile = columns[8 * group : 8 * group + 8, LANES * pair : LANES * pair + LANES]
            swapped = rolled(tile, 64, 1)
            even = jnp.where(lane < 64, tile, rolled(swapped, 4, 0))
            odd = jnp.where(lane < 64, swapped, rolled(tile, 4, 0))
            for block, value in ((2 * pair, even), (2 * pair + 1, odd)):
                at = slice(8 * block, 8 * block + 8)
                if group < 3:
                    u_ref[group, at, :] = value
                elif group < 6:
                    p_ref[group - 3, at, :] = value
                elif block < 25:
                    scale_ref[at, :] = step_square / (value * mass_ref[at, :])
                else:
                    scale_ref[at, :] = jnp.zeros((8, LANES), F32)
    decays = [decay_ref[l : l + 1, :] for l in range(3)]
    for part in range(5):
        m1_ref[part] = weighted_memory(memory_ref, decays, part, 1)


def later_kernel(index_ref, memory_ref, decay_ref, owner_ref, m2_ref, m3_ref, select_ref):
    decays = [decay_ref[l : l + 1, :] for l in range(3)]
    for part in range(5):
        m2_ref[part] = weighted_memory(memory_ref, decays, part, 2)
        m3_ref[part] = weighted_memory(memory_ref, decays, part, 3)
    owner = jnp.concatenate([owner_ref[0], owner_ref[1]], axis=1)
    named = jnp.where(lax.broadcasted_iota(jnp.int32, (16, LANES), 0) == owner, 1.0, 0.0)
    earlier = lax.broadcasted_iota(jnp.int32, (LANES, LANES), 0)
    later = lax.broadcasted_iota(jnp.int32, (LANES, LANES), 1)
    ahead = jnp.where((earlier < later) & ((earlier // 64) == (later // 64)), 1.0, 0.0)
    rank = jnp.sum(named * dot(named.astype(BF16), ahead.astype(BF16)), axis=0, keepdims=True).astype(jnp.int32)
    subs = select_ref.shape[0] // LANES
    slots = 4 * EY * EZ // subs
    row = lax.broadcasted_iota(jnp.int32, select_ref.shape, 0)
    toward = (row // LANES) ^ index_ref[0]
    wanted = (lanes_of((1, LANES)) // 64) * (slots // 2) + rank
    chosen = (owner == toward) & (wanted == row % slots)
    select_ref[...] = jnp.where(chosen, 1.0, 0.0).astype(BF16)


def rim_kernel(rim_ref, u_in, p_in, scale_in, spread_ref, mass_ref, u_ref, p_ref, scale_ref, low_ref, window_ref, rows_ref):
    columns = to_columns(rim_ref[...], window_ref, spread_ref)
    for pair in range(BLOCKS // 2):
        tile = columns[:, LANES * pair : LANES * pair + LANES]
        rows_ref[16 * pair : 16 * pair + 8, :] = rolled(tile, 64, 1)
        rows_ref[16 * pair + 8 : 16 * pair + 16, :] = tile
    u_ref[...] = u_in[...]
    p_ref[...] = p_in[...]
    scale_ref[...] = scale_in[...]
    upper = lanes_of((25, LANES)) >= 64
    last = pl.ds(4, 25, stride=8)
    for c in range(3):
        u_ref[c, last, :] = jnp.where(upper, rows_ref[pl.ds(c, 25, stride=8), :], u_ref[c, last, :])
        p_ref[c, last, :] = jnp.where(upper, rows_ref[pl.ds(3 + c, 25, stride=8), :], p_ref[c, last, :])
    rim = step_square / (rows_ref[pl.ds(6, 25, stride=8), :] * mass_ref[last, :])
    scale_ref[last, :] = jnp.where(upper, rim, scale_ref[last, :])
    low_ref[...] = u_ref[...].astype(BF16)


def strains(grad, rows):
    def at(direction, c):
        return grad[direction * 128 + rows.start : direction * 128 + rows.stop, c * LANES : (c + 1) * LANES]

    return [
        at(0, 0),
        at(1, 1),
        at(2, 2),
        0.5 * (at(1, 0) + at(0, 1)),
        0.5 * (at(2, 0) + at(0, 2)),
        0.5 * (at(2, 1) + at(1, 2)),
    ]


CHUNKS = [slice(0, 32), slice(32, 64), slice(64, 96), slice(96, 125)]


def pack_face(face, upper):
    parts = [face[:, c * LANES : (c + 1) * LANES] for c in range(3)]
    lower_lane = lanes_of((16, LANES)) < 64
    lower_lanes = lanes_of((32, LANES)) < 64
    if upper:
        first = jnp.where(lower_lanes, rolled(parts[0], 64, 1), parts[1])
        second = jnp.where(lower_lane, rolled(parts[2][0:16], 64, 1), parts[2][16:32])
    else:
        first = jnp.where(lower_lanes, parts[0], rolled(parts[1], 64, 1))
        second = jnp.where(lower_lane, parts[2][0:16], rolled(parts[2][16:32], 64, 1))
    return jnp.concatenate([first, second], axis=0)


def step_kernel(step, *refs):
    index_ref, u_ref, lame_ref, mu_ref, m_ref, decay_ref, grad_table, face_table = refs[0:8]
    older = refs[8 : 8 + step]
    refs = refs[8 + step :]
    strain_ref, sigma_ref, odd_ref, even_ref = refs[0:4]
    keep_ref = refs[4] if step < STEPS - 1 else None
    grad_ref = refs[-1]
    grad_ref[...] = dot_six(grad_table, beside(u_ref))
    for block in range(9):
        sigma_ref[(block // 3) * 128 + 120 : (block // 3) * 128 + 128, (block % 3) * LANES : (block % 3) * LANES + LANES] = (
            jnp.zeros((8, LANES), F32)
        )
    decays = [decay_ref[l : l + 1, :] for l in range(3)]
    shares = [(1.0 - decays[l]) * relax_strength[l] for l in range(3)]
    factors = []
    for _ in range(step + 1):
        factors.append(shares[0] + shares[1] + shares[2])
        shares = [decays[l] * shares[l] for l in range(3)]
    for rows in CHUNKS:
        strain = strains(grad_ref, rows)
        for part in range(6):
            strain_ref[part, rows, :] = strain[part]
        lame = lame_ref[rows, :]
        twice_mu = 2.0 * mu_ref[rows, :]
        trace = strain[0] + strain[1] + strain[2]
        third = trace * (1.0 / 3.0)
        pulls = [twice_mu * s for s in strain]
        pull_third = twice_mu * third
        fresh = [pulls[0] - pull_third, pulls[1] - pull_third, pulls[3], pulls[4], pulls[5]]
        relax = []
        for part in range(5):
            value = m_ref[part, rows, :] + factors[0] * fresh[part]
            for back in range(step):
                value = value + factors[back + 1] * older[step - 1 - back][part, rows, :]
            relax.append(value)
            if keep_ref is not None:
                keep_ref[part, rows, :] = fresh[part]
        bulk = lame * trace
        xx = bulk + pulls[0] - relax[0]
        yy = bulk + pulls[1] - relax[1]
        zz = bulk + pulls[2] + relax[0] + relax[1]
        xy = pulls[3] - relax[2]
        xz = pulls[4] - relax[3]
        yz = pulls[5] - relax[4]
        for direction, values in enumerate(((xx, xy, xz), (xy, yy, yz), (xz, yz, zz))):
            for c in range(3):
                sigma_ref[direction * 128 + rows.start : direction * 128 + rows.stop, c * LANES : (c + 1) * LANES] = values[c]
    faces = dot_six(face_table, sigma_ref[...])
    first, last = pack_face(faces[0:32], False), pack_face(faces[32:64], True)
    if step < STEPS - 1:
        even_ring = index_ref[2] == 0
        odd_ref[...] = jnp.where(even_ring, first, last)
        even_ref[...] = jnp.where(even_ring, last, first)
    else:
        odd_ref[...] = first
        even_ref[...] = last


def rest_kernel(sigma_ref, u_ref, p_ref, scale_ref, force_table, next_ref):
    force = dot_six(force_table, sigma_ref[...])
    blocks = {}
    for c in range(3):
        for b in range(5):
            for d in range(5):
                blocks[(c, b, d)] = force[block_rows(b, d), c * LANES : (c + 1) * LANES]
    blocks = assembled(blocks)
    lane = lanes_of((8, LANES))
    sub = lax.broadcasted_iota(jnp.int32, (8, LANES), 0)
    inner = ((sub == 4) & (lane < 64)) | ((sub == 0) & (lane >= 64))
    for c in range(3):
        for b in range(5):
            for d in range(5):
                value = blocks[(c, b, d)]
                value = value + jnp.where(inner, rolled(rolled(value, 4, 0), 64, 1), 0.0)
                at = block_rows(b, d)
                next_ref[c, at, :] = 2.0 * u_ref[c, at, :] - p_ref[c, at, :] + scale_ref[at, :] * value
        next_ref[c, 200:208, :] = jnp.zeros((8, LANES), F32)


def add_faces(from_before, from_after, partial_ref, scale_ref, u_ref, delta_ref):
    delta_ref[...] = jnp.zeros(delta_ref.shape, F32)
    lower = lanes_of((25, LANES)) < 64
    if from_before is not None:
        packed = from_before
        turned = rolled(packed, 64, 1)
        values = [packed[0:32], turned[0:32], jnp.concatenate([packed[32:48], turned[32:48]], axis=0)]
        for c in range(3):
            delta_ref[c, pl.ds(0, 25, stride=8), :] = jnp.where(lower, values[c][0:25], 0.0)
    if from_after is not None:
        packed = from_after
        turned = rolled(packed, 64, 1)
        values = [turned[0:32], packed[0:32], jnp.concatenate([turned[32:48], packed[32:48]], axis=0)]
        for c in range(3):
            delta_ref[c, pl.ds(4, 25, stride=8), :] = jnp.where(lower, 0.0, values[c][0:25])
    blocks = {}
    for c in range(3):
        for b in range(5):
            for d in range(5):
                blocks[(c, b, d)] = delta_ref[c, block_rows(b, d), :]
    blocks = assembled(blocks)
    for c in range(3):
        for b in range(5):
            for d in range(5):
                at = block_rows(b, d)
                u_ref[c, at, :] = partial_ref[c, at, :] + scale_ref[at, :] * blocks[(c, b, d)]
        u_ref[c, 200:208, :] = jnp.zeros((8, LANES), F32)


def update_kernel(index_ref, odd_ref, even_ref, partial_ref, scale_ref, u_ref, low_ref, delta_ref):
    even_ring = index_ref[2] == 0
    odd, even = odd_ref[...], even_ref[...]
    before, after = jnp.where(even_ring, odd, even), jnp.where(even_ring, even, odd)
    add_faces(before, after, partial_ref, scale_ref, u_ref, delta_ref)
    low_ref[...] = u_ref[...].astype(BF16)


def kernel_parts(index_ref, strain_ref, low_ref, far_ref, lame_ref, mu_ref, grad_table, grad_ref, kernel_ref):
    forward = jnp.where(index_ref[1] == 0, beside(low_ref), beside(far_ref))
    grad_ref[...] = dot(grad_table[0], forward) + (dot(grad_table[1], forward) + dot(grad_table[2], forward))
    for rows in CHUNKS:
        far = strains(grad_ref, rows)
        own = [strain_ref[part, rows, :] for part in range(6)]
        trace_own = own[0] + own[1] + own[2]
        trace_far = far[0] + far[1] + far[2]
        third_own, third_far = trace_own * (1.0 / 3.0), trace_far * (1.0 / 3.0)
        twice_mu = 2.0 * mu_ref[rows, :]
        kappa = lame_ref[rows, :] + twice_mu * (1.0 / 3.0)
        kernel_ref[rows, :] = time_step * kappa * trace_far * trace_own
        product = (
            (own[0] - third_own) * (far[0] - third_far)
            + (own[1] - third_own) * (far[1] - third_far)
            + (own[2] - third_own) * (far[2] - third_far)
            + 2.0 * (own[3] * far[3] + own[4] * far[4] + own[5] * far[5])
        )
        kernel_ref[125 + rows.start : 125 + rows.stop, :] = time_step * twice_mu * product
    kernel_ref[250:256, :] = jnp.zeros((6, LANES), F32)
    return kernel_ref[...].astype(BF16)


def parts_kernel(
    index_ref, strain_ref, low_ref, far_ref, lame_ref, mu_ref, grad_table, part_ref, grad_ref, kernel_ref
):
    part_ref[...] = kernel_parts(
        index_ref, strain_ref, low_ref, far_ref, lame_ref, mu_ref, grad_table, grad_ref, kernel_ref
    )


def send_kernel(
    index_ref, strain_ref, low_ref, far_ref, lame_ref, mu_ref, grad_table, one_ref, two_ref, select_ref, *refs
):
    out_refs, (grad_ref, kernel_ref) = refs[:-2], refs[-2:]
    three = kernel_parts(index_ref, strain_ref, low_ref, far_ref, lame_ref, mu_ref, grad_table, grad_ref, kernel_ref)
    rows = out_refs[0].shape[0]
    slots = rows // 2
    group = lanes_of((rows, LANES)) // slots
    over_lanes = (((1,), (1,)), ((), ()))
    for k, ref in enumerate(out_refs):
        chosen = select_ref[k * LANES : (k + 1) * LANES, :]
        total = 0.0
        for part in (one_ref[...], two_ref[...], three):
            total = total + lax.dot_general(part, chosen, over_lanes, preferred_element_type=F32)
        value = total[0:rows]
        for j in range(1, 256 // rows):
            value = jnp.where(group == j, total[j * rows : (j + 1) * rows], value)
        ref[...] = value


def sum_kernel(index_ref, *refs):
    in_refs, out_ref = refs[:-1], refs[-1]
    rows = in_refs[0].shape[0]
    slots = rows // 2
    pieces = 256 // rows
    group = lanes_of((rows, LANES)) // slots
    blocks = [[jnp.zeros((rows, LANES), F32)] * 2 for _ in range(pieces)]
    for k, ref in enumerate(in_refs):
        source = index_ref[0] ^ k
        spot = source % pieces
        value = ref[...]
        for j in range(pieces):
            moved = pltpu.roll(value, ((spot + pieces - j) % pieces) * slots, 1)
            for t in range(2):
                here = (group == spot) & (source // pieces == t)
                blocks[j][t] = jnp.where(here, moved, blocks[j][t])
    value = jnp.concatenate([jnp.concatenate(row, axis=1) for row in blocks], axis=0)
    out_ref[:, 0, :] = value[0:250]


def finish_kernel(before_ref, partial_ref, scale_ref, collect_ref, out_ref, u_ref, delta_ref):
    add_faces(before_ref[...], None, partial_ref, scale_ref, u_ref, delta_ref)
    lane = lanes_of((8, LANES))
    sub = lax.broadcasted_iota(jnp.int32, (8, LANES), 0)
    tiles = []
    for c in range(3):
        row = []
        for pair in range(BLOCKS // 2):
            even = u_ref[c, 16 * pair : 16 * pair + 8, :]
            odd = u_ref[c, 16 * pair + 8 : 16 * pair + 16, :]
            low = jnp.where(sub < 4, even, rolled(rolled(even, 64, 1), 4, 0))
            high = jnp.where(sub < 4, rolled(odd, 64, 1), rolled(odd, 4, 0))
            row.append(jnp.where(lane < 64, low, high))
        tiles.append(jnp.concatenate(row, axis=1))
    columns = jnp.concatenate(tiles, axis=0)
    own = (lanes_of((24, WIDE)) // 8) % 8
    spread = jnp.concatenate([jnp.where(own == ey, columns, 0.0) for ey in range(EY)], axis=0)
    high, middle, low = cut(spread)
    collect = collect_ref[...]
    windows = dot(high, collect) + dot(middle, collect) + dot(low, collect)
    for ey in range(EY):
        width = JUMP if ey < EY - 1 else JUMP + SIDE
        for c in range(3):
            out_ref[0, c, :, JUMP * ey : JUMP * ey + width] = windows[24 * ey + 8 * c : 24 * ey + 8 * c + 8, 0:width]


VMEM = pl.BlockSpec(memory_space=pltpu.VMEM)
SMEM = pl.BlockSpec(memory_space=pltpu.SMEM)


def shaped(*shape, dtype=F32):
    return jax.ShapeDtypeStruct(shape, dtype)


def call(kernel, name, outs, scratch, *args, scalars=0, micros=1):
    return pl.pallas_call(
        kernel,
        name=name,
        out_shape=outs,
        in_specs=[SMEM] * scalars + [VMEM] * (len(args) - scalars),
        out_specs=jax.tree.map(lambda _: VMEM, outs),
        scratch_shapes=scratch,
        compiler_params=pltpu.CompilerParams(vmem_limit_bytes=32 * 1024 * 1024),
        cost_estimate=pl.CostEstimate(flops=0, bytes_accessed=micros * 3000000, transcendentals=0),
    )(*args)


def passed_along(value, axis, steps):
    count = lax.axis_size(axis)
    return lax.ppermute(value, axis, [(source, (source + steps) % count) for source in range(count)])


def swapped(value, axis, first):
    count = lax.axis_size(axis)
    pairs = []
    for source in range(first, count, 2):
        other = (source + 1) % count
        pairs += [(source, other), (other, source)]
    return lax.ppermute(value, axis, pairs)


def per_device(disp_now, disp_prev, memory_init, density, lame_lambda, shear_mu, sls_decay, owner_map):
    ring = ("cuts", "sub")
    subs = lax.axis_size("sub")
    groups = lax.axis_size("group")
    index = jnp.stack([lax.axis_index("sub"), lax.axis_index("group"), lax.axis_index(ring) % 2]).astype(jnp.int32)

    rim = call(gather_kernel, "gather", shaped(8, FACE), [], disp_now, disp_prev, density)
    rim = passed_along(rim, ring, -1)

    grad_table = jnp.asarray(cut_table(GRAD))
    force_table = jnp.asarray(cut_table(FORCE))
    face_table = jnp.asarray(cut_table(FACES))
    spread = jnp.asarray(SPREAD, BF16)
    collect = jnp.asarray(COLLECT, BF16)
    mass = jnp.asarray(MASS)
    memory = jnp.transpose(memory_init, (1, 2, 3, 0, 4))
    owner = jnp.transpose(owner_map, (0, 2, 1))

    state = shaped(3, ROWS, LANES)
    state_low = shaped(3, ROWS, LANES, dtype=BF16)
    scale_shape = shaped(ROWS, LANES)
    five = shaped(5, 125, LANES)
    part_shape = shaped(256, LANES, dtype=BF16)
    grad_scratch = pltpu.VMEM((384, 384), F32)
    part_scratch = [grad_scratch, pltpu.VMEM((256, LANES), F32)]
    face = shaped(48, LANES)
    u, p, scale, m1 = call(
        prologue_kernel, "prologue", [state, state, scale_shape, five], [pltpu.VMEM((8, 56, WINDOW), F32)],
        disp_now, disp_prev, density, memory, sls_decay, spread, mass, micros=3,
    )
    u, p, scale, low = call(
        rim_kernel, "rim", [state, state, scale_shape, state_low],
        [pltpu.VMEM((8, 8, WINDOW), F32), pltpu.VMEM((ROWS, LANES), F32)],
        rim, u, p, scale, spread, mass,
    )
    memories = [m1]
    kept = []
    parts = []
    for step in range(STEPS):
        outs = [shaped(6, 125, LANES), shaped(384, 384), face, face]
        if step < STEPS - 1:
            outs.append(five)
        results = call(
            lambda *refs, step=step: step_kernel(step, *refs), "step", outs, [grad_scratch],
            index, u, lame_lambda, shear_mu, memories[step], sls_decay, grad_table, face_table, *kept, scalars=1,
        )
        strain, sigma, odd, even = results[0:4]
        kept.extend(results[4:])
        if step < STEPS - 1:
            odd = swapped(odd, ring, 1)
            even = swapped(even, ring, 0)
        else:
            before = passed_along(even, ring, 1)
        far = None
        for k in range(1, groups):
            moved = passed_along(low, "group", k)
            far = moved if far is None else jnp.where(lax.axis_index("group") == k, moved, far)
        partial = call(rest_kernel, "rest", state, [], sigma, u, p, scale, force_table)
        shared = (index, strain, low, far, lame_lambda, shear_mu, grad_table)
        if step < STEPS - 1:
            parts.append(call(parts_kernel, "parts", part_shape, part_scratch, *shared, scalars=1))
            if step == 0:
                m2, m3, select = call(
                    later_kernel, "later", [five, five, shaped(subs * LANES, LANES, dtype=BF16)], [],
                    index, memory, sls_decay, owner, scalars=1,
                )
                memories += [m2, m3]
                partial, parts[0], select, memories[2] = lax.optimization_barrier((partial, parts[0], select, m3))
            else:
                partial, parts[1] = lax.optimization_barrier((partial, parts[1]))
            p = u
            u, low = call(
                update_kernel, "update", [state, state_low], [pltpu.VMEM((3, ROWS, LANES), F32)],
                index, odd, even, partial, scale, scalars=1,
            )
        else:
            sent = list(call(
                send_kernel, "send", [shaped(512 // subs, LANES)] * subs, part_scratch, *shared, *parts, select, scalars=1)
            )
            for k in range(subs - 1, 0, -1):
                sent[k] = lax.ppermute(sent[k], "sub", [(j, j ^ k) for j in range(subs)])
    final = call(
        finish_kernel, "finish", shaped(1, 3, 8, FACE),
        [pltpu.VMEM((3, ROWS, LANES), F32), pltpu.VMEM((3, ROWS, LANES), F32)],
        before, partial, scale, collect,
    )
    kernels = call(sum_kernel, "sum", shaped(250, 1, 256), [], index, *sent, scalars=1)
    return final, jnp.transpose(kernels, (1, 2, 0))


def solution(mesh):
    in_specs = (
        P("group", None, ("cuts", "sub"), None),
        P("group", None, ("cuts", "sub"), None),
        P("group", None, None, None, ("cuts", "sub")),
        P(("cuts", "sub"), None),
        P(None, ("cuts", "sub")),
        P(None, ("cuts", "sub")),
        P(None, ("cuts", "sub")),
        P(("cuts", "sub"), None, None),
    )
    out_specs = (P("group", None, ("cuts", "sub"), None), P("group", ("cuts", "sub"), None))
    return jax.shard_map(
        per_device, mesh=mesh, in_specs=in_specs, out_specs=out_specs, check_vma=False
    )
```

```python
import math

import jax
import jax.numpy as jnp
import numpy as np
from jax import lax
from jax.experimental import pallas as pl
from jax.experimental.pallas import tpu as pltpu
from jax.sharding import PartitionSpec as P

STEPS = 3
PAD = 144
EY = 8
EZ = 8
LANES = 128
SIDE = 33
FACE = SIDE * SIDE
BLOCKS = 26
ROWS = 8 * BLOCKS
WIDE = 64 * BLOCKS
JUMP = 4 * SIDE
WINDOW = 256

time_step = 0.03
step_square = 0.0009
relax_strength = (0.12, 0.08, 0.05)

F32 = jnp.float32
BF16 = jnp.bfloat16


def gll_tables():
    root_value = math.sqrt(3.0 / 7.0)
    points = [-1.0, -root_value, 0.0, root_value, 1.0]
    weights = [0.1, 49.0 / 90.0, 32.0 / 45.0, 49.0 / 90.0, 0.1]
    derivative = np.zeros((5, 5))
    for p in range(5):
        for a in range(5):
            accum = 0.0
            for m in range(5):
                if m != a:
                    factor = 1.0 / (points[a] - points[m])
                    for k in range(5):
                        if k != a and k != m:
                            factor = factor * (points[p] - points[k]) / (points[a] - points[k])
                    accum = accum + factor
            derivative[p, a] = accum
    return derivative.astype(np.float32).astype(np.float64), np.array(weights).astype(np.float32).astype(np.float64)


def node(a, b, d):
    return a * 25 + b * 5 + d


def place(a, b, d):
    return (b * 5 + d) * 8 + a


def make_tables():
    derivative, weights = gll_tables()
    grad = np.zeros((3 * 128, ROWS))
    force = np.zeros((ROWS, 3 * 128))
    for a in range(5):
        for b in range(5):
            for d in range(5):
                for m in range(5):
                    grad[node(a, b, d), place(m, b, d)] = derivative[a, m]
                    grad[128 + node(a, b, d), place(a, m, d)] = derivative[b, m]
                    grad[256 + node(a, b, d), place(a, b, m)] = derivative[d, m]
                    row = place(a, b, d)
                    force[row, node(m, b, d)] = -derivative[m, a] * weights[m] * weights[b] * weights[d]
                    force[row, 128 + node(a, m, d)] = -derivative[m, b] * weights[a] * weights[m] * weights[d]
                    force[row, 256 + node(a, b, m)] = -derivative[m, d] * weights[a] * weights[b] * weights[m]
    face = np.zeros((64, 3 * 128))
    face[0:25] = force[0:200:8]
    face[32:57] = force[4:200:8]
    collect = np.zeros((WIDE, WINDOW), np.float32)
    line = np.zeros(SIDE)
    for e in range(8):
        line[4 * e : 4 * e + 5] += weights
    layer = np.array([2 * weights[0], weights[1], weights[2], weights[3], 2 * weights[0], 1.0, 1.0, 1.0])
    mass = np.ones((ROWS, LANES), np.float32)
    for b in range(5):
        for d in range(5):
            for ey in range(8):
                for ez in range(8):
                    column = (b * 5 + d) * 64 + ey * 8 + ez
                    spot = b * SIDE + 4 * ez + d
                    if d < 4 or ez == 7:
                        collect[column, spot] = 1.0
                    for slab in range(2):
                        at = (b * 5 + d) * 8
                        mass[at : at + 8, slab * 64 + ey * 8 + ez] = layer * line[4 * ey + b] * line[4 * ez + d]
    return grad, force, face, collect, mass


def cut_table(table):
    value = table.astype(np.float32)
    pieces = []
    for _ in range(3):
        piece = value.astype(jnp.bfloat16)
        pieces.append(piece)
        value = value - piece.astype(np.float32)
    return np.stack(pieces)


GRAD, FORCE, FACES, COLLECT, MASS = make_tables()


def cut(value):
    high = value.astype(BF16)
    rest = value - high.astype(F32)
    middle = rest.astype(BF16)
    low = (rest - middle.astype(F32)).astype(BF16)
    return high, middle, low


def dot(left, right):
    return jnp.dot(left, right, preferred_element_type=F32)


def dot_six(table, value):
    rows = table.shape[1]
    stacked = table[...].reshape(3 * rows, table.shape[2])
    high, middle, low = cut(value)
    first = dot(stacked, high)
    second = dot(stacked[0 : 2 * rows], middle)
    small = first[2 * rows : 3 * rows] + second[rows : 2 * rows] + dot(stacked[0:rows], low)
    return first[0:rows] + (first[rows : 2 * rows] + second[0:rows] + small)


def dot_three(table, value):
    rows = table.shape[1]
    stacked = table[0:2].reshape(2 * rows, table.shape[2])
    high, middle, _ = cut(value)
    first = dot(stacked, high)
    return first[0:rows] + (first[rows : 2 * rows] + dot(stacked[0:rows], middle))


def lanes_of(shape):
    return lax.broadcasted_iota(jnp.int32, shape, len(shape) - 1)


def rolled(value, shift, axis):
    return pltpu.roll(value, shift % value.shape[axis], axis)


def window_rows(value, window_ref):
    for ey in range(EY):
        width = min(WINDOW, FACE - JUMP * ey)
        if width < WINDOW:
            window_ref[ey] = jnp.zeros(window_ref.shape[1:], F32)
        window_ref[ey, :, 0:width] = value[:, JUMP * ey : JUMP * ey + width]
    return window_ref[...].reshape(-1, WINDOW)


def to_columns(value, window_ref, spread_ref):
    rows = value.shape[0]
    pieces = jnp.concatenate(cut(window_rows(value, window_ref)), axis=0)
    wide = dot(pieces, spread_ref[...])
    half = EY * rows
    own = (lanes_of((rows, WIDE)) // 8) % 8
    picked = 0.0
    for ey in range(EY):
        at = slice(ey * rows, (ey + 1) * rows)
        value = wide[at] + wide[half : 2 * half][at] + wide[2 * half : 3 * half][at]
        picked = jnp.where(own == ey, value, picked)
    return picked


def assembled(blocks):
    lane = lanes_of((8, LANES))
    blocks = dict(blocks)
    for shift, at, pairs in (
        (1, lane % 8, [((b, 0), (b, 4)) for b in range(5)]),
        (8, (lane // 8) % 8, [((0, d), (4, d)) for d in range(5)]),
    ):
        for c in range(3):
            for near, far in pairs:
                first, last = blocks[(c,) + near], blocks[(c,) + far]
                blocks[(c,) + near] = first + jnp.where(at > 0, rolled(last, shift, 1), 0.0)
                blocks[(c,) + far] = last + jnp.where(at < 7, rolled(first, -shift, 1), 0.0)
    return blocks


def block_rows(b, d):
    return slice((b * 5 + d) * 8, (b * 5 + d) * 8 + 8)


def beside(value):
    return jnp.concatenate([value[0], value[1], value[2]], axis=1)


def gather_kernel(now_ref, prev_ref, density_ref, rim_ref, now_copy, prev_copy, density_copy, sems):
    copies = [
        pltpu.make_async_copy(now_ref.at[0], now_copy, sems.at[0]),
        pltpu.make_async_copy(prev_ref.at[0], prev_copy, sems.at[1]),
        pltpu.make_async_copy(density_ref, density_copy, sems.at[2]),
    ]
    for copy in copies:
        copy.start()
    for copy in copies:
        copy.wait()
    for c in range(3):
        rim_ref[c : c + 1, :] = now_copy[c, 0:1, :]
        rim_ref[3 + c : 4 + c, :] = prev_copy[c, 0:1, :]
    rim_ref[6:7, :] = density_copy[0:1, :]
    rim_ref[7:8, :] = density_copy[0:1, :]


def weighted_memory(memory_ref, decays, part, power):
    value = 0.0
    for l in range(3):
        factor = decays[l]
        for _ in range(power - 1):
            factor = factor * decays[l]
        value = value + factor * memory_ref[l, part]
    return value


def spread_table():
    column = lanes_of((1, WIDE))
    block = column // 64
    spot = (block // 5) * SIDE + (block % 5) + 4 * (column % 8)
    spot = jnp.where(block < 25, spot, WINDOW)
    return jnp.where(lax.broadcasted_iota(jnp.int32, (WINDOW, WIDE), 0) == spot, 1.0, 0.0).astype(BF16)


def prologue_kernel(now_ref, prev_ref, density_ref, memory_ref, decay_ref, mass_ref, *refs):
    u_ref, p_ref, scale_ref, m1_ref, spread_ref, window_ref = refs[-6:]
    spread_ref[...] = spread_table()
    rows = jnp.concatenate([now_ref[0].reshape(24, FACE), prev_ref[0].reshape(24, FACE), density_ref[...]], axis=0)
    columns = to_columns(rows, window_ref, spread_ref)
    lane = lanes_of((8, LANES))
    for group in range(7):
        for pair in range(BLOCKS // 2):
            tile = columns[8 * group : 8 * group + 8, LANES * pair : LANES * pair + LANES]
            swapped = rolled(tile, 64, 1)
            even = jnp.where(lane < 64, tile, rolled(swapped, 4, 0))
            odd = jnp.where(lane < 64, swapped, rolled(tile, 4, 0))
            for block, value in ((2 * pair, even), (2 * pair + 1, odd)):
                at = slice(8 * block, 8 * block + 8)
                if group < 3:
                    u_ref[group, at, :] = value
                elif group < 6:
                    p_ref[group - 3, at, :] = value
                elif block < 25:
                    scale_ref[at, :] = step_square / (value * mass_ref[at, :])
                else:
                    scale_ref[at, :] = jnp.zeros((8, LANES), F32)
    decays = [decay_ref[l : l + 1, :] for l in range(3)]
    for part in range(5):
        m1_ref[part] = weighted_memory(memory_ref, decays, part, 1)


def later_kernel(memory_ref, decay_ref, owner_ref, m2_ref, m3_ref, select_ref):
    decays = [decay_ref[l : l + 1, :] for l in range(3)]
    for part in range(5):
        m2_ref[part] = weighted_memory(memory_ref, decays, part, 2)
        m3_ref[part] = weighted_memory(memory_ref, decays, part, 3)
    owner = jnp.concatenate([owner_ref[0], owner_ref[1]], axis=1)
    named = jnp.where(lax.broadcasted_iota(jnp.int32, (16, LANES), 0) == owner, 1.0, 0.0)
    earlier = lax.broadcasted_iota(jnp.int32, (LANES, LANES), 0)
    later = lax.broadcasted_iota(jnp.int32, (LANES, LANES), 1)
    ahead = jnp.where((earlier < later) & ((earlier // 64) == (later // 64)), 1.0, 0.0)
    rank = jnp.sum(named * dot(named.astype(BF16), ahead.astype(BF16)), axis=0, keepdims=True).astype(jnp.int32)
    subs = select_ref.shape[0] // LANES
    slots = 4 * EY * EZ // subs
    row = lax.broadcasted_iota(jnp.int32, select_ref.shape, 0)
    toward = (row // LANES) ^ lax.axis_index("sub")
    wanted = (lanes_of((1, LANES)) // 64) * (slots // 2) + rank
    chosen = (owner == toward) & (wanted == row % slots)
    select_ref[...] = jnp.where(chosen, 1.0, 0.0).astype(BF16)


def rim_kernel(rim_ref, u_in, p_in, scale_in, spread_ref, mass_ref, u_ref, p_ref, scale_ref, low_ref, window_ref, rows_ref):
    columns = to_columns(rim_ref[...], window_ref, spread_ref)
    for pair in range(BLOCKS // 2):
        tile = columns[:, LANES * pair : LANES * pair + LANES]
        rows_ref[16 * pair : 16 * pair + 8, :] = rolled(tile, 64, 1)
        rows_ref[16 * pair + 8 : 16 * pair + 16, :] = tile
    u_ref[...] = u_in[...]
    p_ref[...] = p_in[...]
    scale_ref[...] = scale_in[...]
    upper = lanes_of((25, LANES)) >= 64
    last = pl.ds(4, 25, stride=8)
    for c in range(3):
        u_ref[c, last, :] = jnp.where(upper, rows_ref[pl.ds(c, 25, stride=8), :], u_ref[c, last, :])
        p_ref[c, last, :] = jnp.where(upper, rows_ref[pl.ds(3 + c, 25, stride=8), :], p_ref[c, last, :])
    rim = step_square / (rows_ref[pl.ds(6, 25, stride=8), :] * mass_ref[last, :])
    scale_ref[last, :] = jnp.where(upper, rim, scale_ref[last, :])
    low_ref[...] = u_ref[...].astype(BF16)


def strains(grad, rows):
    def at(direction, c):
        return grad[direction * 128 + rows.start : direction * 128 + rows.stop, c * LANES : (c + 1) * LANES]

    return [
        at(0, 0),
        at(1, 1),
        at(2, 2),
        0.5 * (at(1, 0) + at(0, 1)),
        0.5 * (at(2, 0) + at(0, 2)),
        0.5 * (at(2, 1) + at(1, 2)),
    ]


CHUNKS = [slice(0, 32), slice(32, 64), slice(64, 96), slice(96, 125)]


def pack_face(face, upper):
    parts = [face[:, c * LANES : (c + 1) * LANES] for c in range(3)]
    lower_lane = lanes_of((16, LANES)) < 64
    lower_lanes = lanes_of((32, LANES)) < 64
    if upper:
        first = jnp.where(lower_lanes, rolled(parts[0], 64, 1), parts[1])
        second = jnp.where(lower_lane, rolled(parts[2][0:16], 64, 1), parts[2][16:32])
    else:
        first = jnp.where(lower_lanes, parts[0], rolled(parts[1], 64, 1))
        second = jnp.where(lower_lane, parts[2][0:16], rolled(parts[2][16:32], 64, 1))
    return jnp.concatenate([first, second], axis=0)


def step_kernel(step, *refs):
    u_ref, lame_ref, mu_ref, m_ref, decay_ref, grad_table, face_table = refs[0:7]
    older = refs[7 : 7 + step]
    refs = refs[7 + step :]
    strain_ref, sigma_ref, even_ref = refs[0:3]
    odd_ref, keep_ref = refs[3:5] if step < STEPS - 1 else (None, None)
    grad_ref = refs[-1]
    grad_ref[...] = dot_six(grad_table, beside(u_ref))
    for block in range(9):
        sigma_ref[(block // 3) * 128 + 120 : (block // 3) * 128 + 128, (block % 3) * LANES : (block % 3) * LANES + LANES] = (
            jnp.zeros((8, LANES), F32)
        )
    decays = [decay_ref[l : l + 1, :] for l in range(3)]
    shares = [(1.0 - decays[l]) * relax_strength[l] for l in range(3)]
    factors = []
    for _ in range(step + 1):
        factors.append(shares[0] + shares[1] + shares[2])
        shares = [decays[l] * shares[l] for l in range(3)]
    for rows in CHUNKS:
        strain = strains(grad_ref, rows)
        for part in range(6):
            strain_ref[part, rows, :] = strain[part]
        lame = lame_ref[rows, :]
        twice_mu = 2.0 * mu_ref[rows, :]
        trace = strain[0] + strain[1] + strain[2]
        third = trace * (1.0 / 3.0)
        pulls = [twice_mu * s for s in strain]
        pull_third = twice_mu * third
        fresh = [pulls[0] - pull_third, pulls[1] - pull_third, pulls[3], pulls[4], pulls[5]]
        relax = []
        for part in range(5):
            value = m_ref[part, rows, :] + factors[0] * fresh[part]
            for back in range(step):
                value = value + factors[back + 1] * older[step - 1 - back][part, rows, :]
            relax.append(value)
            if keep_ref is not None:
                keep_ref[part, rows, :] = fresh[part]
        bulk = lame * trace
        xx = bulk + pulls[0] - relax[0]
        yy = bulk + pulls[1] - relax[1]
        zz = bulk + pulls[2] + relax[0] + relax[1]
        xy = pulls[3] - relax[2]
        xz = pulls[4] - relax[3]
        yz = pulls[5] - relax[4]
        for direction, values in enumerate(((xx, xy, xz), (xy, yy, yz), (xz, yz, zz))):
            for c in range(3):
                sigma_ref[direction * 128 + rows.start : direction * 128 + rows.stop, c * LANES : (c + 1) * LANES] = values[c]
    faces = dot_three(face_table, sigma_ref[...])
    first, last = pack_face(faces[0:32], False), pack_face(faces[32:64], True)
    if step < STEPS - 1:
        even_ring = lax.axis_index(("cuts", "sub")) % 2 == 0
        odd_ref[...] = jnp.where(even_ring, first, last)
        even_ref[...] = jnp.where(even_ring, last, first)
    else:
        even_ref[0:48, :] = last
        even_ref[48:, :] = jnp.zeros((even_ref.shape[0] - 48, LANES), F32)


def rest_kernel(sigma_ref, u_ref, p_ref, scale_ref, force_table, next_ref):
    force = dot_three(force_table, sigma_ref[...])
    blocks = {}
    for c in range(3):
        for b in range(5):
            for d in range(5):
                blocks[(c, b, d)] = force[block_rows(b, d), c * LANES : (c + 1) * LANES]
    blocks = assembled(blocks)
    lane = lanes_of((8, LANES))
    sub = lax.broadcasted_iota(jnp.int32, (8, LANES), 0)
    inner = ((sub == 4) & (lane < 64)) | ((sub == 0) & (lane >= 64))
    for c in range(3):
        for b in range(5):
            for d in range(5):
                value = blocks[(c, b, d)]
                value = value + jnp.where(inner, rolled(rolled(value, 4, 0), 64, 1), 0.0)
                at = block_rows(b, d)
                next_ref[c, at, :] = 2.0 * u_ref[c, at, :] - p_ref[c, at, :] + scale_ref[at, :] * value
        next_ref[c, 200:208, :] = jnp.zeros((8, LANES), F32)


def add_faces(from_before, from_after, partial_ref, scale_ref, u_ref, delta_ref):
    delta_ref[...] = jnp.zeros(delta_ref.shape, F32)
    lower = lanes_of((25, LANES)) < 64
    if from_before is not None:
        packed = from_before
        turned = rolled(packed, 64, 1)
        values = [packed[0:32], turned[0:32], jnp.concatenate([packed[32:48], turned[32:48]], axis=0)]
        for c in range(3):
            delta_ref[c, pl.ds(0, 25, stride=8), :] = jnp.where(lower, values[c][0:25], 0.0)
    if from_after is not None:
        packed = from_after
        turned = rolled(packed, 64, 1)
        values = [turned[0:32], packed[0:32], jnp.concatenate([turned[32:48], packed[32:48]], axis=0)]
        for c in range(3):
            delta_ref[c, pl.ds(4, 25, stride=8), :] = jnp.where(lower, 0.0, values[c][0:25])
    blocks = {}
    for c in range(3):
        for b in range(5):
            for d in range(5):
                blocks[(c, b, d)] = delta_ref[c, block_rows(b, d), :]
    blocks = assembled(blocks)
    for c in range(3):
        for b in range(5):
            for d in range(5):
                at = block_rows(b, d)
                u_ref[c, at, :] = partial_ref[c, at, :] + scale_ref[at, :] * blocks[(c, b, d)]
        u_ref[c, 200:208, :] = jnp.zeros((8, LANES), F32)


def update_kernel(odd_ref, even_ref, partial_ref, scale_ref, u_ref, low_ref, delta_ref):
    even_ring = lax.axis_index(("cuts", "sub")) % 2 == 0
    odd, even = odd_ref[...], even_ref[...]
    before, after = jnp.where(even_ring, odd, even), jnp.where(even_ring, even, odd)
    add_faces(before, after, partial_ref, scale_ref, u_ref, delta_ref)
    low_ref[...] = u_ref[...].astype(BF16)


def kernel_parts(strain_ref, low_ref, far_ref, lame_ref, mu_ref, grad_table, grad_ref, kernel_ref):
    forward = jnp.where(lax.axis_index("group") == 0, beside(low_ref), beside(far_ref))
    grads = dot(grad_table[...].reshape(3 * 384, ROWS), forward)
    grad_ref[...] = grads[0:384] + (grads[384:768] + grads[768:1152])
    for rows in CHUNKS:
        far = strains(grad_ref, rows)
        own = [strain_ref[part, rows, :] for part in range(6)]
        trace_own = own[0] + own[1] + own[2]
        trace_far = far[0] + far[1] + far[2]
        third_own, third_far = trace_own * (1.0 / 3.0), trace_far * (1.0 / 3.0)
        twice_mu = 2.0 * mu_ref[rows, :]
        kappa = lame_ref[rows, :] + twice_mu * (1.0 / 3.0)
        kernel_ref[rows, :] = time_step * kappa * trace_far * trace_own
        product = (
            (own[0] - third_own) * (far[0] - third_far)
            + (own[1] - third_own) * (far[1] - third_far)
            + (own[2] - third_own) * (far[2] - third_far)
            + 2.0 * (own[3] * far[3] + own[4] * far[4] + own[5] * far[5])
        )
        kernel_ref[125 + rows.start : 125 + rows.stop, :] = time_step * twice_mu * product
    kernel_ref[250:256, :] = jnp.zeros((6, LANES), F32)
    return kernel_ref[...].astype(BF16)


def parts_kernel(
    strain_ref, low_ref, far_ref, lame_ref, mu_ref, grad_table, part_ref, grad_ref, kernel_ref
):
    part_ref[...] = kernel_parts(
        strain_ref, low_ref, far_ref, lame_ref, mu_ref, grad_table, grad_ref, kernel_ref
    )


def send_kernel(
    strain_ref, low_ref, far_ref, lame_ref, mu_ref, grad_table, one_ref, two_ref, select_ref, *refs
):
    out_refs, (grad_ref, kernel_ref) = refs[:-2], refs[-2:]
    three = kernel_parts(strain_ref, low_ref, far_ref, lame_ref, mu_ref, grad_table, grad_ref, kernel_ref)
    rows = out_refs[0].shape[0]
    slots = rows // 2
    group = lanes_of((rows, LANES)) // slots
    over_lanes = (((1,), (1,)), ((), ()))
    for k, ref in enumerate(out_refs):
        chosen = select_ref[k * LANES : (k + 1) * LANES, :]
        total = 0.0
        for part in (one_ref[...], two_ref[...], three):
            total = total + lax.dot_general(part, chosen, over_lanes, preferred_element_type=F32)
        value = total[0:rows]
        for j in range(1, 256 // rows):
            value = jnp.where(group == j, total[j * rows : (j + 1) * rows], value)
        ref[...] = value


def sum_kernel(*refs):
    in_refs, out_ref = refs[:-1], refs[-1]
    rows = in_refs[0].shape[0]
    slots = rows // 2
    pieces = 256 // rows
    group = lanes_of((rows, LANES)) // slots
    blocks = [[jnp.zeros((rows, LANES), F32)] * 2 for _ in range(pieces)]
    for k, ref in enumerate(in_refs):
        source = lax.axis_index("sub") ^ k
        spot = source % pieces
        value = ref[...]
        for j in range(pieces):
            moved = pltpu.roll(value, ((spot + pieces - j) % pieces) * slots, 1)
            for t in range(2):
                here = (group == spot) & (source // pieces == t)
                blocks[j][t] = jnp.where(here, moved, blocks[j][t])
    value = jnp.concatenate([jnp.concatenate(row, axis=1) for row in blocks], axis=0)
    out_ref[:, 0, :] = value[0:250]


def finish_kernel(before_ref, partial_ref, scale_ref, collect_ref, out_ref, u_ref, delta_ref):
    add_faces(before_ref[0:48], None, partial_ref, scale_ref, u_ref, delta_ref)
    lane = lanes_of((8, LANES))
    sub = lax.broadcasted_iota(jnp.int32, (8, LANES), 0)
    tiles = []
    for c in range(3):
        row = []
        for pair in range(BLOCKS // 2):
            even = u_ref[c, 16 * pair : 16 * pair + 8, :]
            odd = u_ref[c, 16 * pair + 8 : 16 * pair + 16, :]
            low = jnp.where(sub < 4, even, rolled(rolled(even, 64, 1), 4, 0))
            high = jnp.where(sub < 4, rolled(odd, 64, 1), rolled(odd, 4, 0))
            row.append(jnp.where(lane < 64, low, high))
        tiles.append(jnp.concatenate(row, axis=1))
    columns = jnp.concatenate(tiles, axis=0)
    own = (lanes_of((24, WIDE)) // 8) % 8
    spread = jnp.concatenate([jnp.where(own == ey, columns, 0.0) for ey in range(EY)], axis=0)
    high, middle, low = cut(spread)
    collect = collect_ref[...]
    windows = dot(high, collect) + dot(middle, collect) + dot(low, collect)
    for ey in range(EY):
        width = JUMP if ey < EY - 1 else JUMP + SIDE
        for c in range(3):
            out_ref[0, c, :, JUMP * ey : JUMP * ey + width] = windows[24 * ey + 8 * c : 24 * ey + 8 * c + 8, 0:width]


VMEM = pl.BlockSpec(memory_space=pltpu.VMEM)
HBM = pl.BlockSpec(memory_space=pltpu.HBM)


def shaped(*shape, dtype=F32):
    return jax.ShapeDtypeStruct(shape, dtype)


def call(kernel, name, outs, scratch, *args, outside=(), micros=1, room=32 * 1024):
    return pl.pallas_call(
        kernel,
        name=name,
        out_shape=outs,
        in_specs=[HBM if at in outside else VMEM for at in range(len(args))],
        out_specs=jax.tree.map(lambda _: VMEM, outs),
        scratch_shapes=scratch,
        compiler_params=pltpu.CompilerParams(vmem_limit_bytes=room * 1024),
        cost_estimate=pl.CostEstimate(flops=0, bytes_accessed=micros * 3000000, transcendentals=0),
    )(*args)


def passed_along(value, axis, steps):
    count = lax.axis_size(axis)
    return lax.ppermute(value, axis, [(source, (source + steps) % count) for source in range(count)])


def swapped(value, axis, first):
    count = lax.axis_size(axis)
    pairs = []
    for source in range(first, count, 2):
        other = (source + 1) % count
        pairs += [(source, other), (other, source)]
    return lax.ppermute(value, axis, pairs)


def far_field(low, groups):
    far = None
    for k in range(1, groups):
        moved = passed_along(low, "group", k)
        far = moved if far is None else jnp.where(lax.axis_index("group") == k, moved, far)
    return far


def per_device(disp_now, disp_prev, memory_init, density, lame_lambda, shear_mu, sls_decay, owner_map):
    ring = ("cuts", "sub")
    subs = lax.axis_size("sub")
    groups = lax.axis_size("group")

    rim = call(
        gather_kernel, "gather", shaped(8, FACE),
        [pltpu.VMEM((3, 8, FACE), F32)] * 2 + [pltpu.VMEM((8, FACE), F32), pltpu.SemaphoreType.DMA((3,))],
        disp_now, disp_prev, density, outside=(0, 1, 2), room=54 * 1024 - 120,
    )
    rim = passed_along(rim, ring, -1)

    grad_table = jnp.asarray(cut_table(GRAD))
    force_table = jnp.asarray(cut_table(FORCE))
    face_table = jnp.asarray(cut_table(FACES))
    collect = jnp.asarray(COLLECT, BF16)
    mass = jnp.asarray(MASS)
    memory = memory_init[0]
    owner = jnp.transpose(owner_map, (0, 2, 1))

    state = shaped(3, ROWS, LANES)
    state_low = shaped(3, ROWS, LANES, dtype=BF16)
    scale_shape = shaped(ROWS, LANES)
    five = shaped(5, 125, LANES)
    part_shape = shaped(256, LANES, dtype=BF16)
    grad_scratch = pltpu.VMEM((384, 384), F32)
    part_scratch = [grad_scratch, pltpu.VMEM((256, LANES), F32)]
    face = shaped(48, LANES)
    window_scratch = [pltpu.VMEM((8, 8, WINDOW), F32), pltpu.VMEM((ROWS, LANES), F32)]
    u, p, scale, m1, spread = call(
        prologue_kernel, "prologue", [state, state, scale_shape, five, shaped(WINDOW, WIDE, dtype=BF16)],
        [pltpu.VMEM((8, 56, WINDOW), F32)],
        disp_now, disp_prev, density, memory, sls_decay, mass, grad_table, face_table, force_table, lame_lambda, shear_mu,
    )
    u, p, scale, low = call(
        rim_kernel, "rim", [state, state, scale_shape, state_low], window_scratch, rim, u, p, scale, spread, mass
    )
    memories = [m1]
    kept = []
    parts = []
    for step in range(STEPS):
        if step == STEPS - 1:
            far = far_field(low, groups)
        outs = [shaped(6, 125, LANES), shaped(384, 384), face if step < STEPS - 1 else shaped(PAD, LANES)]
        if step < STEPS - 1:
            outs += [face, five]
        results = call(
            lambda *refs, step=step: step_kernel(step, *refs), "step", outs, [grad_scratch],
            u, lame_lambda, shear_mu, memories[step], sls_decay, grad_table, face_table, *kept,
        )
        strain, sigma, even = results[0:3]
        if step < STEPS - 1:
            odd = results[3]
            kept.append(results[4])
            odd = swapped(odd, ring, 1)
            even = swapped(even, ring, 0)
        else:
            before = passed_along(even, ring, 1)
        partial = call(rest_kernel, "rest", state, [], sigma, u, p, scale, force_table)
        if step < STEPS - 1:
            low, sigma = lax.optimization_barrier((low, sigma))
            far = far_field(low, groups)
        shared = (strain, low, far, lame_lambda, shear_mu, grad_table)
        if step < STEPS - 1:
            parts.append(call(parts_kernel, "parts", part_shape, part_scratch, *shared))
            if step == 0:
                m2, m3, select = call(
                    later_kernel, "later", [five, five, shaped(subs * LANES, LANES, dtype=BF16)], [],
                    memory, sls_decay, owner,
                )
                memories += [m2, m3]
                partial, parts[0], select, memories[2] = lax.optimization_barrier((partial, parts[0], select, m3))
            else:
                partial, parts[1] = lax.optimization_barrier((partial, parts[1]))
            p = u
            u, low = call(
                update_kernel, "update", [state, state_low], [pltpu.VMEM((3, ROWS, LANES), F32)],
                odd, even, partial, scale,
            )
        else:
            sent = list(call(
                send_kernel, "send", [shaped(512 // subs, LANES)] * subs, part_scratch, *shared, *parts, select)
            )
            for k in range(subs - 1, 0, -1):
                sent[k] = lax.ppermute(sent[k], "sub", [(j, j ^ k) for j in range(subs)])
    final = call(
        finish_kernel, "finish", shaped(1, 3, 8, FACE),
        [pltpu.VMEM((3, ROWS, LANES), F32), pltpu.VMEM((3, ROWS, LANES), F32)],
        before, partial, scale, collect, micros=20,
    )
    kernels = call(sum_kernel, "sum", shaped(250, 1, 256), [], *sent)
    return final, jnp.transpose(kernels, (1, 2, 0))


def solution(mesh):
    in_specs = (
        P("group", None, ("cuts", "sub"), None),
        P("group", None, ("cuts", "sub"), None),
        P("group", None, None, None, ("cuts", "sub")),
        P(("cuts", "sub"), None),
        P(None, ("cuts", "sub")),
        P(None, ("cuts", "sub")),
        P(None, ("cuts", "sub")),
        P(("cuts", "sub"), None, None),
    )
    out_specs = (P("group", None, ("cuts", "sub"), None), P("group", ("cuts", "sub"), None))
    return jax.shard_map(
        per_device, mesh=mesh, in_specs=in_specs, out_specs=out_specs, check_vma=False
    )
```

```python
import math

import jax
import jax.numpy as jnp
import numpy as np
from jax import lax
from jax.experimental import pallas as pl
from jax.experimental.pallas import tpu as pltpu
from jax.sharding import PartitionSpec as P

STEPS = 3
PAD = 136
EY = 8
EZ = 8
LANES = 128
SIDE = 33
FACE = SIDE * SIDE
BLOCKS = 26
ROWS = 8 * BLOCKS
WIDE = 64 * BLOCKS
JUMP = 4 * SIDE
WINDOW = 256

time_step = 0.03
step_square = 0.0009
relax_strength = (0.12, 0.08, 0.05)

F32 = jnp.float32
BF16 = jnp.bfloat16


def gll_tables():
    root_value = math.sqrt(3.0 / 7.0)
    points = [-1.0, -root_value, 0.0, root_value, 1.0]
    weights = [0.1, 49.0 / 90.0, 32.0 / 45.0, 49.0 / 90.0, 0.1]
    derivative = np.zeros((5, 5))
    for p in range(5):
        for a in range(5):
            accum = 0.0
            for m in range(5):
                if m != a:
                    factor = 1.0 / (points[a] - points[m])
                    for k in range(5):
                        if k != a and k != m:
                            factor = factor * (points[p] - points[k]) / (points[a] - points[k])
                    accum = accum + factor
            derivative[p, a] = accum
    return derivative.astype(np.float32).astype(np.float64), np.array(weights).astype(np.float32).astype(np.float64)


def node(a, b, d):
    return a * 25 + b * 5 + d


def place(a, b, d):
    return (b * 5 + d) * 8 + a


def make_tables():
    derivative, weights = gll_tables()
    grad = np.zeros((3 * 128, 128))
    force = np.zeros((ROWS, 3 * 128))
    for a in range(5):
        for b in range(5):
            for d in range(5):
                for m in range(5):
                    grad[node(a, b, d), node(m, b, d)] = derivative[a, m]
                    grad[128 + node(a, b, d), node(a, m, d)] = derivative[b, m]
                    grad[256 + node(a, b, d), node(a, b, m)] = derivative[d, m]
                    row = place(a, b, d)
                    force[row, node(m, b, d)] = -derivative[m, a] * weights[m] * weights[b] * weights[d]
                    force[row, 128 + node(a, m, d)] = -derivative[m, b] * weights[a] * weights[m] * weights[d]
                    force[row, 256 + node(a, b, m)] = -derivative[m, d] * weights[a] * weights[b] * weights[m]
    face = np.zeros((64, 3 * 128))
    face[0:25] = force[0:200:8]
    face[32:57] = force[4:200:8]
    line = np.zeros(SIDE)
    for e in range(8):
        line[4 * e : 4 * e + 5] += weights
    layer = np.array([2 * weights[0], weights[1], weights[2], weights[3], 2 * weights[0], 1.0, 1.0, 1.0])
    mass = np.ones((ROWS, LANES), np.float32)
    for b in range(5):
        for d in range(5):
            for ey in range(8):
                for ez in range(8):
                    for slab in range(2):
                        at = (b * 5 + d) * 8
                        mass[at : at + 8, slab * 64 + ey * 8 + ez] = layer * line[4 * ey + b] * line[4 * ez + d]
    face_mass = (layer[0] * np.outer(line, line)).reshape(1, FACE).astype(np.float32)
    return grad, force, face, mass, face_mass


def side_by_side(table):
    high, middle, low = cut_table(table)
    pairs = ((high, middle), (middle, high), (low, high))
    return np.stack([np.concatenate(pair, axis=1) for pair in pairs])


def cut_table(table):
    value = table.astype(np.float32)
    pieces = []
    for _ in range(3):
        piece = value.astype(jnp.bfloat16)
        pieces.append(piece)
        value = value - piece.astype(np.float32)
    return np.stack(pieces)


GRAD, FORCE, FACES, MASS, FACE_MASS = make_tables()


def cut(value):
    high = value.astype(BF16)
    rest = value - high.astype(F32)
    middle = rest.astype(BF16)
    low = (rest - middle.astype(F32)).astype(BF16)
    return high, middle, low


def dot(left, right):
    return jnp.dot(left, right, preferred_element_type=F32)


def gradients(table, flat):
    high, middle, low = cut(flat)
    first = dot(table[0:2].reshape(768, 256), jnp.concatenate([high, middle], axis=0))
    return first[0:384] + (first[384:768] + dot(table[2], jnp.concatenate([high, low], axis=0)))


def low_gradients(table, low):
    return dot(table[0], jnp.concatenate([low, low], axis=0)) + dot(table[2, :, 0:128], low)


def flatten(u_ref, flat_ref):
    for c in range(3):
        flat_ref[c, 120:128, :] = jnp.zeros((8, LANES), F32)
        for a in range(5):
            flat_ref[c, 25 * a : 25 * a + 25, :] = u_ref[c, pl.ds(a, 25, stride=8), :]


def dot_three(table, value):
    rows = table.shape[1]
    stacked = table[0:2].reshape(2 * rows, table.shape[2])
    high, middle, _ = cut(value)
    first = dot(stacked, high)
    return first[0:rows] + (first[rows : 2 * rows] + dot(stacked[0:rows], middle))


def lanes_of(shape):
    return lax.broadcasted_iota(jnp.int32, shape, len(shape) - 1)


def rolled(value, shift, axis):
    return pltpu.roll(value, shift % value.shape[axis], axis)


def window_rows(value, window_ref):
    for ey in range(EY):
        width = min(WINDOW, FACE - JUMP * ey)
        if width < WINDOW:
            window_ref[ey] = jnp.zeros(window_ref.shape[1:], F32)
        window_ref[ey, :, 0:width] = value[:, JUMP * ey : JUMP * ey + width]
    return window_ref[...].reshape(-1, WINDOW)


def to_columns(value, window_ref, spread_ref):
    rows = value.shape[0]
    pieces = jnp.concatenate(cut(window_rows(value, window_ref)), axis=0)
    wide = dot(pieces, spread_ref[...])
    half = EY * rows
    own = (lanes_of((rows, WIDE)) // 8) % 8
    picked = 0.0
    for ey in range(EY):
        at = slice(ey * rows, (ey + 1) * rows)
        value = wide[at] + wide[half : 2 * half][at] + wide[2 * half : 3 * half][at]
        picked = jnp.where(own == ey, value, picked)
    return picked


def assembled(blocks):
    lane = lanes_of((8, LANES))
    blocks = dict(blocks)
    for shift, at, pairs in (
        (1, lane % 8, [((b, 0), (b, 4)) for b in range(5)]),
        (8, (lane // 8) % 8, [((0, d), (4, d)) for d in range(5)]),
    ):
        for c in range(3):
            for near, far in pairs:
                first, last = blocks[(c,) + near], blocks[(c,) + far]
                blocks[(c,) + near] = first + jnp.where(at > 0, rolled(last, shift, 1), 0.0)
                blocks[(c,) + far] = last + jnp.where(at < 7, rolled(first, -shift, 1), 0.0)
    return blocks


def block_rows(b, d):
    return slice((b * 5 + d) * 8, (b * 5 + d) * 8 + 8)


def beside(value):
    return jnp.concatenate([value[0], value[1], value[2]], axis=1)


def gather_kernel(now_ref, prev_ref, density_ref, rim_ref, now_copy, prev_copy, density_copy, sems):
    copies = [
        pltpu.make_async_copy(now_ref.at[0], now_copy, sems.at[0]),
        pltpu.make_async_copy(prev_ref.at[0], prev_copy, sems.at[1]),
        pltpu.make_async_copy(density_ref, density_copy, sems.at[2]),
    ]
    for copy in copies:
        copy.start()
    for copy in copies:
        copy.wait()
    for c in range(3):
        rim_ref[c : c + 1, :] = now_copy[c, 0:1, :]
        rim_ref[3 + c : 4 + c, :] = prev_copy[c, 0:1, :]
    rim_ref[6:7, :] = density_copy[0:1, :]
    rim_ref[7:8, :] = density_copy[0:1, :]


def weighted_memory(memory_ref, decays, part, power):
    value = 0.0
    for l in range(3):
        factor = decays[l]
        for _ in range(power - 1):
            factor = factor * decays[l]
        value = value + factor * memory_ref[l, part]
    return value


def spread_table():
    column = lanes_of((1, WIDE))
    block = column // 64
    spot = (block // 5) * SIDE + (block % 5) + 4 * (column % 8)
    spot = jnp.where(block < 25, spot, WINDOW)
    return jnp.where(lax.broadcasted_iota(jnp.int32, (WINDOW, WIDE), 0) == spot, 1.0, 0.0).astype(BF16)


def prologue_kernel(now_ref, prev_ref, density_ref, memory_ref, decay_ref, mass_ref, *refs):
    u_ref, p_ref, scale_ref, m1_ref, spread_ref, window_ref = refs[-6:]
    spread_ref[...] = spread_table()
    rows = jnp.concatenate([now_ref[0].reshape(24, FACE), prev_ref[0].reshape(24, FACE), density_ref[...]], axis=0)
    columns = to_columns(rows, window_ref, spread_ref)
    lane = lanes_of((8, LANES))
    for group in range(7):
        for pair in range(BLOCKS // 2):
            tile = columns[8 * group : 8 * group + 8, LANES * pair : LANES * pair + LANES]
            swapped = rolled(tile, 64, 1)
            even = jnp.where(lane < 64, tile, rolled(swapped, 4, 0))
            odd = jnp.where(lane < 64, swapped, rolled(tile, 4, 0))
            for block, value in ((2 * pair, even), (2 * pair + 1, odd)):
                at = slice(8 * block, 8 * block + 8)
                if group < 3:
                    u_ref[group, at, :] = value
                elif group < 6:
                    p_ref[group - 3, at, :] = value
                elif block < 25:
                    scale_ref[at, :] = step_square / (value * mass_ref[at, :])
                else:
                    scale_ref[at, :] = jnp.zeros((8, LANES), F32)
    decays = [decay_ref[l : l + 1, :] for l in range(3)]
    for part in range(5):
        m1_ref[part] = weighted_memory(memory_ref, decays, part, 1)


def later_kernel(memory_ref, decay_ref, owner_ref, m2_ref, m3_ref, select_ref):
    decays = [decay_ref[l : l + 1, :] for l in range(3)]
    for part in range(5):
        m2_ref[part] = weighted_memory(memory_ref, decays, part, 2)
        m3_ref[part] = weighted_memory(memory_ref, decays, part, 3)
    owner = jnp.concatenate([owner_ref[0], owner_ref[1]], axis=1)
    named = jnp.where(lax.broadcasted_iota(jnp.int32, (16, LANES), 0) == owner, 1.0, 0.0)
    earlier = lax.broadcasted_iota(jnp.int32, (LANES, LANES), 0)
    later = lax.broadcasted_iota(jnp.int32, (LANES, LANES), 1)
    ahead = jnp.where((earlier < later) & ((earlier // 64) == (later // 64)), 1.0, 0.0)
    rank = jnp.sum(named * dot(named.astype(BF16), ahead.astype(BF16)), axis=0, keepdims=True).astype(jnp.int32)
    subs = select_ref.shape[0] // LANES
    slots = 4 * EY * EZ // subs
    row = lax.broadcasted_iota(jnp.int32, select_ref.shape, 0)
    toward = (row // LANES) ^ lax.axis_index("sub")
    wanted = (lanes_of((1, LANES)) // 64) * (slots // 2) + rank
    chosen = (owner == toward) & (wanted == row % slots)
    select_ref[...] = jnp.where(chosen, 1.0, 0.0).astype(BF16)


def rim_kernel(rim_ref, u_in, p_in, scale_in, spread_ref, mass_ref, u_ref, p_ref, scale_ref, flat_ref, low_ref, window_ref, rows_ref):
    columns = to_columns(rim_ref[...], window_ref, spread_ref)
    for pair in range(BLOCKS // 2):
        tile = columns[:, LANES * pair : LANES * pair + LANES]
        rows_ref[16 * pair : 16 * pair + 8, :] = rolled(tile, 64, 1)
        rows_ref[16 * pair + 8 : 16 * pair + 16, :] = tile
    u_ref[...] = u_in[...]
    p_ref[...] = p_in[...]
    scale_ref[...] = scale_in[...]
    upper = lanes_of((25, LANES)) >= 64
    last = pl.ds(4, 25, stride=8)
    for c in range(3):
        u_ref[c, last, :] = jnp.where(upper, rows_ref[pl.ds(c, 25, stride=8), :], u_ref[c, last, :])
        p_ref[c, last, :] = jnp.where(upper, rows_ref[pl.ds(3 + c, 25, stride=8), :], p_ref[c, last, :])
    rim = step_square / (rows_ref[pl.ds(6, 25, stride=8), :] * mass_ref[last, :])
    scale_ref[last, :] = jnp.where(upper, rim, scale_ref[last, :])
    flatten(u_ref, flat_ref)
    low_ref[...] = flat_ref[...].astype(BF16)


def strains(grad, rows):
    def at(direction, c):
        return grad[direction * 128 + rows.start : direction * 128 + rows.stop, c * LANES : (c + 1) * LANES]

    return [
        at(0, 0),
        at(1, 1),
        at(2, 2),
        0.5 * (at(1, 0) + at(0, 1)),
        0.5 * (at(2, 0) + at(0, 2)),
        0.5 * (at(2, 1) + at(1, 2)),
    ]


CHUNKS = [slice(0, 32), slice(32, 64), slice(64, 96), slice(96, 125)]


def pack_face(face, upper):
    parts = [face[:, c * LANES : (c + 1) * LANES] for c in range(3)]
    lower_lane = lanes_of((16, LANES)) < 64
    lower_lanes = lanes_of((32, LANES)) < 64
    if upper:
        first = jnp.where(lower_lanes, rolled(parts[0], 64, 1), parts[1])
        second = jnp.where(lower_lane, rolled(parts[2][0:16], 64, 1), parts[2][16:32])
    else:
        first = jnp.where(lower_lanes, parts[0], rolled(parts[1], 64, 1))
        second = jnp.where(lower_lane, parts[2][0:16], rolled(parts[2][16:32], 64, 1))
    return jnp.concatenate([first, second], axis=0)


def step_kernel(step, *refs):
    flat_ref, lame_ref, mu_ref, m_ref, decay_ref, grad_table, face_table = refs[0:7]
    older = refs[7 : 7 + step]
    refs = refs[7 + step :]
    strain_ref, sigma_ref, even_ref = refs[0:3]
    odd_ref, keep_ref = refs[3:5] if step < STEPS - 1 else (None, None)
    grad_ref = refs[-1]
    grad_ref[...] = gradients(grad_table, beside(flat_ref))
    for block in range(9):
        sigma_ref[(block // 3) * 128 + 120 : (block // 3) * 128 + 128, (block % 3) * LANES : (block % 3) * LANES + LANES] = (
            jnp.zeros((8, LANES), F32)
        )
    decays = [decay_ref[l : l + 1, :] for l in range(3)]
    shares = [(1.0 - decays[l]) * relax_strength[l] for l in range(3)]
    factors = []
    for _ in range(step + 1):
        factors.append(shares[0] + shares[1] + shares[2])
        shares = [decays[l] * shares[l] for l in range(3)]
    for rows in CHUNKS:
        strain = strains(grad_ref, rows)
        for part in range(6):
            strain_ref[part, rows, :] = strain[part]
        lame = lame_ref[rows, :]
        twice_mu = 2.0 * mu_ref[rows, :]
        trace = strain[0] + strain[1] + strain[2]
        third = trace * (1.0 / 3.0)
        pulls = [twice_mu * s for s in strain]
        pull_third = twice_mu * third
        fresh = [pulls[0] - pull_third, pulls[1] - pull_third, pulls[3], pulls[4], pulls[5]]
        relax = []
        for part in range(5):
            value = m_ref[part, rows, :] + factors[0] * fresh[part]
            for back in range(step):
                value = value + factors[back + 1] * older[step - 1 - back][part, rows, :]
            relax.append(value)
            if keep_ref is not None:
                keep_ref[part, rows, :] = fresh[part]
        bulk = lame * trace
        xx = bulk + pulls[0] - relax[0]
        yy = bulk + pulls[1] - relax[1]
        zz = bulk + pulls[2] + relax[0] + relax[1]
        xy = pulls[3] - relax[2]
        xz = pulls[4] - relax[3]
        yz = pulls[5] - relax[4]
        for direction, values in enumerate(((xx, xy, xz), (xy, yy, yz), (xz, yz, zz))):
            for c in range(3):
                sigma_ref[direction * 128 + rows.start : direction * 128 + rows.stop, c * LANES : (c + 1) * LANES] = values[c]
    faces = dot_three(face_table, sigma_ref[...])
    first, last = pack_face(faces[0:32], False), pack_face(faces[32:64], True)
    if step < STEPS - 1:
        even_ring = lax.axis_index(("cuts", "sub")) % 2 == 0
        odd_ref[...] = jnp.where(even_ring, first, last)
        even_ref[...] = jnp.where(even_ring, last, first)
    else:
        even_ref[0:48, :] = last
        even_ref[48:, :] = jnp.zeros((even_ref.shape[0] - 48, LANES), F32)


def rest_kernel(sigma_ref, u_ref, p_ref, scale_ref, force_table, next_ref):
    force = dot_three(force_table, sigma_ref[...])
    blocks = {}
    for c in range(3):
        for b in range(5):
            for d in range(5):
                blocks[(c, b, d)] = force[block_rows(b, d), c * LANES : (c + 1) * LANES]
    blocks = assembled(blocks)
    lane = lanes_of((8, LANES))
    sub = lax.broadcasted_iota(jnp.int32, (8, LANES), 0)
    inner = ((sub == 4) & (lane < 64)) | ((sub == 0) & (lane >= 64))
    for c in range(3):
        for b in range(5):
            for d in range(5):
                value = blocks[(c, b, d)]
                value = value + jnp.where(inner, rolled(rolled(value, 4, 0), 64, 1), 0.0)
                at = block_rows(b, d)
                next_ref[c, at, :] = 2.0 * u_ref[c, at, :] - p_ref[c, at, :] + scale_ref[at, :] * value
        next_ref[c, 200:208, :] = jnp.zeros((8, LANES), F32)


def add_faces(packed_before, packed_after, partial_ref, scale_ref, u_ref, delta_ref):
    delta_ref[...] = jnp.zeros(delta_ref.shape, F32)
    lower = lanes_of((25, LANES)) < 64
    turned = rolled(packed_before, 64, 1)
    values = [packed_before[0:32], turned[0:32], jnp.concatenate([packed_before[32:48], turned[32:48]], axis=0)]
    for c in range(3):
        delta_ref[c, pl.ds(0, 25, stride=8), :] = jnp.where(lower, values[c][0:25], 0.0)
    turned = rolled(packed_after, 64, 1)
    values = [turned[0:32], packed_after[0:32], jnp.concatenate([turned[32:48], packed_after[32:48]], axis=0)]
    for c in range(3):
        delta_ref[c, pl.ds(4, 25, stride=8), :] = jnp.where(lower, 0.0, values[c][0:25])
    blocks = {}
    for c in range(3):
        for b in range(5):
            for d in range(5):
                blocks[(c, b, d)] = delta_ref[c, block_rows(b, d), :]
    blocks = assembled(blocks)
    for c in range(3):
        for b in range(5):
            for d in range(5):
                at = block_rows(b, d)
                u_ref[c, at, :] = partial_ref[c, at, :] + scale_ref[at, :] * blocks[(c, b, d)]
        u_ref[c, 200:208, :] = jnp.zeros((8, LANES), F32)


def update_kernel(odd_ref, even_ref, partial_ref, scale_ref, u_ref, flat_ref, low_ref, delta_ref):
    even_ring = lax.axis_index(("cuts", "sub")) % 2 == 0
    odd, even = odd_ref[...], even_ref[...]
    before, after = jnp.where(even_ring, odd, even), jnp.where(even_ring, even, odd)
    add_faces(before, after, partial_ref, scale_ref, u_ref, delta_ref)
    flatten(u_ref, flat_ref)
    low_ref[...] = flat_ref[...].astype(BF16)


def kernel_parts(strain_ref, low_ref, far_ref, lame_ref, mu_ref, grad_table, grad_ref, kernel_ref):
    forward = jnp.where(lax.axis_index("group") == 0, beside(low_ref), beside(far_ref))
    grad_ref[...] = low_gradients(grad_table, forward)
    for rows in CHUNKS:
        far = strains(grad_ref, rows)
        own = [strain_ref[part, rows, :] for part in range(6)]
        trace_own = own[0] + own[1] + own[2]
        trace_far = far[0] + far[1] + far[2]
        third_own, third_far = trace_own * (1.0 / 3.0), trace_far * (1.0 / 3.0)
        twice_mu = 2.0 * mu_ref[rows, :]
        kappa = lame_ref[rows, :] + twice_mu * (1.0 / 3.0)
        kernel_ref[rows, :] = time_step * kappa * trace_far * trace_own
        product = (
            (own[0] - third_own) * (far[0] - third_far)
            + (own[1] - third_own) * (far[1] - third_far)
            + (own[2] - third_own) * (far[2] - third_far)
            + 2.0 * (own[3] * far[3] + own[4] * far[4] + own[5] * far[5])
        )
        kernel_ref[125 + rows.start : 125 + rows.stop, :] = time_step * twice_mu * product
    kernel_ref[250:256, :] = jnp.zeros((6, LANES), F32)
    return kernel_ref[...].astype(BF16)


def parts_kernel(
    strain_ref, low_ref, far_ref, lame_ref, mu_ref, grad_table, part_ref, grad_ref, kernel_ref
):
    part_ref[...] = kernel_parts(
        strain_ref, low_ref, far_ref, lame_ref, mu_ref, grad_table, grad_ref, kernel_ref
    )


def send_kernel(
    strain_ref, low_ref, far_ref, lame_ref, mu_ref, grad_table, one_ref, two_ref, select_ref, *refs
):
    out_refs, (grad_ref, kernel_ref) = refs[:-2], refs[-2:]
    three = kernel_parts(strain_ref, low_ref, far_ref, lame_ref, mu_ref, grad_table, grad_ref, kernel_ref)
    rows = out_refs[0].shape[0]
    slots = rows // 2
    group = lanes_of((rows, LANES)) // slots
    over_lanes = (((1,), (1,)), ((), ()))
    for k, ref in enumerate(out_refs):
        chosen = select_ref[k * LANES : (k + 1) * LANES, :]
        total = 0.0
        for part in (one_ref[...], two_ref[...], three):
            total = total + lax.dot_general(part, chosen, over_lanes, preferred_element_type=F32)
        value = total[0:rows]
        for j in range(1, 256 // rows):
            value = jnp.where(group == j, total[j * rows : (j + 1) * rows], value)
        ref[...] = value


def sum_kernel(*refs):
    in_refs, out_ref = refs[:-1], refs[-1]
    rows = in_refs[0].shape[0]
    slots = rows // 2
    pieces = 256 // rows
    group = lanes_of((rows, LANES)) // slots
    blocks = [[jnp.zeros((rows, LANES), F32)] * 2 for _ in range(pieces)]
    for k, ref in enumerate(in_refs):
        source = lax.axis_index("sub") ^ k
        spot = source % pieces
        value = ref[...]
        for j in range(pieces):
            moved = pltpu.roll(value, ((spot + pieces - j) % pieces) * slots, 1)
            for t in range(2):
                here = (group == spot) & (source // pieces == t)
                blocks[j][t] = jnp.where(here, moved, blocks[j][t])
    value = jnp.concatenate([jnp.concatenate(row, axis=1) for row in blocks], axis=0)
    out_ref[:, 0, :] = value[0:250]


def to_nodal(columns, spread_ref, nodal_ref):
    rows = columns.shape[0]
    own = (lanes_of((rows, WIDE)) // 8) % 8
    expanded = jnp.concatenate([jnp.where(own == ey, columns, 0.0) for ey in range(EY)], axis=0)
    over_lanes = (((1,), (1,)), ((), ()))
    pieces = jnp.concatenate(cut(expanded), axis=0)
    windows = lax.dot_general(pieces, spread_ref[...], over_lanes, preferred_element_type=F32)
    half = EY * rows
    windows = windows[0:half] + windows[half : 2 * half] + windows[2 * half : 3 * half]
    nodal_ref[...] = jnp.zeros(nodal_ref.shape, F32)
    for ey in range(EY):
        at = slice(JUMP * ey, JUMP * ey + 5 * SIDE)
        nodal_ref[:, at] = nodal_ref[:, at] + windows[ey * rows : (ey + 1) * rows, 0 : 5 * SIDE]


def nodal_kernel(partial_ref, spread_ref, nodal_ref):
    lane = lanes_of((8, LANES))
    sub = lax.broadcasted_iota(jnp.int32, (8, LANES), 0)
    tiles = []
    for c in range(3):
        row = []
        for pair in range(BLOCKS // 2):
            even = partial_ref[c, 16 * pair : 16 * pair + 8, :]
            odd = partial_ref[c, 16 * pair + 8 : 16 * pair + 16, :]
            low = jnp.where(sub < 4, even, rolled(rolled(even, 64, 1), 4, 0))
            high = jnp.where(sub < 4, rolled(odd, 64, 1), rolled(odd, 4, 0))
            row.append(jnp.where(lane < 64, low, high))
        tiles.append(jnp.concatenate(row, axis=1))
    columns = jnp.concatenate(tiles, axis=0)
    column = lanes_of((24, WIDE))
    block = column // 64
    once = ((block % 5 < 4) | (column % 8 == 7)) & ((block // 5 < 4) | ((column // 8) % 8 == 7))
    to_nodal(jnp.where(once, columns, 0.0), spread_ref, nodal_ref)


def finish_kernel(before_ref, nodal_ref, density_ref, face_mass_ref, spread_ref, out_ref, rows_ref, face_ref):
    packed = before_ref[0:48]
    turned = rolled(packed, 64, 1)
    values = [packed[0:32], turned[0:32], jnp.concatenate([packed[32:48], turned[32:48]], axis=0)]
    rows_ref[...] = jnp.zeros(rows_ref.shape, F32)
    for c in range(3):
        rows_ref[pl.ds(c, 25, stride=8), :] = values[c][0:25]
    lane = lanes_of((8, LANES))
    tiles = []
    for pair in range(BLOCKS // 2):
        even, odd = rows_ref[16 * pair : 16 * pair + 8, :], rows_ref[16 * pair + 8 : 16 * pair + 16, :]
        tiles.append(jnp.where(lane < 64, even, rolled(odd, 64, 1)))
    to_nodal(jnp.concatenate(tiles, axis=1), spread_ref, face_ref)
    scale = step_square / (density_ref[0:1, :] * face_mass_ref[...])
    first = lax.broadcasted_iota(jnp.int32, (8, FACE), 0) == 0
    for c in range(3):
        share = face_ref[c : c + 1, :] * scale
        out_ref[0, c] = nodal_ref[8 * c : 8 * c + 8, :] + jnp.where(first, share, 0.0)


VMEM = pl.BlockSpec(memory_space=pltpu.VMEM)
HBM = pl.BlockSpec(memory_space=pltpu.HBM)


def shaped(*shape, dtype=F32):
    return jax.ShapeDtypeStruct(shape, dtype)


def call(kernel, name, outs, scratch, *args, outside=(), micros=1, room=32 * 1024):
    return pl.pallas_call(
        kernel,
        name=name,
        out_shape=outs,
        in_specs=[HBM if at in outside else VMEM for at in range(len(args))],
        out_specs=jax.tree.map(lambda _: VMEM, outs),
        scratch_shapes=scratch,
        compiler_params=pltpu.CompilerParams(vmem_limit_bytes=room * 1024),
        cost_estimate=pl.CostEstimate(flops=0, bytes_accessed=micros * 3000000, transcendentals=0),
    )(*args)


def passed_along(value, axis, steps):
    count = lax.axis_size(axis)
    return lax.ppermute(value, axis, [(source, (source + steps) % count) for source in range(count)])


def swapped(value, axis, first):
    count = lax.axis_size(axis)
    pairs = []
    for source in range(first, count, 2):
        other = (source + 1) % count
        pairs += [(source, other), (other, source)]
    return lax.ppermute(value, axis, pairs)


def far_field(low, groups):
    far = None
    for k in range(1, groups):
        moved = passed_along(low, "group", k)
        far = moved if far is None else jnp.where(lax.axis_index("group") == k, moved, far)
    return far


def per_device(disp_now, disp_prev, memory_init, density, lame_lambda, shear_mu, sls_decay, owner_map):
    ring = ("cuts", "sub")
    subs = lax.axis_size("sub")
    groups = lax.axis_size("group")

    rim = call(
        gather_kernel, "gather", shaped(8, FACE),
        [pltpu.VMEM((3, 8, FACE), F32)] * 2 + [pltpu.VMEM((8, FACE), F32), pltpu.SemaphoreType.DMA((3,))],
        disp_now, disp_prev, density, outside=(0, 1, 2), room=54 * 1024 - 120,
    )
    rim = passed_along(rim, ring, -1)

    grad_table = jnp.asarray(side_by_side(GRAD))
    force_table = jnp.asarray(cut_table(FORCE))
    face_table = jnp.asarray(cut_table(FACES))
    face_mass = jnp.asarray(FACE_MASS)
    mass = jnp.asarray(MASS)
    memory = memory_init[0]
    owner = jnp.transpose(owner_map, (0, 2, 1))

    state = shaped(3, ROWS, LANES)
    flat_shape = shaped(3, 128, LANES)
    low_shape = shaped(3, 128, LANES, dtype=BF16)
    scale_shape = shaped(ROWS, LANES)
    five = shaped(5, 125, LANES)
    part_shape = shaped(256, LANES, dtype=BF16)
    grad_scratch = pltpu.VMEM((384, 384), F32)
    part_scratch = [grad_scratch, pltpu.VMEM((256, LANES), F32)]
    face = shaped(48, LANES)
    window_scratch = [pltpu.VMEM((8, 8, WINDOW), F32), pltpu.VMEM((ROWS, LANES), F32)]
    u, p, scale, m1, spread = call(
        prologue_kernel, "prologue", [state, state, scale_shape, five, shaped(WINDOW, WIDE, dtype=BF16)],
        [pltpu.VMEM((8, 56, WINDOW), F32)],
        disp_now, disp_prev, density, memory, sls_decay, mass, grad_table, face_table, force_table, lame_lambda, shear_mu,
    )
    u, p, scale, flat, low = call(
        rim_kernel, "rim", [state, state, scale_shape, flat_shape, low_shape], window_scratch, rim, u, p, scale, spread, mass
    )
    memories = [m1]
    kept = []
    parts = []
    for step in range(STEPS):
        if step == STEPS - 1:
            far = far_field(low, groups)
        outs = [shaped(6, 125, LANES), shaped(384, 384), face if step < STEPS - 1 else shaped(PAD, LANES)]
        if step < STEPS - 1:
            outs += [face, five]
        results = call(
            lambda *refs, step=step: step_kernel(step, *refs), "step", outs, [grad_scratch],
            flat, lame_lambda, shear_mu, memories[step], sls_decay, grad_table, face_table, *kept,
        )
        strain, sigma, even = results[0:3]
        if step < STEPS - 1:
            odd = results[3]
            kept.append(results[4])
            odd = swapped(odd, ring, 1)
            even = swapped(even, ring, 0)
        else:
            before = passed_along(even, ring, 1)
        partial = call(rest_kernel, "rest", state, [], sigma, u, p, scale, force_table)
        if step < STEPS - 1:
            low, sigma = lax.optimization_barrier((low, sigma))
            far = far_field(low, groups)
        shared = (strain, low, far, lame_lambda, shear_mu, grad_table)
        if step < STEPS - 1:
            parts.append(call(parts_kernel, "parts", part_shape, part_scratch, *shared))
            if step == 0:
                m2, m3, select = call(
                    later_kernel, "later", [five, five, shaped(subs * LANES, LANES, dtype=BF16)], [],
                    memory, sls_decay, owner,
                )
                memories += [m2, m3]
                partial, parts[0], select, memories[2] = lax.optimization_barrier((partial, parts[0], select, m3))
            else:
                partial, parts[1] = lax.optimization_barrier((partial, parts[1]))
            p = u
            u, flat, low = call(
                update_kernel, "update", [state, flat_shape, low_shape], [pltpu.VMEM((3, ROWS, LANES), F32)],
                odd, even, partial, scale,
            )
        else:
            sent = list(call(
                send_kernel, "send", [shaped(512 // subs, LANES)] * subs, part_scratch, *shared, *parts, select)
            )
            for k in [at ^ (at >> 1) for at in range(subs - 1, 0, -1)]:
                sent[k] = lax.ppermute(sent[k], "sub", [(j, j ^ k) for j in range(subs)])
    nodal = call(nodal_kernel, "nodal", shaped(24, FACE), [], partial, spread)
    final = call(
        finish_kernel, "finish", shaped(1, 3, 8, FACE), [pltpu.VMEM((ROWS, LANES), F32), pltpu.VMEM((8, FACE), F32)],
        before, nodal, density, face_mass, spread,
    )
    kernels = call(sum_kernel, "sum", shaped(250, 1, 256), [], *sent)
    return final, jnp.transpose(kernels, (1, 2, 0))


def solution(mesh):
    in_specs = (
        P("group", None, ("cuts", "sub"), None),
        P("group", None, ("cuts", "sub"), None),
        P("group", None, None, None, ("cuts", "sub")),
        P(("cuts", "sub"), None),
        P(None, ("cuts", "sub")),
        P(None, ("cuts", "sub")),
        P(None, ("cuts", "sub")),
        P(("cuts", "sub"), None, None),
    )
    out_specs = (P("group", None, ("cuts", "sub"), None), P("group", ("cuts", "sub"), None))
    return jax.shard_map(
        per_device, mesh=mesh, in_specs=in_specs, out_specs=out_specs, check_vma=False
    )
```

```python
import math

import jax
import jax.numpy as jnp
import numpy as np
from jax import lax
from jax.experimental import pallas as pl
from jax.experimental.pallas import tpu as pltpu
from jax.sharding import PartitionSpec as P

STEPS = 3
PAD = 136
EY = 8
EZ = 8
LANES = 128
SIDE = 33
FACE = SIDE * SIDE
BLOCKS = 26
ROWS = 8 * BLOCKS
WIDE = 64 * BLOCKS
JUMP = 4 * SIDE
WINDOW = 256

time_step = 0.03
step_square = 0.0009
relax_strength = (0.12, 0.08, 0.05)

F32 = jnp.float32
BF16 = jnp.bfloat16


def gll_tables():
    root_value = math.sqrt(3.0 / 7.0)
    points = [-1.0, -root_value, 0.0, root_value, 1.0]
    weights = [0.1, 49.0 / 90.0, 32.0 / 45.0, 49.0 / 90.0, 0.1]
    derivative = np.zeros((5, 5))
    for p in range(5):
        for a in range(5):
            accum = 0.0
            for m in range(5):
                if m != a:
                    factor = 1.0 / (points[a] - points[m])
                    for k in range(5):
                        if k != a and k != m:
                            factor = factor * (points[p] - points[k]) / (points[a] - points[k])
                    accum = accum + factor
            derivative[p, a] = accum
    return derivative.astype(np.float32).astype(np.float64), np.array(weights).astype(np.float32).astype(np.float64)


def node(a, b, d):
    return a * 25 + b * 5 + d


def place(a, b, d):
    return (b * 5 + d) * 8 + a


FACE_ROWS = [slice(0, 128), slice(128, 160), slice(224, 256), slice(256, 288), slice(352, 384)]


def make_tables():
    derivative, weights = gll_tables()
    grad = np.zeros((3 * 128, 128))
    force = np.zeros((ROWS, 3 * 128))
    for a in range(5):
        for b in range(5):
            for d in range(5):
                for m in range(5):
                    grad[node(a, b, d), node(m, b, d)] = derivative[a, m]
                    grad[128 + node(a, b, d), node(a, m, d)] = derivative[b, m]
                    grad[256 + node(a, b, d), node(a, b, m)] = derivative[d, m]
                    row = place(a, b, d)
                    force[row, node(m, b, d)] = -derivative[m, a] * weights[m] * weights[b] * weights[d]
                    force[row, 128 + node(a, m, d)] = -derivative[m, b] * weights[a] * weights[m] * weights[d]
                    force[row, 256 + node(a, b, m)] = -derivative[m, d] * weights[a] * weights[b] * weights[m]
    full = np.zeros((80, 3 * 128))
    first_grad, last_grad = np.zeros((3 * 128, 40)), np.zeros((3 * 128, 40))
    for b in range(5):
        for d in range(5):
            full[d * 8 + b] = force[place(0, b, d)]
            full[40 + d * 8 + b] = force[place(4, b, d)]
            first_grad[:, d * 8 + b] = grad[:, node(0, b, d)]
            last_grad[:, d * 8 + b] = grad[:, node(4, b, d)]
    face = np.concatenate([full[:, rows] for rows in FACE_ROWS], axis=1)
    first, last = cut_table(first_grad), cut_table(last_grad)
    share = np.concatenate([first[0], first[0], first[1], last[0], last[0], last[1]], axis=1)
    rim = np.concatenate([last[0], last[0], last[1], last[1], last[0], last[2]], axis=1)
    line = np.zeros(SIDE)
    for e in range(8):
        line[4 * e : 4 * e + 5] += weights
    layer = np.array([2 * weights[0], weights[1], weights[2], weights[3], 2 * weights[0], 1.0, 1.0, 1.0])
    mass = np.ones((ROWS, LANES), np.float32)
    for b in range(5):
        for d in range(5):
            for ey in range(8):
                for ez in range(8):
                    for slab in range(2):
                        at = (b * 5 + d) * 8
                        mass[at : at + 8, slab * 64 + ey * 8 + ez] = layer * line[4 * ey + b] * line[4 * ez + d]
    face_mass = (layer[0] * np.outer(line, line)).reshape(1, FACE).astype(np.float32)
    return grad, force, face, mass, face_mass, share, rim


def side_by_side(table):
    high, middle, low = cut_table(table)
    pairs = ((high, middle), (middle, high), (low, high))
    return np.stack([np.concatenate(pair, axis=1) for pair in pairs])


def cut_table(table):
    value = table.astype(np.float32)
    pieces = []
    for _ in range(3):
        piece = value.astype(jnp.bfloat16)
        pieces.append(piece)
        value = value - piece.astype(np.float32)
    return np.stack(pieces)


GRAD, FORCE, FACES, MASS, FACE_MASS, SHARE, RIM = make_tables()


def cut(value):
    high = value.astype(BF16)
    rest = value - high.astype(F32)
    middle = rest.astype(BF16)
    low = (rest - middle.astype(F32)).astype(BF16)
    return high, middle, low


def dot(left, right):
    return jnp.dot(left, right, preferred_element_type=F32)


def gradients(table, flat):
    high, middle, low = cut(flat)
    first = dot(table[0:2].reshape(768, 256), jnp.concatenate([high, middle], axis=0))
    return first[0:384] + (first[384:768] + dot(table[2], jnp.concatenate([high, low], axis=0)))


def low_gradients(table, low):
    return dot(table[0], jnp.concatenate([low, low], axis=0)) + dot(table[2, :, 0:128], low)


def flatten(u_ref, flat_ref):
    for c in range(3):
        flat_ref[c, 120:128, :] = jnp.zeros((8, LANES), F32)
        for a in range(5):
            flat_ref[c, 25 * a : 25 * a + 25, :] = u_ref[c, pl.ds(a, 25, stride=8), :]


def dot_three(table, value):
    rows = table.shape[1]
    stacked = table[0:2].reshape(2 * rows, table.shape[2])
    high, middle, _ = cut(value)
    first = dot(stacked, high)
    return first[0:rows] + (first[rows : 2 * rows] + dot(stacked[0:rows], middle))


def lanes_of(shape):
    return lax.broadcasted_iota(jnp.int32, shape, len(shape) - 1)


def rolled(value, shift, axis):
    return pltpu.roll(value, shift % value.shape[axis], axis)


def window_rows(value, window_ref):
    for ey in range(EY):
        width = min(WINDOW, FACE - JUMP * ey)
        if width < WINDOW:
            window_ref[ey] = jnp.zeros(window_ref.shape[1:], F32)
        window_ref[ey, :, 0:width] = value[:, JUMP * ey : JUMP * ey + width]
    return window_ref[...].reshape(-1, WINDOW)


def to_columns(value, window_ref, spread_ref):
    rows = value.shape[0]
    pieces = jnp.concatenate(cut(window_rows(value, window_ref)), axis=0)
    wide = dot(pieces, spread_ref[...])
    half = EY * rows
    own = (lanes_of((rows, WIDE)) // 8) % 8
    picked = 0.0
    for ey in range(EY):
        at = slice(ey * rows, (ey + 1) * rows)
        value = wide[at] + wide[half : 2 * half][at] + wide[2 * half : 3 * half][at]
        picked = jnp.where(own == ey, value, picked)
    return picked


def assembled(blocks):
    lane = lanes_of((8, LANES))
    blocks = dict(blocks)
    for shift, at, pairs in (
        (1, lane % 8, [((b, 0), (b, 4)) for b in range(5)]),
        (8, (lane // 8) % 8, [((0, d), (4, d)) for d in range(5)]),
    ):
        for c in range(3):
            for near, far in pairs:
                first, last = blocks[(c,) + near], blocks[(c,) + far]
                blocks[(c,) + near] = first + jnp.where(at > 0, rolled(last, shift, 1), 0.0)
                blocks[(c,) + far] = last + jnp.where(at < 7, rolled(first, -shift, 1), 0.0)
    return blocks


def block_rows(b, d):
    return slice((b * 5 + d) * 8, (b * 5 + d) * 8 + 8)


def beside(value):
    return jnp.concatenate([value[0], value[1], value[2]], axis=1)


def gather_kernel(now_ref, prev_ref, density_ref, rim_ref, now_copy, prev_copy, density_copy, sems):
    copies = [
        pltpu.make_async_copy(now_ref.at[0], now_copy, sems.at[0]),
        pltpu.make_async_copy(prev_ref.at[0], prev_copy, sems.at[1]),
        pltpu.make_async_copy(density_ref, density_copy, sems.at[2]),
    ]
    for copy in copies:
        copy.start()
    for copy in copies:
        copy.wait()
    for c in range(3):
        rim_ref[c : c + 1, :] = now_copy[c, 0:1, :]
        rim_ref[3 + c : 4 + c, :] = prev_copy[c, 0:1, :]
    rim_ref[6:7, :] = density_copy[0:1, :]
    rim_ref[7:8, :] = density_copy[0:1, :]


def weighted_memory(memory_ref, decays, part, power):
    value = 0.0
    for l in range(3):
        factor = decays[l]
        for _ in range(power - 1):
            factor = factor * decays[l]
        value = value + factor * memory_ref[l, part]
    return value


def spread_table():
    column = lanes_of((1, WIDE))
    block = column // 64
    spot = (block // 5) * SIDE + (block % 5) + 4 * (column % 8)
    spot = jnp.where(block < 25, spot, WINDOW)
    return jnp.where(lax.broadcasted_iota(jnp.int32, (WINDOW, WIDE), 0) == spot, 1.0, 0.0).astype(BF16)


def prologue_kernel(now_ref, prev_ref, density_ref, memory_ref, decay_ref, mass_ref, *refs):
    grad_table = refs[0]
    u_ref, p_ref, scale_ref, m1_ref, spread_ref, flat_ref, grad_ref, window_ref = refs[-8:]
    spread_ref[...] = spread_table()
    rows = jnp.concatenate([now_ref[0].reshape(24, FACE), prev_ref[0].reshape(24, FACE), density_ref[...]], axis=0)
    columns = to_columns(rows, window_ref, spread_ref)
    lane = lanes_of((8, LANES))
    for group in range(7):
        for pair in range(BLOCKS // 2):
            tile = columns[8 * group : 8 * group + 8, LANES * pair : LANES * pair + LANES]
            swapped = rolled(tile, 64, 1)
            even = jnp.where(lane < 64, tile, rolled(swapped, 4, 0))
            odd = jnp.where(lane < 64, swapped, rolled(tile, 4, 0))
            for block, value in ((2 * pair, even), (2 * pair + 1, odd)):
                at = slice(8 * block, 8 * block + 8)
                if group < 3:
                    u_ref[group, at, :] = value
                elif group < 6:
                    p_ref[group - 3, at, :] = value
                elif block < 25:
                    scale_ref[at, :] = step_square / (value * mass_ref[at, :])
                else:
                    scale_ref[at, :] = jnp.zeros((8, LANES), F32)
    decays = [decay_ref[l : l + 1, :] for l in range(3)]
    for part in range(5):
        m1_ref[part] = weighted_memory(memory_ref, decays, part, 1)
    flatten(u_ref, flat_ref)
    lower = lanes_of((25, LANES)) < 64
    for c in range(3):
        flat_ref[c, 100:125, :] = jnp.where(lower, flat_ref[c, 100:125, :], 0.0)
    grad_ref[...] = gradients(grad_table, beside(flat_ref))


def later_kernel(memory_ref, decay_ref, owner_ref, m2_ref, m3_ref, select_ref):
    decays = [decay_ref[l : l + 1, :] for l in range(3)]
    for part in range(5):
        m2_ref[part] = weighted_memory(memory_ref, decays, part, 2)
        m3_ref[part] = weighted_memory(memory_ref, decays, part, 3)
    owner = jnp.concatenate([owner_ref[0], owner_ref[1]], axis=1)
    named = jnp.where(lax.broadcasted_iota(jnp.int32, (16, LANES), 0) == owner, 1.0, 0.0)
    earlier = lax.broadcasted_iota(jnp.int32, (LANES, LANES), 0)
    later = lax.broadcasted_iota(jnp.int32, (LANES, LANES), 1)
    ahead = jnp.where((earlier < later) & ((earlier // 64) == (later // 64)), 1.0, 0.0)
    rank = jnp.sum(named * dot(named.astype(BF16), ahead.astype(BF16)), axis=0, keepdims=True).astype(jnp.int32)
    subs = select_ref.shape[0] // LANES
    slots = 4 * EY * EZ // subs
    row = lax.broadcasted_iota(jnp.int32, select_ref.shape, 0)
    toward = (row // LANES) ^ lax.axis_index("sub")
    wanted = (lanes_of((1, LANES)) // 64) * (slots // 2) + rank
    chosen = (owner == toward) & (wanted == row % slots)
    select_ref[...] = jnp.where(chosen, 1.0, 0.0).astype(BF16)


def rim_rows(rim_ref, spread_ref, window_ref, rows_ref):
    columns = to_columns(rim_ref[...], window_ref, spread_ref)
    for pair in range(BLOCKS // 2):
        tile = columns[:, LANES * pair : LANES * pair + LANES]
        rows_ref[16 * pair : 16 * pair + 8, :] = rolled(tile, 64, 1)
        rows_ref[16 * pair + 8 : 16 * pair + 16, :] = tile


def unpack_face(here, there):
    top = lax.broadcasted_iota(jnp.int32, (8, LANES), 0) < 3
    parts = [[], [], []]
    for d in range(5):
        first, second = here[8 * d : 8 * d + 8], there[8 * d : 8 * d + 8]
        third = jnp.where(top, rolled(first, 3, 0), rolled(second, 6, 0))
        for part, line in zip(parts, (first, second, third)):
            part.append(line)
    return parts


def face_shares(odd_ref, even_ref, face_scale_ref):
    even_ring = lax.axis_index(("cuts", "sub")) % 2 == 0
    odd, even = odd_ref[...], even_ref[...]
    lower = (lanes_of((40, LANES)) < 64) == even_ring
    rows = unpack_face(jnp.where(lower, odd, even), rolled(jnp.where(lower, even, odd), 64, 1))
    lane = lanes_of((8, LANES))
    sub = lax.broadcasted_iota(jnp.int32, (8, LANES), 0)
    ez, ey = lane % 8, (lane // 8) % 8
    up, down = (sub == 0) & (ey > 0), (sub == 4) & (ey < 7)
    shares = []
    for c in range(3):
        lines = rows[c]
        first, last = lines[0], lines[4]
        lines[0] = first + jnp.where(ez > 0, rolled(last, 1, 1), 0.0)
        lines[4] = last + jnp.where(ez < 7, rolled(first, -1, 1), 0.0)
        for d in range(5):
            turned = rolled(lines[d], 4, 0)
            added = jnp.where(up, rolled(turned, 8, 1), jnp.where(down, rolled(turned, -8, 1), 0.0))
            lines[d] = face_scale_ref[8 * d : 8 * d + 8, :] * (lines[d] + added)
        shares.append(lines)
    return shares


def strains(grad, rows):
    def at(direction, c):
        return grad[direction * 128 + rows.start : direction * 128 + rows.stop, c * LANES : (c + 1) * LANES]

    return [
        at(0, 0),
        at(1, 1),
        at(2, 2),
        0.5 * (at(1, 0) + at(0, 1)),
        0.5 * (at(2, 0) + at(0, 2)),
        0.5 * (at(2, 1) + at(1, 2)),
    ]


CHUNKS = [slice(row, min(row + 8, 125)) for row in range(0, 125, 8)]


def pack_face(face, upper):
    lane = lanes_of((8, LANES))
    target = lane < 64 if upper else lane >= 64
    own = lax.broadcasted_iota(jnp.int32, (8, LANES), 0) < 5
    lines = []
    for d in range(5):
        first, second, third = [face[8 * d : 8 * d + 8, c * LANES : (c + 1) * LANES] for c in range(3)]
        moved = rolled(jnp.where(own, first, rolled(third, 5, 0)), 64, 1)
        lines.append(jnp.where(target, moved, jnp.where(own, second, rolled(third, 2, 0))))
    return jnp.concatenate(lines, axis=0)


def step_kernel(step, *refs):
    lame_ref, mu_ref, m_ref, decay_ref, share_table, face_table, base_ref, flat_in = refs[0:8]
    arrived = refs[8 : 10 if step == 0 else 11]
    refs = refs[8 + len(arrived) :]
    older, refs = refs[:step], refs[step:]
    strain_ref, sigma_ref, even_ref, low_ref, extra_ref = refs[0:5]
    odd_ref, keep_ref = refs[5:7] if step < STEPS - 1 else (None, None)
    grad_ref, flat_ref, window_ref, rim_ref = refs[-4:]
    flat_ref[...] = flat_in[...]
    upper = lanes_of((40, 3 * LANES)) % LANES >= 64
    if step == 0:
        rim_rows(arrived[0], arrived[1], window_ref, extra_ref)
        rim_ref[...] = jnp.zeros(rim_ref.shape, F32)
        for c in range(3):
            for d in range(5):
                rim_ref[8 * d : 8 * d + 5, c * LANES : (c + 1) * LANES] = extra_ref[pl.ds(8 * d + c, 5, stride=40), :]
        high, middle, low = [piece.astype(F32) for piece in cut(jnp.where(upper, rim_ref[...], 0.0))]
        stacked = [high, middle, high, middle, low, high]
        at_upper = lanes_of((25, LANES)) >= 64
        for c in range(3):
            flat_ref[c, 100:125, :] = jnp.where(at_upper, extra_ref[pl.ds(c, 25, stride=8), :], flat_ref[c, 100:125, :])
    else:
        shares = face_shares(*arrived)
        value = jnp.concatenate([jnp.concatenate(lines, axis=0) for lines in shares], axis=1)
        high, middle, _ = [piece.astype(F32) for piece in cut(value)]
        stacked = []
        for at in (~upper, upper):
            stacked += [jnp.where(at, high, 0.0), jnp.where(at, middle, 0.0), jnp.where(at, high, 0.0)]
        at_upper = lanes_of((5, LANES)) >= 64
        for c in range(3):
            for d in range(5):
                extra_ref[c, 8 * d : 8 * d + 8, :] = shares[c][d]
                share = shares[c][d][0:5]
                first, last = pl.ds(d, 5, stride=5), pl.ds(100 + d, 5, stride=5)
                flat_ref[c, first, :] = flat_ref[c, first, :] + jnp.where(at_upper, 0.0, share)
                flat_ref[c, last, :] = flat_ref[c, last, :] + jnp.where(at_upper, share, 0.0)
    grad_ref[...] = base_ref[...] + dot(share_table[...], jnp.concatenate(stacked, axis=0).astype(BF16))
    low_ref[...] = flat_ref[...].astype(BF16)
    for block in range(9):
        sigma_ref[(block // 3) * 128 + 120 : (block // 3) * 128 + 128, (block % 3) * LANES : (block % 3) * LANES + LANES] = (
            jnp.zeros((8, LANES), F32)
        )
    decays = [decay_ref[l : l + 1, :] for l in range(3)]
    shares = [(1.0 - decays[l]) * relax_strength[l] for l in range(3)]
    factors = []
    for _ in range(step + 1):
        factors.append(shares[0] + shares[1] + shares[2])
        shares = [decays[l] * shares[l] for l in range(3)]
    for rows in CHUNKS:
        strain = strains(grad_ref, rows)
        for part in range(6):
            strain_ref[part, rows, :] = strain[part]
        lame = lame_ref[rows, :]
        twice_mu = 2.0 * mu_ref[rows, :]
        trace = strain[0] + strain[1] + strain[2]
        third = trace * (1.0 / 3.0)
        pulls = [twice_mu * s for s in strain]
        pull_third = twice_mu * third
        fresh = [pulls[0] - pull_third, pulls[1] - pull_third, pulls[3], pulls[4], pulls[5]]
        relax = []
        for part in range(5):
            value = m_ref[part, rows, :] + factors[0] * fresh[part]
            for back in range(step):
                value = value + factors[back + 1] * older[step - 1 - back][part, rows, :]
            relax.append(value)
            if keep_ref is not None:
                keep_ref[part, rows, :] = fresh[part]
        bulk = lame * trace
        xx = bulk + pulls[0] - relax[0]
        yy = bulk + pulls[1] - relax[1]
        zz = bulk + pulls[2] + relax[0] + relax[1]
        xy = pulls[3] - relax[2]
        xz = pulls[4] - relax[3]
        yz = pulls[5] - relax[4]
        for direction, values in enumerate(((xx, xy, xz), (xy, yy, yz), (xz, yz, zz))):
            for c in range(3):
                sigma_ref[direction * 128 + rows.start : direction * 128 + rows.stop, c * LANES : (c + 1) * LANES] = values[c]
    faces = dot_three(face_table, jnp.concatenate([sigma_ref[rows, :] for rows in FACE_ROWS], axis=0))
    first, last = pack_face(faces[0:40], False), pack_face(faces[40:80], True)
    if step < STEPS - 1:
        even_ring = lax.axis_index(("cuts", "sub")) % 2 == 0
        odd_ref[...] = jnp.where(even_ring, first, last)
        even_ref[...] = jnp.where(even_ring, last, first)
    else:
        even_ref[0:40, :] = last
        even_ref[40:, :] = jnp.zeros((even_ref.shape[0] - 40, LANES), F32)


def next_state(sigma_ref, force_table, u_ref, p_ref, scale_ref, next_ref):
    force = dot_three(force_table, sigma_ref[...])
    blocks = {}
    for c in range(3):
        for b in range(5):
            for d in range(5):
                blocks[(c, b, d)] = force[block_rows(b, d), c * LANES : (c + 1) * LANES]
    blocks = assembled(blocks)
    lane = lanes_of((8, LANES))
    sub = lax.broadcasted_iota(jnp.int32, (8, LANES), 0)
    inner = ((sub == 4) & (lane < 64)) | ((sub == 0) & (lane >= 64))
    for c in range(3):
        for b in range(5):
            for d in range(5):
                value = blocks[(c, b, d)]
                value = value + jnp.where(inner, rolled(rolled(value, 4, 0), 64, 1), 0.0)
                at = block_rows(b, d)
                next_ref[c, at, :] = 2.0 * u_ref[c, at, :] - p_ref[c, at, :] + scale_ref[at, :] * value
        next_ref[c, 200:208, :] = jnp.zeros((8, LANES), F32)


def first_rest_kernel(
    sigma_ref, force_table, u_in, p_in, scale_in, rows_ref, mass_ref, grad_table,
    u_ref, scale_ref, next_ref, flat_ref, grad_ref, face_scale_ref, p_ref
):
    u_ref[...] = u_in[...]
    p_ref[...] = p_in[...]
    scale_ref[...] = scale_in[...]
    upper = lanes_of((25, LANES)) >= 64
    last = pl.ds(4, 25, stride=8)
    for c in range(3):
        u_ref[c, last, :] = jnp.where(upper, rows_ref[pl.ds(c, 25, stride=8), :], u_ref[c, last, :])
        p_ref[c, last, :] = jnp.where(upper, rows_ref[pl.ds(3 + c, 25, stride=8), :], p_ref[c, last, :])
    rim = step_square / (rows_ref[pl.ds(6, 25, stride=8), :] * mass_ref[last, :])
    scale_ref[last, :] = jnp.where(upper, rim, scale_ref[last, :])
    face_scale_ref[...] = jnp.zeros(face_scale_ref.shape, F32)
    lower = lanes_of((5, LANES)) < 64
    for d in range(5):
        first, last = pl.ds(8 * d, 5, stride=40), pl.ds(8 * d + 4, 5, stride=40)
        face_scale_ref[8 * d : 8 * d + 5, :] = jnp.where(lower, scale_ref[first, :], scale_ref[last, :])
    next_state(sigma_ref, force_table, u_ref, p_ref, scale_ref, next_ref)
    flatten(next_ref, flat_ref)
    grad_ref[...] = gradients(grad_table, beside(flat_ref))


def rest_kernel(sigma_ref, force_table, partial_ref, delta_ref, p_ref, scale_ref, grad_table, next_ref, u_ref, *refs):
    u_ref[...] = partial_ref[...]
    upper = lanes_of((5, LANES)) >= 64
    for c in range(3):
        for d in range(5):
            share = delta_ref[c, 8 * d : 8 * d + 5, :]
            first, last = pl.ds(8 * d, 5, stride=40), pl.ds(8 * d + 4, 5, stride=40)
            u_ref[c, first, :] = u_ref[c, first, :] + jnp.where(upper, 0.0, share)
            u_ref[c, last, :] = u_ref[c, last, :] + jnp.where(upper, share, 0.0)
    next_state(sigma_ref, force_table, u_ref, p_ref, scale_ref, next_ref)
    if refs:
        flat_ref, grad_ref = refs
        flatten(next_ref, flat_ref)
        grad_ref[...] = gradients(grad_table, beside(flat_ref))


def kernel_parts(strain_ref, low_ref, far_ref, lame_ref, mu_ref, grad_table, grad_ref, kernel_ref):
    forward = jnp.where(lax.axis_index("group") == 0, beside(low_ref), beside(far_ref))
    grad_ref[...] = low_gradients(grad_table, forward)
    for rows in CHUNKS:
        far = strains(grad_ref, rows)
        own = [strain_ref[part, rows, :] for part in range(6)]
        trace_own = own[0] + own[1] + own[2]
        trace_far = far[0] + far[1] + far[2]
        third_own, third_far = trace_own * (1.0 / 3.0), trace_far * (1.0 / 3.0)
        twice_mu = 2.0 * mu_ref[rows, :]
        kappa = lame_ref[rows, :] + twice_mu * (1.0 / 3.0)
        kernel_ref[rows, :] = time_step * kappa * trace_far * trace_own
        product = (
            (own[0] - third_own) * (far[0] - third_far)
            + (own[1] - third_own) * (far[1] - third_far)
            + (own[2] - third_own) * (far[2] - third_far)
            + 2.0 * (own[3] * far[3] + own[4] * far[4] + own[5] * far[5])
        )
        kernel_ref[125 + rows.start : 125 + rows.stop, :] = time_step * twice_mu * product
    kernel_ref[250:256, :] = jnp.zeros((6, LANES), F32)
    return kernel_ref[...].astype(BF16)


def placed(part, select_ref, rows):
    slots = rows // 2
    group = lanes_of((rows, LANES)) // slots
    total = lax.dot_general(part, select_ref[...], (((1,), (1,)), ((), ())), preferred_element_type=F32)
    blocks = []
    for k in range(select_ref.shape[0] // LANES):
        value = total[0:rows, k * LANES : (k + 1) * LANES]
        for j in range(1, 256 // rows):
            value = jnp.where(group == j, total[j * rows : (j + 1) * rows, k * LANES : (k + 1) * LANES], value)
        blocks.append(value)
    return blocks


def parts_kernel(strain_ref, low_ref, far_ref, lame_ref, mu_ref, grad_table, part_ref, grad_ref, kernel_ref):
    part_ref[...] = kernel_parts(strain_ref, low_ref, far_ref, lame_ref, mu_ref, grad_table, grad_ref, kernel_ref)


def both_parts_kernel(
    strain_ref, low_ref, far_ref, lame_ref, mu_ref, grad_table, one_ref, select_ref, both_ref, grad_ref, kernel_ref
):
    two = kernel_parts(strain_ref, low_ref, far_ref, lame_ref, mu_ref, grad_table, grad_ref, kernel_ref)
    rows = both_ref.shape[1]
    for k, (first, second) in enumerate(zip(placed(one_ref[...], select_ref, rows), placed(two, select_ref, rows))):
        both_ref[k] = first + second


def send_kernel(strain_ref, low_ref, far_ref, lame_ref, mu_ref, grad_table, both_ref, select_ref, *refs):
    out_refs, (grad_ref, kernel_ref) = refs[:-2], refs[-2:]
    three = kernel_parts(strain_ref, low_ref, far_ref, lame_ref, mu_ref, grad_table, grad_ref, kernel_ref)
    for k, (ref, value) in enumerate(zip(out_refs, placed(three, select_ref, out_refs[0].shape[0]))):
        ref[...] = both_ref[k] + value


def sum_kernel(order, *refs):
    in_refs, out_ref = refs[:-1], refs[-1]
    rows = in_refs[0].shape[0]
    slots = rows // 2
    pieces = 256 // rows
    group = lanes_of((rows, LANES)) // slots
    blocks = [[jnp.zeros((rows, LANES), F32)] * 2 for _ in range(pieces)]
    for k, ref in zip(order, in_refs):
        source = lax.axis_index("sub") ^ k
        spot = source % pieces
        value = ref[...]
        for j in range(pieces):
            moved = pltpu.roll(value, ((spot + pieces - j) % pieces) * slots, 1)
            for t in range(2):
                here = (group == spot) & (source // pieces == t)
                blocks[j][t] = jnp.where(here, moved, blocks[j][t])
    value = jnp.concatenate([jnp.concatenate(row, axis=1) for row in blocks], axis=0)
    out_ref[:, 0, :] = value[0:250]


def to_nodal(columns, spread_ref, nodal_ref):
    rows = columns.shape[0]
    own = (lanes_of((rows, WIDE)) // 8) % 8
    expanded = jnp.concatenate([jnp.where(own == ey, columns, 0.0) for ey in range(EY)], axis=0)
    over_lanes = (((1,), (1,)), ((), ()))
    pieces = jnp.concatenate(cut(expanded), axis=0)
    windows = lax.dot_general(pieces, spread_ref[...], over_lanes, preferred_element_type=F32)
    half = EY * rows
    windows = windows[0:half] + windows[half : 2 * half] + windows[2 * half : 3 * half]
    nodal_ref[...] = jnp.zeros(nodal_ref.shape, F32)
    for ey in range(EY):
        at = slice(JUMP * ey, JUMP * ey + 5 * SIDE)
        nodal_ref[:, at] = nodal_ref[:, at] + windows[ey * rows : (ey + 1) * rows, 0 : 5 * SIDE]


def nodal_kernel(partial_ref, spread_ref, nodal_ref):
    lane = lanes_of((8, LANES))
    sub = lax.broadcasted_iota(jnp.int32, (8, LANES), 0)
    tiles = []
    for c in range(3):
        row = []
        for pair in range(BLOCKS // 2):
            even = partial_ref[c, 16 * pair : 16 * pair + 8, :]
            odd = partial_ref[c, 16 * pair + 8 : 16 * pair + 16, :]
            low = jnp.where(sub < 4, even, rolled(rolled(even, 64, 1), 4, 0))
            high = jnp.where(sub < 4, rolled(odd, 64, 1), rolled(odd, 4, 0))
            row.append(jnp.where(lane < 64, low, high))
        tiles.append(jnp.concatenate(row, axis=1))
    columns = jnp.concatenate(tiles, axis=0)
    column = lanes_of((24, WIDE))
    block = column // 64
    once = ((block % 5 < 4) | (column % 8 == 7)) & ((block // 5 < 4) | ((column // 8) % 8 == 7))
    to_nodal(jnp.where(once, columns, 0.0), spread_ref, nodal_ref)


def finish_kernel(before_ref, nodal_ref, density_ref, face_mass_ref, spread_ref, out_ref, rows_ref, face_ref):
    packed = before_ref[0:40]
    values = unpack_face(packed, rolled(packed, 64, 1))
    rows_ref[...] = jnp.zeros(rows_ref.shape, F32)
    for c in range(3):
        for d in range(5):
            rows_ref[pl.ds(8 * d + c, 5, stride=40), :] = values[c][d][0:5]
    lane = lanes_of((8, LANES))
    tiles = []
    for pair in range(BLOCKS // 2):
        even, odd = rows_ref[16 * pair : 16 * pair + 8, :], rows_ref[16 * pair + 8 : 16 * pair + 16, :]
        tiles.append(jnp.where(lane < 64, even, rolled(odd, 64, 1)))
    to_nodal(jnp.concatenate(tiles, axis=1), spread_ref, face_ref)
    scale = step_square / (density_ref[0:1, :] * face_mass_ref[...])
    first = lax.broadcasted_iota(jnp.int32, (8, FACE), 0) == 0
    for c in range(3):
        share = face_ref[c : c + 1, :] * scale
        out_ref[0, c] = nodal_ref[8 * c : 8 * c + 8, :] + jnp.where(first, share, 0.0)


VMEM = pl.BlockSpec(memory_space=pltpu.VMEM)
HBM = pl.BlockSpec(memory_space=pltpu.HBM)


def shaped(*shape, dtype=F32):
    return jax.ShapeDtypeStruct(shape, dtype)


def call(kernel, name, outs, scratch, *args, outside=(), micros=1, room=32 * 1024):
    return pl.pallas_call(
        kernel,
        name=name,
        out_shape=outs,
        in_specs=[HBM if at in outside else VMEM for at in range(len(args))],
        out_specs=jax.tree.map(lambda _: VMEM, outs),
        scratch_shapes=scratch,
        compiler_params=pltpu.CompilerParams(vmem_limit_bytes=room * 1024),
        cost_estimate=pl.CostEstimate(flops=0, bytes_accessed=micros * 3000000, transcendentals=0),
    )(*args)


def passed_along(value, axis, steps):
    count = lax.axis_size(axis)
    return lax.ppermute(value, axis, [(source, (source + steps) % count) for source in range(count)])


def swapped(value, axis, first):
    count = lax.axis_size(axis)
    pairs = []
    for source in range(first, count, 2):
        other = (source + 1) % count
        pairs += [(source, other), (other, source)]
    return lax.ppermute(value, axis, pairs)


def far_field(low, groups):
    far = None
    for k in range(1, groups):
        moved = passed_along(low, "group", k)
        far = moved if far is None else jnp.where(lax.axis_index("group") == k, moved, far)
    return far


def per_device(disp_now, disp_prev, memory_init, density, lame_lambda, shear_mu, sls_decay, owner_map):
    ring = ("cuts", "sub")
    subs = lax.axis_size("sub")
    groups = lax.axis_size("group")

    rim = call(
        gather_kernel, "gather", shaped(8, FACE),
        [pltpu.VMEM((3, 8, FACE), F32)] * 2 + [pltpu.VMEM((8, FACE), F32), pltpu.SemaphoreType.DMA((3,))],
        disp_now, disp_prev, density, outside=(0, 1, 2), room=54 * 1024 - 120,
    )
    rim = passed_along(rim, ring, -1)

    grad_table = jnp.asarray(side_by_side(GRAD))
    force_table = jnp.asarray(cut_table(FORCE))
    face_table = jnp.asarray(cut_table(FACES))
    share_table = jnp.asarray(SHARE)
    rim_table = jnp.asarray(RIM)
    face_mass = jnp.asarray(FACE_MASS)
    mass = jnp.asarray(MASS)
    memory = memory_init[0]
    owner = jnp.transpose(owner_map, (0, 2, 1))

    state = shaped(3, ROWS, LANES)
    scale_shape = shaped(ROWS, LANES)
    five = shaped(5, 125, LANES)
    part_shape = shaped(256, LANES, dtype=BF16)
    grad_scratch = pltpu.VMEM((384, 384), F32)
    part_scratch = [grad_scratch, pltpu.VMEM((256, LANES), F32)]
    face = shaped(40, LANES)
    grad_shape = shaped(384, 384)
    flat_shape = shaped(3, 128, LANES)
    u, p, scale, m1, spread, flat, base = call(
        prologue_kernel, "prologue", [state, state, scale_shape, five, shaped(WINDOW, WIDE, dtype=BF16), flat_shape, grad_shape],
        [pltpu.VMEM((8, 56, WINDOW), F32)],
        disp_now, disp_prev, density, memory, sls_decay, mass, grad_table, face_table, force_table, rim_table, share_table, lame_lambda, shear_mu,
    )
    rows = 512 // subs
    memories = [m1]
    kept = []
    for step in range(STEPS):
        last_step = step == STEPS - 1
        arrived = (rim, spread) if step == 0 else (odd, even, face_scale)
        outs = [
            shaped(6, 125, LANES), shaped(384, 384), shaped(PAD, LANES) if last_step else face,
            shaped(3, 128, LANES, dtype=BF16), scale_shape if step == 0 else shaped(3, 40, LANES),
        ]
        if not last_step:
            outs += [face, five]
        results = call(
            lambda *refs, step=step: step_kernel(step, *refs), "step", outs,
            [grad_scratch, pltpu.VMEM((3, 128, LANES), F32), pltpu.VMEM((8, 8, WINDOW), F32), pltpu.VMEM((40, 384), F32)],
            lame_lambda, shear_mu, memories[step], sls_decay, rim_table if step == 0 else share_table, face_table, base, flat, *arrived, *kept,
        )
        strain, sigma, even, low, extra = results[0:5]
        if last_step:
            before = passed_along(even, ring, 1)
        else:
            kept.append(results[6])
            odd = swapped(results[5], ring, 1)
            even = swapped(even, ring, 0)
        far = far_field(low, groups)
        if step == 0:
            p, scale, partial, flat, base, face_scale = call(
                first_rest_kernel, "rest", [state, scale_shape, state, flat_shape, grad_shape, shaped(40, LANES)],
                [pltpu.VMEM((3, ROWS, LANES), F32)], sigma, force_table, u, p, scale, extra, mass, grad_table,
            )
        else:
            results = call(
                rest_kernel, "rest", [state] if last_step else [state, state, flat_shape, grad_shape],
                [pltpu.VMEM((3, ROWS, LANES), F32)] if last_step else [], sigma, force_table, partial, extra, p, scale, grad_table,
            )
            if last_step:
                partial = results[0]
            else:
                partial, p, flat, base = results
        shared = (strain, low, far, lame_lambda, shear_mu, grad_table)
        if step == 0:
            one = call(parts_kernel, "parts", part_shape, part_scratch, *shared)
            m2, m3, select = call(
                later_kernel, "later", [five, five, shaped(subs * LANES, LANES, dtype=BF16)], [], memory, sls_decay, owner
            )
            memories += [m2, m3]
            base, one, select, memories[2] = lax.optimization_barrier((base, one, select, m3))
        elif not last_step:
            both = call(
                both_parts_kernel, "parts", shaped(subs, rows, LANES), part_scratch, *shared, one, select
            )
            base, both = lax.optimization_barrier((base, both))
        else:
            sent = list(
                call(send_kernel, "send", [shaped(rows, LANES)] * subs, part_scratch, *shared, both, select)
            )
            order = [at ^ (at >> 1) for at in range(subs - 1, -1, -1)]
            for k in order[:-1]:
                sent[k] = lax.ppermute(sent[k], "sub", [(j, j ^ k) for j in range(subs)])
    nodal = call(nodal_kernel, "nodal", shaped(24, FACE), [], partial, spread)
    final = call(
        finish_kernel, "finish", shaped(1, 3, 8, FACE), [pltpu.VMEM((ROWS, LANES), F32), pltpu.VMEM((8, FACE), F32)],
        before, nodal, density, face_mass, spread,
    )
    kernels = call(
        lambda *refs: sum_kernel(order, *refs), "sum", shaped(250, 1, 256), [], *[sent[k] for k in order]
    )
    return final, jnp.transpose(kernels, (1, 2, 0))


def solution(mesh):
    in_specs = (
        P("group", None, ("cuts", "sub"), None),
        P("group", None, ("cuts", "sub"), None),
        P("group", None, None, None, ("cuts", "sub")),
        P(("cuts", "sub"), None),
        P(None, ("cuts", "sub")),
        P(None, ("cuts", "sub")),
        P(None, ("cuts", "sub")),
        P(("cuts", "sub"), None, None),
    )
    out_specs = (P("group", None, ("cuts", "sub"), None), P("group", ("cuts", "sub"), None))
    return jax.shard_map(
        per_device, mesh=mesh, in_specs=in_specs, out_specs=out_specs, check_vma=False
    )
```

```python
import math

import jax
import jax.numpy as jnp
import numpy as np
from jax import lax
from jax.experimental import pallas as pl
from jax.experimental.pallas import tpu as pltpu
from jax.sharding import PartitionSpec as P

STEPS = 3
EY = 8
EZ = 8
LANES = 128
SIDE = 33
FACE = SIDE * SIDE
BLOCKS = 26
ROWS = 8 * BLOCKS
WIDE = 64 * BLOCKS
JUMP = 4 * SIDE
WINDOW = 256

time_step = 0.03
step_square = 0.0009
relax_strength = (0.12, 0.08, 0.05)

F32 = jnp.float32
BF16 = jnp.bfloat16


def gll_tables():
    root_value = math.sqrt(3.0 / 7.0)
    points = [-1.0, -root_value, 0.0, root_value, 1.0]
    weights = [0.1, 49.0 / 90.0, 32.0 / 45.0, 49.0 / 90.0, 0.1]
    derivative = np.zeros((5, 5))
    for p in range(5):
        for a in range(5):
            accum = 0.0
            for m in range(5):
                if m != a:
                    factor = 1.0 / (points[a] - points[m])
                    for k in range(5):
                        if k != a and k != m:
                            factor = factor * (points[p] - points[k]) / (points[a] - points[k])
                    accum = accum + factor
            derivative[p, a] = accum
    return derivative.astype(np.float32).astype(np.float64), np.array(weights).astype(np.float32).astype(np.float64)


def node(a, b, d):
    return a * 25 + b * 5 + d


def place(a, b, d):
    return (b * 5 + d) * 8 + a


FACE_ROWS = [slice(0, 128), slice(128, 160), slice(224, 256), slice(256, 288), slice(352, 384)]


def make_tables():
    derivative, weights = gll_tables()
    grad = np.zeros((3 * 128, 128))
    force = np.zeros((ROWS, 3 * 128))
    for a in range(5):
        for b in range(5):
            for d in range(5):
                for m in range(5):
                    grad[node(a, b, d), node(m, b, d)] = derivative[a, m]
                    grad[128 + node(a, b, d), node(a, m, d)] = derivative[b, m]
                    grad[256 + node(a, b, d), node(a, b, m)] = derivative[d, m]
                    row = place(a, b, d)
                    force[row, node(m, b, d)] = -derivative[m, a] * weights[m] * weights[b] * weights[d]
                    force[row, 128 + node(a, m, d)] = -derivative[m, b] * weights[a] * weights[m] * weights[d]
                    force[row, 256 + node(a, b, m)] = -derivative[m, d] * weights[a] * weights[b] * weights[m]
    full = np.zeros((80, 3 * 128))
    first_grad, last_grad = np.zeros((3 * 128, 40)), np.zeros((3 * 128, 40))
    for b in range(5):
        for d in range(5):
            full[d * 8 + b] = force[place(0, b, d)]
            full[40 + d * 8 + b] = force[place(4, b, d)]
            first_grad[:, d * 8 + b] = grad[:, node(0, b, d)]
            last_grad[:, d * 8 + b] = grad[:, node(4, b, d)]
    face = np.concatenate([full[:, rows] for rows in FACE_ROWS], axis=1)
    first, last = cut_table(first_grad), cut_table(last_grad)
    share = np.concatenate([first[0], first[0], first[1], last[0], last[0], last[1]], axis=1)
    rim = np.concatenate([last[0], last[0], last[1], last[1], last[0], last[2]], axis=1)
    line = np.zeros(SIDE)
    for e in range(8):
        line[4 * e : 4 * e + 5] += weights
    layer = np.array([2 * weights[0], weights[1], weights[2], weights[3], 2 * weights[0], 1.0, 1.0, 1.0])
    mass = np.ones((ROWS, LANES), np.float32)
    for b in range(5):
        for d in range(5):
            for ey in range(8):
                for ez in range(8):
                    for slab in range(2):
                        at = (b * 5 + d) * 8
                        mass[at : at + 8, slab * 64 + ey * 8 + ez] = layer * line[4 * ey + b] * line[4 * ez + d]
    face_mass = (layer[0] * np.outer(line, line)).reshape(1, FACE).astype(np.float32)
    return grad, force, face, mass, face_mass, share, rim


def side_by_side(table):
    high, middle, low = cut_table(table)
    pairs = ((high, middle), (middle, high), (low, high))
    return np.stack([np.concatenate(pair, axis=1) for pair in pairs])


def cut_table(table):
    value = table.astype(np.float32)
    pieces = []
    for _ in range(3):
        piece = value.astype(jnp.bfloat16)
        pieces.append(piece)
        value = value - piece.astype(np.float32)
    return np.stack(pieces)


GRAD, FORCE, FACES, MASS, FACE_MASS, SHARE, RIM = make_tables()


def cut(value):
    high = value.astype(BF16)
    rest = value - high.astype(F32)
    middle = rest.astype(BF16)
    low = (rest - middle.astype(F32)).astype(BF16)
    return high, middle, low


def dot(left, right):
    return jnp.dot(left, right, preferred_element_type=F32)


def gradients(table, flat):
    high, middle, low = cut(flat)
    first = dot(table[0:2].reshape(768, 256), jnp.concatenate([high, middle], axis=0))
    return first[0:384] + (first[384:768] + dot(table[2], jnp.concatenate([high, low], axis=0)))


def low_gradients(table, low):
    return dot(table[0], jnp.concatenate([low, low], axis=0)) + dot(table[2, :, 0:128], low)


def flatten(u_ref, flat_ref):
    for c in range(3):
        flat_ref[c, 120:128, :] = jnp.zeros((8, LANES), F32)
        for a in range(5):
            flat_ref[c, 25 * a : 25 * a + 25, :] = u_ref[c, pl.ds(a, 25, stride=8), :]


def dot_three(table, value):
    rows = table.shape[1]
    stacked = table[0:2].reshape(2 * rows, table.shape[2])
    high, middle, _ = cut(value)
    first = dot(stacked, high)
    return first[0:rows] + (first[rows : 2 * rows] + dot(stacked[0:rows], middle))


def lanes_of(shape):
    return lax.broadcasted_iota(jnp.int32, shape, len(shape) - 1)


def rolled(value, shift, axis):
    return pltpu.roll(value, shift % value.shape[axis], axis)


def window_rows(value, window_ref):
    for ey in range(EY):
        width = min(WINDOW, FACE - JUMP * ey)
        if width < WINDOW:
            window_ref[ey] = jnp.zeros(window_ref.shape[1:], F32)
        window_ref[ey, :, 0:width] = value[:, JUMP * ey : JUMP * ey + width]
    return window_ref[...].reshape(-1, WINDOW)


def to_columns(value, window_ref, spread_ref):
    rows = value.shape[0]
    pieces = jnp.concatenate(cut(window_rows(value, window_ref)), axis=0)
    wide = dot(pieces, spread_ref[...])
    half = EY * rows
    own = (lanes_of((rows, WIDE)) // 8) % 8
    picked = 0.0
    for ey in range(EY):
        at = slice(ey * rows, (ey + 1) * rows)
        value = wide[at] + wide[half : 2 * half][at] + wide[2 * half : 3 * half][at]
        picked = jnp.where(own == ey, value, picked)
    return picked


def assembled(blocks):
    lane = lanes_of((8, LANES))
    blocks = dict(blocks)
    for shift, at, pairs in (
        (1, lane % 8, [((b, 0), (b, 4)) for b in range(5)]),
        (8, (lane // 8) % 8, [((0, d), (4, d)) for d in range(5)]),
    ):
        for c in range(3):
            for near, far in pairs:
                first, last = blocks[(c,) + near], blocks[(c,) + far]
                blocks[(c,) + near] = first + jnp.where(at > 0, rolled(last, shift, 1), 0.0)
                blocks[(c,) + far] = last + jnp.where(at < 7, rolled(first, -shift, 1), 0.0)
    return blocks


def block_rows(b, d):
    return slice((b * 5 + d) * 8, (b * 5 + d) * 8 + 8)


def beside(value):
    return jnp.concatenate([value[0], value[1], value[2]], axis=1)


def gather_kernel(now_ref, prev_ref, density_ref, rim_ref, now_copy, prev_copy, density_copy, sems):
    copies = [
        pltpu.make_async_copy(now_ref.at[0], now_copy, sems.at[0]),
        pltpu.make_async_copy(prev_ref.at[0], prev_copy, sems.at[1]),
        pltpu.make_async_copy(density_ref, density_copy, sems.at[2]),
    ]
    for copy in copies:
        copy.start()
    for copy in copies:
        copy.wait()
    for c in range(3):
        rim_ref[c : c + 1, :] = now_copy[c, 0:1, :]
        rim_ref[3 + c : 4 + c, :] = prev_copy[c, 0:1, :]
    rim_ref[6:7, :] = density_copy[0:1, :]
    rim_ref[7:8, :] = density_copy[0:1, :]


def weighted_memory(memory_ref, decays, part, power):
    value = 0.0
    for l in range(3):
        factor = decays[l]
        for _ in range(power - 1):
            factor = factor * decays[l]
        value = value + factor * memory_ref[l, part]
    return value


def spread_table():
    column = lanes_of((1, WIDE))
    block = column // 64
    spot = (block // 5) * SIDE + (block % 5) + 4 * (column % 8)
    spot = jnp.where(block < 25, spot, WINDOW)
    return jnp.where(lax.broadcasted_iota(jnp.int32, (WINDOW, WIDE), 0) == spot, 1.0, 0.0).astype(BF16)


def prologue_kernel(now_ref, prev_ref, density_ref, memory_ref, decay_ref, mass_ref, *refs):
    grad_table = refs[0]
    u_ref, p_ref, scale_ref, m1_ref, spread_ref, flat_ref, grad_ref, window_ref = refs[-8:]
    spread_ref[...] = spread_table()
    rows = jnp.concatenate([now_ref[0].reshape(24, FACE), prev_ref[0].reshape(24, FACE), density_ref[...]], axis=0)
    columns = to_columns(rows, window_ref, spread_ref)
    lane = lanes_of((8, LANES))
    for group in range(7):
        for pair in range(BLOCKS // 2):
            tile = columns[8 * group : 8 * group + 8, LANES * pair : LANES * pair + LANES]
            swapped = rolled(tile, 64, 1)
            even = jnp.where(lane < 64, tile, rolled(swapped, 4, 0))
            odd = jnp.where(lane < 64, swapped, rolled(tile, 4, 0))
            for block, value in ((2 * pair, even), (2 * pair + 1, odd)):
                at = slice(8 * block, 8 * block + 8)
                if group < 3:
                    u_ref[group, at, :] = value
                elif group < 6:
                    p_ref[group - 3, at, :] = value
                elif block < 25:
                    scale_ref[at, :] = step_square / (value * mass_ref[at, :])
                else:
                    scale_ref[at, :] = jnp.zeros((8, LANES), F32)
    decays = [decay_ref[l : l + 1, :] for l in range(3)]
    for part in range(5):
        m1_ref[part] = weighted_memory(memory_ref, decays, part, 1)
    flatten(u_ref, flat_ref)
    lower = lanes_of((25, LANES)) < 64
    for c in range(3):
        flat_ref[c, 100:125, :] = jnp.where(lower, flat_ref[c, 100:125, :], 0.0)
    grad_ref[...] = gradients(grad_table, beside(flat_ref))


def later_kernel(memory_ref, decay_ref, owner_ref, m2_ref, m3_ref, select_ref):
    decays = [decay_ref[l : l + 1, :] for l in range(3)]
    for part in range(5):
        m2_ref[part] = weighted_memory(memory_ref, decays, part, 2)
        m3_ref[part] = weighted_memory(memory_ref, decays, part, 3)
    owner = jnp.concatenate([owner_ref[0], owner_ref[1]], axis=1)
    named = jnp.where(lax.broadcasted_iota(jnp.int32, (16, LANES), 0) == owner, 1.0, 0.0)
    earlier = lax.broadcasted_iota(jnp.int32, (LANES, LANES), 0)
    later = lax.broadcasted_iota(jnp.int32, (LANES, LANES), 1)
    ahead = jnp.where((earlier < later) & ((earlier // 64) == (later // 64)), 1.0, 0.0)
    rank = jnp.sum(named * dot(named.astype(BF16), ahead.astype(BF16)), axis=0, keepdims=True).astype(jnp.int32)
    subs = select_ref.shape[0] // LANES
    slots = 4 * EY * EZ // subs
    row = lax.broadcasted_iota(jnp.int32, select_ref.shape, 0)
    toward = (row // LANES) ^ lax.axis_index("sub")
    wanted = (lanes_of((1, LANES)) // 64) * (slots // 2) + rank
    chosen = (owner == toward) & (wanted == row % slots)
    select_ref[...] = jnp.where(chosen, 1.0, 0.0).astype(BF16)


def rim_rows(rim_ref, spread_ref, window_ref, rows_ref):
    columns = to_columns(rim_ref[...], window_ref, spread_ref)
    for pair in range(BLOCKS // 2):
        tile = columns[:, LANES * pair : LANES * pair + LANES]
        rows_ref[16 * pair : 16 * pair + 8, :] = rolled(tile, 64, 1)
        rows_ref[16 * pair + 8 : 16 * pair + 16, :] = tile


def unpack_face(here, there):
    top = lax.broadcasted_iota(jnp.int32, (8, LANES), 0) < 3
    parts = [[], [], []]
    for d in range(5):
        first, second = here[8 * d : 8 * d + 8], there[8 * d : 8 * d + 8]
        third = jnp.where(top, rolled(first, 3, 0), rolled(second, 6, 0))
        for part, line in zip(parts, (first, second, third)):
            part.append(line)
    return parts


def face_shares(odd_ref, even_ref, face_scale_ref):
    even_ring = lax.axis_index(("cuts", "sub")) % 2 == 0
    odd, even = odd_ref[...], even_ref[...]
    lower = (lanes_of((40, LANES)) < 64) == even_ring
    rows = unpack_face(jnp.where(lower, odd, even), rolled(jnp.where(lower, even, odd), 64, 1))
    lane = lanes_of((8, LANES))
    sub = lax.broadcasted_iota(jnp.int32, (8, LANES), 0)
    ez, ey = lane % 8, (lane // 8) % 8
    up, down = (sub == 0) & (ey > 0), (sub == 4) & (ey < 7)
    shares = []
    for c in range(3):
        lines = rows[c]
        first, last = lines[0], lines[4]
        lines[0] = first + jnp.where(ez > 0, rolled(last, 1, 1), 0.0)
        lines[4] = last + jnp.where(ez < 7, rolled(first, -1, 1), 0.0)
        for d in range(5):
            turned = rolled(lines[d], 4, 0)
            added = jnp.where(up, rolled(turned, 8, 1), jnp.where(down, rolled(turned, -8, 1), 0.0))
            lines[d] = face_scale_ref[8 * d : 8 * d + 8, :] * (lines[d] + added)
        shares.append(lines)
    return shares


def strains(grad, rows):
    def at(direction, c):
        return grad[direction * 128 + rows.start : direction * 128 + rows.stop, c * LANES : (c + 1) * LANES]

    return [
        at(0, 0),
        at(1, 1),
        at(2, 2),
        0.5 * (at(1, 0) + at(0, 1)),
        0.5 * (at(2, 0) + at(0, 2)),
        0.5 * (at(2, 1) + at(1, 2)),
    ]


CHUNKS = [slice(row, min(row + 8, 125)) for row in range(0, 125, 8)]


def pack_face(face, upper):
    lane = lanes_of((8, LANES))
    target = lane < 64 if upper else lane >= 64
    own = lax.broadcasted_iota(jnp.int32, (8, LANES), 0) < 5
    lines = []
    for d in range(5):
        first, second, third = [face[8 * d : 8 * d + 8, c * LANES : (c + 1) * LANES] for c in range(3)]
        moved = rolled(jnp.where(own, first, rolled(third, 5, 0)), 64, 1)
        lines.append(jnp.where(target, moved, jnp.where(own, second, rolled(third, 2, 0))))
    return jnp.concatenate(lines, axis=0)


def add_shares(shares, flat_ref):
    upper = lanes_of((5, LANES)) >= 64
    for c in range(3):
        for d in range(5):
            first, last = pl.ds(d, 5, stride=5), pl.ds(100 + d, 5, stride=5)
            flat_ref[c, first, :] = flat_ref[c, first, :] + jnp.where(upper, 0.0, shares[c][d][0:5])
            flat_ref[c, last, :] = flat_ref[c, last, :] + jnp.where(upper, shares[c][d][0:5], 0.0)


def shares_kernel(odd_ref, even_ref, face_scale_ref, flat_in, delta_ref, low_ref, flat_ref):
    shares = face_shares(odd_ref, even_ref, face_scale_ref)
    for c in range(3):
        delta_ref[c] = jnp.concatenate(shares[c], axis=0)
    flat_ref[...] = flat_in[...]
    add_shares(shares, flat_ref)
    low_ref[...] = flat_ref[...].astype(BF16)


def step_kernel(step, *refs):
    lame_ref, mu_ref, m_ref, decay_ref, share_table, face_table, base_ref = refs[0:7]
    arrived = refs[7 : 7 + (3, 4, 1)[step]]
    refs = refs[7 + len(arrived) :]
    older, refs = refs[:step], refs[step:]
    strain_ref, sigma_ref, even_ref = refs[0:3]
    if step < STEPS - 1:
        odd_ref, keep_ref, low_ref, extra_ref = refs[3:7]
    grad_ref, flat_ref, window_ref, rim_ref = refs[-4:]
    upper = lanes_of((40, 3 * LANES)) % LANES >= 64
    if step == 0:
        flat_ref[...] = arrived[0][...]
        rim_rows(arrived[1], arrived[2], window_ref, extra_ref)
        rim_ref[...] = jnp.zeros(rim_ref.shape, F32)
        for c in range(3):
            for d in range(5):
                rim_ref[8 * d : 8 * d + 5, c * LANES : (c + 1) * LANES] = extra_ref[pl.ds(8 * d + c, 5, stride=40), :]
        high, middle, low = [piece.astype(F32) for piece in cut(jnp.where(upper, rim_ref[...], 0.0))]
        stacked = [high, middle, high, middle, low, high]
        at_upper = lanes_of((25, LANES)) >= 64
        for c in range(3):
            flat_ref[c, 100:125, :] = jnp.where(at_upper, extra_ref[pl.ds(c, 25, stride=8), :], flat_ref[c, 100:125, :])
    else:
        if step == STEPS - 1:
            value = jnp.concatenate([arrived[0][c] for c in range(3)], axis=1)
        else:
            shares = face_shares(*arrived[1:4])
            value = jnp.concatenate([jnp.concatenate(lines, axis=0) for lines in shares], axis=1)
            for c in range(3):
                extra_ref[c] = value[:, c * LANES : (c + 1) * LANES]
            flat_ref[...] = arrived[0][...]
            add_shares(shares, flat_ref)
        high, middle, _ = [piece.astype(F32) for piece in cut(value)]
        stacked = []
        for at in (~upper, upper):
            stacked += [jnp.where(at, high, 0.0), jnp.where(at, middle, 0.0), jnp.where(at, high, 0.0)]
    grad_ref[...] = base_ref[...] + dot(share_table[...], jnp.concatenate(stacked, axis=0).astype(BF16))
    if step < STEPS - 1:
        low_ref[...] = flat_ref[...].astype(BF16)
    for block in range(9):
        sigma_ref[(block // 3) * 128 + 120 : (block // 3) * 128 + 128, (block % 3) * LANES : (block % 3) * LANES + LANES] = (
            jnp.zeros((8, LANES), F32)
        )
    decays = [decay_ref[l : l + 1, :] for l in range(3)]
    shares = [(1.0 - decays[l]) * relax_strength[l] for l in range(3)]
    factors = []
    for _ in range(step + 1):
        factors.append(shares[0] + shares[1] + shares[2])
        shares = [decays[l] * shares[l] for l in range(3)]
    for rows in CHUNKS:
        strain = strains(grad_ref, rows)
        for part in range(6):
            strain_ref[part, rows, :] = strain[part]
        lame = lame_ref[rows, :]
        twice_mu = 2.0 * mu_ref[rows, :]
        trace = strain[0] + strain[1] + strain[2]
        third = trace * (1.0 / 3.0)
        pulls = [twice_mu * s for s in strain]
        pull_third = twice_mu * third
        fresh = [pulls[0] - pull_third, pulls[1] - pull_third, pulls[3], pulls[4], pulls[5]]
        relax = []
        for part in range(5):
            value = m_ref[part, rows, :] + factors[0] * fresh[part]
            for back in range(step):
                value = value + factors[back + 1] * older[step - 1 - back][part, rows, :]
            relax.append(value)
            if step < STEPS - 1:
                keep_ref[part, rows, :] = fresh[part]
        bulk = lame * trace
        xx = bulk + pulls[0] - relax[0]
        yy = bulk + pulls[1] - relax[1]
        zz = bulk + pulls[2] + relax[0] + relax[1]
        xy = pulls[3] - relax[2]
        xz = pulls[4] - relax[3]
        yz = pulls[5] - relax[4]
        for direction, values in enumerate(((xx, xy, xz), (xy, yy, yz), (xz, yz, zz))):
            for c in range(3):
                sigma_ref[direction * 128 + rows.start : direction * 128 + rows.stop, c * LANES : (c + 1) * LANES] = values[c]
    faces = dot_three(face_table, jnp.concatenate([sigma_ref[rows, :] for rows in FACE_ROWS], axis=0))
    first, last = pack_face(faces[0:40], False), pack_face(faces[40:80], True)
    if step < STEPS - 1:
        even_ring = lax.axis_index(("cuts", "sub")) % 2 == 0
        odd_ref[...] = jnp.where(even_ring, first, last)
        even_ref[...] = jnp.where(even_ring, last, first)
    else:
        even_ref[...] = last


def next_state(sigma_ref, force_table, u_ref, p_ref, scale_ref, next_ref):
    force = dot_three(force_table, sigma_ref[...])
    blocks = {}
    for c in range(3):
        for b in range(5):
            for d in range(5):
                blocks[(c, b, d)] = force[block_rows(b, d), c * LANES : (c + 1) * LANES]
    blocks = assembled(blocks)
    lane = lanes_of((8, LANES))
    sub = lax.broadcasted_iota(jnp.int32, (8, LANES), 0)
    inner = ((sub == 4) & (lane < 64)) | ((sub == 0) & (lane >= 64))
    for c in range(3):
        for b in range(5):
            for d in range(5):
                value = blocks[(c, b, d)]
                value = value + jnp.where(inner, rolled(rolled(value, 4, 0), 64, 1), 0.0)
                at = block_rows(b, d)
                next_ref[c, at, :] = 2.0 * u_ref[c, at, :] - p_ref[c, at, :] + scale_ref[at, :] * value
        next_ref[c, 200:208, :] = jnp.zeros((8, LANES), F32)


def first_rest_kernel(
    sigma_ref, force_table, u_in, p_in, scale_in, rows_ref, mass_ref, grad_table,
    u_ref, scale_ref, next_ref, flat_ref, grad_ref, face_scale_ref, p_ref
):
    u_ref[...] = u_in[...]
    p_ref[...] = p_in[...]
    scale_ref[...] = scale_in[...]
    upper = lanes_of((25, LANES)) >= 64
    last = pl.ds(4, 25, stride=8)
    for c in range(3):
        u_ref[c, last, :] = jnp.where(upper, rows_ref[pl.ds(c, 25, stride=8), :], u_ref[c, last, :])
        p_ref[c, last, :] = jnp.where(upper, rows_ref[pl.ds(3 + c, 25, stride=8), :], p_ref[c, last, :])
    rim = step_square / (rows_ref[pl.ds(6, 25, stride=8), :] * mass_ref[last, :])
    scale_ref[last, :] = jnp.where(upper, rim, scale_ref[last, :])
    face_scale_ref[...] = jnp.zeros(face_scale_ref.shape, F32)
    lower = lanes_of((5, LANES)) < 64
    for d in range(5):
        first, last = pl.ds(8 * d, 5, stride=40), pl.ds(8 * d + 4, 5, stride=40)
        face_scale_ref[8 * d : 8 * d + 5, :] = jnp.where(lower, scale_ref[first, :], scale_ref[last, :])
    next_state(sigma_ref, force_table, u_ref, p_ref, scale_ref, next_ref)
    flatten(next_ref, flat_ref)
    grad_ref[...] = gradients(grad_table, beside(flat_ref))


def rest_kernel(sigma_ref, force_table, partial_ref, delta_ref, p_ref, scale_ref, grad_table, next_ref, u_ref, *refs):
    u_ref[...] = partial_ref[...]
    upper = lanes_of((5, LANES)) >= 64
    for c in range(3):
        for d in range(5):
            share = delta_ref[c, 8 * d : 8 * d + 5, :]
            first, last = pl.ds(8 * d, 5, stride=40), pl.ds(8 * d + 4, 5, stride=40)
            u_ref[c, first, :] = u_ref[c, first, :] + jnp.where(upper, 0.0, share)
            u_ref[c, last, :] = u_ref[c, last, :] + jnp.where(upper, share, 0.0)
    next_state(sigma_ref, force_table, u_ref, p_ref, scale_ref, next_ref)
    if refs:
        flat_ref, grad_ref = refs
        flatten(next_ref, flat_ref)
        grad_ref[...] = gradients(grad_table, beside(flat_ref))


def kernel_parts(strain_ref, low_ref, far_ref, lame_ref, mu_ref, grad_table, grad_ref, kernel_ref):
    forward = jnp.where(lax.axis_index("group") == 0, beside(low_ref), beside(far_ref))
    grad_ref[...] = low_gradients(grad_table, forward)
    for rows in CHUNKS:
        far = strains(grad_ref, rows)
        own = [strain_ref[part, rows, :] for part in range(6)]
        trace_own = own[0] + own[1] + own[2]
        trace_far = far[0] + far[1] + far[2]
        third_own, third_far = trace_own * (1.0 / 3.0), trace_far * (1.0 / 3.0)
        twice_mu = 2.0 * mu_ref[rows, :]
        kappa = lame_ref[rows, :] + twice_mu * (1.0 / 3.0)
        kernel_ref[rows, :] = time_step * kappa * trace_far * trace_own
        product = (
            (own[0] - third_own) * (far[0] - third_far)
            + (own[1] - third_own) * (far[1] - third_far)
            + (own[2] - third_own) * (far[2] - third_far)
            + 2.0 * (own[3] * far[3] + own[4] * far[4] + own[5] * far[5])
        )
        kernel_ref[125 + rows.start : 125 + rows.stop, :] = time_step * twice_mu * product
    kernel_ref[250:256, :] = jnp.zeros((6, LANES), F32)
    return kernel_ref[...].astype(BF16)


def placed(part, select_ref, rows):
    slots = rows // 2
    group = lanes_of((rows, LANES)) // slots
    total = lax.dot_general(part, select_ref[...], (((1,), (1,)), ((), ())), preferred_element_type=F32)
    blocks = []
    for k in range(select_ref.shape[0] // LANES):
        value = total[0:rows, k * LANES : (k + 1) * LANES]
        for j in range(1, 256 // rows):
            value = jnp.where(group == j, total[j * rows : (j + 1) * rows, k * LANES : (k + 1) * LANES], value)
        blocks.append(value)
    return blocks


def parts_kernel(strain_ref, low_ref, far_ref, lame_ref, mu_ref, grad_table, part_ref, grad_ref, kernel_ref):
    part_ref[...] = kernel_parts(strain_ref, low_ref, far_ref, lame_ref, mu_ref, grad_table, grad_ref, kernel_ref)


def both_parts_kernel(
    strain_ref, low_ref, far_ref, lame_ref, mu_ref, grad_table, one_ref, select_ref, both_ref, grad_ref, kernel_ref
):
    two = kernel_parts(strain_ref, low_ref, far_ref, lame_ref, mu_ref, grad_table, grad_ref, kernel_ref)
    rows = both_ref.shape[1]
    for k, (first, second) in enumerate(zip(placed(one_ref[...], select_ref, rows), placed(two, select_ref, rows))):
        both_ref[k] = first + second


def send_kernel(strain_ref, low_ref, far_ref, lame_ref, mu_ref, grad_table, both_ref, select_ref, *refs):
    out_refs, (grad_ref, kernel_ref) = refs[:-2], refs[-2:]
    three = kernel_parts(strain_ref, low_ref, far_ref, lame_ref, mu_ref, grad_table, grad_ref, kernel_ref)
    for k, (ref, value) in enumerate(zip(out_refs, placed(three, select_ref, out_refs[0].shape[0]))):
        ref[...] = both_ref[k] + value


def sum_kernel(order, *refs):
    in_refs, out_ref = refs[:-1], refs[-1]
    rows = in_refs[0].shape[0]
    slots = rows // 2
    pieces = 256 // rows
    group = lanes_of((rows, LANES)) // slots
    blocks = [[jnp.zeros((rows, LANES), F32)] * 2 for _ in range(pieces)]
    for k, ref in zip(order, in_refs):
        source = lax.axis_index("sub") ^ k
        spot = source % pieces
        value = ref[...]
        for j in range(pieces):
            moved = pltpu.roll(value, ((spot + pieces - j) % pieces) * slots, 1)
            for t in range(2):
                here = (group == spot) & (source // pieces == t)
                blocks[j][t] = jnp.where(here, moved, blocks[j][t])
    value = jnp.concatenate([jnp.concatenate(row, axis=1) for row in blocks], axis=0)
    out_ref[:, 0, :] = value[0:250]


def to_nodal(columns, spread_ref, nodal_ref):
    rows = columns.shape[0]
    own = (lanes_of((rows, WIDE)) // 8) % 8
    expanded = jnp.concatenate([jnp.where(own == ey, columns, 0.0) for ey in range(EY)], axis=0)
    over_lanes = (((1,), (1,)), ((), ()))
    pieces = jnp.concatenate(cut(expanded), axis=0)
    windows = lax.dot_general(pieces, spread_ref[...], over_lanes, preferred_element_type=F32)
    half = EY * rows
    windows = windows[0:half] + windows[half : 2 * half] + windows[2 * half : 3 * half]
    nodal_ref[...] = jnp.zeros(nodal_ref.shape, F32)
    for ey in range(EY):
        at = slice(JUMP * ey, JUMP * ey + 5 * SIDE)
        nodal_ref[:, at] = nodal_ref[:, at] + windows[ey * rows : (ey + 1) * rows, 0 : 5 * SIDE]


def nodal_kernel(partial_ref, spread_ref, nodal_ref):
    lane = lanes_of((8, LANES))
    sub = lax.broadcasted_iota(jnp.int32, (8, LANES), 0)
    tiles = []
    for c in range(3):
        row = []
        for pair in range(BLOCKS // 2):
            even = partial_ref[c, 16 * pair : 16 * pair + 8, :]
            odd = partial_ref[c, 16 * pair + 8 : 16 * pair + 16, :]
            low = jnp.where(sub < 4, even, rolled(rolled(even, 64, 1), 4, 0))
            high = jnp.where(sub < 4, rolled(odd, 64, 1), rolled(odd, 4, 0))
            row.append(jnp.where(lane < 64, low, high))
        tiles.append(jnp.concatenate(row, axis=1))
    columns = jnp.concatenate(tiles, axis=0)
    column = lanes_of((24, WIDE))
    block = column // 64
    once = ((block % 5 < 4) | (column % 8 == 7)) & ((block // 5 < 4) | ((column // 8) % 8 == 7))
    to_nodal(jnp.where(once, columns, 0.0), spread_ref, nodal_ref)


def finish_kernel(before_ref, nodal_ref, density_ref, face_mass_ref, spread_ref, out_ref, rows_ref, face_ref):
    packed = before_ref[...]
    values = unpack_face(packed, rolled(packed, 64, 1))
    rows_ref[...] = jnp.zeros(rows_ref.shape, F32)
    for c in range(3):
        for d in range(5):
            rows_ref[pl.ds(8 * d + c, 5, stride=40), :] = values[c][d][0:5]
    lane = lanes_of((8, LANES))
    tiles = []
    for pair in range(BLOCKS // 2):
        even, odd = rows_ref[16 * pair : 16 * pair + 8, :], rows_ref[16 * pair + 8 : 16 * pair + 16, :]
        tiles.append(jnp.where(lane < 64, even, rolled(odd, 64, 1)))
    to_nodal(jnp.concatenate(tiles, axis=1), spread_ref, face_ref)
    scale = step_square / (density_ref[0:1, :] * face_mass_ref[...])
    first = lax.broadcasted_iota(jnp.int32, (8, FACE), 0) == 0
    for c in range(3):
        share = face_ref[c : c + 1, :] * scale
        out_ref[0, c] = nodal_ref[8 * c : 8 * c + 8, :] + jnp.where(first, share, 0.0)


VMEM = pl.BlockSpec(memory_space=pltpu.VMEM)
HBM = pl.BlockSpec(memory_space=pltpu.HBM)


def shaped(*shape, dtype=F32):
    return jax.ShapeDtypeStruct(shape, dtype)


def call(kernel, name, outs, scratch, *args, outside=(), flops=0, room=32 * 1024):
    return pl.pallas_call(
        kernel,
        name=name,
        out_shape=outs,
        in_specs=[HBM if at in outside else VMEM for at in range(len(args))],
        out_specs=jax.tree.map(lambda _: VMEM, outs),
        scratch_shapes=scratch,
        compiler_params=pltpu.CompilerParams(vmem_limit_bytes=room * 1024),
        cost_estimate=pl.CostEstimate(flops=flops, bytes_accessed=3000000, transcendentals=0),
    )(*args)


def passed_along(value, axis, steps):
    count = lax.axis_size(axis)
    return lax.ppermute(value, axis, [(source, (source + steps) % count) for source in range(count)])


def swapped(value, axis, first):
    count = lax.axis_size(axis)
    pairs = []
    for source in range(first, count, 2):
        other = (source + 1) % count
        pairs += [(source, other), (other, source)]
    return lax.ppermute(value, axis, pairs)


def far_field(low, groups):
    far = None
    for k in range(1, groups):
        moved = passed_along(low, "group", k)
        far = moved if far is None else jnp.where(lax.axis_index("group") == k, moved, far)
    return far


def per_device(disp_now, disp_prev, memory_init, density, lame_lambda, shear_mu, sls_decay, owner_map):
    ring = ("cuts", "sub")
    subs = lax.axis_size("sub")
    groups = lax.axis_size("group")

    rim = call(
        gather_kernel, "gather", shaped(8, FACE),
        [pltpu.VMEM((3, 8, FACE), F32)] * 2 + [pltpu.VMEM((8, FACE), F32), pltpu.SemaphoreType.DMA((3,))],
        disp_now, disp_prev, density, outside=(0, 1, 2), room=54 * 1024 - 120,
    )
    rim = passed_along(rim, ring, -1)

    grad_table = jnp.asarray(side_by_side(GRAD))
    force_table = jnp.asarray(cut_table(FORCE))
    face_table = jnp.asarray(cut_table(FACES))
    share_table = jnp.asarray(SHARE)
    rim_table = jnp.asarray(RIM)
    face_mass = jnp.asarray(FACE_MASS)
    mass = jnp.asarray(MASS)
    memory = memory_init[0]
    owner = jnp.transpose(owner_map, (0, 2, 1))

    state = shaped(3, ROWS, LANES)
    scale_shape = shaped(ROWS, LANES)
    five = shaped(5, 125, LANES)
    part_shape = shaped(256, LANES, dtype=BF16)
    grad_scratch = pltpu.VMEM((384, 384), F32)
    part_scratch = [grad_scratch, pltpu.VMEM((256, LANES), F32)]
    face = shaped(40, LANES)
    grad_shape = shaped(384, 384)
    flat_shape = shaped(3, 128, LANES)
    u, p, scale, m1, spread, flat, base = call(
        prologue_kernel, "prologue", [state, state, scale_shape, five, shaped(WINDOW, WIDE, dtype=BF16), flat_shape, grad_shape],
        [pltpu.VMEM((8, 56, WINDOW), F32)],
        disp_now, disp_prev, density, memory, sls_decay, mass, grad_table, face_table, force_table, rim_table, share_table, lame_lambda, shear_mu,
    )
    rows = 512 // subs
    memories = [m1]
    kept = []
    for step in range(STEPS):
        last_step = step == STEPS - 1
        low_shape = shaped(3, 128, LANES, dtype=BF16)
        if last_step:
            extra, low = call(
                shares_kernel, "shares", [shaped(3, 40, LANES), low_shape], [pltpu.VMEM((3, 128, LANES), F32)],
                odd, even, face_scale, flat,
            )
            far = far_field(low, groups)
            arrived = (extra,)
        else:
            arrived = (flat, rim, spread) if step == 0 else (flat, odd, even, face_scale)
        outs = [shaped(6, 125, LANES), grad_shape, face]
        if not last_step:
            outs += [face, five, low_shape, scale_shape if step == 0 else shaped(3, 40, LANES)]
        results = call(
            lambda *refs, step=step: step_kernel(step, *refs), "step", outs,
            [grad_scratch, pltpu.VMEM((3, 128, LANES), F32), pltpu.VMEM((8, 8, WINDOW), F32), pltpu.VMEM((40, 384), F32)],
            lame_lambda, shear_mu, memories[step], sls_decay, rim_table if step == 0 else share_table, face_table, base, *arrived, *kept,
        )
        strain, sigma, even = results[0:3]
        if last_step:
            before = passed_along(even, ring, 1)
        else:
            odd, keep, low, extra = results[3:7]
            kept.append(keep)
            odd = swapped(odd, ring, 1)
            even = swapped(even, ring, 0)
            far = far_field(low, groups)
        if step == 0:
            p, scale, partial, flat, base, face_scale = call(
                first_rest_kernel, "rest", [state, scale_shape, state, flat_shape, grad_shape, shaped(40, LANES)],
                [pltpu.VMEM((3, ROWS, LANES), F32)], sigma, force_table, u, p, scale, extra, mass, grad_table,
            )
        else:
            results = call(
                rest_kernel, "rest", [state] if last_step else [state, state, flat_shape, grad_shape],
                [pltpu.VMEM((3, ROWS, LANES), F32)] if last_step else [], sigma, force_table, partial, extra, p, scale, grad_table,
            )
            if last_step:
                partial = results[0]
            else:
                partial, p, flat, base = results
        shared = (strain, low, far, lame_lambda, shear_mu, grad_table)
        if step == 0:
            one = call(parts_kernel, "parts", part_shape, part_scratch, *shared)
            m2, m3, select = call(
                later_kernel, "later", [five, five, shaped(subs * LANES, LANES, dtype=BF16)], [], memory, sls_decay, owner
            )
            memories += [m2, m3]
            base, one, select, memories[2] = lax.optimization_barrier((base, one, select, m3))
        elif not last_step:
            both = call(
                both_parts_kernel, "parts", shaped(subs, rows, LANES), part_scratch, *shared, one, select
            )
            base, flat, both = lax.optimization_barrier((base, flat, both))
        else:
            sent = list(
                call(send_kernel, "send", [shaped(rows, LANES)] * subs, part_scratch, *shared, both, select)
            )
            order = [at ^ (at >> 1) for at in range(subs - 1, -1, -1)]
            for k in order[:-1]:
                sent[k] = lax.ppermute(sent[k], "sub", [(j, j ^ k) for j in range(subs)])
    nodal = call(nodal_kernel, "nodal", shaped(24, FACE), [], partial, spread)
    final = call(
        finish_kernel, "finish", shaped(1, 3, 8, FACE), [pltpu.VMEM((ROWS, LANES), F32), pltpu.VMEM((8, FACE), F32)],
        before, nodal, density, face_mass, spread, flops=550000000,
    )
    kernels = call(
        lambda *refs: sum_kernel(order, *refs), "sum", shaped(250, 1, 256), [], *[sent[k] for k in order]
    )
    return final, jnp.transpose(kernels, (1, 2, 0))


def solution(mesh):
    in_specs = (
        P("group", None, ("cuts", "sub"), None),
        P("group", None, ("cuts", "sub"), None),
        P("group", None, None, None, ("cuts", "sub")),
        P(("cuts", "sub"), None),
        P(None, ("cuts", "sub")),
        P(None, ("cuts", "sub")),
        P(None, ("cuts", "sub")),
        P(("cuts", "sub"), None, None),
    )
    out_specs = (P("group", None, ("cuts", "sub"), None), P("group", ("cuts", "sub"), None))
    return jax.shard_map(
        per_device, mesh=mesh, in_specs=in_specs, out_specs=out_specs, check_vma=False
    )
```

```python
import math

import jax
import jax.numpy as jnp
import numpy as np
from jax import lax
from jax.experimental import pallas as pl
from jax.experimental.pallas import tpu as pltpu
from jax.sharding import PartitionSpec as P

STEPS = 3
EY = 8
EZ = 8
LANES = 128
SIDE = 33
FACE = SIDE * SIDE
BLOCKS = 26
ROWS = 8 * BLOCKS
WIDE = 64 * BLOCKS
JUMP = 4 * SIDE
WINDOW = 256

time_step = 0.03
step_square = 0.0009
relax_strength = (0.12, 0.08, 0.05)

F32 = jnp.float32
BF16 = jnp.bfloat16


def gll_tables():
    root_value = math.sqrt(3.0 / 7.0)
    points = [-1.0, -root_value, 0.0, root_value, 1.0]
    weights = [0.1, 49.0 / 90.0, 32.0 / 45.0, 49.0 / 90.0, 0.1]
    derivative = np.zeros((5, 5))
    for p in range(5):
        for a in range(5):
            accum = 0.0
            for m in range(5):
                if m != a:
                    factor = 1.0 / (points[a] - points[m])
                    for k in range(5):
                        if k != a and k != m:
                            factor = factor * (points[p] - points[k]) / (points[a] - points[k])
                    accum = accum + factor
            derivative[p, a] = accum
    return derivative.astype(np.float32).astype(np.float64), np.array(weights).astype(np.float32).astype(np.float64)


def node(a, b, d):
    return a * 25 + b * 5 + d


def place(a, b, d):
    return (b * 5 + d) * 8 + a


FACE_ROWS = [slice(0, 128), slice(128, 160), slice(224, 256), slice(256, 288), slice(352, 384)]


def make_tables():
    derivative, weights = gll_tables()
    grad = np.zeros((3 * 128, 128))
    force = np.zeros((ROWS, 3 * 128))
    for a in range(5):
        for b in range(5):
            for d in range(5):
                for m in range(5):
                    grad[node(a, b, d), node(m, b, d)] = derivative[a, m]
                    grad[128 + node(a, b, d), node(a, m, d)] = derivative[b, m]
                    grad[256 + node(a, b, d), node(a, b, m)] = derivative[d, m]
                    row = place(a, b, d)
                    force[row, node(m, b, d)] = -derivative[m, a] * weights[m] * weights[b] * weights[d]
                    force[row, 128 + node(a, m, d)] = -derivative[m, b] * weights[a] * weights[m] * weights[d]
                    force[row, 256 + node(a, b, m)] = -derivative[m, d] * weights[a] * weights[b] * weights[m]
    full = np.zeros((80, 3 * 128))
    first_grad, last_grad = np.zeros((3 * 128, 40)), np.zeros((3 * 128, 40))
    for b in range(5):
        for d in range(5):
            full[d * 8 + b] = force[place(0, b, d)]
            full[40 + d * 8 + b] = force[place(4, b, d)]
            first_grad[:, d * 8 + b] = grad[:, node(0, b, d)]
            last_grad[:, d * 8 + b] = grad[:, node(4, b, d)]
    face = np.concatenate([full[:, rows] for rows in FACE_ROWS], axis=1)
    first, last = cut_table(first_grad), cut_table(last_grad)
    share = np.concatenate([first[0], first[0], first[1], last[0], last[0], last[1]], axis=1)
    rim = np.concatenate([last[0], last[0], last[1], last[1], last[0], last[2]], axis=1)
    line = np.zeros(SIDE)
    for e in range(8):
        line[4 * e : 4 * e + 5] += weights
    layer = np.array([2 * weights[0], weights[1], weights[2], weights[3], 2 * weights[0], 1.0, 1.0, 1.0])
    mass = np.ones((ROWS, LANES), np.float32)
    for b in range(5):
        for d in range(5):
            for ey in range(8):
                for ez in range(8):
                    for slab in range(2):
                        at = (b * 5 + d) * 8
                        mass[at : at + 8, slab * 64 + ey * 8 + ez] = layer * line[4 * ey + b] * line[4 * ez + d]
    face_mass = (layer[0] * np.outer(line, line)).reshape(1, FACE).astype(np.float32)
    return grad, force, face, mass, face_mass, share, rim


def side_by_side(table):
    high, middle, low = cut_table(table)
    pairs = ((high, middle), (middle, high), (low, high))
    return np.stack([np.concatenate(pair, axis=1) for pair in pairs])


def cut_table(table):
    value = table.astype(np.float32)
    pieces = []
    for _ in range(3):
        piece = value.astype(jnp.bfloat16)
        pieces.append(piece)
        value = value - piece.astype(np.float32)
    return np.stack(pieces)


GRAD, FORCE, FACES, MASS, FACE_MASS, SHARE, RIM = make_tables()


def cut(value):
    high = value.astype(BF16)
    rest = value - high.astype(F32)
    middle = rest.astype(BF16)
    low = (rest - middle.astype(F32)).astype(BF16)
    return high, middle, low


def dot(left, right):
    return jnp.dot(left, right, preferred_element_type=F32)


def gradients(table, flat):
    high, middle, low = cut(flat)
    first = dot(table[0:2].reshape(768, 256), jnp.concatenate([high, middle], axis=0))
    return first[0:384] + (first[384:768] + dot(table[2], jnp.concatenate([high, low], axis=0)))


def low_gradients(table, low):
    return dot(table[0], jnp.concatenate([low, low], axis=0)) + dot(table[2, :, 0:128], low)


def flatten(u_ref, flat_ref):
    for c in range(3):
        flat_ref[c, 120:128, :] = jnp.zeros((8, LANES), F32)
        for a in range(5):
            flat_ref[c, 25 * a : 25 * a + 25, :] = u_ref[c, pl.ds(a, 25, stride=8), :]


def dot_three(table, value):
    rows = table.shape[1]
    stacked = table[0:2].reshape(2 * rows, table.shape[2])
    high, middle, _ = cut(value)
    first = dot(stacked, high)
    return first[0:rows] + (first[rows : 2 * rows] + dot(stacked[0:rows], middle))


def lanes_of(shape):
    return lax.broadcasted_iota(jnp.int32, shape, len(shape) - 1)


def rolled(value, shift, axis):
    return pltpu.roll(value, shift % value.shape[axis], axis)


def window_rows(value, window_ref):
    for ey in range(EY):
        width = min(WINDOW, FACE - JUMP * ey)
        if width < WINDOW:
            window_ref[ey] = jnp.zeros(window_ref.shape[1:], F32)
        window_ref[ey, :, 0:width] = value[:, JUMP * ey : JUMP * ey + width]
    return window_ref[...].reshape(-1, WINDOW)


def to_columns(value, window_ref, spread_ref):
    rows = value.shape[0]
    pieces = jnp.concatenate(cut(window_rows(value, window_ref)), axis=0)
    wide = dot(pieces, spread_ref[...])
    half = EY * rows
    own = (lanes_of((rows, WIDE)) // 8) % 8
    picked = 0.0
    for ey in range(EY):
        at = slice(ey * rows, (ey + 1) * rows)
        value = wide[at] + wide[half : 2 * half][at] + wide[2 * half : 3 * half][at]
        picked = jnp.where(own == ey, value, picked)
    return picked


def assembled(blocks):
    lane = lanes_of((8, LANES))
    blocks = dict(blocks)
    for shift, at, pairs in (
        (1, lane % 8, [((b, 0), (b, 4)) for b in range(5)]),
        (8, (lane // 8) % 8, [((0, d), (4, d)) for d in range(5)]),
    ):
        for c in range(3):
            for near, far in pairs:
                first, last = blocks[(c,) + near], blocks[(c,) + far]
                blocks[(c,) + near] = first + jnp.where(at > 0, rolled(last, shift, 1), 0.0)
                blocks[(c,) + far] = last + jnp.where(at < 7, rolled(first, -shift, 1), 0.0)
    return blocks


def block_rows(b, d):
    return slice((b * 5 + d) * 8, (b * 5 + d) * 8 + 8)


def beside(value):
    return jnp.concatenate([value[0], value[1], value[2]], axis=1)


def gather_kernel(now_ref, prev_ref, density_ref, rim_ref, now_copy, prev_copy, density_copy, sems):
    copies = [
        pltpu.make_async_copy(now_ref.at[0], now_copy, sems.at[0]),
        pltpu.make_async_copy(prev_ref.at[0], prev_copy, sems.at[1]),
        pltpu.make_async_copy(density_ref, density_copy, sems.at[2]),
    ]
    for copy in copies:
        copy.start()
    for copy in copies:
        copy.wait()
    for c in range(3):
        rim_ref[c : c + 1, :] = now_copy[c, 0:1, :]
        rim_ref[3 + c : 4 + c, :] = prev_copy[c, 0:1, :]
    rim_ref[6:7, :] = density_copy[0:1, :]
    rim_ref[7:8, :] = density_copy[0:1, :]


def weighted_memory(memory_ref, decays, part, power):
    value = 0.0
    for l in range(3):
        factor = decays[l]
        for _ in range(power - 1):
            factor = factor * decays[l]
        value = value + factor * memory_ref[l, part]
    return value


def spread_table():
    column = lanes_of((1, WIDE))
    block = column // 64
    spot = (block // 5) * SIDE + (block % 5) + 4 * (column % 8)
    spot = jnp.where(block < 25, spot, WINDOW)
    return jnp.where(lax.broadcasted_iota(jnp.int32, (WINDOW, WIDE), 0) == spot, 1.0, 0.0).astype(BF16)


def prologue_kernel(now_ref, prev_ref, density_ref, memory_ref, decay_ref, mass_ref, *refs):
    grad_table = refs[0]
    u_ref, p_ref, scale_ref, m1_ref, spread_ref, flat_ref, grad_ref, window_ref = refs[-8:]
    spread_ref[...] = spread_table()
    rows = jnp.concatenate([now_ref[0].reshape(24, FACE), prev_ref[0].reshape(24, FACE), density_ref[...]], axis=0)
    columns = to_columns(rows, window_ref, spread_ref)
    lane = lanes_of((8, LANES))
    for group in range(7):
        for pair in range(BLOCKS // 2):
            tile = columns[8 * group : 8 * group + 8, LANES * pair : LANES * pair + LANES]
            swapped = rolled(tile, 64, 1)
            even = jnp.where(lane < 64, tile, rolled(swapped, 4, 0))
            odd = jnp.where(lane < 64, swapped, rolled(tile, 4, 0))
            for block, value in ((2 * pair, even), (2 * pair + 1, odd)):
                at = slice(8 * block, 8 * block + 8)
                if group < 3:
                    u_ref[group, at, :] = value
                elif group < 6:
                    p_ref[group - 3, at, :] = value
                elif block < 25:
                    scale_ref[at, :] = step_square / (value * mass_ref[at, :])
                else:
                    scale_ref[at, :] = jnp.zeros((8, LANES), F32)
    decays = [decay_ref[l : l + 1, :] for l in range(3)]
    for part in range(5):
        m1_ref[part] = weighted_memory(memory_ref, decays, part, 1)
    flatten(u_ref, flat_ref)
    lower = lanes_of((25, LANES)) < 64
    for c in range(3):
        flat_ref[c, 100:125, :] = jnp.where(lower, flat_ref[c, 100:125, :], 0.0)
    grad_ref[...] = gradients(grad_table, beside(flat_ref))


def later_kernel(memory_ref, decay_ref, owner_ref, m2_ref, m3_ref, select_ref):
    decays = [decay_ref[l : l + 1, :] for l in range(3)]
    for part in range(5):
        m2_ref[part] = weighted_memory(memory_ref, decays, part, 2)
        m3_ref[part] = weighted_memory(memory_ref, decays, part, 3)
    owner = jnp.concatenate([owner_ref[0], owner_ref[1]], axis=1)
    named = jnp.where(lax.broadcasted_iota(jnp.int32, (16, LANES), 0) == owner, 1.0, 0.0)
    earlier = lax.broadcasted_iota(jnp.int32, (LANES, LANES), 0)
    later = lax.broadcasted_iota(jnp.int32, (LANES, LANES), 1)
    ahead = jnp.where((earlier < later) & ((earlier // 64) == (later // 64)), 1.0, 0.0)
    rank = jnp.sum(named * dot(named.astype(BF16), ahead.astype(BF16)), axis=0, keepdims=True).astype(jnp.int32)
    subs = select_ref.shape[0] // LANES
    slots = 4 * EY * EZ // subs
    row = lax.broadcasted_iota(jnp.int32, select_ref.shape, 0)
    toward = (row // LANES) ^ lax.axis_index("sub")
    wanted = (lanes_of((1, LANES)) // 64) * (slots // 2) + rank
    chosen = (owner == toward) & (wanted == row % slots)
    select_ref[...] = jnp.where(chosen, 1.0, 0.0).astype(BF16)


def rim_rows(rim_ref, spread_ref, window_ref, rows_ref):
    columns = to_columns(rim_ref[...], window_ref, spread_ref)
    for pair in range(BLOCKS // 2):
        tile = columns[:, LANES * pair : LANES * pair + LANES]
        rows_ref[16 * pair : 16 * pair + 8, :] = rolled(tile, 64, 1)
        rows_ref[16 * pair + 8 : 16 * pair + 16, :] = tile


def unpack_face(here, there):
    top = lax.broadcasted_iota(jnp.int32, (8, LANES), 0) < 3
    parts = [[], [], []]
    for d in range(5):
        first, second = here[8 * d : 8 * d + 8], there[8 * d : 8 * d + 8]
        third = jnp.where(top, rolled(first, 3, 0), rolled(second, 6, 0))
        for part, line in zip(parts, (first, second, third)):
            part.append(line)
    return parts


def face_shares(odd_ref, even_ref, face_scale_ref):
    even_ring = lax.axis_index(("cuts", "sub")) % 2 == 0
    odd, even = odd_ref[...], even_ref[...]
    lower = (lanes_of((40, LANES)) < 64) == even_ring
    rows = unpack_face(jnp.where(lower, odd, even), rolled(jnp.where(lower, even, odd), 64, 1))
    lane = lanes_of((8, LANES))
    sub = lax.broadcasted_iota(jnp.int32, (8, LANES), 0)
    ez, ey = lane % 8, (lane // 8) % 8
    up, down = (sub == 0) & (ey > 0), (sub == 4) & (ey < 7)
    shares = []
    for c in range(3):
        lines = rows[c]
        first, last = lines[0], lines[4]
        lines[0] = first + jnp.where(ez > 0, rolled(last, 1, 1), 0.0)
        lines[4] = last + jnp.where(ez < 7, rolled(first, -1, 1), 0.0)
        for d in range(5):
            turned = rolled(lines[d], 4, 0)
            added = jnp.where(up, rolled(turned, 8, 1), jnp.where(down, rolled(turned, -8, 1), 0.0))
            lines[d] = face_scale_ref[8 * d : 8 * d + 8, :] * (lines[d] + added)
        shares.append(lines)
    return shares


def strains(grad, rows):
    def at(direction, c):
        return grad[direction * 128 + rows.start : direction * 128 + rows.stop, c * LANES : (c + 1) * LANES]

    return [
        at(0, 0),
        at(1, 1),
        at(2, 2),
        0.5 * (at(1, 0) + at(0, 1)),
        0.5 * (at(2, 0) + at(0, 2)),
        0.5 * (at(2, 1) + at(1, 2)),
    ]


CHUNKS = [slice(row, min(row + 8, 125)) for row in range(0, 125, 8)]


def pack_face(face, upper):
    lane = lanes_of((8, LANES))
    target = lane < 64 if upper else lane >= 64
    own = lax.broadcasted_iota(jnp.int32, (8, LANES), 0) < 5
    lines = []
    for d in range(5):
        first, second, third = [face[8 * d : 8 * d + 8, c * LANES : (c + 1) * LANES] for c in range(3)]
        moved = rolled(jnp.where(own, first, rolled(third, 5, 0)), 64, 1)
        lines.append(jnp.where(target, moved, jnp.where(own, second, rolled(third, 2, 0))))
    return jnp.concatenate(lines, axis=0)


def add_shares(shares, flat_ref):
    upper = lanes_of((5, LANES)) >= 64
    for c in range(3):
        for d in range(5):
            first, last = pl.ds(d, 5, stride=5), pl.ds(100 + d, 5, stride=5)
            flat_ref[c, first, :] = flat_ref[c, first, :] + jnp.where(upper, 0.0, shares[c][d][0:5])
            flat_ref[c, last, :] = flat_ref[c, last, :] + jnp.where(upper, shares[c][d][0:5], 0.0)


def shares_kernel(odd_ref, even_ref, face_scale_ref, flat_in, delta_ref, low_ref, flat_ref):
    shares = face_shares(odd_ref, even_ref, face_scale_ref)
    for c in range(3):
        delta_ref[c] = jnp.concatenate(shares[c], axis=0)
    flat_ref[...] = flat_in[...]
    add_shares(shares, flat_ref)
    low_ref[...] = flat_ref[...].astype(BF16)


def step_kernel(step, *refs):
    lame_ref, mu_ref, m_ref, decay_ref, share_table, face_table, base_ref = refs[0:7]
    arrived = refs[7 : 7 + (3, 4, 1)[step]]
    refs = refs[7 + len(arrived) :]
    older, refs = refs[:step], refs[step:]
    strain_ref, sigma_ref, even_ref = refs[0:3]
    if step < STEPS - 1:
        odd_ref, keep_ref, low_ref, extra_ref = refs[3:7]
    grad_ref, flat_ref, window_ref, rim_ref = refs[-4:]
    upper = lanes_of((40, 3 * LANES)) % LANES >= 64
    if step == 0:
        flat_ref[...] = arrived[0][...]
        rim_rows(arrived[1], arrived[2], window_ref, extra_ref)
        rim_ref[...] = jnp.zeros(rim_ref.shape, F32)
        for c in range(3):
            for d in range(5):
                rim_ref[8 * d : 8 * d + 5, c * LANES : (c + 1) * LANES] = extra_ref[pl.ds(8 * d + c, 5, stride=40), :]
        high, middle, low = [piece.astype(F32) for piece in cut(jnp.where(upper, rim_ref[...], 0.0))]
        stacked = [high, middle, high, middle, low, high]
        at_upper = lanes_of((25, LANES)) >= 64
        for c in range(3):
            flat_ref[c, 100:125, :] = jnp.where(at_upper, extra_ref[pl.ds(c, 25, stride=8), :], flat_ref[c, 100:125, :])
    else:
        if step == STEPS - 1:
            value = jnp.concatenate([arrived[0][c] for c in range(3)], axis=1)
        else:
            shares = face_shares(*arrived[1:4])
            value = jnp.concatenate([jnp.concatenate(lines, axis=0) for lines in shares], axis=1)
            for c in range(3):
                extra_ref[c] = value[:, c * LANES : (c + 1) * LANES]
            flat_ref[...] = arrived[0][...]
            add_shares(shares, flat_ref)
        high, middle, _ = [piece.astype(F32) for piece in cut(value)]
        stacked = []
        for at in (~upper, upper):
            stacked += [jnp.where(at, high, 0.0), jnp.where(at, middle, 0.0), jnp.where(at, high, 0.0)]
    grad_ref[...] = base_ref[...] + dot(share_table[...], jnp.concatenate(stacked, axis=0).astype(BF16))
    if step < STEPS - 1:
        low_ref[...] = flat_ref[...].astype(BF16)
    for block in range(9):
        sigma_ref[(block // 3) * 128 + 120 : (block // 3) * 128 + 128, (block % 3) * LANES : (block % 3) * LANES + LANES] = (
            jnp.zeros((8, LANES), F32)
        )
    decays = [decay_ref[l : l + 1, :] for l in range(3)]
    shares = [(1.0 - decays[l]) * relax_strength[l] for l in range(3)]
    factors = []
    for _ in range(step + 1):
        factors.append(shares[0] + shares[1] + shares[2])
        shares = [decays[l] * shares[l] for l in range(3)]
    for rows in CHUNKS:
        strain = strains(grad_ref, rows)
        for part in range(6):
            strain_ref[part, rows, :] = strain[part]
        lame = lame_ref[rows, :]
        twice_mu = 2.0 * mu_ref[rows, :]
        trace = strain[0] + strain[1] + strain[2]
        third = trace * (1.0 / 3.0)
        pulls = [twice_mu * s for s in strain]
        pull_third = twice_mu * third
        fresh = [pulls[0] - pull_third, pulls[1] - pull_third, pulls[3], pulls[4], pulls[5]]
        relax = []
        for part in range(5):
            value = m_ref[part, rows, :] + factors[0] * fresh[part]
            for back in range(step):
                value = value + factors[back + 1] * older[step - 1 - back][part, rows, :]
            relax.append(value)
            if step < STEPS - 1:
                keep_ref[part, rows, :] = fresh[part]
        bulk = lame * trace
        xx = bulk + pulls[0] - relax[0]
        yy = bulk + pulls[1] - relax[1]
        zz = bulk + pulls[2] + relax[0] + relax[1]
        xy = pulls[3] - relax[2]
        xz = pulls[4] - relax[3]
        yz = pulls[5] - relax[4]
        for direction, values in enumerate(((xx, xy, xz), (xy, yy, yz), (xz, yz, zz))):
            for c in range(3):
                sigma_ref[direction * 128 + rows.start : direction * 128 + rows.stop, c * LANES : (c + 1) * LANES] = values[c]
    faces = dot_three(face_table, jnp.concatenate([sigma_ref[rows, :] for rows in FACE_ROWS], axis=0))
    first, last = pack_face(faces[0:40], False), pack_face(faces[40:80], True)
    if step < STEPS - 1:
        even_ring = lax.axis_index(("cuts", "sub")) % 2 == 0
        odd_ref[...] = jnp.where(even_ring, first, last)
        even_ref[...] = jnp.where(even_ring, last, first)
    else:
        even_ref[...] = last


def next_state(sigma_ref, force_table, u_ref, p_ref, scale_ref, next_ref):
    force = dot_three(force_table, sigma_ref[...])
    blocks = {}
    for c in range(3):
        for b in range(5):
            for d in range(5):
                blocks[(c, b, d)] = force[block_rows(b, d), c * LANES : (c + 1) * LANES]
    blocks = assembled(blocks)
    lane = lanes_of((8, LANES))
    sub = lax.broadcasted_iota(jnp.int32, (8, LANES), 0)
    inner = ((sub == 4) & (lane < 64)) | ((sub == 0) & (lane >= 64))
    for c in range(3):
        for b in range(5):
            for d in range(5):
                value = blocks[(c, b, d)]
                value = value + jnp.where(inner, rolled(rolled(value, 4, 0), 64, 1), 0.0)
                at = block_rows(b, d)
                next_ref[c, at, :] = 2.0 * u_ref[c, at, :] - p_ref[c, at, :] + scale_ref[at, :] * value
        next_ref[c, 200:208, :] = jnp.zeros((8, LANES), F32)


def first_rest_kernel(
    sigma_ref, force_table, u_in, p_in, scale_in, rows_ref, mass_ref, grad_table,
    u_ref, scale_ref, next_ref, flat_ref, grad_ref, face_scale_ref, p_ref
):
    u_ref[...] = u_in[...]
    p_ref[...] = p_in[...]
    scale_ref[...] = scale_in[...]
    upper = lanes_of((25, LANES)) >= 64
    last = pl.ds(4, 25, stride=8)
    for c in range(3):
        u_ref[c, last, :] = jnp.where(upper, rows_ref[pl.ds(c, 25, stride=8), :], u_ref[c, last, :])
        p_ref[c, last, :] = jnp.where(upper, rows_ref[pl.ds(3 + c, 25, stride=8), :], p_ref[c, last, :])
    rim = step_square / (rows_ref[pl.ds(6, 25, stride=8), :] * mass_ref[last, :])
    scale_ref[last, :] = jnp.where(upper, rim, scale_ref[last, :])
    face_scale_ref[...] = jnp.zeros(face_scale_ref.shape, F32)
    lower = lanes_of((5, LANES)) < 64
    for d in range(5):
        first, last = pl.ds(8 * d, 5, stride=40), pl.ds(8 * d + 4, 5, stride=40)
        face_scale_ref[8 * d : 8 * d + 5, :] = jnp.where(lower, scale_ref[first, :], scale_ref[last, :])
    next_state(sigma_ref, force_table, u_ref, p_ref, scale_ref, next_ref)
    flatten(next_ref, flat_ref)
    grad_ref[...] = gradients(grad_table, beside(flat_ref))


def rest_kernel(sigma_ref, force_table, partial_ref, delta_ref, p_ref, scale_ref, grad_table, next_ref, u_ref, *refs):
    u_ref[...] = partial_ref[...]
    upper = lanes_of((5, LANES)) >= 64
    for c in range(3):
        for d in range(5):
            share = delta_ref[c, 8 * d : 8 * d + 5, :]
            first, last = pl.ds(8 * d, 5, stride=40), pl.ds(8 * d + 4, 5, stride=40)
            u_ref[c, first, :] = u_ref[c, first, :] + jnp.where(upper, 0.0, share)
            u_ref[c, last, :] = u_ref[c, last, :] + jnp.where(upper, share, 0.0)
    next_state(sigma_ref, force_table, u_ref, p_ref, scale_ref, next_ref)
    if refs:
        flat_ref, grad_ref = refs
        flatten(next_ref, flat_ref)
        grad_ref[...] = gradients(grad_table, beside(flat_ref))


def kernel_parts(strain_ref, low_ref, far_ref, lame_ref, mu_ref, grad_table, grad_ref, kernel_ref):
    forward = jnp.where(lax.axis_index("group") == 0, beside(low_ref), beside(far_ref))
    grad_ref[...] = low_gradients(grad_table, forward)
    for rows in CHUNKS:
        far = strains(grad_ref, rows)
        own = [strain_ref[part, rows, :] for part in range(6)]
        trace_own = own[0] + own[1] + own[2]
        trace_far = far[0] + far[1] + far[2]
        third_own, third_far = trace_own * (1.0 / 3.0), trace_far * (1.0 / 3.0)
        twice_mu = 2.0 * mu_ref[rows, :]
        kappa = lame_ref[rows, :] + twice_mu * (1.0 / 3.0)
        kernel_ref[rows, :] = time_step * kappa * trace_far * trace_own
        product = (
            (own[0] - third_own) * (far[0] - third_far)
            + (own[1] - third_own) * (far[1] - third_far)
            + (own[2] - third_own) * (far[2] - third_far)
            + 2.0 * (own[3] * far[3] + own[4] * far[4] + own[5] * far[5])
        )
        kernel_ref[125 + rows.start : 125 + rows.stop, :] = time_step * twice_mu * product
    kernel_ref[250:256, :] = jnp.zeros((6, LANES), F32)
    return kernel_ref[...].astype(BF16)


def placed(pieces, select, rows):
    slots = rows // 2
    group = lanes_of((rows, LANES)) // slots
    total = 0.0
    for piece in pieces:
        total = total + lax.dot_general(piece, select, (((1,), (1,)), ((), ())), preferred_element_type=F32)
    blocks = []
    for k in range(select.shape[0] // LANES):
        value = total[0:rows, k * LANES : (k + 1) * LANES]
        for j in range(1, 256 // rows):
            value = jnp.where(group == j, total[j * rows : (j + 1) * rows, k * LANES : (k + 1) * LANES], value)
        blocks.append(value)
    return blocks


def group_scale(mantissa, exponent):
    return mantissa * jnp.exp2(exponent) * (1.0 / (4096.0 * 32767.0))


def parts_kernel(strain_ref, low_ref, far_ref, lame_ref, mu_ref, grad_table, part_ref, grad_ref, kernel_ref):
    part_ref[...] = kernel_parts(strain_ref, low_ref, far_ref, lame_ref, mu_ref, grad_table, grad_ref, kernel_ref)


def both_parts_kernel(strain_ref, low_ref, far_ref, lame_ref, mu_ref, grad_table, one_ref, both_ref, grad_ref, kernel_ref):
    two = kernel_parts(strain_ref, low_ref, far_ref, lame_ref, mu_ref, grad_table, grad_ref, kernel_ref)
    both_ref[...] = one_ref[...].astype(F32) + two.astype(F32)


def send_kernel(strain_ref, low_ref, far_ref, lame_ref, mu_ref, grad_table, both_ref, select_ref, total_ref, *refs):
    out_refs, (grad_ref, kernel_ref) = refs[:-2], refs[-2:]
    three = kernel_parts(strain_ref, low_ref, far_ref, lame_ref, mu_ref, grad_table, grad_ref, kernel_ref)
    kernel_ref[...] = both_ref[...] + three.astype(F32)
    total_ref[...] = kernel_ref[...]
    for k in range(2):
        rows = slice(125 * k, 125 * k + 125)
        value = kernel_ref[rows, :]
        largest = jnp.maximum(jnp.max(jnp.abs(value), axis=0, keepdims=True), 1e-33)
        exponent = jnp.floor(jnp.log2(largest))
        mantissa = jnp.floor(largest * jnp.exp2(-exponent) * 4096.0) + 2.0
        kernel_ref[rows, :] = jnp.floor(value * (1.0 / group_scale(mantissa, exponent)) + 0.5)
        kernel_ref[250 + 2 * k : 251 + 2 * k, :] = mantissa
        kernel_ref[251 + 2 * k : 252 + 2 * k, :] = exponent
    high, middle, _ = cut(kernel_ref[...])
    for ref, value in zip(out_refs, placed((high, middle), select_ref[LANES:, :], out_refs[0].shape[0])):
        ref[...] = value.astype(jnp.int32).astype(jnp.int16)


def own_kernel(total_ref, select_ref, own_ref):
    row = lax.broadcasted_iota(jnp.int32, (256, LANES), 0)
    unit = jnp.where((row == 250) | (row == 252), 4096.0 * 32767.0, 0.0)
    value = jnp.where(row < 250, total_ref[...], unit)
    own_ref[...] = placed(cut(value), select_ref[0:LANES, :], own_ref.shape[0])[0]


def sum_kernel(order, *refs):
    in_refs, out_ref = refs[:-1], refs[-1]
    rows = in_refs[0].shape[0]
    slots = rows // 2
    pieces = 256 // rows
    group = lanes_of((rows, LANES)) // slots
    blocks = [[jnp.zeros((rows, LANES), F32)] * 2 for _ in range(pieces)]
    for k, ref in zip(order, in_refs):
        source = lax.axis_index("sub") ^ k
        spot = source % pieces
        value = ref[...].astype(jnp.int32).astype(F32) if k > 0 else ref[...]
        for j in range(pieces):
            moved = pltpu.roll(value, ((spot + pieces - j) % pieces) * slots, 1)
            for t in range(2):
                here = (group == spot) & (source // pieces == t)
                blocks[j][t] = jnp.where(here, moved, blocks[j][t])
    value = jnp.concatenate([jnp.concatenate(row, axis=1) for row in blocks], axis=0)
    first, second = [group_scale(value[row : row + 1], value[row + 1 : row + 2]) for row in (250, 252)]
    row = lax.broadcasted_iota(jnp.int32, (256, 256), 0)
    value = value * jnp.where(row < 125, first, second)
    out_ref[:, 0, :] = value[0:250]


def to_nodal(columns, spread_ref, nodal_ref):
    rows = columns.shape[0]
    own = (lanes_of((rows, WIDE)) // 8) % 8
    expanded = jnp.concatenate([jnp.where(own == ey, columns, 0.0) for ey in range(EY)], axis=0)
    over_lanes = (((1,), (1,)), ((), ()))
    pieces = jnp.concatenate(cut(expanded), axis=0)
    windows = lax.dot_general(pieces, spread_ref[...], over_lanes, preferred_element_type=F32)
    half = EY * rows
    windows = windows[0:half] + windows[half : 2 * half] + windows[2 * half : 3 * half]
    nodal_ref[...] = jnp.zeros(nodal_ref.shape, F32)
    for ey in range(EY):
        at = slice(JUMP * ey, JUMP * ey + 5 * SIDE)
        nodal_ref[:, at] = nodal_ref[:, at] + windows[ey * rows : (ey + 1) * rows, 0 : 5 * SIDE]


def nodal_kernel(partial_ref, spread_ref, nodal_ref):
    lane = lanes_of((8, LANES))
    sub = lax.broadcasted_iota(jnp.int32, (8, LANES), 0)
    tiles = []
    for c in range(3):
        row = []
        for pair in range(BLOCKS // 2):
            even = partial_ref[c, 16 * pair : 16 * pair + 8, :]
            odd = partial_ref[c, 16 * pair + 8 : 16 * pair + 16, :]
            low = jnp.where(sub < 4, even, rolled(rolled(even, 64, 1), 4, 0))
            high = jnp.where(sub < 4, rolled(odd, 64, 1), rolled(odd, 4, 0))
            row.append(jnp.where(lane < 64, low, high))
        tiles.append(jnp.concatenate(row, axis=1))
    columns = jnp.concatenate(tiles, axis=0)
    column = lanes_of((24, WIDE))
    block = column // 64
    once = ((block % 5 < 4) | (column % 8 == 7)) & ((block // 5 < 4) | ((column // 8) % 8 == 7))
    to_nodal(jnp.where(once, columns, 0.0), spread_ref, nodal_ref)


def finish_kernel(before_ref, nodal_ref, density_ref, face_mass_ref, spread_ref, out_ref, rows_ref, face_ref):
    packed = before_ref[...]
    values = unpack_face(packed, rolled(packed, 64, 1))
    rows_ref[...] = jnp.zeros(rows_ref.shape, F32)
    for c in range(3):
        for d in range(5):
            rows_ref[pl.ds(8 * d + c, 5, stride=40), :] = values[c][d][0:5]
    lane = lanes_of((8, LANES))
    tiles = []
    for pair in range(BLOCKS // 2):
        even, odd = rows_ref[16 * pair : 16 * pair + 8, :], rows_ref[16 * pair + 8 : 16 * pair + 16, :]
        tiles.append(jnp.where(lane < 64, even, rolled(odd, 64, 1)))
    to_nodal(jnp.concatenate(tiles, axis=1), spread_ref, face_ref)
    scale = step_square / (density_ref[0:1, :] * face_mass_ref[...])
    first = lax.broadcasted_iota(jnp.int32, (8, FACE), 0) == 0
    for c in range(3):
        share = face_ref[c : c + 1, :] * scale
        out_ref[0, c] = nodal_ref[8 * c : 8 * c + 8, :] + jnp.where(first, share, 0.0)


VMEM = pl.BlockSpec(memory_space=pltpu.VMEM)
HBM = pl.BlockSpec(memory_space=pltpu.HBM)


def shaped(*shape, dtype=F32):
    return jax.ShapeDtypeStruct(shape, dtype)


def call(kernel, name, outs, scratch, *args, outside=(), flops=0, room=32 * 1024):
    return pl.pallas_call(
        kernel,
        name=name,
        out_shape=outs,
        in_specs=[HBM if at in outside else VMEM for at in range(len(args))],
        out_specs=jax.tree.map(lambda _: VMEM, outs),
        scratch_shapes=scratch,
        compiler_params=pltpu.CompilerParams(vmem_limit_bytes=room * 1024),
        cost_estimate=pl.CostEstimate(flops=flops, bytes_accessed=3000000, transcendentals=0),
    )(*args)


def passed_along(value, axis, steps):
    count = lax.axis_size(axis)
    return lax.ppermute(value, axis, [(source, (source + steps) % count) for source in range(count)])


def swapped(value, axis, first):
    count = lax.axis_size(axis)
    pairs = []
    for source in range(first, count, 2):
        other = (source + 1) % count
        pairs += [(source, other), (other, source)]
    return lax.ppermute(value, axis, pairs)


def far_field(low, groups):
    far = None
    for k in range(1, groups):
        moved = passed_along(low, "group", k)
        far = moved if far is None else jnp.where(lax.axis_index("group") == k, moved, far)
    return far


def per_device(disp_now, disp_prev, memory_init, density, lame_lambda, shear_mu, sls_decay, owner_map):
    ring = ("cuts", "sub")
    subs = lax.axis_size("sub")
    groups = lax.axis_size("group")

    rim = call(
        gather_kernel, "gather", shaped(8, FACE),
        [pltpu.VMEM((3, 8, FACE), F32)] * 2 + [pltpu.VMEM((8, FACE), F32), pltpu.SemaphoreType.DMA((3,))],
        disp_now, disp_prev, density, outside=(0, 1, 2), room=54 * 1024 - 120,
    )
    rim = passed_along(rim, ring, -1)

    grad_table = jnp.asarray(side_by_side(GRAD))
    force_table = jnp.asarray(cut_table(FORCE))
    face_table = jnp.asarray(cut_table(FACES))
    share_table = jnp.asarray(SHARE)
    rim_table = jnp.asarray(RIM)
    face_mass = jnp.asarray(FACE_MASS)
    mass = jnp.asarray(MASS)
    memory = memory_init[0]
    owner = jnp.transpose(owner_map, (0, 2, 1))

    state = shaped(3, ROWS, LANES)
    scale_shape = shaped(ROWS, LANES)
    five = shaped(5, 125, LANES)
    part_shape = shaped(256, LANES, dtype=BF16)
    grad_scratch = pltpu.VMEM((384, 384), F32)
    part_scratch = [grad_scratch, pltpu.VMEM((256, LANES), F32)]
    face = shaped(40, LANES)
    grad_shape = shaped(384, 384)
    flat_shape = shaped(3, 128, LANES)
    u, p, scale, m1, spread, flat, base = call(
        prologue_kernel, "prologue", [state, state, scale_shape, five, shaped(WINDOW, WIDE, dtype=BF16), flat_shape, grad_shape],
        [pltpu.VMEM((8, 56, WINDOW), F32)],
        disp_now, disp_prev, density, memory, sls_decay, mass, grad_table, face_table, force_table, rim_table, share_table, lame_lambda, shear_mu,
    )
    rows = 512 // subs
    memories = [m1]
    kept = []
    for step in range(STEPS):
        last_step = step == STEPS - 1
        low_shape = shaped(3, 128, LANES, dtype=BF16)
        if last_step:
            extra, low = call(
                shares_kernel, "shares", [shaped(3, 40, LANES), low_shape], [pltpu.VMEM((3, 128, LANES), F32)],
                odd, even, face_scale, flat,
            )
            far = far_field(low, groups)
            arrived = (extra,)
        else:
            arrived = (flat, rim, spread) if step == 0 else (flat, odd, even, face_scale)
        outs = [shaped(6, 125, LANES), grad_shape, face]
        if not last_step:
            outs += [face, five, low_shape, scale_shape if step == 0 else shaped(3, 40, LANES)]
        results = call(
            lambda *refs, step=step: step_kernel(step, *refs), "step", outs,
            [grad_scratch, pltpu.VMEM((3, 128, LANES), F32), pltpu.VMEM((8, 8, WINDOW), F32), pltpu.VMEM((40, 384), F32)],
            lame_lambda, shear_mu, memories[step], sls_decay, rim_table if step == 0 else share_table, face_table, base, *arrived, *kept,
        )
        strain, sigma, even = results[0:3]
        if last_step:
            before = passed_along(even, ring, 1)
        else:
            odd, keep, low, extra = results[3:7]
            kept.append(keep)
            odd = swapped(odd, ring, 1)
            even = swapped(even, ring, 0)
            far = far_field(low, groups)
        if step == 0:
            p, scale, partial, flat, base, face_scale = call(
                first_rest_kernel, "rest", [state, scale_shape, state, flat_shape, grad_shape, shaped(40, LANES)],
                [pltpu.VMEM((3, ROWS, LANES), F32)], sigma, force_table, u, p, scale, extra, mass, grad_table,
            )
        else:
            results = call(
                rest_kernel, "rest", [state] if last_step else [state, state, flat_shape, grad_shape],
                [pltpu.VMEM((3, ROWS, LANES), F32)] if last_step else [], sigma, force_table, partial, extra, p, scale, grad_table,
            )
            if last_step:
                partial = results[0]
            else:
                partial, p, flat, base = results
        shared = (strain, low, far, lame_lambda, shear_mu, grad_table)
        if step == 0:
            one = call(parts_kernel, "parts", part_shape, part_scratch, *shared)
            m2, m3, select = call(
                later_kernel, "later", [five, five, shaped(subs * LANES, LANES, dtype=BF16)], [], memory, sls_decay, owner
            )
            memories += [m2, m3]
            base, one, select, memories[2] = lax.optimization_barrier((base, one, select, m3))
        elif not last_step:
            both = call(
                both_parts_kernel, "parts", shaped(256, LANES), part_scratch, *shared, one
            )
            base, flat, both = lax.optimization_barrier((base, flat, both))
        else:
            total, *blocks = call(
                send_kernel, "send", [shaped(256, LANES)] + [shaped(rows, LANES, dtype=jnp.int16)] * (subs - 1),
                part_scratch, *shared, both, select,
            )
            order = [*range(subs - 1, 0, -1), 0]
            sent = [lax.ppermute(blocks[k - 1], "sub", [(j, j ^ k) for j in range(subs)]) for k in order[:-1]]
            sent.append(call(own_kernel, "own", shaped(rows, LANES), [], total, select))
    nodal = call(nodal_kernel, "nodal", shaped(24, FACE), [], partial, spread)
    final = call(
        finish_kernel, "finish", shaped(1, 3, 8, FACE), [pltpu.VMEM((ROWS, LANES), F32), pltpu.VMEM((8, FACE), F32)],
        before, nodal, density, face_mass, spread, flops=250000000,
    )
    kernels = call(
        lambda *refs: sum_kernel(order, *refs), "sum", shaped(250, 1, 256), [], *sent
    )
    return final, jnp.transpose(kernels, (1, 2, 0))


def solution(mesh):
    in_specs = (
        P("group", None, ("cuts", "sub"), None),
        P("group", None, ("cuts", "sub"), None),
        P("group", None, None, None, ("cuts", "sub")),
        P(("cuts", "sub"), None),
        P(None, ("cuts", "sub")),
        P(None, ("cuts", "sub")),
        P(None, ("cuts", "sub")),
        P(("cuts", "sub"), None, None),
    )
    out_specs = (P("group", None, ("cuts", "sub"), None), P("group", ("cuts", "sub"), None))
    return jax.shard_map(
        per_device, mesh=mesh, in_specs=in_specs, out_specs=out_specs, check_vma=False
    )
```

```python
import math

import jax
import jax.numpy as jnp
import numpy as np
from jax import lax
from jax.experimental import pallas as pl
from jax.experimental.pallas import tpu as pltpu
from jax.sharding import PartitionSpec as P

STEPS = 3
EY = 8
EZ = 8
LANES = 128
SIDE = 33
FACE = SIDE * SIDE
BLOCKS = 26
ROWS = 8 * BLOCKS
WIDE = 64 * BLOCKS
JUMP = 4 * SIDE
WIDE_FACE = 1152
WINDOW = 256

time_step = 0.03
step_square = 0.0009
relax_strength = (0.12, 0.08, 0.05)

F32 = jnp.float32
BF16 = jnp.bfloat16


def gll_tables():
    root_value = math.sqrt(3.0 / 7.0)
    points = [-1.0, -root_value, 0.0, root_value, 1.0]
    weights = [0.1, 49.0 / 90.0, 32.0 / 45.0, 49.0 / 90.0, 0.1]
    derivative = np.zeros((5, 5))
    for p in range(5):
        for a in range(5):
            accum = 0.0
            for m in range(5):
                if m != a:
                    factor = 1.0 / (points[a] - points[m])
                    for k in range(5):
                        if k != a and k != m:
                            factor = factor * (points[p] - points[k]) / (points[a] - points[k])
                    accum = accum + factor
            derivative[p, a] = accum
    return derivative.astype(np.float32).astype(np.float64), np.array(weights).astype(np.float32).astype(np.float64)


def node(a, b, d):
    return a * 25 + b * 5 + d


def place(a, b, d):
    return (b * 5 + d) * 8 + a


FACE_ROWS = [slice(0, 128), slice(128, 160), slice(224, 256), slice(256, 288), slice(352, 384)]


def make_tables():
    derivative, weights = gll_tables()
    grad = np.zeros((3 * 128, 128))
    force = np.zeros((ROWS, 3 * 128))
    for a in range(5):
        for b in range(5):
            for d in range(5):
                for m in range(5):
                    grad[node(a, b, d), node(m, b, d)] = derivative[a, m]
                    grad[128 + node(a, b, d), node(a, m, d)] = derivative[b, m]
                    grad[256 + node(a, b, d), node(a, b, m)] = derivative[d, m]
                    row = place(a, b, d)
                    force[row, node(m, b, d)] = -derivative[m, a] * weights[m] * weights[b] * weights[d]
                    force[row, 128 + node(a, m, d)] = -derivative[m, b] * weights[a] * weights[m] * weights[d]
                    force[row, 256 + node(a, b, m)] = -derivative[m, d] * weights[a] * weights[b] * weights[m]
    full = np.zeros((80, 3 * 128))
    first_grad, last_grad = np.zeros((3 * 128, 40)), np.zeros((3 * 128, 40))
    for b in range(5):
        for d in range(5):
            full[d * 8 + b] = force[place(0, b, d)]
            full[40 + d * 8 + b] = force[place(4, b, d)]
            first_grad[:, d * 8 + b] = grad[:, node(0, b, d)]
            last_grad[:, d * 8 + b] = grad[:, node(4, b, d)]
    face = np.concatenate([full[:, rows] for rows in FACE_ROWS], axis=1)
    first, last = cut_table(first_grad), cut_table(last_grad)
    share = np.concatenate([first[0], first[0], first[1], last[0], last[0], last[1]], axis=1)
    rim = np.concatenate([last[0], last[0], last[1], last[1], last[0], last[2]], axis=1)
    line = np.zeros(SIDE)
    for e in range(8):
        line[4 * e : 4 * e + 5] += weights
    layer = np.array([2 * weights[0], weights[1], weights[2], weights[3], 2 * weights[0], 1.0, 1.0, 1.0])
    mass = np.ones((ROWS, LANES), np.float32)
    for b in range(5):
        for d in range(5):
            for ey in range(8):
                for ez in range(8):
                    for slab in range(2):
                        at = (b * 5 + d) * 8
                        mass[at : at + 8, slab * 64 + ey * 8 + ez] = layer * line[4 * ey + b] * line[4 * ez + d]
    return grad, force, face, mass, share, rim


def side_by_side(table):
    high, middle, low = cut_table(table)
    pairs = ((high, middle), (middle, high), (low, high))
    return np.stack([np.concatenate(pair, axis=1) for pair in pairs])


def cut_table(table):
    value = table.astype(np.float32)
    pieces = []
    for _ in range(3):
        piece = value.astype(jnp.bfloat16)
        pieces.append(piece)
        value = value - piece.astype(np.float32)
    return np.stack(pieces)


GRAD, FORCE, FACES, MASS, SHARE, RIM = make_tables()


def make_gathers():
    columns = np.zeros((BLOCKS // 2, LANES), np.int32)
    for b in range(5):
        for d in range(5):
            block = b * 5 + d
            for ey in range(8):
                for ez in range(8):
                    columns[block // 2, (block % 2) * 64 + ey * 8 + ez] = (4 * ey + b) * SIDE + 4 * ez + d
    nodes = np.zeros((WIDE_FACE // LANES, LANES), np.int32)
    for y in range(SIDE):
        for z in range(SIDE):
            ey, ez = min(y // 4, 7), min(z // 4, 7)
            block = (y - 4 * ey) * 5 + z - 4 * ez
            spot = y * SIDE + z
            nodes[spot // LANES, spot % LANES] = (block // 2) * LANES + (block % 2) * 64 + ey * 8 + ez
    return columns, nodes


COLUMN_LANES, NODE_LANES = make_gathers()


def gathered(tiles, table, table_ref):
    results = []
    for row in range(table.shape[0]):
        spots = jnp.broadcast_to(table_ref[row : row + 1, :], (8, LANES))
        tile_of, lane_of = spots // LANES, spots % LANES
        value = jnp.zeros((8, LANES), F32)
        for at in sorted(set((table[row] // LANES).tolist())):
            moved = jnp.take_along_axis(tiles[at], lane_of, axis=1, mode="promise_in_bounds")
            value = jnp.where(tile_of == at, moved, value)
        results.append(value)
    return results


def cut(value):
    high = value.astype(BF16)
    rest = value - high.astype(F32)
    middle = rest.astype(BF16)
    low = (rest - middle.astype(F32)).astype(BF16)
    return high, middle, low


def dot(left, right):
    return jnp.dot(left, right, preferred_element_type=F32)


def gradients(table, flat):
    high, middle, low = cut(flat)
    first = dot(table[0:2].reshape(768, 256), jnp.concatenate([high, middle], axis=0))
    return first[0:384] + (first[384:768] + dot(table[2], jnp.concatenate([high, low], axis=0)))


def low_gradients(table, low):
    return dot(table[0], jnp.concatenate([low, low], axis=0)) + dot(table[2, :, 0:128], low)


def flatten(u_ref, flat_ref):
    for c in range(3):
        flat_ref[c, 120:128, :] = jnp.zeros((8, LANES), F32)
        for a in range(5):
            flat_ref[c, 25 * a : 25 * a + 25, :] = u_ref[c, pl.ds(a, 25, stride=8), :]


def dot_three(table, value):
    rows = table.shape[1]
    stacked = table[0:2].reshape(2 * rows, table.shape[2])
    high, middle, _ = cut(value)
    first = dot(stacked, high)
    return first[0:rows] + (first[rows : 2 * rows] + dot(stacked[0:rows], middle))


def lanes_of(shape):
    return lax.broadcasted_iota(jnp.int32, shape, len(shape) - 1)


def rolled(value, shift, axis):
    return pltpu.roll(value, shift % value.shape[axis], axis)


def window_rows(value, window_ref):
    for ey in range(EY):
        width = min(WINDOW, FACE - JUMP * ey)
        if width < WINDOW:
            window_ref[ey] = jnp.zeros(window_ref.shape[1:], F32)
        window_ref[ey, :, 0:width] = value[:, JUMP * ey : JUMP * ey + width]
    return window_ref[...].reshape(-1, WINDOW)


def to_columns(value, window_ref, spread_ref):
    rows = value.shape[0]
    pieces = jnp.concatenate(cut(window_rows(value, window_ref)), axis=0)
    wide = dot(pieces, spread_ref[...])
    half = EY * rows
    own = (lanes_of((rows, WIDE)) // 8) % 8
    picked = 0.0
    for ey in range(EY):
        at = slice(ey * rows, (ey + 1) * rows)
        value = wide[at] + wide[half : 2 * half][at] + wide[2 * half : 3 * half][at]
        picked = jnp.where(own == ey, value, picked)
    return picked


def assembled(blocks):
    lane = lanes_of((8, LANES))
    blocks = dict(blocks)
    for shift, at, pairs in (
        (1, lane % 8, [((b, 0), (b, 4)) for b in range(5)]),
        (8, (lane // 8) % 8, [((0, d), (4, d)) for d in range(5)]),
    ):
        for c in range(3):
            for near, far in pairs:
                first, last = blocks[(c,) + near], blocks[(c,) + far]
                blocks[(c,) + near] = first + jnp.where(at > 0, rolled(last, shift, 1), 0.0)
                blocks[(c,) + far] = last + jnp.where(at < 7, rolled(first, -shift, 1), 0.0)
    return blocks


def block_rows(b, d):
    return slice((b * 5 + d) * 8, (b * 5 + d) * 8 + 8)


def beside(value):
    return jnp.concatenate([value[0], value[1], value[2]], axis=1)


def gather_kernel(now_ref, prev_ref, density_ref, rim_ref, now_copy, prev_copy, density_copy, sems):
    copies = [
        pltpu.make_async_copy(now_ref.at[0], now_copy, sems.at[0]),
        pltpu.make_async_copy(prev_ref.at[0], prev_copy, sems.at[1]),
        pltpu.make_async_copy(density_ref, density_copy, sems.at[2]),
    ]
    for copy in copies:
        copy.start()
    for copy in copies:
        copy.wait()
    rim_ref[:, 1024:] = jnp.zeros((8, WIDE_FACE - 1024), F32)
    for c in range(3):
        rim_ref[c : c + 1, 0:FACE] = now_copy[c, 0:1, :]
        rim_ref[3 + c : 4 + c, 0:FACE] = prev_copy[c, 0:1, :]
    rim_ref[6:7, 0:FACE] = density_copy[0:1, :]
    rim_ref[7:8, 0:FACE] = density_copy[0:1, :]


def weighted_memory(memory_ref, decays, part, power):
    value = 0.0
    for l in range(3):
        factor = decays[l]
        for _ in range(power - 1):
            factor = factor * decays[l]
        value = value + factor * memory_ref[l, part]
    return value


def spread_table():
    column = lanes_of((1, WIDE))
    block = column // 64
    spot = (block // 5) * SIDE + (block % 5) + 4 * (column % 8)
    spot = jnp.where(block < 25, spot, WINDOW)
    return jnp.where(lax.broadcasted_iota(jnp.int32, (WINDOW, WIDE), 0) == spot, 1.0, 0.0).astype(BF16)


def prologue_kernel(now_ref, prev_ref, density_ref, memory_ref, decay_ref, mass_ref, *refs):
    grad_table = refs[0]
    u_ref, p_ref, scale_ref, m1_ref, spread_ref, flat_ref, grad_ref, window_ref = refs[-8:]
    spread_ref[...] = spread_table()
    rows = jnp.concatenate([now_ref[0].reshape(24, FACE), prev_ref[0].reshape(24, FACE), density_ref[...]], axis=0)
    columns = to_columns(rows, window_ref, spread_ref)
    lane = lanes_of((8, LANES))
    for group in range(7):
        for pair in range(BLOCKS // 2):
            tile = columns[8 * group : 8 * group + 8, LANES * pair : LANES * pair + LANES]
            swapped = rolled(tile, 64, 1)
            even = jnp.where(lane < 64, tile, rolled(swapped, 4, 0))
            odd = jnp.where(lane < 64, swapped, rolled(tile, 4, 0))
            for block, value in ((2 * pair, even), (2 * pair + 1, odd)):
                at = slice(8 * block, 8 * block + 8)
                if group < 3:
                    u_ref[group, at, :] = value
                elif group < 6:
                    p_ref[group - 3, at, :] = value
                elif block < 25:
                    scale_ref[at, :] = step_square / (value * mass_ref[at, :])
                else:
                    scale_ref[at, :] = jnp.zeros((8, LANES), F32)
    decays = [decay_ref[l : l + 1, :] for l in range(3)]
    for part in range(5):
        m1_ref[part] = weighted_memory(memory_ref, decays, part, 1)
    flatten(u_ref, flat_ref)
    lower = lanes_of((25, LANES)) < 64
    for c in range(3):
        flat_ref[c, 100:125, :] = jnp.where(lower, flat_ref[c, 100:125, :], 0.0)
    grad_ref[...] = gradients(grad_table, beside(flat_ref))


def later_kernel(memory_ref, decay_ref, owner_ref, m2_ref, m3_ref, select_ref):
    decays = [decay_ref[l : l + 1, :] for l in range(3)]
    for part in range(5):
        m2_ref[part] = weighted_memory(memory_ref, decays, part, 2)
        m3_ref[part] = weighted_memory(memory_ref, decays, part, 3)
    owner = jnp.concatenate([owner_ref[0], owner_ref[1]], axis=1)
    named = jnp.where(lax.broadcasted_iota(jnp.int32, (16, LANES), 0) == owner, 1.0, 0.0)
    earlier = lax.broadcasted_iota(jnp.int32, (LANES, LANES), 0)
    later = lax.broadcasted_iota(jnp.int32, (LANES, LANES), 1)
    ahead = jnp.where((earlier < later) & ((earlier // 64) == (later // 64)), 1.0, 0.0)
    rank = jnp.sum(named * dot(named.astype(BF16), ahead.astype(BF16)), axis=0, keepdims=True).astype(jnp.int32)
    subs = select_ref.shape[0] // LANES
    slots = 4 * EY * EZ // subs
    row = lax.broadcasted_iota(jnp.int32, select_ref.shape, 0)
    toward = (row // LANES) ^ lax.axis_index("sub")
    wanted = (lanes_of((1, LANES)) // 64) * (slots // 2) + rank
    chosen = (owner == toward) & (wanted == row % slots)
    select_ref[...] = jnp.where(chosen, 1.0, 0.0).astype(BF16)


def rim_rows(rim_ref, lanes_ref, rows_ref):
    tiles = [rim_ref[:, at : at + LANES] for at in range(0, WIDE_FACE, LANES)]
    for pair, tile in enumerate(gathered(tiles, COLUMN_LANES, lanes_ref)):
        rows_ref[16 * pair : 16 * pair + 8, :] = rolled(tile, 64, 1)
        rows_ref[16 * pair + 8 : 16 * pair + 16, :] = tile


def unpack_face(here, there):
    top = lax.broadcasted_iota(jnp.int32, (8, LANES), 0) < 3
    parts = [[], [], []]
    for d in range(5):
        first, second = here[8 * d : 8 * d + 8], there[8 * d : 8 * d + 8]
        third = jnp.where(top, rolled(first, 3, 0), rolled(second, 6, 0))
        for part, line in zip(parts, (first, second, third)):
            part.append(line)
    return parts


def face_shares(odd_ref, even_ref, face_scale_ref):
    even_ring = lax.axis_index(("cuts", "sub")) % 2 == 0
    odd, even = odd_ref[...], even_ref[...]
    lower = (lanes_of((40, LANES)) < 64) == even_ring
    rows = unpack_face(jnp.where(lower, odd, even), rolled(jnp.where(lower, even, odd), 64, 1))
    return [assembled_lines(lines, face_scale_ref) for lines in rows]


def assembled_lines(lines, face_scale_ref):
    lane = lanes_of((8, LANES))
    sub = lax.broadcasted_iota(jnp.int32, (8, LANES), 0)
    ez, ey = lane % 8, (lane // 8) % 8
    up, down = (sub == 0) & (ey > 0), (sub == 4) & (ey < 7)
    first, last = lines[0], lines[4]
    lines = list(lines)
    lines[0] = first + jnp.where(ez > 0, rolled(last, 1, 1), 0.0)
    lines[4] = last + jnp.where(ez < 7, rolled(first, -1, 1), 0.0)
    for d in range(5):
        turned = rolled(lines[d], 4, 0)
        added = jnp.where(up, rolled(turned, 8, 1), jnp.where(down, rolled(turned, -8, 1), 0.0))
        lines[d] = face_scale_ref[8 * d : 8 * d + 8, :] * (lines[d] + added)
    return lines


def strains(grad, rows):
    def at(direction, c):
        return grad[direction * 128 + rows.start : direction * 128 + rows.stop, c * LANES : (c + 1) * LANES]

    return [
        at(0, 0),
        at(1, 1),
        at(2, 2),
        0.5 * (at(1, 0) + at(0, 1)),
        0.5 * (at(2, 0) + at(0, 2)),
        0.5 * (at(2, 1) + at(1, 2)),
    ]


CHUNKS = [slice(row, min(row + 8, 125)) for row in range(0, 125, 8)]


def pack_face(face, upper):
    lane = lanes_of((8, LANES))
    target = lane < 64 if upper else lane >= 64
    own = lax.broadcasted_iota(jnp.int32, (8, LANES), 0) < 5
    lines = []
    for d in range(5):
        first, second, third = [face[8 * d : 8 * d + 8, c * LANES : (c + 1) * LANES] for c in range(3)]
        moved = rolled(jnp.where(own, first, rolled(third, 5, 0)), 64, 1)
        lines.append(jnp.where(target, moved, jnp.where(own, second, rolled(third, 2, 0))))
    return jnp.concatenate(lines, axis=0)


def add_shares(shares, flat_ref):
    upper = lanes_of((5, LANES)) >= 64
    for c in range(3):
        for d in range(5):
            first, last = pl.ds(d, 5, stride=5), pl.ds(100 + d, 5, stride=5)
            flat_ref[c, first, :] = flat_ref[c, first, :] + jnp.where(upper, 0.0, shares[c][d][0:5])
            flat_ref[c, last, :] = flat_ref[c, last, :] + jnp.where(upper, shares[c][d][0:5], 0.0)


def shares_kernel(odd_ref, even_ref, face_scale_ref, flat_in, delta_ref, low_ref, flat_ref):
    shares = face_shares(odd_ref, even_ref, face_scale_ref)
    for c in range(3):
        delta_ref[c] = jnp.concatenate(shares[c], axis=0)
    flat_ref[...] = flat_in[...]
    add_shares(shares, flat_ref)
    low_ref[...] = flat_ref[...].astype(BF16)


def step_kernel(step, *refs):
    lame_ref, mu_ref, m_ref, decay_ref, share_table, face_table, base_ref = refs[0:7]
    arrived = refs[7 : 7 + (3, 4, 1)[step]]
    refs = refs[7 + len(arrived) :]
    older, refs = refs[:step], refs[step:]
    strain_ref, sigma_ref, even_ref = refs[0:3]
    if step < STEPS - 1:
        odd_ref, keep_ref, low_ref, extra_ref = refs[3:7]
    grad_ref, flat_ref, rim_ref = refs[-3:]
    upper = lanes_of((40, 3 * LANES)) % LANES >= 64
    if step == 0:
        flat_ref[...] = arrived[0][...]
        rim_rows(arrived[1], arrived[2], extra_ref)
        rim_ref[...] = jnp.zeros(rim_ref.shape, F32)
        for c in range(3):
            for d in range(5):
                rim_ref[8 * d : 8 * d + 5, c * LANES : (c + 1) * LANES] = extra_ref[pl.ds(8 * d + c, 5, stride=40), :]
        high, middle, low = [piece.astype(F32) for piece in cut(jnp.where(upper, rim_ref[...], 0.0))]
        stacked = [high, middle, high, middle, low, high]
        at_upper = lanes_of((25, LANES)) >= 64
        for c in range(3):
            flat_ref[c, 100:125, :] = jnp.where(at_upper, extra_ref[pl.ds(c, 25, stride=8), :], flat_ref[c, 100:125, :])
    else:
        if step == STEPS - 1:
            value = jnp.concatenate([arrived[0][c] for c in range(3)], axis=1)
        else:
            shares = face_shares(*arrived[1:4])
            value = jnp.concatenate([jnp.concatenate(lines, axis=0) for lines in shares], axis=1)
            for c in range(3):
                extra_ref[c] = value[:, c * LANES : (c + 1) * LANES]
            flat_ref[...] = arrived[0][...]
            add_shares(shares, flat_ref)
        high, middle, _ = [piece.astype(F32) for piece in cut(value)]
        stacked = []
        for at in (~upper, upper):
            stacked += [jnp.where(at, high, 0.0), jnp.where(at, middle, 0.0), jnp.where(at, high, 0.0)]
    grad_ref[...] = base_ref[...] + dot(share_table[...], jnp.concatenate(stacked, axis=0).astype(BF16))
    if step < STEPS - 1:
        low_ref[...] = flat_ref[...].astype(BF16)
    for block in range(9):
        sigma_ref[(block // 3) * 128 + 120 : (block // 3) * 128 + 128, (block % 3) * LANES : (block % 3) * LANES + LANES] = (
            jnp.zeros((8, LANES), F32)
        )
    decays = [decay_ref[l : l + 1, :] for l in range(3)]
    shares = [(1.0 - decays[l]) * relax_strength[l] for l in range(3)]
    factors = []
    for _ in range(step + 1):
        factors.append(shares[0] + shares[1] + shares[2])
        shares = [decays[l] * shares[l] for l in range(3)]
    for rows in CHUNKS:
        strain = strains(grad_ref, rows)
        for part in range(6):
            strain_ref[part, rows, :] = strain[part]
        lame = lame_ref[rows, :]
        twice_mu = 2.0 * mu_ref[rows, :]
        trace = strain[0] + strain[1] + strain[2]
        third = trace * (1.0 / 3.0)
        pulls = [twice_mu * s for s in strain]
        pull_third = twice_mu * third
        fresh = [pulls[0] - pull_third, pulls[1] - pull_third, pulls[3], pulls[4], pulls[5]]
        relax = []
        for part in range(5):
            value = m_ref[part, rows, :] + factors[0] * fresh[part]
            for back in range(step):
                value = value + factors[back + 1] * older[step - 1 - back][part, rows, :]
            relax.append(value)
            if step < STEPS - 1:
                keep_ref[part, rows, :] = fresh[part]
        bulk = lame * trace
        xx = bulk + pulls[0] - relax[0]
        yy = bulk + pulls[1] - relax[1]
        zz = bulk + pulls[2] + relax[0] + relax[1]
        xy = pulls[3] - relax[2]
        xz = pulls[4] - relax[3]
        yz = pulls[5] - relax[4]
        for direction, values in enumerate(((xx, xy, xz), (xy, yy, yz), (xz, yz, zz))):
            for c in range(3):
                sigma_ref[direction * 128 + rows.start : direction * 128 + rows.stop, c * LANES : (c + 1) * LANES] = values[c]
    faces = dot_three(face_table, jnp.concatenate([sigma_ref[rows, :] for rows in FACE_ROWS], axis=0))
    first, last = pack_face(faces[0:40], False), pack_face(faces[40:80], True)
    if step < STEPS - 1:
        even_ring = lax.axis_index(("cuts", "sub")) % 2 == 0
        odd_ref[...] = jnp.where(even_ring, first, last)
        even_ref[...] = jnp.where(even_ring, last, first)
    else:
        even_ref[...] = last


def next_state(sigma_ref, force_table, u_ref, p_ref, scale_ref, next_ref):
    force = dot_three(force_table, sigma_ref[...])
    blocks = {}
    for c in range(3):
        for b in range(5):
            for d in range(5):
                blocks[(c, b, d)] = force[block_rows(b, d), c * LANES : (c + 1) * LANES]
    blocks = assembled(blocks)
    lane = lanes_of((8, LANES))
    sub = lax.broadcasted_iota(jnp.int32, (8, LANES), 0)
    inner = ((sub == 4) & (lane < 64)) | ((sub == 0) & (lane >= 64))
    for c in range(3):
        for b in range(5):
            for d in range(5):
                value = blocks[(c, b, d)]
                value = value + jnp.where(inner, rolled(rolled(value, 4, 0), 64, 1), 0.0)
                at = block_rows(b, d)
                next_ref[c, at, :] = 2.0 * u_ref[c, at, :] - p_ref[c, at, :] + scale_ref[at, :] * value
        next_ref[c, 200:208, :] = jnp.zeros((8, LANES), F32)


def first_rest_kernel(
    sigma_ref, force_table, u_in, p_in, scale_in, rows_ref, mass_ref, grad_table,
    u_ref, scale_ref, next_ref, flat_ref, grad_ref, face_scale_ref, p_ref
):
    u_ref[...] = u_in[...]
    p_ref[...] = p_in[...]
    scale_ref[...] = scale_in[...]
    upper = lanes_of((25, LANES)) >= 64
    last = pl.ds(4, 25, stride=8)
    for c in range(3):
        u_ref[c, last, :] = jnp.where(upper, rows_ref[pl.ds(c, 25, stride=8), :], u_ref[c, last, :])
        p_ref[c, last, :] = jnp.where(upper, rows_ref[pl.ds(3 + c, 25, stride=8), :], p_ref[c, last, :])
    rim = step_square / (rows_ref[pl.ds(6, 25, stride=8), :] * mass_ref[last, :])
    scale_ref[last, :] = jnp.where(upper, rim, scale_ref[last, :])
    face_scale_ref[...] = jnp.zeros(face_scale_ref.shape, F32)
    lower = lanes_of((5, LANES)) < 64
    for d in range(5):
        first, last = pl.ds(8 * d, 5, stride=40), pl.ds(8 * d + 4, 5, stride=40)
        face_scale_ref[8 * d : 8 * d + 5, :] = jnp.where(lower, scale_ref[first, :], scale_ref[last, :])
    next_state(sigma_ref, force_table, u_ref, p_ref, scale_ref, next_ref)
    flatten(next_ref, flat_ref)
    grad_ref[...] = gradients(grad_table, beside(flat_ref))


def rest_kernel(sigma_ref, force_table, partial_ref, delta_ref, p_ref, scale_ref, grad_table, next_ref, u_ref, *refs):
    u_ref[...] = partial_ref[...]
    upper = lanes_of((5, LANES)) >= 64
    for c in range(3):
        for d in range(5):
            share = delta_ref[c, 8 * d : 8 * d + 5, :]
            first, last = pl.ds(8 * d, 5, stride=40), pl.ds(8 * d + 4, 5, stride=40)
            u_ref[c, first, :] = u_ref[c, first, :] + jnp.where(upper, 0.0, share)
            u_ref[c, last, :] = u_ref[c, last, :] + jnp.where(upper, share, 0.0)
    next_state(sigma_ref, force_table, u_ref, p_ref, scale_ref, next_ref)
    if refs:
        flat_ref, grad_ref = refs
        flatten(next_ref, flat_ref)
        grad_ref[...] = gradients(grad_table, beside(flat_ref))


def kernel_parts(strain_ref, low_ref, far_ref, lame_ref, mu_ref, grad_table, grad_ref, kernel_ref):
    forward = jnp.where(lax.axis_index("group") == 0, beside(low_ref), beside(far_ref))
    grad_ref[...] = low_gradients(grad_table, forward)
    for rows in CHUNKS:
        far = strains(grad_ref, rows)
        own = [strain_ref[part, rows, :] for part in range(6)]
        trace_own = own[0] + own[1] + own[2]
        trace_far = far[0] + far[1] + far[2]
        third_own, third_far = trace_own * (1.0 / 3.0), trace_far * (1.0 / 3.0)
        twice_mu = 2.0 * mu_ref[rows, :]
        kappa = lame_ref[rows, :] + twice_mu * (1.0 / 3.0)
        kernel_ref[rows, :] = time_step * kappa * trace_far * trace_own
        product = (
            (own[0] - third_own) * (far[0] - third_far)
            + (own[1] - third_own) * (far[1] - third_far)
            + (own[2] - third_own) * (far[2] - third_far)
            + 2.0 * (own[3] * far[3] + own[4] * far[4] + own[5] * far[5])
        )
        kernel_ref[125 + rows.start : 125 + rows.stop, :] = time_step * twice_mu * product
    kernel_ref[250:256, :] = jnp.zeros((6, LANES), F32)
    return kernel_ref[...].astype(BF16)


def placed(pieces, select, rows):
    slots = rows // 2
    group = lanes_of((rows, LANES)) // slots
    total = 0.0
    for piece in pieces:
        total = total + lax.dot_general(piece, select, (((1,), (1,)), ((), ())), preferred_element_type=F32)
    blocks = []
    for k in range(select.shape[0] // LANES):
        value = total[0:rows, k * LANES : (k + 1) * LANES]
        for j in range(1, 256 // rows):
            value = jnp.where(group == j, total[j * rows : (j + 1) * rows, k * LANES : (k + 1) * LANES], value)
        blocks.append(value)
    return blocks


def group_scale(mantissa, exponent):
    return mantissa * jnp.exp2(exponent) * (1.0 / (4096.0 * 32767.0))


def parts_kernel(strain_ref, low_ref, far_ref, lame_ref, mu_ref, grad_table, part_ref, grad_ref, kernel_ref):
    part_ref[...] = kernel_parts(strain_ref, low_ref, far_ref, lame_ref, mu_ref, grad_table, grad_ref, kernel_ref)


def both_parts_kernel(strain_ref, low_ref, far_ref, lame_ref, mu_ref, grad_table, one_ref, both_ref, grad_ref, kernel_ref):
    two = kernel_parts(strain_ref, low_ref, far_ref, lame_ref, mu_ref, grad_table, grad_ref, kernel_ref)
    both_ref[...] = one_ref[...].astype(F32) + two.astype(F32)


def send_kernel(strain_ref, low_ref, far_ref, lame_ref, mu_ref, grad_table, both_ref, select_ref, total_ref, *refs):
    out_refs, (grad_ref, kernel_ref) = refs[:-2], refs[-2:]
    three = kernel_parts(strain_ref, low_ref, far_ref, lame_ref, mu_ref, grad_table, grad_ref, kernel_ref)
    kernel_ref[...] = both_ref[...] + three.astype(F32)
    total_ref[...] = kernel_ref[...]
    for k in range(2):
        rows = slice(125 * k, 125 * k + 125)
        value = kernel_ref[rows, :]
        largest = jnp.maximum(jnp.max(jnp.abs(value), axis=0, keepdims=True), 1e-33)
        exponent = jnp.floor(jnp.log2(largest))
        mantissa = jnp.floor(largest * jnp.exp2(-exponent) * 4096.0) + 2.0
        kernel_ref[rows, :] = jnp.floor(value * (1.0 / group_scale(mantissa, exponent)) + 0.5)
        kernel_ref[250 + 2 * k : 251 + 2 * k, :] = mantissa
        kernel_ref[251 + 2 * k : 252 + 2 * k, :] = exponent
    high, middle, _ = cut(kernel_ref[...])
    for ref, value in zip(out_refs, placed((high, middle), select_ref[LANES:, :], out_refs[0].shape[0])):
        ref[...] = value.astype(jnp.int32).astype(jnp.int16)


def own_kernel(total_ref, select_ref, own_ref):
    row = lax.broadcasted_iota(jnp.int32, (256, LANES), 0)
    unit = jnp.where((row == 250) | (row == 252), 4096.0 * 32767.0, 0.0)
    value = jnp.where(row < 250, total_ref[...], unit)
    own_ref[...] = placed(cut(value), select_ref[0:LANES, :], own_ref.shape[0])[0]


def sum_kernel(order, *refs):
    in_refs, out_ref = refs[:-1], refs[-1]
    rows = in_refs[0].shape[0]
    slots = rows // 2
    pieces = 256 // rows
    group = lanes_of((rows, LANES)) // slots
    blocks = [[jnp.zeros((rows, LANES), F32)] * 2 for _ in range(pieces)]
    for k, ref in zip(order, in_refs):
        source = lax.axis_index("sub") ^ k
        spot = source % pieces
        value = ref[...].astype(jnp.int32).astype(F32) if k > 0 else ref[...]
        for j in range(pieces):
            moved = pltpu.roll(value, ((spot + pieces - j) % pieces) * slots, 1)
            for t in range(2):
                here = (group == spot) & (source // pieces == t)
                blocks[j][t] = jnp.where(here, moved, blocks[j][t])
    value = jnp.concatenate([jnp.concatenate(row, axis=1) for row in blocks], axis=0)
    first, second = [group_scale(value[row : row + 1], value[row + 1 : row + 2]) for row in (250, 252)]
    row = lax.broadcasted_iota(jnp.int32, (256, 256), 0)
    value = value * jnp.where(row < 125, first, second)
    out_ref[:, 0, :] = value[0:250]


def to_nodal(columns, spread_ref, nodal_ref):
    rows = columns.shape[0]
    own = (lanes_of((rows, WIDE)) // 8) % 8
    expanded = jnp.concatenate([jnp.where(own == ey, columns, 0.0) for ey in range(EY)], axis=0)
    over_lanes = (((1,), (1,)), ((), ()))
    pieces = jnp.concatenate(cut(expanded), axis=0)
    windows = lax.dot_general(pieces, spread_ref[...], over_lanes, preferred_element_type=F32)
    half = EY * rows
    windows = windows[0:half] + windows[half : 2 * half] + windows[2 * half : 3 * half]
    nodal_ref[...] = jnp.zeros(nodal_ref.shape, F32)
    for ey in range(EY):
        at = slice(JUMP * ey, JUMP * ey + 5 * SIDE)
        nodal_ref[:, at] = nodal_ref[:, at] + windows[ey * rows : (ey + 1) * rows, 0 : 5 * SIDE]


def nodal_kernel(partial_ref, spread_ref, nodal_ref):
    lane = lanes_of((8, LANES))
    sub = lax.broadcasted_iota(jnp.int32, (8, LANES), 0)
    tiles = []
    for c in range(3):
        row = []
        for pair in range(BLOCKS // 2):
            even = partial_ref[c, 16 * pair : 16 * pair + 8, :]
            odd = partial_ref[c, 16 * pair + 8 : 16 * pair + 16, :]
            low = jnp.where(sub < 4, even, rolled(rolled(even, 64, 1), 4, 0))
            high = jnp.where(sub < 4, rolled(odd, 64, 1), rolled(odd, 4, 0))
            row.append(jnp.where(lane < 64, low, high))
        tiles.append(jnp.concatenate(row, axis=1))
    columns = jnp.concatenate(tiles, axis=0)
    column = lanes_of((24, WIDE))
    block = column // 64
    once = ((block % 5 < 4) | (column % 8 == 7)) & ((block // 5 < 4) | ((column // 8) % 8 == 7))
    to_nodal(jnp.where(once, columns, 0.0), spread_ref, nodal_ref)


def finish_kernel(before_ref, nodal_ref, face_scale_ref, lanes_ref, out_ref, rows_ref, face_ref):
    packed = before_ref[...]
    values = unpack_face(packed, rolled(packed, 64, 1))
    rows_ref[...] = jnp.zeros(rows_ref.shape, F32)
    for c in range(3):
        lines = assembled_lines(values[c], face_scale_ref)
        for d in range(5):
            rows_ref[pl.ds(8 * d + c, 5, stride=40), :] = lines[d][0:5]
    lane = lanes_of((8, LANES))
    tiles = []
    for pair in range(BLOCKS // 2):
        even, odd = rows_ref[16 * pair : 16 * pair + 8, :], rows_ref[16 * pair + 8 : 16 * pair + 16, :]
        tiles.append(jnp.where(lane < 64, even, rolled(odd, 64, 1)))
    for at, tile in enumerate(gathered(tiles, NODE_LANES, lanes_ref)):
        face_ref[:, LANES * at : LANES * at + LANES] = tile
    first = lax.broadcasted_iota(jnp.int32, (8, FACE), 0) == 0
    for c in range(3):
        out_ref[0, c] = nodal_ref[8 * c : 8 * c + 8, :] + jnp.where(first, face_ref[c : c + 1, 0:FACE], 0.0)


VMEM = pl.BlockSpec(memory_space=pltpu.VMEM)
HBM = pl.BlockSpec(memory_space=pltpu.HBM)


def shaped(*shape, dtype=F32):
    return jax.ShapeDtypeStruct(shape, dtype)


def call(kernel, name, outs, scratch, *args, outside=(), flops=0, room=32 * 1024):
    return pl.pallas_call(
        kernel,
        name=name,
        out_shape=outs,
        in_specs=[HBM if at in outside else VMEM for at in range(len(args))],
        out_specs=jax.tree.map(lambda _: VMEM, outs),
        scratch_shapes=scratch,
        compiler_params=pltpu.CompilerParams(vmem_limit_bytes=room * 1024),
        cost_estimate=pl.CostEstimate(flops=flops, bytes_accessed=3000000, transcendentals=0),
    )(*args)


def passed_along(value, axis, steps):
    count = lax.axis_size(axis)
    return lax.ppermute(value, axis, [(source, (source + steps) % count) for source in range(count)])


def swapped(value, axis, first):
    count = lax.axis_size(axis)
    pairs = []
    for source in range(first, count, 2):
        other = (source + 1) % count
        pairs += [(source, other), (other, source)]
    return lax.ppermute(value, axis, pairs)


def far_field(low, groups):
    far = None
    for k in range(1, groups):
        moved = passed_along(low, "group", k)
        far = moved if far is None else jnp.where(lax.axis_index("group") == k, moved, far)
    return far


def per_device(disp_now, disp_prev, memory_init, density, lame_lambda, shear_mu, sls_decay, owner_map):
    ring = ("cuts", "sub")
    subs = lax.axis_size("sub")
    groups = lax.axis_size("group")

    rim = call(
        gather_kernel, "gather", shaped(8, WIDE_FACE),
        [pltpu.VMEM((3, 8, FACE), F32)] * 2 + [pltpu.VMEM((8, FACE), F32), pltpu.SemaphoreType.DMA((3,))],
        disp_now, disp_prev, density, outside=(0, 1, 2), room=54 * 1024 - 120,
    )
    rim = passed_along(rim, ring, -1)

    grad_table = jnp.asarray(side_by_side(GRAD))
    force_table = jnp.asarray(cut_table(FORCE))
    face_table = jnp.asarray(cut_table(FACES))
    share_table = jnp.asarray(SHARE)
    rim_table = jnp.asarray(RIM)
    column_lanes = jnp.asarray(COLUMN_LANES)
    node_lanes = jnp.asarray(NODE_LANES)
    mass = jnp.asarray(MASS)
    memory = memory_init[0]
    owner = jnp.transpose(owner_map, (0, 2, 1))

    state = shaped(3, ROWS, LANES)
    scale_shape = shaped(ROWS, LANES)
    five = shaped(5, 125, LANES)
    part_shape = shaped(256, LANES, dtype=BF16)
    grad_scratch = pltpu.VMEM((384, 384), F32)
    part_scratch = [grad_scratch, pltpu.VMEM((256, LANES), F32)]
    face = shaped(40, LANES)
    grad_shape = shaped(384, 384)
    flat_shape = shaped(3, 128, LANES)
    u, p, scale, m1, spread, flat, base = call(
        prologue_kernel, "prologue", [state, state, scale_shape, five, shaped(WINDOW, WIDE, dtype=BF16), flat_shape, grad_shape],
        [pltpu.VMEM((8, 56, WINDOW), F32)],
        disp_now, disp_prev, density, memory, sls_decay, mass, grad_table, face_table, force_table, rim_table, share_table, lame_lambda, shear_mu,
    )
    rows = 512 // subs
    memories = [m1]
    kept = []
    for step in range(STEPS):
        last_step = step == STEPS - 1
        low_shape = shaped(3, 128, LANES, dtype=BF16)
        if last_step:
            extra, low = call(
                shares_kernel, "shares", [shaped(3, 40, LANES), low_shape], [pltpu.VMEM((3, 128, LANES), F32)],
                odd, even, face_scale, flat,
            )
            far = far_field(low, groups)
            arrived = (extra,)
        else:
            arrived = (flat, rim, column_lanes) if step == 0 else (flat, odd, even, face_scale)
        outs = [shaped(6, 125, LANES), grad_shape, face]
        if not last_step:
            outs += [face, five, low_shape, scale_shape if step == 0 else shaped(3, 40, LANES)]
        results = call(
            lambda *refs, step=step: step_kernel(step, *refs), "step", outs,
            [grad_scratch, pltpu.VMEM((3, 128, LANES), F32), pltpu.VMEM((40, 384), F32)],
            lame_lambda, shear_mu, memories[step], sls_decay, rim_table if step == 0 else share_table, face_table, base, *arrived, *kept,
        )
        strain, sigma, even = results[0:3]
        if last_step:
            before = passed_along(even, ring, 1)
        else:
            odd, keep, low, extra = results[3:7]
            kept.append(keep)
            odd = swapped(odd, ring, 1)
            even = swapped(even, ring, 0)
            far = far_field(low, groups)
        if step == 0:
            p, scale, partial, flat, base, face_scale = call(
                first_rest_kernel, "rest", [state, scale_shape, state, flat_shape, grad_shape, shaped(40, LANES)],
                [pltpu.VMEM((3, ROWS, LANES), F32)], sigma, force_table, u, p, scale, extra, mass, grad_table,
            )
        else:
            results = call(
                rest_kernel, "rest", [state] if last_step else [state, state, flat_shape, grad_shape],
                [pltpu.VMEM((3, ROWS, LANES), F32)] if last_step else [], sigma, force_table, partial, extra, p, scale, grad_table,
            )
            if last_step:
                partial = results[0]
            else:
                partial, p, flat, base = results
        shared = (strain, low, far, lame_lambda, shear_mu, grad_table)
        if step == 0:
            one = call(parts_kernel, "parts", part_shape, part_scratch, *shared)
            m2, m3, select = call(
                later_kernel, "later", [five, five, shaped(subs * LANES, LANES, dtype=BF16)], [], memory, sls_decay, owner
            )
            memories += [m2, m3]
            base, one, select, memories[2] = lax.optimization_barrier((base, one, select, m3))
        elif not last_step:
            both = call(
                both_parts_kernel, "parts", shaped(256, LANES), part_scratch, *shared, one
            )
            base, flat, both = lax.optimization_barrier((base, flat, both))
        else:
            total, *blocks = call(
                send_kernel, "send", [shaped(256, LANES)] + [shaped(rows, LANES, dtype=jnp.int16)] * (subs - 1),
                part_scratch, *shared, both, select,
            )
            order = [*range(subs - 1, 0, -1), 0]
            sent = [lax.ppermute(blocks[k - 1], "sub", [(j, j ^ k) for j in range(subs)]) for k in order[:-1]]
            sent.append(call(own_kernel, "own", shaped(rows, LANES), [], total, select))
    nodal = call(nodal_kernel, "nodal", shaped(24, FACE), [], partial, spread)
    final = call(
        finish_kernel, "finish", shaped(1, 3, 8, FACE), [pltpu.VMEM((ROWS, LANES), F32), pltpu.VMEM((8, WIDE_FACE), F32)],
        before, nodal, face_scale, node_lanes, flops=250000000,
    )
    kernels = call(
        lambda *refs: sum_kernel(order, *refs), "sum", shaped(250, 1, 256), [], *sent
    )
    return final, jnp.transpose(kernels, (1, 2, 0))


def solution(mesh):
    in_specs = (
        P("group", None, ("cuts", "sub"), None),
        P("group", None, ("cuts", "sub"), None),
        P("group", None, None, None, ("cuts", "sub")),
        P(("cuts", "sub"), None),
        P(None, ("cuts", "sub")),
        P(None, ("cuts", "sub")),
        P(None, ("cuts", "sub")),
        P(("cuts", "sub"), None, None),
    )
    out_specs = (P("group", None, ("cuts", "sub"), None), P("group", ("cuts", "sub"), None))
    return jax.shard_map(
        per_device, mesh=mesh, in_specs=in_specs, out_specs=out_specs, check_vma=False
    )
```

```python
import math

import jax
import jax.numpy as jnp
import numpy as np
from jax import lax
from jax.experimental import pallas as pl
from jax.experimental.pallas import tpu as pltpu
from jax.sharding import PartitionSpec as P

STEPS = 3
EY = 8
EZ = 8
LANES = 128
SIDE = 33
FACE = SIDE * SIDE
BLOCKS = 26
ROWS = 8 * BLOCKS
WIDE = 64 * BLOCKS
JUMP = 4 * SIDE
WIDE_FACE = 1152
WINDOW = 256

time_step = 0.03
step_square = 0.0009
relax_strength = (0.12, 0.08, 0.05)

F32 = jnp.float32
BF16 = jnp.bfloat16


def gll_tables():
    root_value = math.sqrt(3.0 / 7.0)
    points = [-1.0, -root_value, 0.0, root_value, 1.0]
    weights = [0.1, 49.0 / 90.0, 32.0 / 45.0, 49.0 / 90.0, 0.1]
    derivative = np.zeros((5, 5))
    for p in range(5):
        for a in range(5):
            accum = 0.0
            for m in range(5):
                if m != a:
                    factor = 1.0 / (points[a] - points[m])
                    for k in range(5):
                        if k != a and k != m:
                            factor = factor * (points[p] - points[k]) / (points[a] - points[k])
                    accum = accum + factor
            derivative[p, a] = accum
    return derivative.astype(np.float32).astype(np.float64), np.array(weights).astype(np.float32).astype(np.float64)


def node(a, b, d):
    return a * 25 + b * 5 + d


def place(a, b, d):
    return (b * 5 + d) * 8 + a


FACE_ROWS = [slice(0, 128), slice(128, 160), slice(224, 256), slice(256, 288), slice(352, 384)]


def make_tables():
    derivative, weights = gll_tables()
    grad = np.zeros((3 * 128, 128))
    force = np.zeros((ROWS, 3 * 128))
    for a in range(5):
        for b in range(5):
            for d in range(5):
                for m in range(5):
                    grad[node(a, b, d), node(m, b, d)] = derivative[a, m]
                    grad[128 + node(a, b, d), node(a, m, d)] = derivative[b, m]
                    grad[256 + node(a, b, d), node(a, b, m)] = derivative[d, m]
                    row = place(a, b, d)
                    force[row, node(m, b, d)] = -derivative[m, a] * weights[m] * weights[b] * weights[d]
                    force[row, 128 + node(a, m, d)] = -derivative[m, b] * weights[a] * weights[m] * weights[d]
                    force[row, 256 + node(a, b, m)] = -derivative[m, d] * weights[a] * weights[b] * weights[m]
    full = np.zeros((80, 3 * 128))
    first_grad, last_grad = np.zeros((3 * 128, 40)), np.zeros((3 * 128, 40))
    for b in range(5):
        for d in range(5):
            full[d * 8 + b] = force[place(0, b, d)]
            full[40 + d * 8 + b] = force[place(4, b, d)]
            first_grad[:, d * 8 + b] = grad[:, node(0, b, d)]
            last_grad[:, d * 8 + b] = grad[:, node(4, b, d)]
    face = np.concatenate([full[:, rows] for rows in FACE_ROWS], axis=1)
    first, last = cut_table(first_grad), cut_table(last_grad)
    share = np.concatenate([first[0], first[0], first[1], last[0], last[0], last[1]], axis=1)
    rim = np.concatenate([last[0], last[0], last[1], last[1], last[0], last[2]], axis=1)
    line = np.zeros(SIDE)
    for e in range(8):
        line[4 * e : 4 * e + 5] += weights
    layer = np.array([2 * weights[0], weights[1], weights[2], weights[3], 2 * weights[0], 1.0, 1.0, 1.0])
    mass = np.ones((ROWS, LANES), np.float32)
    for b in range(5):
        for d in range(5):
            for ey in range(8):
                for ez in range(8):
                    for slab in range(2):
                        at = (b * 5 + d) * 8
                        mass[at : at + 8, slab * 64 + ey * 8 + ez] = layer * line[4 * ey + b] * line[4 * ez + d]
    return grad, force, face, mass, share, rim


def side_by_side(table):
    high, middle, low = cut_table(table)
    pairs = ((high, middle), (middle, high), (low, high))
    return np.stack([np.concatenate(pair, axis=1) for pair in pairs])


def cut_table(table):
    value = table.astype(np.float32)
    pieces = []
    for _ in range(3):
        piece = value.astype(jnp.bfloat16)
        pieces.append(piece)
        value = value - piece.astype(np.float32)
    return np.stack(pieces)


GRAD, FORCE, FACES, MASS, SHARE, RIM = make_tables()


def make_gathers():
    columns = np.zeros((BLOCKS // 2, LANES), np.int32)
    for b in range(5):
        for d in range(5):
            block = b * 5 + d
            for ey in range(8):
                for ez in range(8):
                    columns[block // 2, (block % 2) * 64 + ey * 8 + ez] = (4 * ey + b) * SIDE + 4 * ez + d
    nodes = np.zeros((WIDE_FACE // LANES, LANES), np.int32)
    for y in range(SIDE):
        for z in range(SIDE):
            ey, ez = min(y // 4, 7), min(z // 4, 7)
            block = (y - 4 * ey) * 5 + z - 4 * ez
            spot = y * SIDE + z
            nodes[spot // LANES, spot % LANES] = (block // 2) * LANES + (block % 2) * 64 + ey * 8 + ez
    return columns, nodes


COLUMN_LANES, NODE_LANES = make_gathers()


def gathered(tiles, table, table_ref):
    results = []
    for row in range(table.shape[0]):
        spots = jnp.broadcast_to(table_ref[row : row + 1, :], (8, LANES))
        tile_of, lane_of = spots // LANES, spots % LANES
        value = jnp.zeros((8, LANES), F32)
        for at in sorted(set((table[row] // LANES).tolist())):
            moved = jnp.take_along_axis(tiles[at], lane_of, axis=1, mode="promise_in_bounds")
            value = jnp.where(tile_of == at, moved, value)
        results.append(value)
    return results


def cut(value):
    high = value.astype(BF16)
    rest = value - high.astype(F32)
    middle = rest.astype(BF16)
    low = (rest - middle.astype(F32)).astype(BF16)
    return high, middle, low


def dot(left, right):
    return jnp.dot(left, right, preferred_element_type=F32)


def gradients(table, flat):
    high, middle, low = cut(flat)
    first = dot(table[0:2].reshape(768, 256), jnp.concatenate([high, middle], axis=0))
    return first[0:384] + (first[384:768] + dot(table[2], jnp.concatenate([high, low], axis=0)))


def low_gradients(table, low):
    return dot(table[0], jnp.concatenate([low, low], axis=0)) + dot(table[2, :, 0:128], low)


def flatten(u_ref, flat_ref):
    for c in range(3):
        flat_ref[c, 120:128, :] = jnp.zeros((8, LANES), F32)
        for a in range(5):
            flat_ref[c, 25 * a : 25 * a + 25, :] = u_ref[c, pl.ds(a, 25, stride=8), :]


def dot_three(table, value):
    rows = table.shape[1]
    stacked = table[0:2].reshape(2 * rows, table.shape[2])
    high, middle, _ = cut(value)
    first = dot(stacked, high)
    return first[0:rows] + (first[rows : 2 * rows] + dot(stacked[0:rows], middle))


def lanes_of(shape):
    return lax.broadcasted_iota(jnp.int32, shape, len(shape) - 1)


def rolled(value, shift, axis):
    return pltpu.roll(value, shift % value.shape[axis], axis)


def window_rows(value, window_ref):
    for ey in range(EY):
        width = min(WINDOW, FACE - JUMP * ey)
        if width < WINDOW:
            window_ref[ey] = jnp.zeros(window_ref.shape[1:], F32)
        window_ref[ey, :, 0:width] = value[:, JUMP * ey : JUMP * ey + width]
    return window_ref[...].reshape(-1, WINDOW)


def to_columns(value, window_ref, spread_ref):
    rows = value.shape[0]
    pieces = jnp.concatenate(cut(window_rows(value, window_ref)), axis=0)
    wide = dot(pieces, spread_ref[...])
    half = EY * rows
    own = (lanes_of((rows, WIDE)) // 8) % 8
    picked = 0.0
    for ey in range(EY):
        at = slice(ey * rows, (ey + 1) * rows)
        value = wide[at] + wide[half : 2 * half][at] + wide[2 * half : 3 * half][at]
        picked = jnp.where(own == ey, value, picked)
    return picked


def assembled(blocks):
    lane = lanes_of((8, LANES))
    blocks = dict(blocks)
    for shift, at, pairs in (
        (1, lane % 8, [((b, 0), (b, 4)) for b in range(5)]),
        (8, (lane // 8) % 8, [((0, d), (4, d)) for d in range(5)]),
    ):
        for c in range(3):
            for near, far in pairs:
                first, last = blocks[(c,) + near], blocks[(c,) + far]
                blocks[(c,) + near] = first + jnp.where(at > 0, rolled(last, shift, 1), 0.0)
                blocks[(c,) + far] = last + jnp.where(at < 7, rolled(first, -shift, 1), 0.0)
    return blocks


def block_rows(b, d):
    return slice((b * 5 + d) * 8, (b * 5 + d) * 8 + 8)


def beside(value):
    return jnp.concatenate([value[0], value[1], value[2]], axis=1)


def gather_kernel(now_ref, prev_ref, density_ref, rim_ref, now_copy, prev_copy, density_copy, sems):
    copies = [
        pltpu.make_async_copy(now_ref.at[0], now_copy, sems.at[0]),
        pltpu.make_async_copy(prev_ref.at[0], prev_copy, sems.at[1]),
        pltpu.make_async_copy(density_ref, density_copy, sems.at[2]),
    ]
    for copy in copies:
        copy.start()
    for copy in copies:
        copy.wait()
    rim_ref[:, 1024:] = jnp.zeros((8, WIDE_FACE - 1024), F32)
    for c in range(3):
        rim_ref[c : c + 1, 0:FACE] = now_copy[c, 0:1, :]
        rim_ref[3 + c : 4 + c, 0:FACE] = prev_copy[c, 0:1, :]
    rim_ref[6:7, 0:FACE] = density_copy[0:1, :]
    rim_ref[7:8, 0:FACE] = density_copy[0:1, :]


def weighted_memory(memory_ref, decays, part, power):
    value = 0.0
    for l in range(3):
        factor = decays[l]
        for _ in range(power - 1):
            factor = factor * decays[l]
        value = value + factor * memory_ref[l, part]
    return value


def spread_table():
    column = lanes_of((1, WIDE))
    block = column // 64
    spot = (block // 5) * SIDE + (block % 5) + 4 * (column % 8)
    spot = jnp.where(block < 25, spot, WINDOW)
    return jnp.where(lax.broadcasted_iota(jnp.int32, (WINDOW, WIDE), 0) == spot, 1.0, 0.0).astype(BF16)


def prologue_kernel(now_ref, prev_ref, density_ref, memory_ref, decay_ref, mass_ref, *refs):
    grad_table = refs[0]
    u_ref, p_ref, scale_ref, m1_ref, spread_ref, flat_ref, grad_ref, window_ref = refs[-8:]
    spread_ref[...] = spread_table()
    rows = jnp.concatenate([now_ref[0].reshape(24, FACE), prev_ref[0].reshape(24, FACE), density_ref[...]], axis=0)
    columns = to_columns(rows, window_ref, spread_ref)
    lane = lanes_of((8, LANES))
    for group in range(7):
        for pair in range(BLOCKS // 2):
            tile = columns[8 * group : 8 * group + 8, LANES * pair : LANES * pair + LANES]
            swapped = rolled(tile, 64, 1)
            even = jnp.where(lane < 64, tile, rolled(swapped, 4, 0))
            odd = jnp.where(lane < 64, swapped, rolled(tile, 4, 0))
            for block, value in ((2 * pair, even), (2 * pair + 1, odd)):
                at = slice(8 * block, 8 * block + 8)
                if group < 3:
                    u_ref[group, at, :] = value
                elif group < 6:
                    p_ref[group - 3, at, :] = value
                elif block < 25:
                    scale_ref[at, :] = step_square / (value * mass_ref[at, :])
                else:
                    scale_ref[at, :] = jnp.zeros((8, LANES), F32)
    decays = [decay_ref[l : l + 1, :] for l in range(3)]
    for part in range(5):
        m1_ref[part] = weighted_memory(memory_ref, decays, part, 1)
    flatten(u_ref, flat_ref)
    lower = lanes_of((25, LANES)) < 64
    for c in range(3):
        flat_ref[c, 100:125, :] = jnp.where(lower, flat_ref[c, 100:125, :], 0.0)
    grad_ref[...] = gradients(grad_table, beside(flat_ref))


def later_kernel(memory_ref, decay_ref, owner_ref, m2_ref, m3_ref, select_ref):
    decays = [decay_ref[l : l + 1, :] for l in range(3)]
    for part in range(5):
        m2_ref[part] = weighted_memory(memory_ref, decays, part, 2)
        m3_ref[part] = weighted_memory(memory_ref, decays, part, 3)
    owner = jnp.concatenate([owner_ref[0], owner_ref[1]], axis=1)
    named = jnp.where(lax.broadcasted_iota(jnp.int32, (16, LANES), 0) == owner, 1.0, 0.0)
    earlier = lax.broadcasted_iota(jnp.int32, (LANES, LANES), 0)
    later = lax.broadcasted_iota(jnp.int32, (LANES, LANES), 1)
    ahead = jnp.where((earlier < later) & ((earlier // 64) == (later // 64)), 1.0, 0.0)
    rank = jnp.sum(named * dot(named.astype(BF16), ahead.astype(BF16)), axis=0, keepdims=True).astype(jnp.int32)
    subs = select_ref.shape[0] // LANES
    slots = 4 * EY * EZ // subs
    row = lax.broadcasted_iota(jnp.int32, select_ref.shape, 0)
    toward = (row // LANES) ^ lax.axis_index("sub")
    wanted = (lanes_of((1, LANES)) // 64) * (slots // 2) + rank
    chosen = (owner == toward) & (wanted == row % slots)
    select_ref[...] = jnp.where(chosen, 1.0, 0.0).astype(BF16)


def rim_rows(rim_ref, lanes_ref, rows_ref):
    tiles = [rim_ref[:, at : at + LANES] for at in range(0, WIDE_FACE, LANES)]
    for pair, tile in enumerate(gathered(tiles, COLUMN_LANES, lanes_ref)):
        rows_ref[16 * pair : 16 * pair + 8, :] = rolled(tile, 64, 1)
        rows_ref[16 * pair + 8 : 16 * pair + 16, :] = tile


def rim_displacement(rim_ref, lanes_ref, rows_ref):
    sub = lax.broadcasted_iota(jnp.int32, (8, LANES), 0)
    tiles = [rim_ref[:, at : at + LANES] for at in range(0, WIDE_FACE, LANES)]
    tiles.append(tiles[-1])
    pairs = [jnp.where(sub < 3, tiles[at], rolled(tiles[at + 1], 3, 0)) for at in range(0, len(tiles), 2)]
    second = jnp.where(sub < 3, 0, 1)
    for row in range(BLOCKS // 2):
        spots = jnp.broadcast_to(lanes_ref[row : row + 1, :], (8, LANES))
        tile_of, lane_of = spots // LANES, spots % LANES
        value = jnp.zeros((8, LANES), F32)
        for at in sorted(set((COLUMN_LANES[row] // (2 * LANES)).tolist())):
            moved = jnp.take_along_axis(pairs[at], lane_of, axis=1, mode="promise_in_bounds")
            value = jnp.where(tile_of == 2 * at + second, moved, value)
        tile = jnp.where(tile_of % 2 == 0, value, rolled(value, -3, 0))
        rows_ref[16 * row : 16 * row + 8, :] = rolled(tile, 64, 1)
        rows_ref[16 * row + 8 : 16 * row + 16, :] = tile


def unpack_face(here, there):
    top = lax.broadcasted_iota(jnp.int32, (8, LANES), 0) < 3
    parts = [[], [], []]
    for d in range(5):
        first, second = here[8 * d : 8 * d + 8], there[8 * d : 8 * d + 8]
        third = jnp.where(top, rolled(first, 3, 0), rolled(second, 6, 0))
        for part, line in zip(parts, (first, second, third)):
            part.append(line)
    return parts


def face_shares(odd_ref, even_ref, face_scale_ref):
    even_ring = lax.axis_index(("cuts", "sub")) % 2 == 0
    odd, even = odd_ref[...], even_ref[...]
    lower = (lanes_of((40, LANES)) < 64) == even_ring
    rows = unpack_face(jnp.where(lower, odd, even), rolled(jnp.where(lower, even, odd), 64, 1))
    return [assembled_lines(lines, face_scale_ref) for lines in rows]


def assembled_lines(lines, face_scale_ref):
    lane = lanes_of((8, LANES))
    sub = lax.broadcasted_iota(jnp.int32, (8, LANES), 0)
    ez, ey = lane % 8, (lane // 8) % 8
    up, down = (sub == 0) & (ey > 0), (sub == 4) & (ey < 7)
    first, last = lines[0], lines[4]
    lines = list(lines)
    lines[0] = first + jnp.where(ez > 0, rolled(last, 1, 1), 0.0)
    lines[4] = last + jnp.where(ez < 7, rolled(first, -1, 1), 0.0)
    for d in range(5):
        turned = rolled(lines[d], 4, 0)
        added = jnp.where(up, rolled(turned, 8, 1), jnp.where(down, rolled(turned, -8, 1), 0.0))
        lines[d] = face_scale_ref[8 * d : 8 * d + 8, :] * (lines[d] + added)
    return lines


def strains(grad, rows):
    def at(direction, c):
        return grad[direction * 128 + rows.start : direction * 128 + rows.stop, c * LANES : (c + 1) * LANES]

    return [
        at(0, 0),
        at(1, 1),
        at(2, 2),
        0.5 * (at(1, 0) + at(0, 1)),
        0.5 * (at(2, 0) + at(0, 2)),
        0.5 * (at(2, 1) + at(1, 2)),
    ]


CHUNKS = [slice(row, min(row + 8, 125)) for row in range(0, 125, 8)]


def pack_face(face, upper):
    lane = lanes_of((8, LANES))
    target = lane < 64 if upper else lane >= 64
    own = lax.broadcasted_iota(jnp.int32, (8, LANES), 0) < 5
    lines = []
    for d in range(5):
        first, second, third = [face[8 * d : 8 * d + 8, c * LANES : (c + 1) * LANES] for c in range(3)]
        moved = rolled(jnp.where(own, first, rolled(third, 5, 0)), 64, 1)
        lines.append(jnp.where(target, moved, jnp.where(own, second, rolled(third, 2, 0))))
    return jnp.concatenate(lines, axis=0)


def add_shares(shares, flat_ref):
    upper = lanes_of((5, LANES)) >= 64
    for c in range(3):
        for d in range(5):
            first, last = pl.ds(d, 5, stride=5), pl.ds(100 + d, 5, stride=5)
            flat_ref[c, first, :] = flat_ref[c, first, :] + jnp.where(upper, 0.0, shares[c][d][0:5])
            flat_ref[c, last, :] = flat_ref[c, last, :] + jnp.where(upper, shares[c][d][0:5], 0.0)


def shares_kernel(odd_ref, even_ref, face_scale_ref, flat_in, delta_ref, low_ref, flat_ref):
    shares = face_shares(odd_ref, even_ref, face_scale_ref)
    for c in range(3):
        delta_ref[c] = jnp.concatenate(shares[c], axis=0)
    flat_ref[...] = flat_in[...]
    add_shares(shares, flat_ref)
    low_ref[...] = flat_ref[...].astype(BF16)


def step_kernel(step, *refs):
    lame_ref, mu_ref, m_ref, decay_ref, share_table, face_table, base_ref = refs[0:7]
    arrived = refs[7 : 7 + (3, 4, 1)[step]]
    refs = refs[7 + len(arrived) :]
    older, refs = refs[:step], refs[step:]
    strain_ref, sigma_ref, even_ref = refs[0:3]
    if step < STEPS - 1:
        odd_ref, keep_ref, low_ref = refs[3:6]
    grad_ref, flat_ref, rim_ref, rows_ref = refs[-4:]
    upper = lanes_of((40, 3 * LANES)) % LANES >= 64
    if step == 0:
        flat_ref[...] = arrived[0][...]
        rim_displacement(arrived[1], arrived[2], rows_ref)
        rim_ref[...] = jnp.zeros(rim_ref.shape, F32)
        for c in range(3):
            for d in range(5):
                rim_ref[8 * d : 8 * d + 5, c * LANES : (c + 1) * LANES] = rows_ref[pl.ds(8 * d + c, 5, stride=40), :]
        high, middle, low = [piece.astype(F32) for piece in cut(jnp.where(upper, rim_ref[...], 0.0))]
        stacked = [high, middle, high, middle, low, high]
        at_upper = lanes_of((25, LANES)) >= 64
        for c in range(3):
            flat_ref[c, 100:125, :] = jnp.where(at_upper, rows_ref[pl.ds(c, 25, stride=8), :], flat_ref[c, 100:125, :])
    else:
        if step == STEPS - 1:
            value = jnp.concatenate([arrived[0][c] for c in range(3)], axis=1)
        else:
            shares = face_shares(*arrived[1:4])
            value = jnp.concatenate([jnp.concatenate(lines, axis=0) for lines in shares], axis=1)
            for c in range(3):
                refs[6][c] = value[:, c * LANES : (c + 1) * LANES]
            flat_ref[...] = arrived[0][...]
            add_shares(shares, flat_ref)
        high, middle, _ = [piece.astype(F32) for piece in cut(value)]
        stacked = []
        for at in (~upper, upper):
            stacked += [jnp.where(at, high, 0.0), jnp.where(at, middle, 0.0), jnp.where(at, high, 0.0)]
    grad_ref[...] = base_ref[...] + dot(share_table[...], jnp.concatenate(stacked, axis=0).astype(BF16))
    if step < STEPS - 1:
        low_ref[...] = flat_ref[...].astype(BF16)
    for block in range(9):
        sigma_ref[(block // 3) * 128 + 120 : (block // 3) * 128 + 128, (block % 3) * LANES : (block % 3) * LANES + LANES] = (
            jnp.zeros((8, LANES), F32)
        )
    decays = [decay_ref[l : l + 1, :] for l in range(3)]
    shares = [(1.0 - decays[l]) * relax_strength[l] for l in range(3)]
    factors = []
    for _ in range(step + 1):
        factors.append(shares[0] + shares[1] + shares[2])
        shares = [decays[l] * shares[l] for l in range(3)]
    for rows in CHUNKS:
        strain = strains(grad_ref, rows)
        for part in range(6):
            strain_ref[part, rows, :] = strain[part]
        lame = lame_ref[rows, :]
        twice_mu = 2.0 * mu_ref[rows, :]
        trace = strain[0] + strain[1] + strain[2]
        third = trace * (1.0 / 3.0)
        pulls = [twice_mu * s for s in strain]
        pull_third = twice_mu * third
        fresh = [pulls[0] - pull_third, pulls[1] - pull_third, pulls[3], pulls[4], pulls[5]]
        relax = []
        for part in range(5):
            value = m_ref[part, rows, :] + factors[0] * fresh[part]
            for back in range(step):
                value = value + factors[back + 1] * older[step - 1 - back][part, rows, :]
            relax.append(value)
            if step < STEPS - 1:
                keep_ref[part, rows, :] = fresh[part]
        bulk = lame * trace
        xx = bulk + pulls[0] - relax[0]
        yy = bulk + pulls[1] - relax[1]
        zz = bulk + pulls[2] + relax[0] + relax[1]
        xy = pulls[3] - relax[2]
        xz = pulls[4] - relax[3]
        yz = pulls[5] - relax[4]
        for direction, values in enumerate(((xx, xy, xz), (xy, yy, yz), (xz, yz, zz))):
            for c in range(3):
                sigma_ref[direction * 128 + rows.start : direction * 128 + rows.stop, c * LANES : (c + 1) * LANES] = values[c]
    faces = dot_three(face_table, jnp.concatenate([sigma_ref[rows, :] for rows in FACE_ROWS], axis=0))
    first, last = pack_face(faces[0:40], False), pack_face(faces[40:80], True)
    if step < STEPS - 1:
        even_ring = lax.axis_index(("cuts", "sub")) % 2 == 0
        odd_ref[...] = jnp.where(even_ring, first, last)
        even_ref[...] = jnp.where(even_ring, last, first)
    else:
        even_ref[...] = last


def next_state(sigma_ref, force_table, u_ref, p_ref, scale_ref, next_ref):
    force = dot_three(force_table, sigma_ref[...])
    blocks = {}
    for c in range(3):
        for b in range(5):
            for d in range(5):
                blocks[(c, b, d)] = force[block_rows(b, d), c * LANES : (c + 1) * LANES]
    blocks = assembled(blocks)
    lane = lanes_of((8, LANES))
    sub = lax.broadcasted_iota(jnp.int32, (8, LANES), 0)
    inner = ((sub == 4) & (lane < 64)) | ((sub == 0) & (lane >= 64))
    for c in range(3):
        for b in range(5):
            for d in range(5):
                value = blocks[(c, b, d)]
                value = value + jnp.where(inner, rolled(rolled(value, 4, 0), 64, 1), 0.0)
                at = block_rows(b, d)
                next_ref[c, at, :] = 2.0 * u_ref[c, at, :] - p_ref[c, at, :] + scale_ref[at, :] * value
        next_ref[c, 200:208, :] = jnp.zeros((8, LANES), F32)


def first_rest_kernel(
    sigma_ref, force_table, u_in, p_in, scale_in, rim_ref, lanes_ref, mass_ref, grad_table,
    u_ref, scale_ref, next_ref, flat_ref, grad_ref, face_scale_ref, p_ref, rows_ref
):
    rim_rows(rim_ref, lanes_ref, rows_ref)
    u_ref[...] = u_in[...]
    p_ref[...] = p_in[...]
    scale_ref[...] = scale_in[...]
    upper = lanes_of((25, LANES)) >= 64
    last = pl.ds(4, 25, stride=8)
    for c in range(3):
        u_ref[c, last, :] = jnp.where(upper, rows_ref[pl.ds(c, 25, stride=8), :], u_ref[c, last, :])
        p_ref[c, last, :] = jnp.where(upper, rows_ref[pl.ds(3 + c, 25, stride=8), :], p_ref[c, last, :])
    rim = step_square / (rows_ref[pl.ds(6, 25, stride=8), :] * mass_ref[last, :])
    scale_ref[last, :] = jnp.where(upper, rim, scale_ref[last, :])
    face_scale_ref[...] = jnp.zeros(face_scale_ref.shape, F32)
    lower = lanes_of((5, LANES)) < 64
    for d in range(5):
        first, last = pl.ds(8 * d, 5, stride=40), pl.ds(8 * d + 4, 5, stride=40)
        face_scale_ref[8 * d : 8 * d + 5, :] = jnp.where(lower, scale_ref[first, :], scale_ref[last, :])
    next_state(sigma_ref, force_table, u_ref, p_ref, scale_ref, next_ref)
    flatten(next_ref, flat_ref)
    grad_ref[...] = gradients(grad_table, beside(flat_ref))


def rest_kernel(sigma_ref, force_table, partial_ref, delta_ref, p_ref, scale_ref, grad_table, next_ref, u_ref, *refs):
    u_ref[...] = partial_ref[...]
    upper = lanes_of((5, LANES)) >= 64
    for c in range(3):
        for d in range(5):
            share = delta_ref[c, 8 * d : 8 * d + 5, :]
            first, last = pl.ds(8 * d, 5, stride=40), pl.ds(8 * d + 4, 5, stride=40)
            u_ref[c, first, :] = u_ref[c, first, :] + jnp.where(upper, 0.0, share)
            u_ref[c, last, :] = u_ref[c, last, :] + jnp.where(upper, share, 0.0)
    next_state(sigma_ref, force_table, u_ref, p_ref, scale_ref, next_ref)
    if refs:
        flat_ref, grad_ref = refs
        flatten(next_ref, flat_ref)
        grad_ref[...] = gradients(grad_table, beside(flat_ref))


def kernel_parts(strain_ref, low_ref, far_ref, lame_ref, mu_ref, grad_table, grad_ref, kernel_ref):
    forward = jnp.where(lax.axis_index("group") == 0, beside(low_ref), beside(far_ref))
    grad_ref[...] = low_gradients(grad_table, forward)
    for rows in CHUNKS:
        far = strains(grad_ref, rows)
        own = [strain_ref[part, rows, :] for part in range(6)]
        trace_own = own[0] + own[1] + own[2]
        trace_far = far[0] + far[1] + far[2]
        third_own, third_far = trace_own * (1.0 / 3.0), trace_far * (1.0 / 3.0)
        twice_mu = 2.0 * mu_ref[rows, :]
        kappa = lame_ref[rows, :] + twice_mu * (1.0 / 3.0)
        kernel_ref[rows, :] = time_step * kappa * trace_far * trace_own
        product = (
            (own[0] - third_own) * (far[0] - third_far)
            + (own[1] - third_own) * (far[1] - third_far)
            + (own[2] - third_own) * (far[2] - third_far)
            + 2.0 * (own[3] * far[3] + own[4] * far[4] + own[5] * far[5])
        )
        kernel_ref[125 + rows.start : 125 + rows.stop, :] = time_step * twice_mu * product
    kernel_ref[250:256, :] = jnp.zeros((6, LANES), F32)
    return kernel_ref[...].astype(BF16)


def placed(pieces, select, rows):
    slots = rows // 2
    group = lanes_of((rows, LANES)) // slots
    total = 0.0
    for piece in pieces:
        total = total + lax.dot_general(piece, select, (((1,), (1,)), ((), ())), preferred_element_type=F32)
    blocks = []
    for k in range(select.shape[0] // LANES):
        value = total[0:rows, k * LANES : (k + 1) * LANES]
        for j in range(1, 256 // rows):
            value = jnp.where(group == j, total[j * rows : (j + 1) * rows, k * LANES : (k + 1) * LANES], value)
        blocks.append(value)
    return blocks


def group_scale(mantissa, exponent):
    return mantissa * jnp.exp2(exponent) * (1.0 / (4096.0 * 32767.0))


def parts_kernel(strain_ref, low_ref, far_ref, lame_ref, mu_ref, grad_table, part_ref, grad_ref, kernel_ref):
    part_ref[...] = kernel_parts(strain_ref, low_ref, far_ref, lame_ref, mu_ref, grad_table, grad_ref, kernel_ref)


def both_parts_kernel(strain_ref, low_ref, far_ref, lame_ref, mu_ref, grad_table, one_ref, both_ref, grad_ref, kernel_ref):
    two = kernel_parts(strain_ref, low_ref, far_ref, lame_ref, mu_ref, grad_table, grad_ref, kernel_ref)
    both_ref[...] = one_ref[...].astype(F32) + two.astype(F32)


def send_kernel(strain_ref, low_ref, far_ref, lame_ref, mu_ref, grad_table, both_ref, select_ref, total_ref, *refs):
    out_refs, (grad_ref, kernel_ref) = refs[:-2], refs[-2:]
    three = kernel_parts(strain_ref, low_ref, far_ref, lame_ref, mu_ref, grad_table, grad_ref, kernel_ref)
    kernel_ref[...] = both_ref[...] + three.astype(F32)
    total_ref[...] = kernel_ref[...]
    for k in range(2):
        rows = slice(125 * k, 125 * k + 125)
        value = kernel_ref[rows, :]
        largest = jnp.maximum(jnp.max(jnp.abs(value), axis=0, keepdims=True), 1e-33)
        exponent = jnp.floor(jnp.log2(largest))
        mantissa = jnp.floor(largest * jnp.exp2(-exponent) * 4096.0) + 2.0
        kernel_ref[rows, :] = jnp.floor(value * (1.0 / group_scale(mantissa, exponent)) + 0.5)
        kernel_ref[250 + 2 * k : 251 + 2 * k, :] = mantissa
        kernel_ref[251 + 2 * k : 252 + 2 * k, :] = exponent
    high, middle, _ = cut(kernel_ref[...])
    for ref, value in zip(out_refs, placed((high, middle), select_ref[LANES:, :], out_refs[0].shape[0])):
        ref[...] = value.astype(jnp.int32).astype(jnp.int16)


def own_kernel(total_ref, select_ref, own_ref):
    row = lax.broadcasted_iota(jnp.int32, (256, LANES), 0)
    unit = jnp.where((row == 250) | (row == 252), 4096.0 * 32767.0, 0.0)
    value = jnp.where(row < 250, total_ref[...], unit)
    own_ref[...] = placed(cut(value), select_ref[0:LANES, :], own_ref.shape[0])[0]


def sum_kernel(order, *refs):
    in_refs, out_ref = refs[:-1], refs[-1]
    rows = in_refs[0].shape[0]
    slots = rows // 2
    pieces = 256 // rows
    group = lanes_of((rows, LANES)) // slots
    blocks = [[jnp.zeros((rows, LANES), F32)] * 2 for _ in range(pieces)]
    for k, ref in zip(order, in_refs):
        source = lax.axis_index("sub") ^ k
        spot = source % pieces
        value = ref[...].astype(jnp.int32).astype(F32) if k > 0 else ref[...]
        for j in range(pieces):
            moved = pltpu.roll(value, ((spot + pieces - j) % pieces) * slots, 1)
            for t in range(2):
                here = (group == spot) & (source // pieces == t)
                blocks[j][t] = jnp.where(here, moved, blocks[j][t])
    value = jnp.concatenate([jnp.concatenate(row, axis=1) for row in blocks], axis=0)
    first, second = [group_scale(value[row : row + 1], value[row + 1 : row + 2]) for row in (250, 252)]
    row = lax.broadcasted_iota(jnp.int32, (256, 256), 0)
    value = value * jnp.where(row < 125, first, second)
    out_ref[:, 0, :] = value[0:250]


def to_nodal(columns, spread_ref, nodal_ref):
    rows = columns.shape[0]
    own = (lanes_of((rows, WIDE)) // 8) % 8
    expanded = jnp.concatenate([jnp.where(own == ey, columns, 0.0) for ey in range(EY)], axis=0)
    over_lanes = (((1,), (1,)), ((), ()))
    pieces = jnp.concatenate(cut(expanded), axis=0)
    windows = lax.dot_general(pieces, spread_ref[...], over_lanes, preferred_element_type=F32)
    half = EY * rows
    windows = windows[0:half] + windows[half : 2 * half] + windows[2 * half : 3 * half]
    nodal_ref[...] = jnp.zeros(nodal_ref.shape, F32)
    for ey in range(EY):
        at = slice(JUMP * ey, JUMP * ey + 5 * SIDE)
        nodal_ref[:, at] = nodal_ref[:, at] + windows[ey * rows : (ey + 1) * rows, 0 : 5 * SIDE]


def nodal_kernel(partial_ref, spread_ref, nodal_ref):
    lane = lanes_of((8, LANES))
    sub = lax.broadcasted_iota(jnp.int32, (8, LANES), 0)
    tiles = []
    for c in range(3):
        row = []
        for pair in range(BLOCKS // 2):
            even = partial_ref[c, 16 * pair : 16 * pair + 8, :]
            odd = partial_ref[c, 16 * pair + 8 : 16 * pair + 16, :]
            low = jnp.where(sub < 4, even, rolled(rolled(even, 64, 1), 4, 0))
            high = jnp.where(sub < 4, rolled(odd, 64, 1), rolled(odd, 4, 0))
            row.append(jnp.where(lane < 64, low, high))
        tiles.append(jnp.concatenate(row, axis=1))
    columns = jnp.concatenate(tiles, axis=0)
    column = lanes_of((24, WIDE))
    block = column // 64
    once = ((block % 5 < 4) | (column % 8 == 7)) & ((block // 5 < 4) | ((column // 8) % 8 == 7))
    to_nodal(jnp.where(once, columns, 0.0), spread_ref, nodal_ref)


def finish_kernel(before_ref, nodal_ref, face_scale_ref, lanes_ref, out_ref, rows_ref, face_ref):
    packed = before_ref[...]
    values = unpack_face(packed, rolled(packed, 64, 1))
    rows_ref[...] = jnp.zeros(rows_ref.shape, F32)
    for c in range(3):
        lines = assembled_lines(values[c], face_scale_ref)
        for d in range(5):
            rows_ref[pl.ds(8 * d + c, 5, stride=40), :] = lines[d][0:5]
    lane = lanes_of((8, LANES))
    tiles = []
    for pair in range(BLOCKS // 2):
        even, odd = rows_ref[16 * pair : 16 * pair + 8, :], rows_ref[16 * pair + 8 : 16 * pair + 16, :]
        tiles.append(jnp.where(lane < 64, even, rolled(odd, 64, 1)))
    for at, tile in enumerate(gathered(tiles, NODE_LANES, lanes_ref)):
        face_ref[:, LANES * at : LANES * at + LANES] = tile
    first = lax.broadcasted_iota(jnp.int32, (8, FACE), 0) == 0
    for c in range(3):
        out_ref[0, c] = nodal_ref[8 * c : 8 * c + 8, :] + jnp.where(first, face_ref[c : c + 1, 0:FACE], 0.0)


VMEM = pl.BlockSpec(memory_space=pltpu.VMEM)
HBM = pl.BlockSpec(memory_space=pltpu.HBM)


def shaped(*shape, dtype=F32):
    return jax.ShapeDtypeStruct(shape, dtype)


def call(kernel, name, outs, scratch, *args, outside=(), flops=0, room=32 * 1024):
    return pl.pallas_call(
        kernel,
        name=name,
        out_shape=outs,
        in_specs=[HBM if at in outside else VMEM for at in range(len(args))],
        out_specs=jax.tree.map(lambda _: VMEM, outs),
        scratch_shapes=scratch,
        compiler_params=pltpu.CompilerParams(vmem_limit_bytes=room * 1024),
        cost_estimate=pl.CostEstimate(flops=flops, bytes_accessed=3000000, transcendentals=0),
    )(*args)


def passed_along(value, axis, steps):
    count = lax.axis_size(axis)
    return lax.ppermute(value, axis, [(source, (source + steps) % count) for source in range(count)])


def swapped(value, axis, first):
    count = lax.axis_size(axis)
    pairs = []
    for source in range(first, count, 2):
        other = (source + 1) % count
        pairs += [(source, other), (other, source)]
    return lax.ppermute(value, axis, pairs)


def far_field(low, groups):
    far = None
    for k in range(1, groups):
        moved = passed_along(low, "group", k)
        far = moved if far is None else jnp.where(lax.axis_index("group") == k, moved, far)
    return far


def per_device(disp_now, disp_prev, memory_init, density, lame_lambda, shear_mu, sls_decay, owner_map):
    ring = ("cuts", "sub")
    subs = lax.axis_size("sub")
    groups = lax.axis_size("group")

    rim = call(
        gather_kernel, "gather", shaped(8, WIDE_FACE),
        [pltpu.VMEM((3, 8, FACE), F32)] * 2 + [pltpu.VMEM((8, FACE), F32), pltpu.SemaphoreType.DMA((3,))],
        disp_now, disp_prev, density, outside=(0, 1, 2), room=54 * 1024 - 120,
    )
    rim = passed_along(rim, ring, -1)

    grad_table = jnp.asarray(side_by_side(GRAD))
    force_table = jnp.asarray(cut_table(FORCE))
    face_table = jnp.asarray(cut_table(FACES))
    share_table = jnp.asarray(SHARE)
    rim_table = jnp.asarray(RIM)
    column_lanes = jnp.asarray(COLUMN_LANES)
    node_lanes = jnp.asarray(NODE_LANES)
    mass = jnp.asarray(MASS)
    memory = memory_init[0]
    owner = jnp.transpose(owner_map, (0, 2, 1))

    state = shaped(3, ROWS, LANES)
    scale_shape = shaped(ROWS, LANES)
    five = shaped(5, 125, LANES)
    part_shape = shaped(256, LANES, dtype=BF16)
    grad_scratch = pltpu.VMEM((384, 384), F32)
    part_scratch = [grad_scratch, pltpu.VMEM((256, LANES), F32)]
    face = shaped(40, LANES)
    grad_shape = shaped(384, 384)
    flat_shape = shaped(3, 128, LANES)
    u, p, scale, m1, spread, flat, base = call(
        prologue_kernel, "prologue", [state, state, scale_shape, five, shaped(WINDOW, WIDE, dtype=BF16), flat_shape, grad_shape],
        [pltpu.VMEM((8, 56, WINDOW), F32)],
        disp_now, disp_prev, density, memory, sls_decay, mass, grad_table, face_table, force_table, rim_table, share_table, lame_lambda, shear_mu,
    )
    rows = 512 // subs
    memories = [m1]
    kept = []
    for step in range(STEPS):
        last_step = step == STEPS - 1
        low_shape = shaped(3, 128, LANES, dtype=BF16)
        if last_step:
            extra, low = call(
                shares_kernel, "shares", [shaped(3, 40, LANES), low_shape], [pltpu.VMEM((3, 128, LANES), F32)],
                odd, even, face_scale, flat,
            )
            far = far_field(low, groups)
            arrived = (extra,)
        else:
            arrived = (flat, rim, column_lanes) if step == 0 else (flat, odd, even, face_scale)
        outs = [shaped(6, 125, LANES), grad_shape, face]
        if not last_step:
            outs += [face, five, low_shape]
        if step == 1:
            outs.append(shaped(3, 40, LANES))
        results = call(
            lambda *refs, step=step: step_kernel(step, *refs), "step", outs,
            [grad_scratch, pltpu.VMEM((3, 128, LANES), F32), pltpu.VMEM((40, 384), F32), pltpu.VMEM((ROWS, LANES), F32)],
            lame_lambda, shear_mu, memories[step], sls_decay, rim_table if step == 0 else share_table, face_table, base, *arrived, *kept,
        )
        strain, sigma, even = results[0:3]
        if last_step:
            before = passed_along(even, ring, 1)
        else:
            odd, keep, low = results[3:6]
            extra = results[6] if step == 1 else None
            kept.append(keep)
            odd = swapped(odd, ring, 1)
            even = swapped(even, ring, 0)
            far = far_field(low, groups)
        if step == 0:
            p, scale, partial, flat, base, face_scale = call(
                first_rest_kernel, "rest", [state, scale_shape, state, flat_shape, grad_shape, shaped(40, LANES)],
                [pltpu.VMEM((3, ROWS, LANES), F32), pltpu.VMEM((ROWS, LANES), F32)],
                sigma, force_table, u, p, scale, rim, column_lanes, mass, grad_table,
            )
        else:
            results = call(
                rest_kernel, "rest", [state] if last_step else [state, state, flat_shape, grad_shape],
                [pltpu.VMEM((3, ROWS, LANES), F32)] if last_step else [], sigma, force_table, partial, extra, p, scale, grad_table,
            )
            if last_step:
                partial = results[0]
            else:
                partial, p, flat, base = results
        shared = (strain, low, far, lame_lambda, shear_mu, grad_table)
        if step == 0:
            one = call(parts_kernel, "parts", part_shape, part_scratch, *shared)
            m2, m3, select = call(
                later_kernel, "later", [five, five, shaped(subs * LANES, LANES, dtype=BF16)], [], memory, sls_decay, owner
            )
            memories += [m2, m3]
            base, one, select, memories[2] = lax.optimization_barrier((base, one, select, m3))
        elif not last_step:
            both = call(
                both_parts_kernel, "parts", shaped(256, LANES), part_scratch, *shared, one
            )
            base, flat, both = lax.optimization_barrier((base, flat, both))
        else:
            total, *blocks = call(
                send_kernel, "send", [shaped(256, LANES)] + [shaped(rows, LANES, dtype=jnp.int16)] * (subs - 1),
                part_scratch, *shared, both, select,
            )
            order = [*range(subs - 1, 0, -1), 0]
            sent = [lax.ppermute(blocks[k - 1], "sub", [(j, j ^ k) for j in range(subs)]) for k in order[:-1]]
            sent.append(call(own_kernel, "own", shaped(rows, LANES), [], total, select))
    nodal = call(nodal_kernel, "nodal", shaped(24, FACE), [], partial, spread)
    final = call(
        finish_kernel, "finish", shaped(1, 3, 8, FACE), [pltpu.VMEM((ROWS, LANES), F32), pltpu.VMEM((8, WIDE_FACE), F32)],
        before, nodal, face_scale, node_lanes, flops=250000000,
    )
    kernels = call(
        lambda *refs: sum_kernel(order, *refs), "sum", shaped(250, 1, 256), [], *sent
    )
    return final, jnp.transpose(kernels, (1, 2, 0))


def solution(mesh):
    in_specs = (
        P("group", None, ("cuts", "sub"), None),
        P("group", None, ("cuts", "sub"), None),
        P("group", None, None, None, ("cuts", "sub")),
        P(("cuts", "sub"), None),
        P(None, ("cuts", "sub")),
        P(None, ("cuts", "sub")),
        P(None, ("cuts", "sub")),
        P(("cuts", "sub"), None, None),
    )
    out_specs = (P("group", None, ("cuts", "sub"), None), P("group", ("cuts", "sub"), None))
    return jax.shard_map(
        per_device, mesh=mesh, in_specs=in_specs, out_specs=out_specs, check_vma=False
    )
```

```python
import math

import jax
import jax.numpy as jnp
import numpy as np
from jax import lax
from jax.experimental import pallas as pl
from jax.experimental.pallas import tpu as pltpu
from jax.sharding import PartitionSpec as P

STEPS = 3
EY = 8
EZ = 8
LANES = 128
SIDE = 33
FACE = SIDE * SIDE
BLOCKS = 26
ROWS = 8 * BLOCKS
TALL = 320
FLAT = 144
WIDE = 64 * BLOCKS
JUMP = 4 * SIDE
WIDE_FACE = 1152
WINDOW = 256

time_step = 0.03
step_square = 0.0009
relax_strength = (0.12, 0.08, 0.05)

F32 = jnp.float32
BF16 = jnp.bfloat16


def gll_tables():
    root_value = math.sqrt(3.0 / 7.0)
    points = [-1.0, -root_value, 0.0, root_value, 1.0]
    weights = [0.1, 49.0 / 90.0, 32.0 / 45.0, 49.0 / 90.0, 0.1]
    derivative = np.zeros((5, 5))
    for p in range(5):
        for a in range(5):
            accum = 0.0
            for m in range(5):
                if m != a:
                    factor = 1.0 / (points[a] - points[m])
                    for k in range(5):
                        if k != a and k != m:
                            factor = factor * (points[p] - points[k]) / (points[a] - points[k])
                    accum = accum + factor
            derivative[p, a] = accum
    return derivative.astype(np.float32).astype(np.float64), np.array(weights).astype(np.float32).astype(np.float64)


def node(a, b, d):
    return a * 25 + b * 5 + d


def place(a, b, d):
    return (b * 5 + d) * 8 + a


FACE_ROWS = [slice(0, 128), slice(128, 160), slice(224, 256), slice(256, 288), slice(352, 384)]


def make_tables():
    derivative, weights = gll_tables()
    grad = np.zeros((3 * 128, 128))
    force = np.zeros((ROWS, 3 * 128))
    for a in range(5):
        for b in range(5):
            for d in range(5):
                for m in range(5):
                    grad[node(a, b, d), node(m, b, d)] = derivative[a, m]
                    grad[128 + node(a, b, d), node(a, m, d)] = derivative[b, m]
                    grad[256 + node(a, b, d), node(a, b, m)] = derivative[d, m]
                    row = place(a, b, d)
                    force[row, node(m, b, d)] = -derivative[m, a] * weights[m] * weights[b] * weights[d]
                    force[row, 128 + node(a, m, d)] = -derivative[m, b] * weights[a] * weights[m] * weights[d]
                    force[row, 256 + node(a, b, m)] = -derivative[m, d] * weights[a] * weights[b] * weights[m]
    full = np.zeros((80, 3 * 128))
    first_grad, last_grad = np.zeros((3 * 128, 40)), np.zeros((3 * 128, 40))
    for b in range(5):
        for d in range(5):
            full[d * 8 + b] = force[place(0, b, d)]
            full[40 + d * 8 + b] = force[place(4, b, d)]
            first_grad[:, d * 8 + b] = grad[:, node(0, b, d)]
            last_grad[:, d * 8 + b] = grad[:, node(4, b, d)]
    face = np.concatenate([full[:, rows] for rows in FACE_ROWS], axis=1)
    first, last = cut_table(first_grad), cut_table(last_grad)
    share = np.concatenate([first[0], first[0], first[1], last[0], last[0], last[1]], axis=1)
    rim = np.concatenate([last[0], last[0], last[1], last[1], last[0], last[2]], axis=1)
    line = np.zeros(SIDE)
    for e in range(8):
        line[4 * e : 4 * e + 5] += weights
    layer = np.array([2 * weights[0], weights[1], weights[2], weights[3], 2 * weights[0], 1.0, 1.0, 1.0])
    mass = np.ones((TALL, LANES), np.float32)
    for b in range(5):
        for d in range(5):
            for ey in range(8):
                for ez in range(8):
                    for slab in range(2):
                        at = (b * 5 + d) * 8
                        mass[at : at + 8, slab * 64 + ey * 8 + ez] = layer * line[4 * ey + b] * line[4 * ez + d]
    return grad, force, face, mass, share, rim


def side_by_side(table):
    high, middle, low = cut_table(table)
    pairs = ((high, middle), (middle, high), (low, high))
    return np.stack([np.concatenate(pair, axis=1) for pair in pairs])


def cut_table(table):
    value = table.astype(np.float32)
    pieces = []
    for _ in range(3):
        piece = value.astype(jnp.bfloat16)
        pieces.append(piece)
        value = value - piece.astype(np.float32)
    return np.stack(pieces)


GRAD, FORCE, FACES, MASS, SHARE, RIM = make_tables()


def make_gathers():
    columns = np.zeros((BLOCKS // 2, LANES), np.int32)
    for b in range(5):
        for d in range(5):
            block = b * 5 + d
            for ey in range(8):
                for ez in range(8):
                    columns[block // 2, (block % 2) * 64 + ey * 8 + ez] = (4 * ey + b) * SIDE + 4 * ez + d
    nodes = np.zeros((WIDE_FACE // LANES, LANES), np.int32)
    for y in range(SIDE):
        for z in range(SIDE):
            ey, ez = min(y // 4, 7), min(z // 4, 7)
            block = (y - 4 * ey) * 5 + z - 4 * ez
            spot = y * SIDE + z
            nodes[spot // LANES, spot % LANES] = (block // 2) * LANES + (block % 2) * 64 + ey * 8 + ez
    return columns, nodes


COLUMN_LANES, NODE_LANES = make_gathers()


def gathered(tiles, table, table_ref):
    results = []
    for row in range(table.shape[0]):
        spots = jnp.broadcast_to(table_ref[row : row + 1, :], (8, LANES))
        tile_of, lane_of = spots // LANES, spots % LANES
        value = jnp.zeros((8, LANES), F32)
        for at in sorted(set((table[row] // LANES).tolist())):
            moved = jnp.take_along_axis(tiles[at], lane_of, axis=1, mode="promise_in_bounds")
            value = jnp.where(tile_of == at, moved, value)
        results.append(value)
    return results


def cut(value):
    high = value.astype(BF16)
    rest = value - high.astype(F32)
    middle = rest.astype(BF16)
    low = (rest - middle.astype(F32)).astype(BF16)
    return high, middle, low


def dot(left, right):
    return jnp.dot(left, right, preferred_element_type=F32)


def gradients(table, flat):
    high, middle, low = cut(flat)
    first = dot(table[0:2].reshape(768, 256), jnp.concatenate([high, middle], axis=0))
    return first[0:384] + (first[384:768] + dot(table[2], jnp.concatenate([high, low], axis=0)))


def low_gradients(table, low):
    return dot(table[0], jnp.concatenate([low, low], axis=0)) + dot(table[2, :, 0:128], low)


def flatten(u_ref, flat_ref):
    for c in range(3):
        flat_ref[c, 120:128, :] = jnp.zeros((8, LANES), F32)
        for a in range(5):
            flat_ref[c, 25 * a : 25 * a + 25, :] = u_ref[c, pl.ds(a, 25, stride=8), :]


def dot_three(table, value):
    rows = table.shape[1]
    stacked = table[0:2].reshape(2 * rows, table.shape[2])
    high, middle, _ = cut(value)
    first = dot(stacked, high)
    return first[0:rows] + (first[rows : 2 * rows] + dot(stacked[0:rows], middle))


def lanes_of(shape):
    return lax.broadcasted_iota(jnp.int32, shape, len(shape) - 1)


def rolled(value, shift, axis):
    return pltpu.roll(value, shift % value.shape[axis], axis)


def window_rows(value, window_ref):
    for ey in range(EY):
        width = min(WINDOW, FACE - JUMP * ey)
        if width < WINDOW:
            window_ref[ey] = jnp.zeros(window_ref.shape[1:], F32)
        window_ref[ey, :, 0:width] = value[:, JUMP * ey : JUMP * ey + width]
    return window_ref[...].reshape(-1, WINDOW)


def to_columns(value, window_ref, spread_ref):
    rows = value.shape[0]
    pieces = jnp.concatenate(cut(window_rows(value, window_ref)), axis=0)
    wide = dot(pieces, spread_ref[...])
    half = EY * rows
    own = (lanes_of((rows, WIDE)) // 8) % 8
    picked = 0.0
    for ey in range(EY):
        at = slice(ey * rows, (ey + 1) * rows)
        value = wide[at] + wide[half : 2 * half][at] + wide[2 * half : 3 * half][at]
        picked = jnp.where(own == ey, value, picked)
    return picked


def assembled(blocks):
    lane = lanes_of((8, LANES))
    blocks = dict(blocks)
    for shift, at, pairs in (
        (1, lane % 8, [((b, 0), (b, 4)) for b in range(5)]),
        (8, (lane // 8) % 8, [((0, d), (4, d)) for d in range(5)]),
    ):
        for c in range(3):
            for near, far in pairs:
                first, last = blocks[(c,) + near], blocks[(c,) + far]
                blocks[(c,) + near] = first + jnp.where(at > 0, rolled(last, shift, 1), 0.0)
                blocks[(c,) + far] = last + jnp.where(at < 7, rolled(first, -shift, 1), 0.0)
    return blocks


def block_rows(b, d):
    return slice((b * 5 + d) * 8, (b * 5 + d) * 8 + 8)


def beside(value):
    return jnp.concatenate([value[0], value[1], value[2]], axis=1)


def gather_kernel(now_ref, prev_ref, density_ref, rim_ref, now_copy, prev_copy, density_copy, sems):
    copies = [
        pltpu.make_async_copy(now_ref.at[0], now_copy, sems.at[0]),
        pltpu.make_async_copy(prev_ref.at[0], prev_copy, sems.at[1]),
        pltpu.make_async_copy(density_ref, density_copy, sems.at[2]),
    ]
    for copy in copies:
        copy.start()
    for copy in copies:
        copy.wait()
    rim_ref[:, 1024:] = jnp.zeros((8, WIDE_FACE - 1024), F32)
    for c in range(3):
        rim_ref[c : c + 1, 0:FACE] = now_copy[c, 0:1, :]
        rim_ref[3 + c : 4 + c, 0:FACE] = prev_copy[c, 0:1, :]
    rim_ref[6:7, 0:FACE] = density_copy[0:1, :]
    rim_ref[7:8, 0:FACE] = density_copy[0:1, :]


def weighted_memory(memory_ref, decays, part, power):
    value = 0.0
    for l in range(3):
        factor = decays[l]
        for _ in range(power - 1):
            factor = factor * decays[l]
        value = value + factor * memory_ref[l, part]
    return value


def spread_table():
    column = lanes_of((1, WIDE))
    block = column // 64
    spot = (block // 5) * SIDE + (block % 5) + 4 * (column % 8)
    spot = jnp.where(block < 25, spot, WINDOW)
    return jnp.where(lax.broadcasted_iota(jnp.int32, (WINDOW, WIDE), 0) == spot, 1.0, 0.0).astype(BF16)


def prologue_kernel(now_ref, prev_ref, density_ref, memory_ref, decay_ref, mass_ref, *refs):
    grad_table = refs[0]
    u_ref, p_ref, scale_ref, m1_ref, spread_ref, flat_ref, grad_ref, window_ref = refs[-8:]
    spread_ref[...] = spread_table()
    rows = jnp.concatenate([now_ref[0].reshape(24, FACE), prev_ref[0].reshape(24, FACE), density_ref[...]], axis=0)
    columns = to_columns(rows, window_ref, spread_ref)
    lane = lanes_of((8, LANES))
    for group in range(7):
        for pair in range(BLOCKS // 2):
            tile = columns[8 * group : 8 * group + 8, LANES * pair : LANES * pair + LANES]
            swapped = rolled(tile, 64, 1)
            even = jnp.where(lane < 64, tile, rolled(swapped, 4, 0))
            odd = jnp.where(lane < 64, swapped, rolled(tile, 4, 0))
            for block, value in ((2 * pair, even), (2 * pair + 1, odd)):
                at = slice(8 * block, 8 * block + 8)
                if group < 3:
                    u_ref[group, at, :] = value
                elif group < 6:
                    p_ref[group - 3, at, :] = value
                elif block < 25:
                    scale_ref[at, :] = step_square / (value * mass_ref[at, :])
                else:
                    scale_ref[at, :] = jnp.zeros((8, LANES), F32)
    decays = [decay_ref[l : l + 1, :] for l in range(3)]
    for part in range(5):
        m1_ref[part] = weighted_memory(memory_ref, decays, part, 1)
    flatten(u_ref, flat_ref)
    lower = lanes_of((25, LANES)) < 64
    for c in range(3):
        flat_ref[c, 100:125, :] = jnp.where(lower, flat_ref[c, 100:125, :], 0.0)
    grad_ref[...] = gradients(grad_table, beside(flat_ref))


def later_kernel(memory_ref, decay_ref, owner_ref, m2_ref, m3_ref, select_ref):
    decays = [decay_ref[l : l + 1, :] for l in range(3)]
    for part in range(5):
        m2_ref[part] = weighted_memory(memory_ref, decays, part, 2)
        m3_ref[part] = weighted_memory(memory_ref, decays, part, 3)
    owner = jnp.concatenate([owner_ref[0], owner_ref[1]], axis=1)
    named = jnp.where(lax.broadcasted_iota(jnp.int32, (16, LANES), 0) == owner, 1.0, 0.0)
    earlier = lax.broadcasted_iota(jnp.int32, (LANES, LANES), 0)
    later = lax.broadcasted_iota(jnp.int32, (LANES, LANES), 1)
    ahead = jnp.where((earlier < later) & ((earlier // 64) == (later // 64)), 1.0, 0.0)
    rank = jnp.sum(named * dot(named.astype(BF16), ahead.astype(BF16)), axis=0, keepdims=True).astype(jnp.int32)
    subs = select_ref.shape[0] // LANES
    slots = 4 * EY * EZ // subs
    row = lax.broadcasted_iota(jnp.int32, select_ref.shape, 0)
    toward = (row // LANES) ^ lax.axis_index("sub")
    wanted = (lanes_of((1, LANES)) // 64) * (slots // 2) + rank
    chosen = (owner == toward) & (wanted == row % slots)
    select_ref[...] = jnp.where(chosen, 1.0, 0.0).astype(BF16)


def rim_rows(rim_ref, lanes_ref, rows_ref):
    tiles = [rim_ref[:, at : at + LANES] for at in range(0, WIDE_FACE, LANES)]
    for pair, tile in enumerate(gathered(tiles, COLUMN_LANES, lanes_ref)):
        rows_ref[16 * pair : 16 * pair + 8, :] = rolled(tile, 64, 1)
        rows_ref[16 * pair + 8 : 16 * pair + 16, :] = tile


def rim_displacement(rim_ref, lanes_ref, rows_ref):
    sub = lax.broadcasted_iota(jnp.int32, (8, LANES), 0)
    tiles = [rim_ref[:, at : at + LANES] for at in range(0, WIDE_FACE, LANES)]
    tiles.append(tiles[-1])
    pairs = [jnp.where(sub < 3, tiles[at], rolled(tiles[at + 1], 3, 0)) for at in range(0, len(tiles), 2)]
    second = jnp.where(sub < 3, 0, 1)
    for row in range(BLOCKS // 2):
        spots = jnp.broadcast_to(lanes_ref[row : row + 1, :], (8, LANES))
        tile_of, lane_of = spots // LANES, spots % LANES
        value = jnp.zeros((8, LANES), F32)
        for at in sorted(set((COLUMN_LANES[row] // (2 * LANES)).tolist())):
            moved = jnp.take_along_axis(pairs[at], lane_of, axis=1, mode="promise_in_bounds")
            value = jnp.where(tile_of == 2 * at + second, moved, value)
        tile = jnp.where(tile_of % 2 == 0, value, rolled(value, -3, 0))
        rows_ref[16 * row : 16 * row + 8, :] = rolled(tile, 64, 1)
        rows_ref[16 * row + 8 : 16 * row + 16, :] = tile


def unpack_face(here, there):
    top = lax.broadcasted_iota(jnp.int32, (8, LANES), 0) < 3
    parts = [[], [], []]
    for d in range(5):
        first, second = here[8 * d : 8 * d + 8], there[8 * d : 8 * d + 8]
        third = jnp.where(top, rolled(first, 3, 0), rolled(second, 6, 0))
        for part, line in zip(parts, (first, second, third)):
            part.append(line)
    return parts


def face_shares(odd_ref, even_ref, face_scale_ref):
    even_ring = lax.axis_index(("cuts", "sub")) % 2 == 0
    odd, even = odd_ref[...], even_ref[...]
    lower = (lanes_of((40, LANES)) < 64) == even_ring
    rows = unpack_face(jnp.where(lower, odd, even), rolled(jnp.where(lower, even, odd), 64, 1))
    return [assembled_lines(lines, face_scale_ref) for lines in rows]


def assembled_lines(lines, face_scale_ref):
    lane = lanes_of((8, LANES))
    sub = lax.broadcasted_iota(jnp.int32, (8, LANES), 0)
    ez, ey = lane % 8, (lane // 8) % 8
    up, down = (sub == 0) & (ey > 0), (sub == 4) & (ey < 7)
    first, last = lines[0], lines[4]
    lines = list(lines)
    lines[0] = first + jnp.where(ez > 0, rolled(last, 1, 1), 0.0)
    lines[4] = last + jnp.where(ez < 7, rolled(first, -1, 1), 0.0)
    for d in range(5):
        turned = rolled(lines[d], 4, 0)
        added = jnp.where(up, rolled(turned, 8, 1), jnp.where(down, rolled(turned, -8, 1), 0.0))
        lines[d] = face_scale_ref[8 * d : 8 * d + 8, :] * (lines[d] + added)
    return lines


def strains(grad, rows):
    def at(direction, c):
        return grad[direction * 128 + rows.start : direction * 128 + rows.stop, c * LANES : (c + 1) * LANES]

    return [
        at(0, 0),
        at(1, 1),
        at(2, 2),
        0.5 * (at(1, 0) + at(0, 1)),
        0.5 * (at(2, 0) + at(0, 2)),
        0.5 * (at(2, 1) + at(1, 2)),
    ]


CHUNKS = [slice(row, min(row + 8, 125)) for row in range(0, 125, 8)]


def pack_face(face, upper):
    lane = lanes_of((8, LANES))
    target = lane < 64 if upper else lane >= 64
    own = lax.broadcasted_iota(jnp.int32, (8, LANES), 0) < 5
    lines = []
    for d in range(5):
        first, second, third = [face[8 * d : 8 * d + 8, c * LANES : (c + 1) * LANES] for c in range(3)]
        moved = rolled(jnp.where(own, first, rolled(third, 5, 0)), 64, 1)
        lines.append(jnp.where(target, moved, jnp.where(own, second, rolled(third, 2, 0))))
    return jnp.concatenate(lines, axis=0)


def add_shares(shares, flat_ref):
    upper = lanes_of((5, LANES)) >= 64
    for c in range(3):
        for d in range(5):
            first, last = pl.ds(d, 5, stride=5), pl.ds(100 + d, 5, stride=5)
            flat_ref[c, first, :] = flat_ref[c, first, :] + jnp.where(upper, 0.0, shares[c][d][0:5])
            flat_ref[c, last, :] = flat_ref[c, last, :] + jnp.where(upper, shares[c][d][0:5], 0.0)


def shares_kernel(odd_ref, even_ref, face_scale_ref, flat_in, delta_ref, low_ref, flat_ref):
    shares = face_shares(odd_ref, even_ref, face_scale_ref)
    for c in range(3):
        delta_ref[c] = jnp.concatenate(shares[c], axis=0)
    flat_ref[:, 0:128, :] = flat_in[...]
    add_shares(shares, flat_ref)
    low_ref[...] = flat_ref[:, 0:128, :].astype(BF16)


def step_kernel(step, *refs):
    lame_ref, mu_ref, m_ref, decay_ref, share_table, face_table, base_ref = refs[0:7]
    arrived = refs[7 : 7 + (3, 4, 1)[step]]
    refs = refs[7 + len(arrived) :]
    older, refs = refs[:step], refs[step:]
    strain_ref, sigma_ref, even_ref = refs[0:3]
    if step < STEPS - 1:
        odd_ref, keep_ref, low_ref = refs[3:6]
    grad_ref, flat_ref, rim_ref, rows_ref = refs[-4:]
    upper = lanes_of((40, 3 * LANES)) % LANES >= 64
    if step == 0:
        flat_ref[:, 0:128, :] = arrived[0][...]
        rim_displacement(arrived[1], arrived[2], rows_ref)
        rim_ref[...] = jnp.zeros(rim_ref.shape, F32)
        for c in range(3):
            for d in range(5):
                rim_ref[8 * d : 8 * d + 5, c * LANES : (c + 1) * LANES] = rows_ref[pl.ds(8 * d + c, 5, stride=40), :]
        high, middle, low = [piece.astype(F32) for piece in cut(jnp.where(upper, rim_ref[...], 0.0))]
        stacked = [high, middle, high, middle, low, high]
        at_upper = lanes_of((25, LANES)) >= 64
        for c in range(3):
            flat_ref[c, 100:125, :] = jnp.where(at_upper, rows_ref[pl.ds(c, 25, stride=8), :], flat_ref[c, 100:125, :])
    else:
        if step == STEPS - 1:
            value = jnp.concatenate([arrived[0][c] for c in range(3)], axis=1)
        else:
            shares = face_shares(*arrived[1:4])
            value = jnp.concatenate([jnp.concatenate(lines, axis=0) for lines in shares], axis=1)
            for c in range(3):
                refs[6][c] = value[:, c * LANES : (c + 1) * LANES]
            flat_ref[:, 0:128, :] = arrived[0][...]
            add_shares(shares, flat_ref)
        high, middle, _ = [piece.astype(F32) for piece in cut(value)]
        stacked = []
        for at in (~upper, upper):
            stacked += [jnp.where(at, high, 0.0), jnp.where(at, middle, 0.0), jnp.where(at, high, 0.0)]
    grad_ref[...] = base_ref[...] + dot(share_table[...], jnp.concatenate(stacked, axis=0).astype(BF16))
    if step < STEPS - 1:
        low_ref[...] = flat_ref[:, 0:128, :].astype(BF16)
    for block in range(9):
        sigma_ref[(block // 3) * 128 + 120 : (block // 3) * 128 + 128, (block % 3) * LANES : (block % 3) * LANES + LANES] = (
            jnp.zeros((8, LANES), F32)
        )
    decays = [decay_ref[l : l + 1, :] for l in range(3)]
    shares = [(1.0 - decays[l]) * relax_strength[l] for l in range(3)]
    factors = []
    for _ in range(step + 1):
        factors.append(shares[0] + shares[1] + shares[2])
        shares = [decays[l] * shares[l] for l in range(3)]
    for rows in CHUNKS:
        strain = strains(grad_ref, rows)
        for part in range(6):
            strain_ref[part, rows, :] = strain[part]
        lame = lame_ref[rows, :]
        twice_mu = 2.0 * mu_ref[rows, :]
        trace = strain[0] + strain[1] + strain[2]
        third = trace * (1.0 / 3.0)
        pulls = [twice_mu * s for s in strain]
        pull_third = twice_mu * third
        fresh = [pulls[0] - pull_third, pulls[1] - pull_third, pulls[3], pulls[4], pulls[5]]
        relax = []
        for part in range(5):
            value = m_ref[part, rows, :] + factors[0] * fresh[part]
            for back in range(step):
                value = value + factors[back + 1] * older[step - 1 - back][part, rows, :]
            relax.append(value)
            if step < STEPS - 1:
                keep_ref[part, rows, :] = fresh[part]
        bulk = lame * trace
        xx = bulk + pulls[0] - relax[0]
        yy = bulk + pulls[1] - relax[1]
        zz = bulk + pulls[2] + relax[0] + relax[1]
        xy = pulls[3] - relax[2]
        xz = pulls[4] - relax[3]
        yz = pulls[5] - relax[4]
        for direction, values in enumerate(((xx, xy, xz), (xy, yy, yz), (xz, yz, zz))):
            for c in range(3):
                sigma_ref[direction * 128 + rows.start : direction * 128 + rows.stop, c * LANES : (c + 1) * LANES] = values[c]
    faces = dot_three(face_table, jnp.concatenate([sigma_ref[rows, :] for rows in FACE_ROWS], axis=0))
    first, last = pack_face(faces[0:40], False), pack_face(faces[40:80], True)
    if step < STEPS - 1:
        even_ring = lax.axis_index(("cuts", "sub")) % 2 == 0
        odd_ref[...] = jnp.where(even_ring, first, last)
        even_ref[...] = jnp.where(even_ring, last, first)
    else:
        even_ref[...] = last


def next_state(sigma_ref, force_table, u_ref, p_ref, scale_ref, next_ref):
    force = dot_three(force_table, sigma_ref[...])
    blocks = {}
    for c in range(3):
        for b in range(5):
            for d in range(5):
                blocks[(c, b, d)] = force[block_rows(b, d), c * LANES : (c + 1) * LANES]
    blocks = assembled(blocks)
    lane = lanes_of((8, LANES))
    sub = lax.broadcasted_iota(jnp.int32, (8, LANES), 0)
    inner = ((sub == 4) & (lane < 64)) | ((sub == 0) & (lane >= 64))
    for c in range(3):
        for b in range(5):
            for d in range(5):
                value = blocks[(c, b, d)]
                value = value + jnp.where(inner, rolled(rolled(value, 4, 0), 64, 1), 0.0)
                at = block_rows(b, d)
                next_ref[c, at, :] = 2.0 * u_ref[c, at, :] - p_ref[c, at, :] + scale_ref[at, :] * value
        next_ref[c, 200:208, :] = jnp.zeros((8, LANES), F32)


def first_rest_kernel(
    sigma_ref, force_table, u_in, p_in, scale_in, rim_ref, lanes_ref, mass_ref, grad_table,
    u_ref, scale_ref, next_ref, flat_ref, grad_ref, face_scale_ref, p_ref, rows_ref
):
    rim_rows(rim_ref, lanes_ref, rows_ref)
    u_ref[:, 0:ROWS, :] = u_in[:, 0:ROWS, :]
    p_ref[:, 0:ROWS, :] = p_in[:, 0:ROWS, :]
    scale_ref[0:ROWS, :] = scale_in[0:ROWS, :]
    upper = lanes_of((25, LANES)) >= 64
    last = pl.ds(4, 25, stride=8)
    for c in range(3):
        u_ref[c, last, :] = jnp.where(upper, rows_ref[pl.ds(c, 25, stride=8), :], u_ref[c, last, :])
        p_ref[c, last, :] = jnp.where(upper, rows_ref[pl.ds(3 + c, 25, stride=8), :], p_ref[c, last, :])
    rim = step_square / (rows_ref[pl.ds(6, 25, stride=8), :] * mass_ref[last, :])
    scale_ref[last, :] = jnp.where(upper, rim, scale_ref[last, :])
    face_scale_ref[...] = jnp.zeros(face_scale_ref.shape, F32)
    lower = lanes_of((5, LANES)) < 64
    for d in range(5):
        first, last = pl.ds(8 * d, 5, stride=40), pl.ds(8 * d + 4, 5, stride=40)
        face_scale_ref[8 * d : 8 * d + 5, :] = jnp.where(lower, scale_ref[first, :], scale_ref[last, :])
    next_state(sigma_ref, force_table, u_ref, p_ref, scale_ref, next_ref)
    flatten(next_ref, flat_ref)
    grad_ref[...] = gradients(grad_table, beside(flat_ref))


def rest_kernel(sigma_ref, force_table, partial_ref, delta_ref, p_ref, scale_ref, grad_table, next_ref, u_ref, *refs):
    u_ref[:, 0:ROWS, :] = partial_ref[:, 0:ROWS, :]
    upper = lanes_of((5, LANES)) >= 64
    for c in range(3):
        for d in range(5):
            share = delta_ref[c, 8 * d : 8 * d + 5, :]
            first, last = pl.ds(8 * d, 5, stride=40), pl.ds(8 * d + 4, 5, stride=40)
            u_ref[c, first, :] = u_ref[c, first, :] + jnp.where(upper, 0.0, share)
            u_ref[c, last, :] = u_ref[c, last, :] + jnp.where(upper, share, 0.0)
    next_state(sigma_ref, force_table, u_ref, p_ref, scale_ref, next_ref)
    if refs:
        flat_ref, grad_ref = refs
        flatten(next_ref, flat_ref)
        grad_ref[...] = gradients(grad_table, beside(flat_ref))


def kernel_parts(strain_ref, low_ref, far_ref, lame_ref, mu_ref, grad_table, grad_ref, kernel_ref):
    forward = jnp.where(lax.axis_index("group") == 0, beside(low_ref), beside(far_ref))
    grad_ref[...] = low_gradients(grad_table, forward)
    for rows in CHUNKS:
        far = strains(grad_ref, rows)
        own = [strain_ref[part, rows, :] for part in range(6)]
        trace_own = own[0] + own[1] + own[2]
        trace_far = far[0] + far[1] + far[2]
        third_own, third_far = trace_own * (1.0 / 3.0), trace_far * (1.0 / 3.0)
        twice_mu = 2.0 * mu_ref[rows, :]
        kappa = lame_ref[rows, :] + twice_mu * (1.0 / 3.0)
        kernel_ref[rows, :] = time_step * kappa * trace_far * trace_own
        product = (
            (own[0] - third_own) * (far[0] - third_far)
            + (own[1] - third_own) * (far[1] - third_far)
            + (own[2] - third_own) * (far[2] - third_far)
            + 2.0 * (own[3] * far[3] + own[4] * far[4] + own[5] * far[5])
        )
        kernel_ref[125 + rows.start : 125 + rows.stop, :] = time_step * twice_mu * product
    kernel_ref[250:256, :] = jnp.zeros((6, LANES), F32)
    return kernel_ref[...].astype(BF16)


def placed(pieces, select, rows):
    slots = rows // 2
    group = lanes_of((rows, LANES)) // slots
    total = 0.0
    for piece in pieces:
        total = total + lax.dot_general(piece, select, (((1,), (1,)), ((), ())), preferred_element_type=F32)
    blocks = []
    for k in range(select.shape[0] // LANES):
        value = total[0:rows, k * LANES : (k + 1) * LANES]
        for j in range(1, 256 // rows):
            value = jnp.where(group == j, total[j * rows : (j + 1) * rows, k * LANES : (k + 1) * LANES], value)
        blocks.append(value)
    return blocks


def group_scale(mantissa, exponent):
    return mantissa * jnp.exp2(exponent) * (1.0 / (4096.0 * 32767.0))


def parts_kernel(strain_ref, low_ref, far_ref, lame_ref, mu_ref, grad_table, part_ref, grad_ref, kernel_ref):
    part_ref[...] = kernel_parts(strain_ref, low_ref, far_ref, lame_ref, mu_ref, grad_table, grad_ref, kernel_ref)


def both_parts_kernel(strain_ref, low_ref, far_ref, lame_ref, mu_ref, grad_table, one_ref, both_ref, grad_ref, kernel_ref):
    two = kernel_parts(strain_ref, low_ref, far_ref, lame_ref, mu_ref, grad_table, grad_ref, kernel_ref)
    both_ref[...] = one_ref[...].astype(F32) + two.astype(F32)


def send_kernel(strain_ref, low_ref, far_ref, lame_ref, mu_ref, grad_table, both_ref, select_ref, total_ref, *refs):
    out_refs, (grad_ref, kernel_ref) = refs[:-2], refs[-2:]
    three = kernel_parts(strain_ref, low_ref, far_ref, lame_ref, mu_ref, grad_table, grad_ref, kernel_ref)
    kernel_ref[...] = both_ref[...] + three.astype(F32)
    total_ref[...] = kernel_ref[...]
    for k in range(2):
        rows = slice(125 * k, 125 * k + 125)
        value = kernel_ref[rows, :]
        largest = jnp.maximum(jnp.max(jnp.abs(value), axis=0, keepdims=True), 1e-33)
        exponent = jnp.floor(jnp.log2(largest))
        mantissa = jnp.floor(largest * jnp.exp2(-exponent) * 4096.0) + 2.0
        kernel_ref[rows, :] = jnp.floor(value * (1.0 / group_scale(mantissa, exponent)) + 0.5)
        kernel_ref[250 + 2 * k : 251 + 2 * k, :] = mantissa
        kernel_ref[251 + 2 * k : 252 + 2 * k, :] = exponent
    high, middle, _ = cut(kernel_ref[...])
    for ref, value in zip(out_refs, placed((high, middle), select_ref[LANES:, :], out_refs[0].shape[0])):
        ref[...] = value.astype(jnp.int32).astype(jnp.int16)


def own_kernel(total_ref, select_ref, own_ref):
    row = lax.broadcasted_iota(jnp.int32, (256, LANES), 0)
    unit = jnp.where((row == 250) | (row == 252), 4096.0 * 32767.0, 0.0)
    value = jnp.where(row < 250, total_ref[...], unit)
    own_ref[...] = placed(cut(value), select_ref[0:LANES, :], own_ref.shape[0])[0]


def sum_kernel(order, *refs):
    in_refs, out_ref = refs[:-1], refs[-1]
    rows = in_refs[0].shape[0]
    slots = rows // 2
    pieces = 256 // rows
    group = lanes_of((rows, LANES)) // slots
    blocks = [[jnp.zeros((rows, LANES), F32)] * 2 for _ in range(pieces)]
    for k, ref in zip(order, in_refs):
        source = lax.axis_index("sub") ^ k
        spot = source % pieces
        value = ref[...].astype(jnp.int32).astype(F32) if k > 0 else ref[...]
        for j in range(pieces):
            moved = pltpu.roll(value, ((spot + pieces - j) % pieces) * slots, 1)
            for t in range(2):
                here = (group == spot) & (source // pieces == t)
                blocks[j][t] = jnp.where(here, moved, blocks[j][t])
    value = jnp.concatenate([jnp.concatenate(row, axis=1) for row in blocks], axis=0)
    first, second = [group_scale(value[row : row + 1], value[row + 1 : row + 2]) for row in (250, 252)]
    row = lax.broadcasted_iota(jnp.int32, (256, 256), 0)
    value = value * jnp.where(row < 125, first, second)
    out_ref[:, 0, :] = value[0:250]


def to_nodal(columns, spread_ref, nodal_ref):
    rows = columns.shape[0]
    own = (lanes_of((rows, WIDE)) // 8) % 8
    expanded = jnp.concatenate([jnp.where(own == ey, columns, 0.0) for ey in range(EY)], axis=0)
    over_lanes = (((1,), (1,)), ((), ()))
    pieces = jnp.concatenate(cut(expanded), axis=0)
    windows = lax.dot_general(pieces, spread_ref[...], over_lanes, preferred_element_type=F32)
    half = EY * rows
    windows = windows[0:half] + windows[half : 2 * half] + windows[2 * half : 3 * half]
    nodal_ref[...] = jnp.zeros(nodal_ref.shape, F32)
    for ey in range(EY):
        at = slice(JUMP * ey, JUMP * ey + 5 * SIDE)
        nodal_ref[:, at] = nodal_ref[:, at] + windows[ey * rows : (ey + 1) * rows, 0 : 5 * SIDE]


def nodal_kernel(partial_ref, spread_ref, nodal_ref):
    lane = lanes_of((8, LANES))
    sub = lax.broadcasted_iota(jnp.int32, (8, LANES), 0)
    tiles = []
    for c in range(3):
        row = []
        for pair in range(BLOCKS // 2):
            even = partial_ref[c, 16 * pair : 16 * pair + 8, :]
            odd = partial_ref[c, 16 * pair + 8 : 16 * pair + 16, :]
            low = jnp.where(sub < 4, even, rolled(rolled(even, 64, 1), 4, 0))
            high = jnp.where(sub < 4, rolled(odd, 64, 1), rolled(odd, 4, 0))
            row.append(jnp.where(lane < 64, low, high))
        tiles.append(jnp.concatenate(row, axis=1))
    columns = jnp.concatenate(tiles, axis=0)
    column = lanes_of((24, WIDE))
    block = column // 64
    once = ((block % 5 < 4) | (column % 8 == 7)) & ((block // 5 < 4) | ((column // 8) % 8 == 7))
    to_nodal(jnp.where(once, columns, 0.0), spread_ref, nodal_ref)


def finish_kernel(before_ref, nodal_ref, face_scale_ref, lanes_ref, out_ref, rows_ref, face_ref):
    packed = before_ref[...]
    values = unpack_face(packed, rolled(packed, 64, 1))
    rows_ref[...] = jnp.zeros(rows_ref.shape, F32)
    for c in range(3):
        lines = assembled_lines(values[c], face_scale_ref)
        for d in range(5):
            rows_ref[pl.ds(8 * d + c, 5, stride=40), :] = lines[d][0:5]
    lane = lanes_of((8, LANES))
    tiles = []
    for pair in range(BLOCKS // 2):
        even, odd = rows_ref[16 * pair : 16 * pair + 8, :], rows_ref[16 * pair + 8 : 16 * pair + 16, :]
        tiles.append(jnp.where(lane < 64, even, rolled(odd, 64, 1)))
    for at, tile in enumerate(gathered(tiles, NODE_LANES, lanes_ref)):
        face_ref[:, LANES * at : LANES * at + LANES] = tile
    first = lax.broadcasted_iota(jnp.int32, (8, FACE), 0) == 0
    for c in range(3):
        out_ref[0, c] = nodal_ref[8 * c : 8 * c + 8, :] + jnp.where(first, face_ref[c : c + 1, 0:FACE], 0.0)


VMEM = pl.BlockSpec(memory_space=pltpu.VMEM)
HBM = pl.BlockSpec(memory_space=pltpu.HBM)


def shaped(*shape, dtype=F32):
    return jax.ShapeDtypeStruct(shape, dtype)


def call(kernel, name, outs, scratch, *args, outside=(), flops=0, room=32 * 1024):
    return pl.pallas_call(
        kernel,
        name=name,
        out_shape=outs,
        in_specs=[HBM if at in outside else VMEM for at in range(len(args))],
        out_specs=jax.tree.map(lambda _: VMEM, outs),
        scratch_shapes=scratch,
        compiler_params=pltpu.CompilerParams(vmem_limit_bytes=room * 1024),
        cost_estimate=pl.CostEstimate(flops=flops, bytes_accessed=3000000, transcendentals=0),
    )(*args)


def passed_along(value, axis, steps):
    count = lax.axis_size(axis)
    return lax.ppermute(value, axis, [(source, (source + steps) % count) for source in range(count)])


def swapped(value, axis, first):
    count = lax.axis_size(axis)
    pairs = []
    for source in range(first, count, 2):
        other = (source + 1) % count
        pairs += [(source, other), (other, source)]
    return lax.ppermute(value, axis, pairs)


def far_field(low, groups):
    far = None
    for k in range(1, groups):
        moved = passed_along(low, "group", k)
        far = moved if far is None else jnp.where(lax.axis_index("group") == k, moved, far)
    return far


def per_device(disp_now, disp_prev, memory_init, density, lame_lambda, shear_mu, sls_decay, owner_map):
    ring = ("cuts", "sub")
    subs = lax.axis_size("sub")
    groups = lax.axis_size("group")

    rim = call(
        gather_kernel, "gather", shaped(8, WIDE_FACE),
        [pltpu.VMEM((3, 8, FACE), F32)] * 2 + [pltpu.VMEM((8, FACE), F32), pltpu.SemaphoreType.DMA((3,))],
        disp_now, disp_prev, density, outside=(0, 1, 2), room=54 * 1024 - 120,
    )
    rim = passed_along(rim, ring, -1)

    grad_table = jnp.asarray(side_by_side(GRAD))
    force_table = jnp.asarray(cut_table(FORCE))
    face_table = jnp.asarray(cut_table(FACES))
    share_table = jnp.asarray(SHARE)
    rim_table = jnp.asarray(RIM)
    column_lanes = jnp.asarray(COLUMN_LANES)
    node_lanes = jnp.asarray(NODE_LANES)
    mass = jnp.asarray(MASS)
    memory = memory_init[0]
    owner = jnp.transpose(owner_map, (0, 2, 1))

    state = shaped(3, TALL, LANES)
    scale_shape = shaped(TALL, LANES)
    five = shaped(5, 125, LANES)
    part_shape = shaped(256, LANES, dtype=BF16)
    grad_scratch = pltpu.VMEM((384, 384), F32)
    part_scratch = [grad_scratch, pltpu.VMEM((256, LANES), F32)]
    face = shaped(40, LANES)
    grad_shape = shaped(384, 384)
    flat_shape = shaped(3, 128, LANES)
    u, p, scale, m1, spread, flat, base = call(
        prologue_kernel, "prologue", [state, state, scale_shape, five, shaped(WINDOW, WIDE, dtype=BF16), flat_shape, grad_shape],
        [pltpu.VMEM((8, 56, WINDOW), F32)],
        disp_now, disp_prev, density, memory, sls_decay, mass, grad_table, face_table, force_table, rim_table, share_table, lame_lambda, shear_mu,
    )
    rows = 512 // subs
    memories = [m1]
    kept = []
    for step in range(STEPS):
        last_step = step == STEPS - 1
        low_shape = shaped(3, 128, LANES, dtype=BF16)
        if last_step:
            extra, low = call(
                shares_kernel, "shares", [shaped(3, 40, LANES), low_shape], [pltpu.VMEM((3, FLAT, LANES), F32)],
                odd, even, face_scale, flat,
            )
            far = far_field(low, groups)
            arrived = (extra,)
        else:
            arrived = (flat, rim, column_lanes) if step == 0 else (flat, odd, even, face_scale)
        outs = [shaped(6, 125, LANES), grad_shape, face]
        if not last_step:
            outs += [face, five, low_shape]
        if step == 1:
            outs.append(shaped(3, 40, LANES))
        results = call(
            lambda *refs, step=step: step_kernel(step, *refs), "step", outs,
            [grad_scratch, pltpu.VMEM((3, FLAT, LANES), F32), pltpu.VMEM((40, 384), F32), pltpu.VMEM((TALL, LANES), F32)],
            lame_lambda, shear_mu, memories[step], sls_decay, rim_table if step == 0 else share_table, face_table, base, *arrived, *kept,
        )
        strain, sigma, even = results[0:3]
        if last_step:
            before = passed_along(even, ring, 1)
        else:
            odd, keep, low = results[3:6]
            extra = results[6] if step == 1 else None
            kept.append(keep)
            odd = swapped(odd, ring, 1)
            even = swapped(even, ring, 0)
            far = far_field(low, groups)
        if step == 0:
            p, scale, partial, flat, base, face_scale = call(
                first_rest_kernel, "rest", [state, scale_shape, state, flat_shape, grad_shape, shaped(40, LANES)],
                [pltpu.VMEM((3, TALL, LANES), F32), pltpu.VMEM((TALL, LANES), F32)],
                sigma, force_table, u, p, scale, rim, column_lanes, mass, grad_table,
            )
        else:
            results = call(
                rest_kernel, "rest", [state] if last_step else [state, state, flat_shape, grad_shape],
                [pltpu.VMEM((3, TALL, LANES), F32)] if last_step else [], sigma, force_table, partial, extra, p, scale, grad_table,
            )
            if last_step:
                partial = results[0]
            else:
                partial, p, flat, base = results
        shared = (strain, low, far, lame_lambda, shear_mu, grad_table)
        if step == 0:
            one = call(parts_kernel, "parts", part_shape, part_scratch, *shared)
            m2, m3, select = call(
                later_kernel, "later", [five, five, shaped(subs * LANES, LANES, dtype=BF16)], [], memory, sls_decay, owner
            )
            memories += [m2, m3]
            base, one, select, memories[2] = lax.optimization_barrier((base, one, select, m3))
        elif not last_step:
            both = call(
                both_parts_kernel, "parts", shaped(256, LANES), part_scratch, *shared, one
            )
            base, flat, both = lax.optimization_barrier((base, flat, both))
        else:
            total, *blocks = call(
                send_kernel, "send", [shaped(256, LANES)] + [shaped(rows, LANES, dtype=jnp.int16)] * (subs - 1),
                part_scratch, *shared, both, select,
            )
            order = [*range(subs - 1, 0, -1), 0]
            sent = [lax.ppermute(blocks[k - 1], "sub", [(j, j ^ k) for j in range(subs)]) for k in order[:-1]]
            sent.append(call(own_kernel, "own", shaped(rows, LANES), [], total, select))
    nodal = call(nodal_kernel, "nodal", shaped(24, FACE), [], partial, spread)
    final = call(
        finish_kernel, "finish", shaped(1, 3, 8, FACE), [pltpu.VMEM((TALL, LANES), F32), pltpu.VMEM((8, WIDE_FACE), F32)],
        before, nodal, face_scale, node_lanes, flops=250000000,
    )
    kernels = call(
        lambda *refs: sum_kernel(order, *refs), "sum", shaped(250, 1, 256), [], *sent
    )
    return final, jnp.transpose(kernels, (1, 2, 0))


def solution(mesh):
    in_specs = (
        P("group", None, ("cuts", "sub"), None),
        P("group", None, ("cuts", "sub"), None),
        P("group", None, None, None, ("cuts", "sub")),
        P(("cuts", "sub"), None),
        P(None, ("cuts", "sub")),
        P(None, ("cuts", "sub")),
        P(None, ("cuts", "sub")),
        P(("cuts", "sub"), None, None),
    )
    out_specs = (P("group", None, ("cuts", "sub"), None), P("group", ("cuts", "sub"), None))
    return jax.shard_map(
        per_device, mesh=mesh, in_specs=in_specs, out_specs=out_specs, check_vma=False
    )
```

```python
import math

import jax
import jax.numpy as jnp
import numpy as np
from jax import lax
from jax.experimental import pallas as pl
from jax.experimental.pallas import tpu as pltpu
from jax.sharding import PartitionSpec as P

STEPS = 3
EY = 8
EZ = 8
LANES = 128
SIDE = 33
FACE = SIDE * SIDE
BLOCKS = 26
ROWS = 8 * BLOCKS
TALL = 320
FLAT = 144
WIDE = 64 * BLOCKS
JUMP = 4 * SIDE
WIDE_FACE = 1152
WINDOW = 256

time_step = 0.03
step_square = 0.0009
relax_strength = (0.12, 0.08, 0.05)

F32 = jnp.float32
BF16 = jnp.bfloat16


def gll_tables():
    root_value = math.sqrt(3.0 / 7.0)
    points = [-1.0, -root_value, 0.0, root_value, 1.0]
    weights = [0.1, 49.0 / 90.0, 32.0 / 45.0, 49.0 / 90.0, 0.1]
    derivative = np.zeros((5, 5))
    for p in range(5):
        for a in range(5):
            accum = 0.0
            for m in range(5):
                if m != a:
                    factor = 1.0 / (points[a] - points[m])
                    for k in range(5):
                        if k != a and k != m:
                            factor = factor * (points[p] - points[k]) / (points[a] - points[k])
                    accum = accum + factor
            derivative[p, a] = accum
    return derivative.astype(np.float32).astype(np.float64), np.array(weights).astype(np.float32).astype(np.float64)


def node(a, b, d):
    return a * 25 + b * 5 + d


def place(a, b, d):
    return (b * 5 + d) * 8 + a


FACE_ROWS = [slice(0, 128), slice(128, 160), slice(224, 256), slice(256, 288), slice(352, 384)]


def make_tables():
    derivative, weights = gll_tables()
    grad = np.zeros((3 * 128, 128))
    force = np.zeros((ROWS, 3 * 128))
    for a in range(5):
        for b in range(5):
            for d in range(5):
                for m in range(5):
                    grad[node(a, b, d), node(m, b, d)] = derivative[a, m]
                    grad[128 + node(a, b, d), node(a, m, d)] = derivative[b, m]
                    grad[256 + node(a, b, d), node(a, b, m)] = derivative[d, m]
                    row = place(a, b, d)
                    force[row, node(m, b, d)] = -derivative[m, a] * weights[m] * weights[b] * weights[d]
                    force[row, 128 + node(a, m, d)] = -derivative[m, b] * weights[a] * weights[m] * weights[d]
                    force[row, 256 + node(a, b, m)] = -derivative[m, d] * weights[a] * weights[b] * weights[m]
    full = np.zeros((80, 3 * 128))
    first_grad, last_grad = np.zeros((3 * 128, 40)), np.zeros((3 * 128, 40))
    for b in range(5):
        for d in range(5):
            full[d * 8 + b] = force[place(0, b, d)]
            full[40 + d * 8 + b] = force[place(4, b, d)]
            first_grad[:, d * 8 + b] = grad[:, node(0, b, d)]
            last_grad[:, d * 8 + b] = grad[:, node(4, b, d)]
    face = np.concatenate([full[:, rows] for rows in FACE_ROWS], axis=1)
    first, last = cut_table(first_grad), cut_table(last_grad)
    share = np.concatenate([first[0], first[0], first[1], last[0], last[0], last[1]], axis=1)
    rim = np.concatenate([last[0], last[0], last[1], last[1], last[0], last[2]], axis=1)
    line = np.zeros(SIDE)
    for e in range(8):
        line[4 * e : 4 * e + 5] += weights
    layer = np.array([2 * weights[0], weights[1], weights[2], weights[3], 2 * weights[0], 1.0, 1.0, 1.0])
    mass = np.ones((TALL, LANES), np.float32)
    for b in range(5):
        for d in range(5):
            for ey in range(8):
                for ez in range(8):
                    for slab in range(2):
                        at = (b * 5 + d) * 8
                        mass[at : at + 8, slab * 64 + ey * 8 + ez] = layer * line[4 * ey + b] * line[4 * ez + d]
    return grad, force, face, mass, share, rim


def side_by_side(table):
    high, middle, low = cut_table(table)
    pairs = ((high, middle), (middle, high), (low, high))
    return np.stack([np.concatenate(pair, axis=1) for pair in pairs])


def cut_table(table):
    value = table.astype(np.float32)
    pieces = []
    for _ in range(3):
        piece = value.astype(jnp.bfloat16)
        pieces.append(piece)
        value = value - piece.astype(np.float32)
    return np.stack(pieces)


GRAD, FORCE, FACES, MASS, SHARE, RIM = make_tables()


def make_gathers():
    columns = np.zeros((BLOCKS // 2, LANES), np.int32)
    for b in range(5):
        for d in range(5):
            block = b * 5 + d
            for ey in range(8):
                for ez in range(8):
                    columns[block // 2, (block % 2) * 64 + ey * 8 + ez] = (4 * ey + b) * SIDE + 4 * ez + d
    nodes = np.zeros((WIDE_FACE // LANES, LANES), np.int32)
    for y in range(SIDE):
        for z in range(SIDE):
            ey, ez = min(y // 4, 7), min(z // 4, 7)
            block = (y - 4 * ey) * 5 + z - 4 * ez
            spot = y * SIDE + z
            nodes[spot // LANES, spot % LANES] = (block // 2) * LANES + (block % 2) * 64 + ey * 8 + ez
    return columns, nodes


COLUMN_LANES, NODE_LANES = make_gathers()


def gathered(tiles, table, table_ref):
    results = []
    for row in range(table.shape[0]):
        spots = jnp.broadcast_to(table_ref[row : row + 1, :], (8, LANES))
        tile_of, lane_of = spots // LANES, spots % LANES
        value = jnp.zeros((8, LANES), F32)
        for at in sorted(set((table[row] // LANES).tolist())):
            moved = jnp.take_along_axis(tiles[at], lane_of, axis=1, mode="promise_in_bounds")
            value = jnp.where(tile_of == at, moved, value)
        results.append(value)
    return results


def cut(value):
    high = value.astype(BF16)
    rest = value - high.astype(F32)
    middle = rest.astype(BF16)
    low = (rest - middle.astype(F32)).astype(BF16)
    return high, middle, low


def dot(left, right):
    return jnp.dot(left, right, preferred_element_type=F32)


def gradients(table, flat):
    high, middle, low = cut(flat)
    first = dot(table[0:2].reshape(768, 256), jnp.concatenate([high, middle], axis=0))
    return first[0:384] + (first[384:768] + dot(table[2], jnp.concatenate([high, low], axis=0)))


def low_gradients(table, low):
    return dot(table[0], jnp.concatenate([low, low], axis=0)) + dot(table[2, :, 0:128], low)


def flatten(u_ref, flat_ref):
    for c in range(3):
        flat_ref[c, 120:128, :] = jnp.zeros((8, LANES), F32)
        for a in range(5):
            flat_ref[c, 25 * a : 25 * a + 25, :] = u_ref[c, pl.ds(a, 25, stride=8), :]


def dot_three(table, value):
    rows = table.shape[1]
    stacked = table[0:2].reshape(2 * rows, table.shape[2])
    high, middle, _ = cut(value)
    first = dot(stacked, high)
    return first[0:rows] + (first[rows : 2 * rows] + dot(stacked[0:rows], middle))


def lanes_of(shape):
    return lax.broadcasted_iota(jnp.int32, shape, len(shape) - 1)


def rolled(value, shift, axis):
    return pltpu.roll(value, shift % value.shape[axis], axis)


def window_rows(value, window_ref):
    for ey in range(EY):
        width = min(WINDOW, FACE - JUMP * ey)
        if width < WINDOW:
            window_ref[ey] = jnp.zeros(window_ref.shape[1:], F32)
        window_ref[ey, :, 0:width] = value[:, JUMP * ey : JUMP * ey + width]
    return window_ref[...].reshape(-1, WINDOW)


def to_columns(value, window_ref, spread_ref):
    rows = value.shape[0]
    pieces = jnp.concatenate(cut(window_rows(value, window_ref)), axis=0)
    wide = dot(pieces, spread_ref[...])
    half = EY * rows
    own = (lanes_of((rows, WIDE)) // 8) % 8
    picked = 0.0
    for ey in range(EY):
        at = slice(ey * rows, (ey + 1) * rows)
        value = wide[at] + wide[half : 2 * half][at] + wide[2 * half : 3 * half][at]
        picked = jnp.where(own == ey, value, picked)
    return picked


def assembled(blocks):
    lane = lanes_of((8, LANES))
    blocks = dict(blocks)
    for shift, at, pairs in (
        (1, lane % 8, [((b, 0), (b, 4)) for b in range(5)]),
        (8, (lane // 8) % 8, [((0, d), (4, d)) for d in range(5)]),
    ):
        for c in range(3):
            for near, far in pairs:
                first, last = blocks[(c,) + near], blocks[(c,) + far]
                blocks[(c,) + near] = first + jnp.where(at > 0, rolled(last, shift, 1), 0.0)
                blocks[(c,) + far] = last + jnp.where(at < 7, rolled(first, -shift, 1), 0.0)
    return blocks


def block_rows(b, d):
    return slice((b * 5 + d) * 8, (b * 5 + d) * 8 + 8)


def beside(value):
    return jnp.concatenate([value[0], value[1], value[2]], axis=1)


def gather_kernel(now_ref, prev_ref, density_ref, rim_ref, now_copy, prev_copy, density_copy, sems):
    copies = [
        pltpu.make_async_copy(now_ref.at[0], now_copy, sems.at[0]),
        pltpu.make_async_copy(prev_ref.at[0], prev_copy, sems.at[1]),
        pltpu.make_async_copy(density_ref, density_copy, sems.at[2]),
    ]
    for copy in copies:
        copy.start()
    for copy in copies:
        copy.wait()
    rim_ref[:, 1024:] = jnp.zeros((8, WIDE_FACE - 1024), F32)
    for c in range(3):
        rim_ref[c : c + 1, 0:FACE] = now_copy[c, 0:1, :]
        rim_ref[3 + c : 4 + c, 0:FACE] = prev_copy[c, 0:1, :]
    rim_ref[6:7, 0:FACE] = density_copy[0:1, :]
    rim_ref[7:8, 0:FACE] = density_copy[0:1, :]


def weighted_memory(memory_ref, decays, part, power):
    value = 0.0
    for l in range(3):
        factor = decays[l]
        for _ in range(power - 1):
            factor = factor * decays[l]
        value = value + factor * memory_ref[l, part]
    return value


def spread_table():
    column = lanes_of((1, WIDE))
    block = column // 64
    spot = (block // 5) * SIDE + (block % 5) + 4 * (column % 8)
    spot = jnp.where(block < 25, spot, WINDOW)
    return jnp.where(lax.broadcasted_iota(jnp.int32, (WINDOW, WIDE), 0) == spot, 1.0, 0.0).astype(BF16)


def prologue_kernel(now_ref, prev_ref, density_ref, memory_ref, decay_ref, mass_ref, *refs):
    grad_table = refs[0]
    u_ref, p_ref, scale_ref, m1_ref, spread_ref, flat_ref, grad_ref, window_ref = refs[-8:]
    spread_ref[...] = spread_table()
    rows = jnp.concatenate([now_ref[0].reshape(24, FACE), prev_ref[0].reshape(24, FACE), density_ref[...]], axis=0)
    columns = to_columns(rows, window_ref, spread_ref)
    lane = lanes_of((8, LANES))
    for group in range(7):
        for pair in range(BLOCKS // 2):
            tile = columns[8 * group : 8 * group + 8, LANES * pair : LANES * pair + LANES]
            swapped = rolled(tile, 64, 1)
            even = jnp.where(lane < 64, tile, rolled(swapped, 4, 0))
            odd = jnp.where(lane < 64, swapped, rolled(tile, 4, 0))
            for block, value in ((2 * pair, even), (2 * pair + 1, odd)):
                at = slice(8 * block, 8 * block + 8)
                if group < 3:
                    u_ref[group, at, :] = value
                elif group < 6:
                    p_ref[group - 3, at, :] = value
                elif block < 25:
                    scale_ref[at, :] = step_square / (value * mass_ref[at, :])
                else:
                    scale_ref[at, :] = jnp.zeros((8, LANES), F32)
    decays = [decay_ref[l : l + 1, :] for l in range(3)]
    for part in range(5):
        m1_ref[part] = weighted_memory(memory_ref, decays, part, 1)
    flatten(u_ref, flat_ref)
    lower = lanes_of((25, LANES)) < 64
    for c in range(3):
        flat_ref[c, 100:125, :] = jnp.where(lower, flat_ref[c, 100:125, :], 0.0)
    grad_ref[...] = gradients(grad_table, beside(flat_ref))


def later_kernel(memory_ref, decay_ref, owner_ref, m2_ref, m3_ref, select_ref):
    decays = [decay_ref[l : l + 1, :] for l in range(3)]
    for part in range(5):
        m2_ref[part] = weighted_memory(memory_ref, decays, part, 2)
        m3_ref[part] = weighted_memory(memory_ref, decays, part, 3)
    owner = jnp.concatenate([owner_ref[0], owner_ref[1]], axis=1)
    named = jnp.where(lax.broadcasted_iota(jnp.int32, (16, LANES), 0) == owner, 1.0, 0.0)
    earlier = lax.broadcasted_iota(jnp.int32, (LANES, LANES), 0)
    later = lax.broadcasted_iota(jnp.int32, (LANES, LANES), 1)
    ahead = jnp.where((earlier < later) & ((earlier // 64) == (later // 64)), 1.0, 0.0)
    rank = jnp.sum(named * dot(named.astype(BF16), ahead.astype(BF16)), axis=0, keepdims=True).astype(jnp.int32)
    subs = select_ref.shape[0] // LANES
    slots = 4 * EY * EZ // subs
    row = lax.broadcasted_iota(jnp.int32, select_ref.shape, 0)
    toward = (row // LANES) ^ lax.axis_index("sub")
    wanted = (lanes_of((1, LANES)) // 64) * (slots // 2) + rank
    chosen = (owner == toward) & (wanted == row % slots)
    select_ref[...] = jnp.where(chosen, 1.0, 0.0).astype(BF16)


def rim_rows(rim_ref, lanes_ref, rows_ref):
    tiles = [rim_ref[:, at : at + LANES] for at in range(0, WIDE_FACE, LANES)]
    for pair, tile in enumerate(gathered(tiles, COLUMN_LANES, lanes_ref)):
        rows_ref[16 * pair : 16 * pair + 8, :] = rolled(tile, 64, 1)
        rows_ref[16 * pair + 8 : 16 * pair + 16, :] = tile


def rim_displacement(rim_ref, lanes_ref, rows_ref):
    sub = lax.broadcasted_iota(jnp.int32, (8, LANES), 0)
    tiles = [rim_ref[:, at : at + LANES] for at in range(0, WIDE_FACE, LANES)]
    tiles.append(tiles[-1])
    pairs = [jnp.where(sub < 3, tiles[at], rolled(tiles[at + 1], 3, 0)) for at in range(0, len(tiles), 2)]
    second = jnp.where(sub < 3, 0, 1)
    for row in range(BLOCKS // 2):
        spots = jnp.broadcast_to(lanes_ref[row : row + 1, :], (8, LANES))
        tile_of, lane_of = spots // LANES, spots % LANES
        value = jnp.zeros((8, LANES), F32)
        for at in sorted(set((COLUMN_LANES[row] // (2 * LANES)).tolist())):
            moved = jnp.take_along_axis(pairs[at], lane_of, axis=1, mode="promise_in_bounds")
            value = jnp.where(tile_of == 2 * at + second, moved, value)
        tile = jnp.where(tile_of % 2 == 0, value, rolled(value, -3, 0))
        rows_ref[16 * row : 16 * row + 8, :] = rolled(tile, 64, 1)
        rows_ref[16 * row + 8 : 16 * row + 16, :] = tile


def unpack_face(here, there):
    top = lax.broadcasted_iota(jnp.int32, (8, LANES), 0) < 3
    parts = [[], [], []]
    for d in range(5):
        first, second = here[8 * d : 8 * d + 8], there[8 * d : 8 * d + 8]
        third = jnp.where(top, rolled(first, 3, 0), rolled(second, 6, 0))
        for part, line in zip(parts, (first, second, third)):
            part.append(line)
    return parts


def face_shares(odd_ref, even_ref, face_scale_ref):
    even_ring = lax.axis_index(("cuts", "sub")) % 2 == 0
    odd, even = odd_ref[...], even_ref[...]
    lower = (lanes_of((40, LANES)) < 64) == even_ring
    rows = unpack_face(jnp.where(lower, odd, even), rolled(jnp.where(lower, even, odd), 64, 1))
    return [assembled_lines(lines, face_scale_ref) for lines in rows]


def assembled_lines(lines, face_scale_ref):
    lane = lanes_of((8, LANES))
    sub = lax.broadcasted_iota(jnp.int32, (8, LANES), 0)
    ez, ey = lane % 8, (lane // 8) % 8
    up, down = (sub == 0) & (ey > 0), (sub == 4) & (ey < 7)
    first, last = lines[0], lines[4]
    lines = list(lines)
    lines[0] = first + jnp.where(ez > 0, rolled(last, 1, 1), 0.0)
    lines[4] = last + jnp.where(ez < 7, rolled(first, -1, 1), 0.0)
    for d in range(5):
        turned = rolled(lines[d], 4, 0)
        added = jnp.where(up, rolled(turned, 8, 1), jnp.where(down, rolled(turned, -8, 1), 0.0))
        lines[d] = face_scale_ref[8 * d : 8 * d + 8, :] * (lines[d] + added)
    return lines


def strains(grad, rows):
    def at(direction, c):
        return grad[direction * 128 + rows.start : direction * 128 + rows.stop, c * LANES : (c + 1) * LANES]

    return [
        at(0, 0),
        at(1, 1),
        at(2, 2),
        0.5 * (at(1, 0) + at(0, 1)),
        0.5 * (at(2, 0) + at(0, 2)),
        0.5 * (at(2, 1) + at(1, 2)),
    ]


CHUNKS = [slice(row, min(row + 8, 125)) for row in range(0, 125, 8)]


def pack_face(face, upper):
    lane = lanes_of((8, LANES))
    target = lane < 64 if upper else lane >= 64
    own = lax.broadcasted_iota(jnp.int32, (8, LANES), 0) < 5
    lines = []
    for d in range(5):
        first, second, third = [face[8 * d : 8 * d + 8, c * LANES : (c + 1) * LANES] for c in range(3)]
        moved = rolled(jnp.where(own, first, rolled(third, 5, 0)), 64, 1)
        lines.append(jnp.where(target, moved, jnp.where(own, second, rolled(third, 2, 0))))
    return jnp.concatenate(lines, axis=0)


def add_shares(shares, flat_ref):
    upper = lanes_of((5, LANES)) >= 64
    for c in range(3):
        for d in range(5):
            first, last = pl.ds(d, 5, stride=5), pl.ds(100 + d, 5, stride=5)
            flat_ref[c, first, :] = flat_ref[c, first, :] + jnp.where(upper, 0.0, shares[c][d][0:5])
            flat_ref[c, last, :] = flat_ref[c, last, :] + jnp.where(upper, shares[c][d][0:5], 0.0)


def shares_kernel(odd_ref, even_ref, face_scale_ref, flat_in, delta_ref, low_ref, flat_ref):
    shares = face_shares(odd_ref, even_ref, face_scale_ref)
    for c in range(3):
        delta_ref[c] = jnp.concatenate(shares[c], axis=0)
    flat_ref[:, 0:128, :] = flat_in[...]
    add_shares(shares, flat_ref)
    low_ref[...] = flat_ref[:, 0:128, :].astype(BF16)


def step_kernel(step, *refs):
    lame_ref, mu_ref, m_ref, decay_ref, share_table, face_table, base_ref = refs[0:7]
    arrived = refs[7 : 7 + (3, 4, 1)[step]]
    refs = refs[7 + len(arrived) :]
    older, refs = refs[:step], refs[step:]
    strain_ref, sigma_ref, even_ref = refs[0:3]
    if step < STEPS - 1:
        odd_ref, keep_ref, low_ref = refs[3:6]
    grad_ref, flat_ref, rim_ref, rows_ref = refs[-4:]
    upper = lanes_of((40, 3 * LANES)) % LANES >= 64
    if step == 0:
        flat_ref[:, 0:128, :] = arrived[0][...]
        rim_displacement(arrived[1], arrived[2], rows_ref)
        rim_ref[...] = jnp.zeros(rim_ref.shape, F32)
        for c in range(3):
            for d in range(5):
                rim_ref[8 * d : 8 * d + 5, c * LANES : (c + 1) * LANES] = rows_ref[pl.ds(8 * d + c, 5, stride=40), :]
        high, middle, low = [piece.astype(F32) for piece in cut(jnp.where(upper, rim_ref[...], 0.0))]
        stacked = [high, middle, high, middle, low, high]
        at_upper = lanes_of((25, LANES)) >= 64
        for c in range(3):
            flat_ref[c, 100:125, :] = jnp.where(at_upper, rows_ref[pl.ds(c, 25, stride=8), :], flat_ref[c, 100:125, :])
    else:
        if step == STEPS - 1:
            value = jnp.concatenate([arrived[0][c] for c in range(3)], axis=1)
        else:
            shares = face_shares(*arrived[1:4])
            value = jnp.concatenate([jnp.concatenate(lines, axis=0) for lines in shares], axis=1)
            for c in range(3):
                refs[6][c] = value[:, c * LANES : (c + 1) * LANES]
            flat_ref[:, 0:128, :] = arrived[0][...]
            add_shares(shares, flat_ref)
        high, middle, _ = [piece.astype(F32) for piece in cut(value)]
        stacked = []
        for at in (~upper, upper):
            stacked += [jnp.where(at, high, 0.0), jnp.where(at, middle, 0.0), jnp.where(at, high, 0.0)]
    grad_ref[...] = base_ref[...] + dot(share_table[...], jnp.concatenate(stacked, axis=0).astype(BF16))
    if step < STEPS - 1:
        low_ref[...] = flat_ref[:, 0:128, :].astype(BF16)
    for block in range(9):
        sigma_ref[(block // 3) * 128 + 120 : (block // 3) * 128 + 128, (block % 3) * LANES : (block % 3) * LANES + LANES] = (
            jnp.zeros((8, LANES), F32)
        )
    decays = [decay_ref[l : l + 1, :] for l in range(3)]
    shares = [(1.0 - decays[l]) * relax_strength[l] for l in range(3)]
    factors = []
    for _ in range(step + 1):
        factors.append(shares[0] + shares[1] + shares[2])
        shares = [decays[l] * shares[l] for l in range(3)]
    for rows in CHUNKS:
        strain = strains(grad_ref, rows)
        for part in range(6):
            strain_ref[part, rows, :] = strain[part]
        lame = lame_ref[rows, :]
        twice_mu = 2.0 * mu_ref[rows, :]
        trace = strain[0] + strain[1] + strain[2]
        third = trace * (1.0 / 3.0)
        pulls = [twice_mu * s for s in strain]
        pull_third = twice_mu * third
        fresh = [pulls[0] - pull_third, pulls[1] - pull_third, pulls[3], pulls[4], pulls[5]]
        relax = []
        for part in range(5):
            value = m_ref[part, rows, :] + factors[0] * fresh[part]
            for back in range(step):
                value = value + factors[back + 1] * older[step - 1 - back][part, rows, :]
            relax.append(value)
            if step < STEPS - 1:
                keep_ref[part, rows, :] = fresh[part]
        bulk = lame * trace
        xx = bulk + pulls[0] - relax[0]
        yy = bulk + pulls[1] - relax[1]
        zz = bulk + pulls[2] + relax[0] + relax[1]
        xy = pulls[3] - relax[2]
        xz = pulls[4] - relax[3]
        yz = pulls[5] - relax[4]
        for direction, values in enumerate(((xx, xy, xz), (xy, yy, yz), (xz, yz, zz))):
            for c in range(3):
                sigma_ref[direction * 128 + rows.start : direction * 128 + rows.stop, c * LANES : (c + 1) * LANES] = values[c]
    faces = dot_three(face_table, jnp.concatenate([sigma_ref[rows, :] for rows in FACE_ROWS], axis=0))
    first, last = pack_face(faces[0:40], False), pack_face(faces[40:80], True)
    if step < STEPS - 1:
        even_ring = lax.axis_index(("cuts", "sub")) % 2 == 0
        odd_ref[...] = jnp.where(even_ring, first, last)
        even_ref[...] = jnp.where(even_ring, last, first)
    else:
        even_ref[...] = last


def next_state(sigma_ref, force_table, u_ref, p_ref, scale_ref, next_ref):
    force = dot_three(force_table, sigma_ref[...])
    blocks = {}
    for c in range(3):
        for b in range(5):
            for d in range(5):
                blocks[(c, b, d)] = force[block_rows(b, d), c * LANES : (c + 1) * LANES]
    blocks = assembled(blocks)
    lane = lanes_of((8, LANES))
    sub = lax.broadcasted_iota(jnp.int32, (8, LANES), 0)
    inner = ((sub == 4) & (lane < 64)) | ((sub == 0) & (lane >= 64))
    for c in range(3):
        for b in range(5):
            for d in range(5):
                value = blocks[(c, b, d)]
                value = value + jnp.where(inner, rolled(rolled(value, 4, 0), 64, 1), 0.0)
                at = block_rows(b, d)
                next_ref[c, at, :] = 2.0 * u_ref[c, at, :] - p_ref[c, at, :] + scale_ref[at, :] * value
        next_ref[c, 200:208, :] = jnp.zeros((8, LANES), F32)


def first_rest_kernel(
    sigma_ref, force_table, u_in, p_in, scale_in, rim_ref, lanes_ref, mass_ref, grad_table,
    u_ref, scale_ref, next_ref, flat_ref, grad_ref, face_scale_ref, p_ref, rows_ref
):
    rim_rows(rim_ref, lanes_ref, rows_ref)
    u_ref[:, 0:ROWS, :] = u_in[:, 0:ROWS, :]
    p_ref[:, 0:ROWS, :] = p_in[:, 0:ROWS, :]
    scale_ref[0:ROWS, :] = scale_in[0:ROWS, :]
    upper = lanes_of((25, LANES)) >= 64
    last = pl.ds(4, 25, stride=8)
    for c in range(3):
        u_ref[c, last, :] = jnp.where(upper, rows_ref[pl.ds(c, 25, stride=8), :], u_ref[c, last, :])
        p_ref[c, last, :] = jnp.where(upper, rows_ref[pl.ds(3 + c, 25, stride=8), :], p_ref[c, last, :])
    rim = step_square / (rows_ref[pl.ds(6, 25, stride=8), :] * mass_ref[last, :])
    scale_ref[last, :] = jnp.where(upper, rim, scale_ref[last, :])
    face_scale_ref[...] = jnp.zeros(face_scale_ref.shape, F32)
    lower = lanes_of((5, LANES)) < 64
    for d in range(5):
        first, last = pl.ds(8 * d, 5, stride=40), pl.ds(8 * d + 4, 5, stride=40)
        face_scale_ref[8 * d : 8 * d + 5, :] = jnp.where(lower, scale_ref[first, :], scale_ref[last, :])
    next_state(sigma_ref, force_table, u_ref, p_ref, scale_ref, next_ref)
    flatten(next_ref, flat_ref)
    grad_ref[...] = gradients(grad_table, beside(flat_ref))


def rest_kernel(sigma_ref, force_table, partial_ref, delta_ref, p_ref, scale_ref, grad_table, next_ref, u_ref, *refs):
    u_ref[:, 0:ROWS, :] = partial_ref[:, 0:ROWS, :]
    upper = lanes_of((5, LANES)) >= 64
    for c in range(3):
        for d in range(5):
            share = delta_ref[c, 8 * d : 8 * d + 5, :]
            first, last = pl.ds(8 * d, 5, stride=40), pl.ds(8 * d + 4, 5, stride=40)
            u_ref[c, first, :] = u_ref[c, first, :] + jnp.where(upper, 0.0, share)
            u_ref[c, last, :] = u_ref[c, last, :] + jnp.where(upper, share, 0.0)
    next_state(sigma_ref, force_table, u_ref, p_ref, scale_ref, next_ref)
    if refs:
        flat_ref, grad_ref = refs
        flatten(next_ref, flat_ref)
        grad_ref[...] = gradients(grad_table, beside(flat_ref))


def kernel_parts(strain_ref, low_ref, far_ref, lame_ref, mu_ref, grad_table, grad_ref, kernel_ref):
    forward = jnp.where(lax.axis_index("group") == 0, beside(low_ref), beside(far_ref))
    grad_ref[...] = low_gradients(grad_table, forward)
    for rows in CHUNKS:
        far = strains(grad_ref, rows)
        own = [strain_ref[part, rows, :] for part in range(6)]
        trace_own = own[0] + own[1] + own[2]
        trace_far = far[0] + far[1] + far[2]
        third_own, third_far = trace_own * (1.0 / 3.0), trace_far * (1.0 / 3.0)
        twice_mu = 2.0 * mu_ref[rows, :]
        kappa = lame_ref[rows, :] + twice_mu * (1.0 / 3.0)
        kernel_ref[rows, :] = time_step * kappa * trace_far * trace_own
        product = (
            (own[0] - third_own) * (far[0] - third_far)
            + (own[1] - third_own) * (far[1] - third_far)
            + (own[2] - third_own) * (far[2] - third_far)
            + 2.0 * (own[3] * far[3] + own[4] * far[4] + own[5] * far[5])
        )
        kernel_ref[125 + rows.start : 125 + rows.stop, :] = time_step * twice_mu * product
    kernel_ref[250:256, :] = jnp.zeros((6, LANES), F32)
    return kernel_ref[...].astype(BF16)


def placed(pieces, select, rows):
    slots = rows // 2
    group = lanes_of((rows, LANES)) // slots
    total = 0.0
    for piece in pieces:
        total = total + lax.dot_general(piece, select, (((1,), (1,)), ((), ())), preferred_element_type=F32)
    blocks = []
    for k in range(select.shape[0] // LANES):
        value = total[0:rows, k * LANES : (k + 1) * LANES]
        for j in range(1, 256 // rows):
            value = jnp.where(group == j, total[j * rows : (j + 1) * rows, k * LANES : (k + 1) * LANES], value)
        blocks.append(value)
    return blocks


def group_scale(mantissa, exponent):
    return mantissa * jnp.exp2(exponent) * (1.0 / (4096.0 * 32767.0))


def parts_kernel(strain_ref, low_ref, far_ref, lame_ref, mu_ref, grad_table, part_ref, grad_ref, kernel_ref):
    part_ref[...] = kernel_parts(strain_ref, low_ref, far_ref, lame_ref, mu_ref, grad_table, grad_ref, kernel_ref)


def both_parts_kernel(strain_ref, low_ref, far_ref, lame_ref, mu_ref, grad_table, one_ref, both_ref, grad_ref, kernel_ref):
    two = kernel_parts(strain_ref, low_ref, far_ref, lame_ref, mu_ref, grad_table, grad_ref, kernel_ref)
    both_ref[...] = one_ref[...].astype(F32) + two.astype(F32)


def send_kernel(strain_ref, low_ref, far_ref, lame_ref, mu_ref, grad_table, both_ref, select_ref, total_ref, *refs):
    out_refs, (grad_ref, kernel_ref) = refs[:-2], refs[-2:]
    three = kernel_parts(strain_ref, low_ref, far_ref, lame_ref, mu_ref, grad_table, grad_ref, kernel_ref)
    kernel_ref[...] = both_ref[...] + three.astype(F32)
    total_ref[...] = kernel_ref[...]
    for k in range(2):
        rows = slice(125 * k, 125 * k + 125)
        value = kernel_ref[rows, :]
        largest = jnp.maximum(jnp.max(jnp.abs(value), axis=0, keepdims=True), 1e-33)
        exponent = jnp.floor(jnp.log2(largest))
        mantissa = jnp.floor(largest * jnp.exp2(-exponent) * 4096.0) + 2.0
        kernel_ref[rows, :] = jnp.floor(value * (1.0 / group_scale(mantissa, exponent)) + 0.5)
        kernel_ref[250 + 2 * k : 251 + 2 * k, :] = mantissa
        kernel_ref[251 + 2 * k : 252 + 2 * k, :] = exponent
    high, middle, _ = cut(kernel_ref[...])
    for ref, value in zip(out_refs, placed((high, middle), select_ref[LANES:, :], out_refs[0].shape[0])):
        ref[...] = value.astype(jnp.int32).astype(jnp.int16)


def own_kernel(total_ref, select_ref, own_ref):
    row = lax.broadcasted_iota(jnp.int32, (256, LANES), 0)
    unit = jnp.where((row == 250) | (row == 252), 4096.0 * 32767.0, 0.0)
    value = jnp.where(row < 250, total_ref[...], unit)
    own_ref[...] = placed(cut(value), select_ref[0:LANES, :], own_ref.shape[0])[0]


def sum_kernel(order, *refs):
    in_refs, (out_ref, rows_ref, sems) = refs[:-3], refs[-3:]
    rows = in_refs[0].shape[0]
    slots = rows // 2
    pieces = 256 // rows
    group = lanes_of((rows, LANES)) // slots
    sources = [lax.axis_index("sub") ^ k for k in order]
    values = [ref[...].astype(jnp.int32).astype(F32) if k > 0 else ref[...] for k, ref in zip(order, in_refs)]
    scales = None
    copies = []
    for j in range(pieces - 1, -1, -1):
        halves = [jnp.zeros((rows, LANES), F32)] * 2
        for source, value in zip(sources, values):
            spot = source % pieces
            moved = pltpu.roll(value, ((spot + pieces - j) % pieces) * slots, 1)
            for t in range(2):
                halves[t] = jnp.where((group == spot) & (source // pieces == t), moved, halves[t])
        value = jnp.concatenate(halves, axis=1)
        if scales is None:
            at = 250 - j * rows
            scales = [group_scale(value[row : row + 1], value[row + 1 : row + 2]) for row in (at, at + 2)]
        row = lax.broadcasted_iota(jnp.int32, (rows, 256), 0) + j * rows
        value = value * jnp.where(row < 125, scales[0], scales[1])
        for start in range(0, rows, 64):
            first, last = j * rows + start, min(j * rows + start + 64, 250)
            rows_ref[first:last, 0, :] = value[start : start + last - first]
            at = pl.ds(first, last - first)
            copy = pltpu.make_async_copy(rows_ref.at[at], out_ref.at[at], sems.at[len(copies)])
            copy.start()
            copies.append(copy)
    for copy in copies:
        copy.wait()


def to_nodal(columns, spread_ref, nodal_ref):
    rows = columns.shape[0]
    own = (lanes_of((rows, WIDE)) // 8) % 8
    expanded = jnp.concatenate([jnp.where(own == ey, columns, 0.0) for ey in range(EY)], axis=0)
    over_lanes = (((1,), (1,)), ((), ()))
    pieces = jnp.concatenate(cut(expanded), axis=0)
    windows = lax.dot_general(pieces, spread_ref[...], over_lanes, preferred_element_type=F32)
    half = EY * rows
    windows = windows[0:half] + windows[half : 2 * half] + windows[2 * half : 3 * half]
    nodal_ref[...] = jnp.zeros(nodal_ref.shape, F32)
    for ey in range(EY):
        at = slice(JUMP * ey, JUMP * ey + 5 * SIDE)
        nodal_ref[:, at] = nodal_ref[:, at] + windows[ey * rows : (ey + 1) * rows, 0 : 5 * SIDE]


def nodal_kernel(partial_ref, spread_ref, nodal_ref):
    lane = lanes_of((8, LANES))
    sub = lax.broadcasted_iota(jnp.int32, (8, LANES), 0)
    tiles = []
    for c in range(3):
        row = []
        for pair in range(BLOCKS // 2):
            even = partial_ref[c, 16 * pair : 16 * pair + 8, :]
            odd = partial_ref[c, 16 * pair + 8 : 16 * pair + 16, :]
            low = jnp.where(sub < 4, even, rolled(rolled(even, 64, 1), 4, 0))
            high = jnp.where(sub < 4, rolled(odd, 64, 1), rolled(odd, 4, 0))
            row.append(jnp.where(lane < 64, low, high))
        tiles.append(jnp.concatenate(row, axis=1))
    columns = jnp.concatenate(tiles, axis=0)
    column = lanes_of((24, WIDE))
    block = column // 64
    once = ((block % 5 < 4) | (column % 8 == 7)) & ((block // 5 < 4) | ((column // 8) % 8 == 7))
    to_nodal(jnp.where(once, columns, 0.0), spread_ref, nodal_ref)


def finish_kernel(before_ref, nodal_ref, face_scale_ref, lanes_ref, out_ref, rows_ref, face_ref):
    packed = before_ref[...]
    values = unpack_face(packed, rolled(packed, 64, 1))
    rows_ref[...] = jnp.zeros(rows_ref.shape, F32)
    for c in range(3):
        lines = assembled_lines(values[c], face_scale_ref)
        for d in range(5):
            rows_ref[pl.ds(8 * d + c, 5, stride=40), :] = lines[d][0:5]
    lane = lanes_of((8, LANES))
    tiles = []
    for pair in range(BLOCKS // 2):
        even, odd = rows_ref[16 * pair : 16 * pair + 8, :], rows_ref[16 * pair + 8 : 16 * pair + 16, :]
        tiles.append(jnp.where(lane < 64, even, rolled(odd, 64, 1)))
    for at, tile in enumerate(gathered(tiles, NODE_LANES, lanes_ref)):
        face_ref[:, LANES * at : LANES * at + LANES] = tile
    first = lax.broadcasted_iota(jnp.int32, (8, FACE), 0) == 0
    for c in range(3):
        out_ref[0, c] = nodal_ref[8 * c : 8 * c + 8, :] + jnp.where(first, face_ref[c : c + 1, 0:FACE], 0.0)


VMEM = pl.BlockSpec(memory_space=pltpu.VMEM)
HBM = pl.BlockSpec(memory_space=pltpu.HBM)


def shaped(*shape, dtype=F32):
    return jax.ShapeDtypeStruct(shape, dtype)


def call(kernel, name, outs, scratch, *args, outside=(), written_outside=False, flops=0, room=32 * 1024):
    return pl.pallas_call(
        kernel,
        name=name,
        out_shape=outs,
        in_specs=[HBM if at in outside else VMEM for at in range(len(args))],
        out_specs=jax.tree.map(lambda _: HBM if written_outside else VMEM, outs),
        scratch_shapes=scratch,
        compiler_params=pltpu.CompilerParams(vmem_limit_bytes=room * 1024),
        cost_estimate=pl.CostEstimate(flops=flops, bytes_accessed=3000000, transcendentals=0),
    )(*args)


def passed_along(value, axis, steps):
    count = lax.axis_size(axis)
    return lax.ppermute(value, axis, [(source, (source + steps) % count) for source in range(count)])


def swapped(value, axis, first):
    count = lax.axis_size(axis)
    pairs = []
    for source in range(first, count, 2):
        other = (source + 1) % count
        pairs += [(source, other), (other, source)]
    return lax.ppermute(value, axis, pairs)


def far_field(low, groups):
    far = None
    for k in range(1, groups):
        moved = passed_along(low, "group", k)
        far = moved if far is None else jnp.where(lax.axis_index("group") == k, moved, far)
    return far


def per_device(disp_now, disp_prev, memory_init, density, lame_lambda, shear_mu, sls_decay, owner_map):
    ring = ("cuts", "sub")
    subs = lax.axis_size("sub")
    groups = lax.axis_size("group")

    rim = call(
        gather_kernel, "gather", shaped(8, WIDE_FACE),
        [pltpu.VMEM((3, 8, FACE), F32)] * 2 + [pltpu.VMEM((8, FACE), F32), pltpu.SemaphoreType.DMA((3,))],
        disp_now, disp_prev, density, outside=(0, 1, 2), room=54 * 1024 - 120,
    )
    rim = passed_along(rim, ring, -1)

    grad_table = jnp.asarray(side_by_side(GRAD))
    force_table = jnp.asarray(cut_table(FORCE))
    face_table = jnp.asarray(cut_table(FACES))
    share_table = jnp.asarray(SHARE)
    rim_table = jnp.asarray(RIM)
    column_lanes = jnp.asarray(COLUMN_LANES)
    node_lanes = jnp.asarray(NODE_LANES)
    mass = jnp.asarray(MASS)
    memory = memory_init[0]
    owner = jnp.transpose(owner_map, (0, 2, 1))

    state = shaped(3, TALL, LANES)
    scale_shape = shaped(TALL, LANES)
    five = shaped(5, 125, LANES)
    part_shape = shaped(256, LANES, dtype=BF16)
    grad_scratch = pltpu.VMEM((384, 384), F32)
    part_scratch = [grad_scratch, pltpu.VMEM((256, LANES), F32)]
    face = shaped(40, LANES)
    grad_shape = shaped(384, 384)
    flat_shape = shaped(3, 128, LANES)
    u, p, scale, m1, spread, flat, base = call(
        prologue_kernel, "prologue", [state, state, scale_shape, five, shaped(WINDOW, WIDE, dtype=BF16), flat_shape, grad_shape],
        [pltpu.VMEM((8, 56, WINDOW), F32)],
        disp_now, disp_prev, density, memory, sls_decay, mass, grad_table, face_table, force_table, rim_table, share_table, lame_lambda, shear_mu,
    )
    rows = 512 // subs
    memories = [m1]
    kept = []
    for step in range(STEPS):
        last_step = step == STEPS - 1
        low_shape = shaped(3, 128, LANES, dtype=BF16)
        if last_step:
            extra, low = call(
                shares_kernel, "shares", [shaped(3, 40, LANES), low_shape], [pltpu.VMEM((3, FLAT, LANES), F32)],
                odd, even, face_scale, flat,
            )
            far = far_field(low, groups)
            arrived = (extra,)
        else:
            arrived = (flat, rim, column_lanes) if step == 0 else (flat, odd, even, face_scale)
        outs = [shaped(6, 125, LANES), grad_shape, face]
        if not last_step:
            outs += [face, five, low_shape]
        if step == 1:
            outs.append(shaped(3, 40, LANES))
        results = call(
            lambda *refs, step=step: step_kernel(step, *refs), "step", outs,
            [grad_scratch, pltpu.VMEM((3, FLAT, LANES), F32), pltpu.VMEM((40, 384), F32), pltpu.VMEM((TALL, LANES), F32)],
            lame_lambda, shear_mu, memories[step], sls_decay, rim_table if step == 0 else share_table, face_table, base, *arrived, *kept,
        )
        strain, sigma, even = results[0:3]
        if last_step:
            before = passed_along(even, ring, 1)
        else:
            odd, keep, low = results[3:6]
            extra = results[6] if step == 1 else None
            kept.append(keep)
            odd = swapped(odd, ring, 1)
            even = swapped(even, ring, 0)
            far = far_field(low, groups)
        if step == 0:
            p, scale, partial, flat, base, face_scale = call(
                first_rest_kernel, "rest", [state, scale_shape, state, flat_shape, grad_shape, shaped(40, LANES)],
                [pltpu.VMEM((3, TALL, LANES), F32), pltpu.VMEM((TALL, LANES), F32)],
                sigma, force_table, u, p, scale, rim, column_lanes, mass, grad_table,
            )
        else:
            results = call(
                rest_kernel, "rest", [state] if last_step else [state, state, flat_shape, grad_shape],
                [pltpu.VMEM((3, TALL, LANES), F32)] if last_step else [], sigma, force_table, partial, extra, p, scale, grad_table,
            )
            if last_step:
                partial = results[0]
            else:
                partial, p, flat, base = results
        shared = (strain, low, far, lame_lambda, shear_mu, grad_table)
        if step == 0:
            one = call(parts_kernel, "parts", part_shape, part_scratch, *shared)
            m2, m3, select = call(
                later_kernel, "later", [five, five, shaped(subs * LANES, LANES, dtype=BF16)], [], memory, sls_decay, owner
            )
            memories += [m2, m3]
            base, one, select, memories[2] = lax.optimization_barrier((base, one, select, m3))
        elif not last_step:
            both = call(
                both_parts_kernel, "parts", shaped(256, LANES), part_scratch, *shared, one
            )
            base, flat, both = lax.optimization_barrier((base, flat, both))
        else:
            total, *blocks = call(
                send_kernel, "send", [shaped(256, LANES)] + [shaped(rows, LANES, dtype=jnp.int16)] * (subs - 1),
                part_scratch, *shared, both, select,
            )
            order = [*range(subs - 1, 0, -1), 0]
            sent = [lax.ppermute(blocks[k - 1], "sub", [(j, j ^ k) for j in range(subs)]) for k in order[:-1]]
            sent.append(call(own_kernel, "own", shaped(rows, LANES), [], total, select))
    nodal = call(nodal_kernel, "nodal", shaped(24, FACE), [], partial, spread)
    final = call(
        finish_kernel, "finish", shaped(1, 3, 8, FACE), [pltpu.VMEM((TALL, LANES), F32), pltpu.VMEM((8, WIDE_FACE), F32)],
        before, nodal, face_scale, node_lanes, flops=250000000,
    )
    kernels = call(
        lambda *refs: sum_kernel(order, *refs), "sum", shaped(250, 1, 256),
        [pltpu.VMEM((250, 1, 256), F32), pltpu.SemaphoreType.DMA((4,))], *sent, written_outside=True,
    )
    return final, jnp.transpose(kernels, (1, 2, 0))


def solution(mesh):
    in_specs = (
        P("group", None, ("cuts", "sub"), None),
        P("group", None, ("cuts", "sub"), None),
        P("group", None, None, None, ("cuts", "sub")),
        P(("cuts", "sub"), None),
        P(None, ("cuts", "sub")),
        P(None, ("cuts", "sub")),
        P(None, ("cuts", "sub")),
        P(("cuts", "sub"), None, None),
    )
    out_specs = (P("group", None, ("cuts", "sub"), None), P("group", ("cuts", "sub"), None))
    return jax.shard_map(
        per_device, mesh=mesh, in_specs=in_specs, out_specs=out_specs, check_vma=False
    )
```
